32 devices in a mesh: ctx: 8 (over z, x), fsdp: 4 (over y, core).
Axes of the slice: x: 2, y: 2, z: 4, core: 2. Of those that a mesh axis runs over, the one named last changes fastest.
Arguments:
- tokens: bfloat16 [4, 1024, 768], P('fsdp', 'ctx'), may hold values from -6 to 6
- doc_lengths: int32 [4, 4], P('fsdp'), may hold values from 1 to 960, as said below
- routes: int32 [4, 1024, 2], P('fsdp', 'ctx'), may hold values from 0 to 3, all different within a row
- cotangent: bfloat16 [4, 1024, 768], P('fsdp', 'ctx'), may hold values from -6 to 6
- attn_gain: bfloat16 [768], P(('ctx', 'fsdp')), may hold values from 0.25 to 1.75
- w_qkv: bfloat16 [768, 2304], P(('ctx', 'fsdp')), may hold values from -0.21875 to 0.21875
- w_out: bfloat16 [768, 768], P(('ctx', 'fsdp')), may hold values from -2.5 to 2.5
- mlp_gain: bfloat16 [768], P(('ctx', 'fsdp')), may hold values from 0.25 to 1.75
- router: bfloat16 [768, 4], P(('ctx', 'fsdp')), may hold values from -0.15625 to 0.15625
- expert_in: bfloat16 [2048, 4, 2, 768], P(('ctx', 'fsdp')), may hold values from -0.21875 to 0.21875
- expert_out: bfloat16 [2048, 4, 768], P(('ctx', 'fsdp')), may hold values from -0.375 to 0.375
- shared_in: bfloat16 [2048, 2, 768], P(('ctx', 'fsdp')), may hold values from -0.21875 to 0.21875
- shared_out: bfloat16 [2048, 768], P(('ctx', 'fsdp')), may hold values from -0.25 to 0.25
Outputs:
- layer_out: bfloat16 [4, 1024, 768], P('fsdp', 'ctx')
- grad_tokens: float32 [4, 1024, 768], P('fsdp', 'ctx')
- grad_attn_gain: float32 [768], P(('ctx', 'fsdp'))
- grad_w_qkv: float32 [768, 2304], P(('ctx', 'fsdp'))
- grad_w_out: float32 [768, 768], P(('ctx', 'fsdp'))
- grad_mlp_gain: float32 [768], P(('ctx', 'fsdp'))
- grad_router: float32 [768, 4], P(('ctx', 'fsdp'))
- grad_expert_in: float32 [2048, 4, 2, 768], P(('ctx', 'fsdp'))
- grad_expert_out: float32 [2048, 4, 768], P(('ctx', 'fsdp'))
- grad_shared_in: float32 [2048, 2, 768], P(('ctx', 'fsdp'))
- grad_shared_out: float32 [2048, 768], P(('ctx', 'fsdp'))
The draws below stay inside these ranges and needn't reach their ends.
Inputs may be any that keep to these rules, and one draw needn't show every extreme that they name: `doc_lengths`: in each slot the lengths sum to less than 1024; rows past the sum are padding. Each slot holds one document of exactly 960 rows and at least one of a single row. `routes`: each token names 2 different experts, in order of priority.
All inputs are finite; a program needn't handle non-finite values.
Results may differ from the reference program's by a relative error of at most 0.035.
Values may be sent and summed in bfloat16 or wider, within the bound.
A program may use at most 448 MiB of HBM per device.

```python
import math
import jax
import jax.numpy as jnp
from jax import lax

D = 768
HEADS = 12
HEAD_DIM = 64
FF = 2048
EXPERTS = 4
TOP = 2
NDOC = 4
TOK_DEV = 128
SLOT = 1024
SLOTS = 4
CAP = 80
N_CTX = 8


def draw_doc_lengths(key, part):
    key = jax.random.fold_in(key, 11)
    eighth = max(TOK_DEV // 8, 1)
    short_key, pick_key = jax.random.split(key, 2)
    shorts = jax.random.randint(short_key, (SLOTS, NDOC), 1, eighth + 1)
    chosen = jax.random.randint(pick_key, (SLOTS, 1), 0, NDOC)
    column = jnp.arange(NDOC, dtype=jnp.int32)[None, :]
    is_long = column == chosen
    lowest = jnp.min(jnp.where(is_long, eighth + 1, shorts), axis=1, keepdims=True)
    shorts = shorts - lowest + 1
    longest = SLOT - TOK_DEV // 2
    return jnp.where(is_long, longest, shorts).astype(jnp.int32)


def block_scale(stream_key, dims, cuts, low, top_value):
    loudness = 1.0
    for dim, blocks in cuts:
        heights = jax.random.uniform(jax.random.fold_in(jax.random.fold_in(stream_key, 6), dim), (blocks,), jnp.float32, low / len(cuts), top_value / len(cuts))
        loudness = loudness * jnp.repeat(jnp.exp(heights), dims[dim] // blocks).reshape((-1,) + (1,) * (len(dims) - 1 - dim))
    return loudness


def different_ones(rng, rows, amount, top, lift):
    ranking = jax.random.permutation(jax.random.fold_in(rng, 1), amount)
    boost = ranking
    for power in range(3):
        boost = boost * boost // amount
    boost = boost * lift // amount
    tickets = jax.random.randint(jax.random.fold_in(rng, 2), (rows, amount), 0, 4096) + boost
    fixed_rows = jax.random.permutation(jax.random.fold_in(rng, 3), rows)[jnp.arange(amount) % rows]
    tickets = jnp.where(jnp.arange(rows)[:, None] == fixed_rows[None, :], 1 << 14, tickets)
    score = tickets * amount + jnp.arange(amount)
    return lax.top_k(score.astype(jnp.int32), top)[1].astype(jnp.int32)


def scatter_about(own_key, shape, spread, reach, shards=(), kind=jnp.bfloat16):
    level = block_scale(own_key, shape, shards, -0.22, 0.18) if shards else 1.0
    values = jax.random.normal(own_key, shape, jnp.float32) * spread * level
    return jnp.minimum(jnp.maximum(values, -reach), reach).astype(kind)


def setup_inputs(seed: int = 0) -> dict:
    keys = jax.random.split(jax.random.key(seed), 14)
    tokens = scatter_about(keys[0], (SLOTS, SLOT, D), 1.0, 6.0, ((0, 4), (1, 8)))
    doc_lengths = draw_doc_lengths(jax.random.fold_in(keys[13], 71), 0)
    routes = different_ones(keys[2], SLOTS * SLOT, EXPERTS, TOP, 4096).reshape((SLOTS, SLOT, TOP))
    cotangent = scatter_about(keys[3], (SLOTS, SLOT, D), 1.0, 6.0, ((0, 4), (1, 8)))
    attn_gain = jnp.clip(1.0 + 0.15 * jax.random.normal(keys[4], (D,), jnp.float32), 0.25, 1.75).astype(jnp.bfloat16)
    w_qkv = scatter_about(keys[5], (D, 3 * D), D ** -0.5, 0.21875, ((0, 32),))
    w_out = scatter_about(keys[6], (D, D), (max(D // 128, 1)) ** -0.5, 2.5, ((0, 32),))
    mlp_gain = jnp.clip(1.0 + 0.15 * jax.random.normal(keys[7], (D,), jnp.float32), 0.25, 1.75).astype(jnp.bfloat16)
    router = scatter_about(keys[8], (D, EXPERTS), (2 * D) ** -0.5, 0.15625, ((0, 32),))
    expert_in = scatter_about(keys[9], (FF, EXPERTS, 2, D), D ** -0.5, 0.21875, ((0, 32),))
    expert_out = scatter_about(keys[10], (FF, EXPERTS, D), (FF // 8) ** -0.5, 0.375, ((0, 32),))
    shared_in = scatter_about(keys[11], (FF, 2, D), D ** -0.5, 0.21875, ((0, 32),))
    shared_out = scatter_about(keys[12], (FF, D), (FF // 4) ** -0.5, 0.25, ((0, 32),))
    return dict(tokens=tokens, doc_lengths=doc_lengths, routes=routes, cotangent=cotangent, attn_gain=attn_gain, w_qkv=w_qkv, w_out=w_out, mlp_gain=mlp_gain, router=router, expert_in=expert_in, expert_out=expert_out, shared_in=shared_in, shared_out=shared_out)


@jax.custom_vjp
def low(v):
    return lax.optimization_barrier(v.astype(jnp.bfloat16)).astype(jnp.float32)

@jax.custom_vjp
def low_back(v):
    return v

def low_keep(v):
    return (low(v), None)

def low_pass(kept, grad):
    return (grad,)

def back_keep(v):
    return (v, None)

def back_low(kept, grad):
    return (low(grad),)
low.defvjp(low_keep, low_pass)
low_back.defvjp(back_keep, back_low)
EPSILON = 1e-05
ROPE_BASE = 10000.0
MASKED = -1e+30
PRECISE = lax.Precision.HIGHEST

def doc_ids(row_index, doc_ends):
    return lax.optimization_barrier(jnp.sum((row_index[:, None] >= doc_ends[None, :]).astype(jnp.int32), axis=1))

def positions(row_index, lengths):
    doc_ends = jnp.cumsum(lengths).astype(jnp.int32)
    doc_starts = doc_ends - lengths
    doc_num = doc_ids(row_index, doc_ends)
    column = jnp.arange(lengths.shape[0], dtype=jnp.int32)
    begins = lax.optimization_barrier(jnp.sum(jnp.where(doc_num[:, None] == column[None, :], doc_starts[None, :], 0), axis=1))
    return (doc_num, (row_index - begins).astype(jnp.int32), doc_ends)

def rope_tables(position, head_dim):
    half_dim = head_dim // 2
    inverse = ROPE_BASE ** (-2.0 * jnp.arange(half_dim, dtype=jnp.float32) / head_dim)
    angles = position.astype(jnp.float32)[:, None] * inverse[None, :]
    return (jnp.cos(angles), jnp.sin(angles))

def rotate(values, cosine, sine_tab):
    half_dim = values.shape[-1] // 2
    lower_half = values[..., :half_dim]
    upper_half = values[..., half_dim:]
    cos_b = cosine[:, None, :]
    sin_b = sine_tab[:, None, :]
    return jnp.concatenate([lower_half * cos_b - upper_half * sin_b, upper_half * cos_b + lower_half * sin_b], axis=-1)

def placement(route_rows, live_rows, expert_count, capacity):
    tok_count = route_rows.shape[0]
    top_k = route_rows.shape[1]
    expert_of = route_rows.T.reshape(-1)
    token_of = jnp.tile(jnp.arange(tok_count, dtype=jnp.int32), top_k)
    pair_live = jnp.tile(live_rows, top_k)
    expert_raw = expert_of[:, None] == jnp.arange(expert_count, dtype=jnp.int32)[None, :]
    expert_hot = (expert_raw & pair_live[:, None]).astype(jnp.int32)
    earlier = jnp.cumsum(expert_hot, axis=0) - expert_hot
    slot_of = lax.optimization_barrier(jnp.sum(earlier * expert_hot, axis=1))
    kept_pair = pair_live & (slot_of < capacity)
    flat_slot = expert_of * capacity + slot_of
    slot_ids = jnp.arange(expert_count * capacity, dtype=jnp.int32)
    pair_place = ((flat_slot[:, None] == slot_ids[None, :]) & kept_pair[:, None]).astype(jnp.float32)
    token_hot = (token_of[:, None] == jnp.arange(tok_count, dtype=jnp.int32)[None, :]).astype(jnp.float32)
    return (pair_place, token_hot, expert_raw.astype(jnp.float32))

def norm_rows(values, gain):
    return values * lax.rsqrt(lax.optimization_barrier(jnp.mean(values * values, axis=-1, keepdims=True)) + EPSILON) * gain

def swiglu(gate_vals, up_vals):
    return gate_vals * jax.nn.sigmoid(gate_vals) * up_vals

def slot_forward(inputs, lengths, route_rows, weights):
    attn_gain, w_qkv, w_out, mlp_gain, router, expert_in, expert_out, shared_in, shared_out = weights
    row_index = jnp.arange(SLOT, dtype=jnp.int32)
    doc_num, position, doc_ends = positions(row_index, lengths)
    live_rows = doc_num < NDOC
    live_mask = live_rows.astype(jnp.float32)[:, None]
    normed = low(norm_rows(inputs, attn_gain))
    proj_qkv = low_back(jnp.dot(normed, w_qkv, precision=PRECISE))
    cosine, sine_tab = rope_tables(position, HEAD_DIM)
    head_shape = (SLOT, HEADS, HEAD_DIM)
    query = low(rotate(proj_qkv[:, :D].reshape(head_shape), cosine, sine_tab))
    keys_all = low(rotate(proj_qkv[:, D:2 * D].reshape(head_shape), cosine, sine_tab))
    values_all = low(proj_qkv[:, 2 * D:].reshape(head_shape))
    width = math.gcd(SLOT, 512)
    blocks = SLOT // width
    score_scale = 1.0 / math.sqrt(HEAD_DIM)

    def attend_block(block_args):
        query_blk, doc_blk, index_blk = block_args
        scores = low_back(jnp.einsum('qhd,khd->hqk', query_blk, keys_all, precision=PRECISE) * score_scale)
        allowed = (doc_num[None, :] == doc_blk[:, None]) & (row_index[None, :] <= index_blk[:, None])
        scores = jnp.where(allowed[None], scores, MASKED)
        row_max = lax.optimization_barrier(jnp.max(scores, axis=-1, keepdims=True))
        expo_vals = jnp.exp(scores - row_max)
        probs = low(expo_vals / lax.optimization_barrier(jnp.sum(expo_vals, axis=-1, keepdims=True)))
        return jnp.einsum('hqk,khd->qhd', probs, values_all, precision=PRECISE)
    attn = lax.map(jax.checkpoint(attend_block), (query.reshape(blocks, width, HEADS, HEAD_DIM), doc_num.reshape(blocks, width), row_index.reshape(blocks, width)))
    attn = low_back(low(attn.reshape(SLOT, D)))
    resid = inputs + low_back(jnp.dot(attn, w_out, precision=PRECISE))
    mixed = low(norm_rows(resid, mlp_gain))

    def group_block(block_args):
        mixed_g, routes_g, live_g = block_args
        logits = low_back(jnp.dot(mixed_g, router, precision=PRECISE))
        shifted = jnp.exp(logits - lax.optimization_barrier(jnp.max(logits, axis=-1, keepdims=True)))
        router_probs = shifted / lax.optimization_barrier(jnp.sum(shifted, axis=-1, keepdims=True))
        pair_place, token_hot, expert_raw = placement(routes_g, live_g, EXPERTS, CAP)
        gate_pair = lax.optimization_barrier(jnp.sum(jnp.dot(token_hot, router_probs, precision=PRECISE) * expert_raw, axis=1))
        dispatch = jnp.dot(pair_place.T, token_hot, precision=PRECISE)
        combine = jnp.dot(pair_place.T, token_hot * gate_pair[:, None], precision=PRECISE)
        slot_in = jnp.dot(dispatch, mixed_g, precision=PRECISE).reshape(EXPERTS, CAP, D)
        gate_e = low_back(jnp.einsum('ecd,fed->ecf', slot_in, expert_in[:, :, 0, :], precision=PRECISE))
        up_e = low_back(jnp.einsum('ecd,fed->ecf', slot_in, expert_in[:, :, 1, :], precision=PRECISE))
        hidden_e = low(swiglu(gate_e, up_e))
        expert_y = low_back(jnp.einsum('ecf,fed->ecd', hidden_e, expert_out, precision=PRECISE))
        routed = jnp.dot(combine.T, expert_y.reshape(EXPERTS * CAP, D), precision=PRECISE)
        gate_s = low_back(jnp.einsum('td,fd->tf', mixed_g, shared_in[:, 0, :], precision=PRECISE))
        up_s = low_back(jnp.einsum('td,fd->tf', mixed_g, shared_in[:, 1, :], precision=PRECISE))
        hidden_s = low(swiglu(gate_s, up_s))
        shared_y = low_back(jnp.dot(hidden_s, shared_out, precision=PRECISE))
        return routed + shared_y
    group_args = (mixed.reshape(N_CTX, TOK_DEV, D), route_rows.reshape(N_CTX, TOK_DEV, TOP), live_rows.reshape(N_CTX, TOK_DEV))
    branch = lax.map(jax.checkpoint(group_block), group_args).reshape(SLOT, D)
    return live_mask * (resid + branch)

def reference(tokens, doc_lengths, routes, cotangent, attn_gain, w_qkv, w_out, mlp_gain, router, expert_in, expert_out, shared_in, shared_out):
    floats = tuple((array.astype(jnp.float32) for array in (tokens, attn_gain, w_qkv, w_out, mlp_gain, router, expert_in, expert_out, shared_in, shared_out)))

    def forward(inputs, *weights):
        outputs = [slot_forward(inputs[number], doc_lengths[number], routes[number], weights) for number in range(SLOTS)]
        return jnp.stack(outputs)
    layer_out, pullback = jax.vjp(forward, *floats)
    grads = pullback(cotangent.astype(jnp.float32))
    return (layer_out.astype(jnp.bfloat16), grads[0], grads[1], grads[2], grads[3], grads[4], grads[5], grads[6], grads[7], grads[8], grads[9])
```

```python
import functools
import math

import jax
import jax.numpy as jnp
from jax import lax
from jax.experimental import pallas as pl
from jax.experimental.pallas import tpu as pltpu
from jax.sharding import PartitionSpec as P

HEAD_DIM = 64
EPSILON = 1e-05
ROPE_BASE = 10000.0
MASKED = -1e30
GROUPS = 4
MESH = pl.DeviceIdType.MESH
DMA = pltpu.SemaphoreType.DMA
BF = jnp.bfloat16
F32 = jnp.float32


class Place:
    def __init__(self, columns):
        ctx, fsdp = lax.axis_index("ctx"), lax.axis_index("fsdp")
        self.columns = columns
        self.a, self.b = ctx // 2, ctx % 2
        self.y, self.c = fsdp // 2, fsdp % 2
        flip_b = (1 - self.b, self.y)
        flip_y = (self.b, 1 - self.y)
        core = self.c == 0
        self.first = tuple(jnp.where(core, p, q) for p, q in zip(flip_b, flip_y))
        self.second = tuple(jnp.where(core, q, p) for p, q in zip(flip_b, flip_y))
        self.plane = [(self.b, self.y), self.first, self.second, (1 - self.b, 1 - self.y)]
        self.sib_plane = [(self.b, self.y), self.second, self.first, (1 - self.b, 1 - self.y)]

    def at(self, step):
        return lax.rem(self.a + step, self.columns)

    def device(self, a=None, plane=None, c=None):
        b, y = plane if plane is not None else (self.b, self.y)
        a = self.a if a is None else a
        c = self.c if c is None else c
        return {"ctx": a * 2 + b, "fsdp": y * 2 + c}

    def column(self, step):
        return self.device(a=self.at(step))

    def flip_b(self):
        return self.device(plane=(1 - self.b, self.y))

    def flip_y(self):
        return self.device(plane=(self.b, 1 - self.y))

    def sibling(self):
        return self.device(c=1 - self.c)

    def chunk(self, step, plane, c):
        return (self.at(step) * 2 + plane[0]) * 4 + plane[1] * 2 + c


def greet(devices):
    barrier = pltpu.get_barrier_semaphore()
    for device in devices:
        pl.semaphore_signal(barrier, inc=1, device_id=device, device_id_type=MESH)
    pl.semaphore_wait(barrier, len(devices))


def remote(src, dst, send, recv, device):
    return pltpu.make_async_remote_copy(
        src_ref=src, dst_ref=dst, send_sem=send, recv_sem=recv, device_id=device, device_id_type=MESH
    )


class Sends:
    def __init__(self, sems):
        self.sems, self.made = sems, []

    def start(self, src, dst, recv, device):
        copy = remote(src, dst, self.sems.at[len(self.made)], recv, device)
        copy.start()
        self.made.append(copy)

    def finish(self):
        for copy in self.made:
            copy.wait_send()


def arrived(dst, recv, device):
    remote(dst, dst, recv, recv, device).wait_recv()


def gather_ctx(pos, src, out, sends, recv, local):
    n = pos.columns
    me = pos.a * 2 + pos.b
    own = pltpu.make_async_copy(src, out.at[me], local)
    own.start()
    for k in range(1, n):
        sends.start(src, out.at[me], recv.at[k], pos.column(k))
    sends.start(src, out.at[me], recv.at[n], pos.flip_b())
    yield
    for k in range(1, n):
        slot = pos.at(n - k) * 2 + pos.b
        arrived(out.at[slot], recv.at[k], pos.column(k))
        sends.start(out.at[slot], out.at[slot], recv.at[n + k], pos.flip_b())
        yield
    for k in range(n):
        slot = pos.at(n - k) * 2 + 1 - pos.b
        arrived(out.at[slot], recv.at[n + k], pos.flip_b())
        yield
    own.wait()


def gather_ctx_sems(n):
    return [DMA((2 * n,)), DMA((2 * n,)), DMA]


def gather_fsdp(pos, src, out, sends, recv, local):
    parts = src.shape[0]
    me = pos.y * 2 + pos.c
    other = (1 - pos.y) * 2 + pos.c
    own = []
    for p in range(parts):
        own.append(pltpu.make_async_copy(src.at[p], out.at[p, me], local.at[p]))
        own[-1].start()
        sends.start(src.at[p], out.at[p, me], recv.at[p], pos.flip_y())
    for p in range(parts):
        sends.start(src.at[p], out.at[p, me], recv.at[parts + p], pos.sibling())
    yield
    for p in range(parts):
        arrived(out.at[p, other], recv.at[p], pos.flip_y())
        sends.start(out.at[p, other], out.at[p, other], recv.at[2 * parts + p], pos.sibling())
        yield
    for p in range(parts):
        arrived(out.at[p, pos.y * 2 + 1 - pos.c], recv.at[parts + p], pos.sibling())
        arrived(out.at[p, (1 - pos.y) * 2 + 1 - pos.c], recv.at[2 * parts + p], pos.sibling())
        own[p].wait()


def gather_fsdp_sems(parts):
    return [DMA((3 * parts,)), DMA((3 * parts,)), DMA((parts,))]


def gather_all(pos, src, out, sends, recv, local, group_of=None):
    n = pos.columns
    me = pos.chunk(0, pos.plane[0], pos.c)
    part = (lambda a: src) if group_of is None else (lambda a: src.at[group_of(a)])
    mine = part(pos.a)
    own = pltpu.make_async_copy(mine, out.at[me], local)
    own.start()
    first, second = pos.device(plane=pos.first), pos.device(plane=pos.second)
    sibling = pos.sibling()
    for k in range(1, n):
        sends.start(part(pos.at(k)), out.at[me], recv.at[k], pos.column(k))
    sends.start(mine, out.at[me], recv.at[n], first)
    sends.start(mine, out.at[me], recv.at[2 * n], second)
    sends.start(mine, out.at[me], recv.at[4 * n], sibling)
    yield
    for k in range(1, n):
        slot = pos.chunk(n - k, pos.plane[0], pos.c)
        arrived(out.at[slot], recv.at[k], first)
        sends.start(out.at[slot], out.at[slot], recv.at[n + k], first)
        sends.start(out.at[slot], out.at[slot], recv.at[2 * n + k], second)
        sends.start(out.at[slot], out.at[slot], recv.at[4 * n + k], sibling)
        yield
    for k in range(n):
        slot = pos.chunk(n - k, pos.first, pos.c)
        arrived(out.at[slot], recv.at[n + k], first)
        sends.start(out.at[slot], out.at[slot], recv.at[3 * n + k], second)
        sends.start(out.at[slot], out.at[slot], recv.at[5 * n + k], sibling)
        yield
    for r in range(2):
        for k in range(n):
            slot = pos.chunk(n - k, pos.plane[2 + r], pos.c)
            arrived(out.at[slot], recv.at[(2 + r) * n + k], second)
            sends.start(out.at[slot], out.at[slot], recv.at[(6 + r) * n + k], sibling)
            yield
    own.wait()
    for r in range(4):
        for k in range(n):
            slot = pos.chunk(n - k, pos.sib_plane[r], 1 - pos.c)
            arrived(out.at[slot], recv.at[(4 + r) * n + k], sibling)


def gather_all_sems(n):
    return [DMA((8 * n,)), DMA((8 * n,)), DMA]


def drive(streams):
    streams = list(streams)
    while streams:
        for stream in list(streams):
            if next(stream, streams) is streams:
                streams.remove(stream)


def all_partners(pos):
    return [pos.column(k) for k in range(1, pos.columns)] + [pos.flip_b(), pos.flip_y(), pos.sibling()]


def gather_start_kernel(columns, group_of, tokens, wq, wo, ffn, cot, o_tokens, o_wq, o_wo, o_ffn, o_cot, *sems):
    pos = Place(columns)
    greet(all_partners(pos))
    s = [Sends(sems[3 * i]) for i in range(5)]
    r = lambda i: (sems[3 * i + 1], sems[3 * i + 2])
    streams = [
        gather_ctx(pos, tokens, o_tokens, s[0], *r(0)),
        gather_all(pos, wq, o_wq, s[1], *r(1), group_of=group_of),
        gather_all(pos, wo, o_wo, s[2], *r(2)),
        gather_fsdp(pos, ffn, o_ffn, s[3], *r(3)),
    ]
    drive(streams)
    drive([gather_ctx(pos, cot, o_cot, s[4], *r(4))])
    for x in s:
        x.finish()


def call(kernel, collective_id, ins, outs, scratch, name, space=pl.ANY, in_space=None):
    return pl.pallas_call(
        kernel,
        out_shape=outs,
        in_specs=[pl.BlockSpec(memory_space=in_space or space)] * len(ins),
        out_specs=jax.tree.map(lambda _: pl.BlockSpec(memory_space=space), outs),
        scratch_shapes=scratch,
        compiler_params=pltpu.CompilerParams(
            collective_id=collective_id, has_side_effects=True, vmem_limit_bytes=60 << 20
        ),
        name=name,
    )(*ins)


def shaped(shape, dtype=BF):
    return jax.ShapeDtypeStruct(tuple(shape), dtype)


def gather_start(nc, tokens, wq, wo, ffn, cot):
    n = nc // 2
    group_of = lambda a: a // (n // GROUPS)
    sems = gather_ctx_sems(n) + gather_all_sems(n) * 2 + gather_fsdp_sems(ffn.shape[0]) + gather_ctx_sems(n)
    outs = (
        shaped((nc,) + tokens.shape),
        shaped((nc * 4,) + wq.shape[1:]),
        shaped((nc * 4,) + wo.shape),
        shaped((ffn.shape[0], 4) + ffn.shape[1:]),
        shaped((nc,) + cot.shape),
    )
    return call(functools.partial(gather_start_kernel, n, group_of), 1, (tokens, wq, wo, ffn, cot), outs, sems, "gather_start")


def gather_ctx_kernel(columns, src, out, send, recv, local):
    pos = Place(columns)
    greet([pos.column(k) for k in range(1, columns)] + [pos.flip_b()])
    s = Sends(send)
    drive([gather_ctx(pos, src, out, s, recv, local)])
    s.finish()


def gather_rows(nc, src, collective_id):
    n = nc // 2
    return call(functools.partial(gather_ctx_kernel, n), collective_id, (src,), shaped((nc,) + src.shape), gather_ctx_sems(n), "gather_rows")


def swap_kernel(nc, src, out, send, recv, local):
    per = nc // GROUPS
    ctx = lax.axis_index("ctx")
    group, place = ctx // per, ctx % per
    peer = lambda k: lax.rem(group + k, GROUPS)
    device = lambda k: {"ctx": peer(k) * per + place}
    greet([device(k) for k in range(1, GROUPS)])
    own = pltpu.make_async_copy(src.at[group], out.at[group], local)
    own.start()
    copies = []
    for k in range(1, GROUPS):
        copies.append(remote(src.at[peer(k)], out.at[group], send.at[k], recv.at[k], device(k)))
        copies[-1].start()
    for k in range(1, GROUPS):
        arrived(out.at[peer(GROUPS - k)], recv.at[k], device(k))
    own.wait()
    for copy in copies:
        copy.wait_send()


def swap(nc, src, collective_id):
    return call(functools.partial(swap_kernel, nc), collective_id, (src,), shaped(src.shape), [DMA((GROUPS,)), DMA((GROUPS,)), DMA], "swap")


def add(acc, *others):
    total = acc[...].astype(F32)
    for other in others:
        total = total + other[...].astype(F32)
    acc[...] = total.astype(acc.dtype)


def scatter_ctx(pos, part, out, acc, from_b, from_col, sends, recv, local):
    n = pos.columns
    loads = []
    for k in range(n):
        loads.append(pltpu.make_async_copy(part.at[pos.at(k) * 2 + pos.b], acc.at[k], local.at[k]))
        loads[-1].start()
    for k in [*range(1, n), 0]:
        sends.start(part.at[pos.at(k) * 2 + 1 - pos.b], from_b.at[k], recv.at[k], pos.flip_b())
    yield
    for k in [*range(1, n), 0]:
        loads[k].wait()
        arrived(from_b.at[k], recv.at[k], pos.flip_b())
        if k:
            add(acc.at[k], from_b.at[k])
            sends.start(acc.at[k], from_col.at[k], recv.at[n + k], pos.column(k))
            yield
    total = acc[0].astype(F32) + from_b[0].astype(F32)
    for k in range(1, n):
        arrived(from_col.at[k], recv.at[n + k], pos.column(k))
        total = total + from_col[k].astype(F32)
        yield
    out[...] = total.astype(out.dtype)


def scatter_ctx_scratch(n, shape):
    v = lambda m: pltpu.VMEM((m,) + tuple(shape), BF)
    return [v(n), v(n), v(n), DMA((2 * n,)), DMA((2 * n,)), DMA((n,))]


def scatter_ctx_kernel(columns, part, out, acc, from_b, from_col, send, recv, local):
    pos = Place(columns)
    greet([pos.column(k) for k in range(1, columns)] + [pos.flip_b()])
    s = Sends(send)
    drive([scatter_ctx(pos, part, out, acc, from_b, from_col, s, recv, local)])
    s.finish()


def scatter_rows(nc, part, collective_id):
    n = nc // 2
    return pl.pallas_call(
        functools.partial(scatter_ctx_kernel, n),
        out_shape=shaped(part.shape[1:], F32),
        in_specs=[pl.BlockSpec(memory_space=pl.ANY)],
        out_specs=pl.BlockSpec(memory_space=pltpu.VMEM),
        scratch_shapes=scatter_ctx_scratch(n, part.shape[1:]),
        compiler_params=pltpu.CompilerParams(collective_id=collective_id, has_side_effects=True, vmem_limit_bytes=60 << 20),
        name="scatter_rows",
    )(part)


def scatter_fsdp(pos, part, out, acc, from_sib, from_y, sends, recv, local):
    parts = part.shape[0]
    loads = []
    mine = [(1 - pos.y) * 2 + pos.c, pos.y * 2 + pos.c]
    his = [(1 - pos.y) * 2 + 1 - pos.c, pos.y * 2 + 1 - pos.c]
    for t in range(2):
        for p in range(parts):
            i = t * parts + p
            loads.append(pltpu.make_async_copy(part.at[p, mine[t]], acc.at[i], local.at[i]))
            loads[-1].start()
            sends.start(part.at[p, his[t]], from_sib.at[i], recv.at[i], pos.sibling())
    yield
    for p in range(parts):
        loads[p].wait()
        arrived(from_sib.at[p], recv.at[p], pos.sibling())
        add(acc.at[p], from_sib.at[p])
        sends.start(acc.at[p], from_y.at[p], recv.at[2 * parts + p], pos.flip_y())
        yield
    for p in range(parts):
        loads[parts + p].wait()
        arrived(from_sib.at[parts + p], recv.at[parts + p], pos.sibling())
        add(acc.at[parts + p], from_sib.at[parts + p])
        yield
    for p in range(parts):
        arrived(from_y.at[p], recv.at[2 * parts + p], pos.flip_y())
        out[p] = acc[parts + p].astype(F32) + from_y[p].astype(F32)
        yield


def scatter_fsdp_scratch(parts, shape):
    v = lambda m: pltpu.VMEM((m,) + tuple(shape), BF)
    return [v(2 * parts), v(2 * parts), v(parts), DMA((3 * parts,)), DMA((3 * parts,)), DMA((2 * parts,))]


def scatter_all(pos, part, out, acc, from_sib, from_2, from_1, from_col, sends, recv, local, per_group=False):
    n = pos.columns
    sibling = pos.sibling()
    first, second = pos.device(plane=pos.first), pos.device(plane=pos.second)
    loads = {}
    for r in (3, 2, 1, 0):
        for k in range(n):
            i = r * n + k
            loads[i] = pltpu.make_async_copy(part.at[pos.chunk(k, pos.plane[r], pos.c)], acc.at[i], local.at[i])
            loads[i].start()
            sends.start(part.at[pos.chunk(k, pos.sib_plane[r], 1 - pos.c)], from_sib.at[i], recv.at[i], sibling)
    yield
    for r in (3, 2):
        for k in range(n):
            i = r * n + k
            loads[i].wait()
            arrived(from_sib.at[i], recv.at[i], sibling)
            add(acc.at[i], from_sib.at[i])
            j = (r - 2) * n + k
            sends.start(acc.at[i], from_2.at[j], recv.at[4 * n + j], second)
        yield
    for k in range(n):
        i = n + k
        loads[i].wait()
        arrived(from_sib.at[i], recv.at[i], sibling)
        arrived(from_2.at[i], recv.at[4 * n + i], second)
        add(acc.at[i], from_sib.at[i], from_2.at[i])
        sends.start(acc.at[i], from_1.at[k], recv.at[6 * n + k], first)
    yield
    for k in [*range(1, n), 0]:
        loads[k].wait()
        arrived(from_sib.at[k], recv.at[k], sibling)
        arrived(from_2.at[k], recv.at[4 * n + k], second)
        arrived(from_1.at[k], recv.at[6 * n + k], first)
        if k:
            add(acc.at[k], from_sib.at[k], from_2.at[k], from_1.at[k])
            sends.start(acc.at[k], from_col.at[k], recv.at[7 * n + k], pos.column(k))
    total = acc[0].astype(F32) + from_sib[0].astype(F32) + from_2[0].astype(F32) + from_1[0].astype(F32)
    yield
    if not per_group:
        for k in range(1, n):
            arrived(from_col.at[k], recv.at[7 * n + k], pos.column(k))
            total = total + from_col[k].astype(F32)
        out[...] = total
        return
    each = n // GROUPS
    for k in range(1, n):
        arrived(from_col.at[k], recv.at[7 * n + k], pos.column(k))
    out[...] = jnp.zeros_like(out)
    for k in range(n):
        value = total if k == 0 else from_col[k].astype(F32)
        group = pos.at(n - k) // each
        out[group] = out[group] + value


def scatter_all_scratch(n, shape):
    v = lambda m: pltpu.VMEM((m,) + tuple(shape), BF)
    return [v(4 * n), v(4 * n), v(2 * n), v(n), v(n), DMA((8 * n,)), DMA((8 * n,)), DMA((4 * n,))]


def scatter_end_kernel(columns, gn, wq, wo, ffn, yy, o_gn, o_wq, o_wo, o_ffn, o_yy, *scratch):
    pos = Place(columns)
    greet(all_partners(pos))
    c1, a1, a2, f1, c2 = scratch[0:6], scratch[6:14], scratch[14:22], scratch[22:28], scratch[28:34]
    s = [Sends(x[-3]) for x in (c1, a1, a2, f1, c2)]
    drive(
        [
            scatter_ctx(pos, gn, o_gn, *c1[:-3], s[0], *c1[-2:]),
            scatter_fsdp(pos, ffn, o_ffn, *f1[:-3], s[3], *f1[-2:]),
            scatter_all(pos, wq, o_wq, *a1[:-3], s[1], *a1[-2:], per_group=True),
            scatter_all(pos, wo, o_wo, *a2[:-3], s[2], *a2[-2:]),
            scatter_ctx(pos, yy, o_yy, *c2[:-3], s[4], *c2[-2:]),
        ]
    )
    for x in s:
        x.finish()


def scatter_end(nc, gn, wq, wo, ffn, yy):
    n = nc // 2
    scratch = (
        scatter_ctx_scratch(n, gn.shape[1:])
        + scatter_all_scratch(n, wq.shape[1:])
        + scatter_all_scratch(n, wo.shape[1:])
        + scatter_fsdp_scratch(ffn.shape[0], ffn.shape[2:])
        + scatter_ctx_scratch(n, yy.shape[1:])
    )
    outs = (
        shaped(gn.shape[1:], F32),
        shaped((GROUPS,) + wq.shape[1:], F32),
        shaped(wo.shape[1:], F32),
        shaped((ffn.shape[0],) + ffn.shape[2:], F32),
        shaped(yy.shape[1:], F32),
    )
    return call(
        functools.partial(scatter_end_kernel, n), 6, (gn, wq, wo, ffn, yy), outs, scratch, "scatter_end",
        space=pltpu.VMEM, in_space=pl.ANY,
    )


def doc_ids(row_index, doc_ends):
    return jnp.sum((row_index[:, None] >= doc_ends[None, :]).astype(jnp.int32), axis=1)


def positions(row_index, lengths):
    doc_ends = jnp.cumsum(lengths)
    doc_starts = doc_ends - lengths
    doc_num = doc_ids(row_index, doc_ends)
    column = jnp.arange(lengths.shape[0], dtype=jnp.int32)
    begins = jnp.sum(jnp.where(doc_num[:, None] == column[None, :], doc_starts[None, :], 0), axis=1)
    return doc_num, row_index - begins


def rope_tables(position):
    half_dim = HEAD_DIM // 2
    inverse = ROPE_BASE ** (-2.0 * jnp.arange(half_dim, dtype=F32) / HEAD_DIM)
    angles = position.astype(F32)[:, None] * inverse[None, :]
    return jnp.cos(angles), jnp.sin(angles)


def rotate(values, cosine, sine):
    half_dim = values.shape[-1] // 2
    lower, upper = values[..., :half_dim], values[..., half_dim:]
    cosine, sine = cosine[:, None, :], sine[:, None, :]
    return jnp.concatenate([lower * cosine - upper * sine, upper * cosine + lower * sine], axis=-1)


def kept_rows(route_rows, live_rows, experts, capacity):
    count, top = route_rows.shape
    hot = (route_rows[:, :, None] == jnp.arange(experts, dtype=jnp.int32)) & live_rows[:, None, None]
    hot = hot.astype(F32)
    before = jnp.tril(jnp.ones((count, count), F32), -1)
    kept = jnp.zeros((count, experts), F32)
    base = jnp.zeros((1, experts), F32)
    for k in range(top):
        earlier = base + jnp.dot(before, hot[:, k])
        kept = kept + hot[:, k] * (earlier < capacity)
        base = base + jnp.sum(hot[:, k], axis=0, keepdims=True)
    return kept


def dot(a, b, dims):
    return lax.dot_general(a, b, (dims, ((), ())), preferred_element_type=F32)


def pad_rows(x, rows):
    return jnp.pad(x, [(0, rows - x.shape[0])] + [(0, 0)] * (x.ndim - 1))


def body(tokens, doc_lengths, routes, cotangent, attn_gain, w_qkv, w_out, mlp_gain, router, expert_in, expert_out, shared_in, shared_out):
    nc = lax.axis_size("ctx")
    nf = lax.axis_size("fsdp")
    rows, width = tokens.shape[1:]
    heads = width // HEAD_DIM
    experts = expert_in.shape[1]
    hidden = expert_in.shape[0]
    top = routes.shape[2]
    capacity = 5 * top * rows // (4 * experts)
    per = nc // GROUPS
    ctx = lax.axis_index("ctx")
    group, place = ctx // per, ctx % per
    slot = nc * rows
    mine = heads // GROUPS
    share = mine * HEAD_DIM
    scale = 1.0 / math.sqrt(HEAD_DIM)
    owned = w_out.shape[0]
    padded = -(-(owned + 2 + experts) // 16) * 16

    wq_send = w_qkv.reshape(owned, 3, GROUPS, share).transpose(2, 0, 1, 3).reshape(GROUPS, owned, 3 * share)
    wq_send = jnp.pad(wq_send, ((0, 0), (0, padded - owned), (0, 0)))
    small = jnp.concatenate([attn_gain[None], mlp_gain[None], router.T], axis=0)
    wo_send = pad_rows(jnp.concatenate([w_out, jnp.pad(small, ((0, 0), (0, width - owned)))], axis=0), padded)
    gate_up = jnp.concatenate([expert_in.transpose(2, 1, 0, 3), shared_in.transpose(1, 0, 2)[:, None]], axis=1)
    down = jnp.concatenate([expert_out.transpose(1, 0, 2), shared_out[None]], axis=0)
    ffn_send = jnp.concatenate([gate_up, down[None]], axis=0).reshape(3, (experts + 1) * hidden, width)

    x_all, wq_all, wo_all, ffn_all, cot_all = gather_start(nc, tokens[0], wq_send, wo_send, ffn_send, cotangent[0])
    units = nf * (experts + 1) * hidden
    w_gate, w_up, w_down = (ffn_all[p].reshape(units, width) for p in range(3))
    wq = wq_all[:, :owned].reshape(width, 3 * share)
    wo = wo_all[:, :owned].reshape(width, width)
    small = wo_all[:, owned : owned + 2 + experts, :owned].transpose(1, 0, 2).reshape(2 + experts, width)
    gain_a, gain_m = small[0].astype(F32), small[1].astype(F32)
    router_t = small[2:]

    all_rows = jnp.arange(slot, dtype=jnp.int32)
    doc_num, position = positions(all_rows, doc_lengths[0])
    cosine, sine = rope_tables(position)
    live_all = (doc_num < doc_lengths.shape[1]).astype(F32)[:, None]
    x_slot = x_all.reshape(slot, width).astype(F32)
    inv_attn = lax.rsqrt(jnp.mean(x_slot * x_slot, axis=-1, keepdims=True) + EPSILON)
    normed = (x_slot * inv_attn * gain_a).astype(BF)

    def queries(v):
        return lax.dynamic_index_in_dim(v.reshape((GROUPS, per, rows) + v.shape[1:]), place, 1, False).reshape((GROUPS * rows,) + v.shape[1:])

    normed_q = queries(normed)
    cos_q, sin_q = queries(cosine), queries(sine)
    q = rotate(dot(normed_q, wq[:, :share], ((1,), (0,))).reshape(-1, mine, HEAD_DIM), cos_q, sin_q).astype(BF)
    k = rotate(dot(normed, wq[:, share : 2 * share], ((1,), (0,))).reshape(slot, mine, HEAD_DIM), cosine, sine).astype(BF)
    v = dot(normed, wq[:, 2 * share :], ((1,), (0,))).reshape(slot, mine, HEAD_DIM).astype(BF)
    rows_q, doc_q = queries(all_rows), queries(doc_num)
    allowed = (doc_q[:, None] == doc_num[None, :]) & (all_rows[None, :] <= rows_q[:, None])
    scores = jnp.einsum("qhd,khd->hqk", q, k, preferred_element_type=F32) * scale
    scores = jnp.where(allowed[None], scores, MASKED)
    expo = jnp.exp(scores - jnp.max(scores, axis=-1, keepdims=True))
    prob = expo / jnp.sum(expo, axis=-1, keepdims=True)
    prob_b = prob.astype(BF)
    o = jnp.einsum("hqk,khd->qhd", prob_b, v, preferred_element_type=F32).astype(BF)

    o_own = swap(nc, o.reshape(GROUPS, rows, share), 2)
    attn = o_own.transpose(1, 0, 2).reshape(rows, width)

    row_index = ctx * rows + jnp.arange(rows, dtype=jnp.int32)
    doc_own, _ = positions(row_index, doc_lengths[0])
    live_rows = doc_own < doc_lengths.shape[1]
    live = live_rows.astype(F32)[:, None]
    x = tokens[0].astype(F32)
    resid = x + dot(attn, wo, ((1,), (0,)))
    inv_mlp = lax.rsqrt(jnp.mean(resid * resid, axis=-1, keepdims=True) + EPSILON)
    mixed = (resid * inv_mlp * gain_m).astype(BF)
    logits = dot(mixed, router_t, ((1,), (1,)))
    router_prob = jax.nn.softmax(logits, axis=-1)
    kept = kept_rows(routes[0], live_rows, experts, capacity)
    weight = router_prob * kept
    high = weight.astype(BF)
    low = (weight - high.astype(F32)).astype(BF)
    extra = pad_rows(jnp.pad(jnp.concatenate([high, low], axis=1).T, ((0, 0), (0, width - rows))), 16)
    mixed_all = gather_rows(nc, jnp.concatenate([mixed, extra], axis=0), 3)

    weights = mixed_all[:, rows : rows + 2 * experts, :rows].astype(F32)
    weights = (weights[:, :experts] + weights[:, experts:]).transpose(0, 2, 1).reshape(slot, experts)
    mix = mixed_all[:, :rows].reshape(slot, width)
    g = (cot_all.reshape(slot, width) * live_all.astype(BF)).astype(BF)
    unit_weight = jnp.concatenate([weights, jnp.ones((slot, 1), F32)], axis=1)
    unit_weight = jnp.tile(jnp.repeat(unit_weight, hidden, axis=1), (1, nf))
    gate = dot(mix, w_gate, ((1,), (1,)))
    up = dot(mix, w_up, ((1,), (1,)))
    sig = jax.nn.sigmoid(gate)
    hid = gate * sig * up
    hid_w = (hid * unit_weight).astype(BF)
    y_part = dot(hid_w, w_down, ((1,), (0,))).astype(BF)
    back = dot(g, w_down, ((1,), (1,)))
    pair = (hid * back).reshape(slot, nf, experts + 1, hidden).sum(axis=(1, 3))[:, :experts]
    back_w = back * unit_weight
    d_gate = (back_w * up * sig * (1.0 + gate * (1.0 - sig))).astype(BF)
    d_up = (back_w * gate * sig).astype(BF)
    gm_part = (dot(d_gate, w_gate, ((1,), (0,))) + dot(d_up, w_up, ((1,), (0,)))).astype(BF)
    d_w = jnp.stack([dot(d_gate, mix, ((0,), (0,))), dot(d_up, mix, ((0,), (0,))), dot(hid_w, g, ((0,), (0,)))]).astype(BF)
    pair_t = pair.reshape(nc, rows, experts).transpose(0, 2, 1)
    pair_t = jnp.pad(pair_t, ((0, 0), (0, 16 - experts), (0, width - rows))).astype(BF)
    gm_all = scatter_rows(nc, jnp.concatenate([gm_part.reshape(nc, rows, width), pair_t], axis=1), 4)

    grad_prob = gm_all[rows : rows + experts, :rows].T * kept
    grad_logits = (router_prob * (grad_prob - jnp.sum(router_prob * grad_prob, axis=-1, keepdims=True))).astype(BF)
    grad_router_t = dot(grad_logits, mixed, ((0,), (0,)))
    grad_mixed = gm_all[:rows] + dot(grad_logits, router_t, ((1,), (0,)))
    grad_top = cotangent[0].astype(F32) * live
    w = grad_mixed * gain_m
    grad_resid = grad_top + inv_mlp * w - resid * jnp.mean(w * resid, axis=-1, keepdims=True) * inv_mlp**3
    grad_gain_m = jnp.sum(grad_mixed * resid * inv_mlp, axis=0)
    grad_resid_b = grad_resid.astype(BF)
    grad_wo = dot(attn, grad_resid_b, ((0,), (0,)))
    grad_attn = dot(grad_resid_b, wo, ((1,), (1,))).astype(BF)
    do = swap(nc, grad_attn.reshape(rows, GROUPS, share).transpose(1, 0, 2), 5).reshape(GROUPS * rows, mine, HEAD_DIM)

    grad_p = jnp.einsum("qhd,khd->hqk", do, v, preferred_element_type=F32)
    delta = jnp.sum(prob * grad_p, axis=-1, keepdims=True)
    grad_s = (prob * (grad_p - delta)).astype(BF)
    dq = jnp.einsum("hqk,khd->qhd", grad_s, k, preferred_element_type=F32) * scale
    dk = jnp.einsum("hqk,qhd->khd", grad_s, q, preferred_element_type=F32) * scale
    dv = jnp.einsum("hqk,qhd->khd", prob_b, do, preferred_element_type=F32)
    dq = rotate(dq, cos_q, -sin_q).reshape(GROUPS * rows, share).astype(BF)
    dk = rotate(dk, cosine, -sine).reshape(slot, share)
    dkv = jnp.concatenate([dk, dv.reshape(slot, share)], axis=1).astype(BF)
    grad_wq = jnp.concatenate([dot(normed_q, dq, ((0,), (0,))), dot(normed, dkv, ((0,), (0,)))], axis=1)
    gn_q = dot(dq, wq[:, :share], ((1,), (1,))).reshape(GROUPS, 1, rows, width)
    here = (jnp.arange(per) == place).astype(F32)[None, :, None, None]
    gn = dot(dkv, wq[:, share:], ((1,), (1,))).reshape(GROUPS, per, rows, width) + gn_q * here
    gn_part = gn.reshape(nc, rows, width).astype(BF)

    gn_full = gn.reshape(slot, width)
    grad_gain_a = jnp.sum(gn_full * x_slot * inv_attn, axis=0)
    small = jnp.concatenate([grad_gain_a[None], grad_gain_m[None], grad_router_t], axis=0)
    small = small.reshape(2 + experts, nc * nf, owned).transpose(1, 0, 2)
    wo_part = jnp.concatenate([grad_wo.reshape(nc * nf, owned, width), jnp.pad(small, ((0, 0), (0, 0), (0, width - owned)))], axis=1)
    wo_part = jnp.pad(wo_part, ((0, 0), (0, padded - wo_part.shape[1]), (0, 0))).astype(BF)
    wq_part = jnp.pad(grad_wq.reshape(nc * nf, owned, 3 * share), ((0, 0), (0, padded - owned), (0, 0))).astype(BF)
    ffn_part = d_w.reshape(3, nf, (experts + 1) * hidden, width)
    gn_own, wq_own, wo_own, ffn_own, y_own = scatter_end(nc, gn_part, wq_part, wo_part, ffn_part, y_part.reshape(nc, rows, width))

    layer_out = (live * (resid + y_own)).astype(BF)[None]
    inv = lax.rsqrt(jnp.mean(x * x, axis=-1, keepdims=True) + EPSILON)
    w = gn_own * gain_a
    grad_tokens = (grad_resid + inv * w - x * jnp.mean(w * x, axis=-1, keepdims=True) * inv**3)[None]
    grad_w_qkv = wq_own[:, :owned].reshape(GROUPS, owned, 3, share).transpose(1, 2, 0, 3).reshape(owned, 3 * width)
    small = wo_own[owned : owned + 2 + experts, :owned]
    out = ffn_own.reshape(3, experts + 1, hidden, width)
    return (
        layer_out,
        grad_tokens,
        small[0],
        grad_w_qkv,
        wo_own[:owned],
        small[1],
        small[2:].T,
        out[:2, :experts].transpose(2, 1, 0, 3),
        out[2, :experts].transpose(1, 0, 2),
        out[:2, experts].transpose(1, 0, 2),
        out[2, experts],
    )


def solution(mesh):
    rows = P("fsdp", "ctx", None)
    flat = ("ctx", "fsdp")
    weights = (P(flat), P(flat, None), P(flat, None), P(flat), P(flat, None))
    ffn = (P(flat, None, None, None), P(flat, None, None), P(flat, None, None), P(flat, None))
    return jax.shard_map(
        body,
        mesh=mesh,
        in_specs=(rows, P("fsdp", None), rows, rows) + weights + ffn,
        out_specs=(rows, rows) + weights + ffn,
        check_vma=False,
    )
```

```python
import functools
import math

import jax
import jax.numpy as jnp
import numpy as np
from jax import lax
from jax.experimental import pallas as pl
from jax.experimental.pallas import tpu as pltpu
from jax.sharding import PartitionSpec as P

HEAD_DIM = 64
EPSILON = 1e-05
ROPE_BASE = 10000.0
MASKED = -1e30
NN, NT, TN = ((1,), (0,)), ((1,), (1,)), ((0,), (0,))
FUSED_BYTES = 2 << 20
GROUPS = 4
MESH = pl.DeviceIdType.MESH
DMA = pltpu.SemaphoreType.DMA
BF = jnp.bfloat16
F32 = jnp.float32


class Place:
    def __init__(self, columns):
        ctx, fsdp = lax.axis_index("ctx"), lax.axis_index("fsdp")
        self.columns = columns
        self.a, self.b = ctx // 2, ctx % 2
        self.y, self.c = fsdp // 2, fsdp % 2
        flip_b = (1 - self.b, self.y)
        flip_y = (self.b, 1 - self.y)
        core = self.c == 0
        self.first = tuple(jnp.where(core, p, q) for p, q in zip(flip_b, flip_y))
        self.second = tuple(jnp.where(core, q, p) for p, q in zip(flip_b, flip_y))
        self.plane = [(self.b, self.y), self.first, self.second, (1 - self.b, 1 - self.y)]
        self.sib_plane = [(self.b, self.y), self.second, self.first, (1 - self.b, 1 - self.y)]

    def at(self, step):
        return lax.rem(self.a + step, self.columns)

    def device(self, a=None, plane=None, c=None):
        b, y = plane if plane is not None else (self.b, self.y)
        a = self.a if a is None else a
        c = self.c if c is None else c
        return {"ctx": a * 2 + b, "fsdp": y * 2 + c}

    def column(self, step):
        return self.device(a=self.at(step))

    def flip_b(self):
        return self.device(plane=(1 - self.b, self.y))

    def flip_y(self):
        return self.device(plane=(self.b, 1 - self.y))

    def sibling(self):
        return self.device(c=1 - self.c)

    def chunk(self, step, plane, c):
        return (self.at(step) * 2 + plane[0]) * 4 + plane[1] * 2 + c


def greet(devices):
    barrier = pltpu.get_barrier_semaphore()
    for device in devices:
        pl.semaphore_signal(barrier, inc=1, device_id=device, device_id_type=MESH)
    pl.semaphore_wait(barrier, len(devices))


def remote(src, dst, send, recv, device):
    return pltpu.make_async_remote_copy(
        src_ref=src, dst_ref=dst, send_sem=send, recv_sem=recv, device_id=device, device_id_type=MESH
    )


class Sends:
    def __init__(self, sems):
        self.sems, self.made = sems, []

    def start(self, src, dst, recv, device):
        copy = remote(src, dst, self.sems.at[len(self.made)], recv, device)
        copy.start()
        self.made.append(copy)

    def finish(self):
        for copy in self.made:
            copy.wait_send()


def arrived(dst, recv, device):
    remote(dst, dst, recv, recv, device).wait_recv()


def gather_ctx(pos, src, out, sends, recv, local, there=lambda slot: None):
    n = pos.columns
    me = pos.a * 2 + pos.b
    own = pltpu.make_async_copy(src, out.at[me], local)
    own.start()
    for k in range(1, n):
        sends.start(src, out.at[me], recv.at[k], pos.column(k))
    sends.start(src, out.at[me], recv.at[n], pos.flip_b())
    yield
    own.wait()
    there(me)
    for k in range(1, n):
        slot = pos.at(n - k) * 2 + pos.b
        arrived(out.at[slot], recv.at[k], pos.column(k))
        sends.start(out.at[slot], out.at[slot], recv.at[n + k], pos.flip_b())
        there(slot)
        yield
    for k in range(n):
        slot = pos.at(n - k) * 2 + 1 - pos.b
        arrived(out.at[slot], recv.at[n + k], pos.flip_b())
        there(slot)
        yield


def gather_ctx_sems(n):
    return [DMA((2 * n,)), DMA((2 * n,)), DMA]


def gather_fsdp(pos, src, out, sends, recv, local):
    parts = src.shape[0]
    me = pos.y * 2 + pos.c
    other = (1 - pos.y) * 2 + pos.c
    own = []
    for p in range(parts):
        own.append(pltpu.make_async_copy(src.at[p], out.at[p, me], local.at[p]))
        own[-1].start()
        sends.start(src.at[p], out.at[p, me], recv.at[p], pos.flip_y())
    for p in range(parts):
        sends.start(src.at[p], out.at[p, me], recv.at[parts + p], pos.sibling())
    yield
    for p in range(parts):
        arrived(out.at[p, other], recv.at[p], pos.flip_y())
        sends.start(out.at[p, other], out.at[p, other], recv.at[2 * parts + p], pos.sibling())
        yield
    for p in range(parts):
        arrived(out.at[p, pos.y * 2 + 1 - pos.c], recv.at[parts + p], pos.sibling())
        arrived(out.at[p, (1 - pos.y) * 2 + 1 - pos.c], recv.at[2 * parts + p], pos.sibling())
        own[p].wait()


def gather_fsdp_sems(parts):
    return [DMA((3 * parts,)), DMA((3 * parts,)), DMA((parts,))]


def gather_all(pos, src, out, sends, recv, local, group_of=None):
    n = pos.columns
    me = pos.chunk(0, pos.plane[0], pos.c)
    part = (lambda a: src) if group_of is None else (lambda a: src.at[group_of(a)])
    mine = part(pos.a)
    own = pltpu.make_async_copy(mine, out.at[me], local)
    own.start()
    first, second = pos.device(plane=pos.first), pos.device(plane=pos.second)
    sibling = pos.sibling()
    for k in range(1, n):
        sends.start(part(pos.at(k)), out.at[me], recv.at[k], pos.column(k))
    sends.start(mine, out.at[me], recv.at[n], first)
    sends.start(mine, out.at[me], recv.at[2 * n], second)
    sends.start(mine, out.at[me], recv.at[4 * n], sibling)
    yield
    for k in range(1, n):
        slot = pos.chunk(n - k, pos.plane[0], pos.c)
        arrived(out.at[slot], recv.at[k], first)
        sends.start(out.at[slot], out.at[slot], recv.at[n + k], first)
        sends.start(out.at[slot], out.at[slot], recv.at[2 * n + k], second)
        sends.start(out.at[slot], out.at[slot], recv.at[4 * n + k], sibling)
        yield
    for k in range(n):
        slot = pos.chunk(n - k, pos.first, pos.c)
        arrived(out.at[slot], recv.at[n + k], first)
        sends.start(out.at[slot], out.at[slot], recv.at[3 * n + k], second)
        sends.start(out.at[slot], out.at[slot], recv.at[5 * n + k], sibling)
        yield
    for r in range(2):
        for k in range(n):
            slot = pos.chunk(n - k, pos.plane[2 + r], pos.c)
            arrived(out.at[slot], recv.at[(2 + r) * n + k], second)
            sends.start(out.at[slot], out.at[slot], recv.at[(6 + r) * n + k], sibling)
            yield
    own.wait()
    for r in range(4):
        for k in range(n):
            slot = pos.chunk(n - k, pos.sib_plane[r], 1 - pos.c)
            arrived(out.at[slot], recv.at[(4 + r) * n + k], sibling)


def gather_all_sems(n):
    return [DMA((8 * n,)), DMA((8 * n,)), DMA]


def drive(streams):
    streams = list(streams)
    while streams:
        for stream in list(streams):
            if next(stream, streams) is streams:
                streams.remove(stream)


def all_partners(pos):
    return [pos.column(k) for k in range(1, pos.columns)] + [pos.flip_b(), pos.flip_y(), pos.sibling()]


def shaped(shape, dtype=BF):
    return jax.ShapeDtypeStruct(tuple(shape), dtype)


def dot(a, b, dims):
    return lax.dot_general(a, b, (dims, ((), ())), preferred_element_type=F32)


def add(acc, *others):
    total = acc[...].astype(F32)
    for other in others:
        total = total + other[...].astype(F32)
    acc[...] = total.astype(acc.dtype)


def scatter_ctx(pos, part, out, acc, from_b, from_col, sends, recv, local):
    n = pos.columns
    loads = []
    for k in range(n):
        loads.append(pltpu.make_async_copy(part.at[pos.at(k) * 2 + pos.b], acc.at[k], local.at[k]))
        loads[-1].start()
    for k in [*range(1, n), 0]:
        sends.start(part.at[pos.at(k) * 2 + 1 - pos.b], from_b.at[k], recv.at[k], pos.flip_b())
    yield
    for k in [*range(1, n), 0]:
        loads[k].wait()
        arrived(from_b.at[k], recv.at[k], pos.flip_b())
        if k:
            add(acc.at[k], from_b.at[k])
            sends.start(acc.at[k], from_col.at[k], recv.at[n + k], pos.column(k))
            yield
    total = acc[0].astype(F32) + from_b[0].astype(F32)
    for k in range(1, n):
        arrived(from_col.at[k], recv.at[n + k], pos.column(k))
        total = total + from_col[k].astype(F32)
        yield
    out[...] = total.astype(out.dtype)


def scatter_ctx_scratch(n, shape):
    v = lambda m: pltpu.VMEM((m,) + tuple(shape), BF)
    return [v(n), v(n), v(n), DMA((2 * n,)), DMA((2 * n,)), DMA((n,))]


def scatter_fsdp(pos, part, out, acc, from_sib, from_y, sends, recv, local):
    parts = len(part)
    loads = []
    mine = [(1 - pos.y) * 2 + pos.c, pos.y * 2 + pos.c]
    his = [(1 - pos.y) * 2 + 1 - pos.c, pos.y * 2 + 1 - pos.c]
    for t in range(2):
        for p in range(parts):
            i = t * parts + p
            loads.append(pltpu.make_async_copy(part[p].at[mine[t]], acc.at[i], local.at[i]))
            loads[-1].start()
            sends.start(part[p].at[his[t]], from_sib.at[i], recv.at[i], pos.sibling())
    yield
    for p in range(parts):
        loads[p].wait()
        arrived(from_sib.at[p], recv.at[p], pos.sibling())
        add(acc.at[p], from_sib.at[p])
        sends.start(acc.at[p], from_y.at[p], recv.at[2 * parts + p], pos.flip_y())
        yield
    for p in range(parts):
        loads[parts + p].wait()
        arrived(from_sib.at[parts + p], recv.at[parts + p], pos.sibling())
        add(acc.at[parts + p], from_sib.at[parts + p])
        yield
    for p in range(parts):
        arrived(from_y.at[p], recv.at[2 * parts + p], pos.flip_y())
        out[p] = acc[parts + p].astype(F32) + from_y[p].astype(F32)
        yield


def scatter_fsdp_scratch(parts, shape):
    v = lambda m: pltpu.VMEM((m,) + tuple(shape), BF)
    return [v(2 * parts), v(2 * parts), v(parts), DMA((3 * parts,)), DMA((3 * parts,)), DMA((2 * parts,))]


def scatter_all(pos, part, out, acc, from_sib, from_2, from_1, from_col, sends, recv, local, per_group=False):
    n = pos.columns
    sibling = pos.sibling()
    first, second = pos.device(plane=pos.first), pos.device(plane=pos.second)
    loads = {}
    for r in (3, 2, 1, 0):
        for k in range(n):
            i = r * n + k
            loads[i] = pltpu.make_async_copy(part.at[pos.chunk(k, pos.plane[r], pos.c)], acc.at[i], local.at[i])
            loads[i].start()
            sends.start(part.at[pos.chunk(k, pos.sib_plane[r], 1 - pos.c)], from_sib.at[i], recv.at[i], sibling)
    yield
    for r in (3, 2):
        for k in range(n):
            i = r * n + k
            loads[i].wait()
            arrived(from_sib.at[i], recv.at[i], sibling)
            add(acc.at[i], from_sib.at[i])
            j = (r - 2) * n + k
            sends.start(acc.at[i], from_2.at[j], recv.at[4 * n + j], second)
        yield
    for k in range(n):
        i = n + k
        loads[i].wait()
        arrived(from_sib.at[i], recv.at[i], sibling)
        arrived(from_2.at[i], recv.at[4 * n + i], second)
        add(acc.at[i], from_sib.at[i], from_2.at[i])
        sends.start(acc.at[i], from_1.at[k], recv.at[6 * n + k], first)
    yield
    for k in [*range(1, n), 0]:
        loads[k].wait()
        arrived(from_sib.at[k], recv.at[k], sibling)
        arrived(from_2.at[k], recv.at[4 * n + k], second)
        arrived(from_1.at[k], recv.at[6 * n + k], first)
        if k:
            add(acc.at[k], from_sib.at[k], from_2.at[k], from_1.at[k])
            sends.start(acc.at[k], from_col.at[k], recv.at[7 * n + k], pos.column(k))
    total = acc[0].astype(F32) + from_sib[0].astype(F32) + from_2[0].astype(F32) + from_1[0].astype(F32)
    yield
    if not per_group:
        for k in range(1, n):
            arrived(from_col.at[k], recv.at[7 * n + k], pos.column(k))
            total = total + from_col[k].astype(F32)
        out[...] = total
        return
    each = n // GROUPS
    for k in range(1, n):
        arrived(from_col.at[k], recv.at[7 * n + k], pos.column(k))
    out[...] = jnp.zeros_like(out)
    for k in range(n):
        value = total if k == 0 else from_col[k].astype(F32)
        group = pos.at(n - k) // each
        out[group] = out[group] + value


def scatter_all_scratch(n, shape):
    v = lambda m: pltpu.VMEM((m,) + tuple(shape), BF)
    return [v(4 * n), v(4 * n), v(2 * n), v(n), v(n), DMA((8 * n,)), DMA((8 * n,)), DMA((4 * n,))]


class Sizes:
    def __init__(self, nc, nf, rows, width, experts, hidden, owned, padded, capacity, top, docs):
        self.nc, self.nf, self.rows, self.width = nc, nf, rows, width
        self.experts, self.hidden, self.owned, self.padded = experts, hidden, owned, padded
        self.capacity, self.top, self.docs = capacity, top, docs
        self.columns, self.per = nc // 2, nc // GROUPS
        self.heads = width // HEAD_DIM // GROUPS
        self.share = self.heads * HEAD_DIM
        self.slot = nc * rows
        self.all = nc * nf


def scalars(sz, lengths):
    sizes = [lengths[0, d] for d in range(sz.docs)]
    ends, total = [], 0
    for size in sizes:
        total = total + size
        ends.append(total)
    return sizes, ends


def starts(index, sizes, ends):
    low = jnp.zeros_like(index)
    for size, end in zip(sizes, ends):
        low = low + jnp.where(index >= end, size, 0)
    return low


def iota(shape, dim):
    return lax.broadcasted_iota(jnp.int32, shape, dim)


def mean_square(x, width):
    return jnp.sum(x * x, axis=-1, keepdims=True) * (1.0 / width)


def turn(value, cosine, sine):
    half = HEAD_DIM // 2
    lower, upper = value[:half], value[half:]
    return jnp.concatenate([lower * cosine - upper * sine, upper * cosine + lower * sine], axis=0)


def head(h):
    return slice(h * HEAD_DIM, (h + 1) * HEAD_DIM)


def blk(index, rows):
    return pl.ds(pl.multiple_of(index * rows, rows), rows)


class Copies:
    def __init__(self, sems):
        self.sems, self.made = sems, []

    def start(self, src, dst):
        self.made.append(pltpu.make_async_copy(src, dst, self.sems.at[len(self.made)]))
        self.made[-1].start()

    def finish(self):
        for copy in self.made:
            copy.wait()


def swap_send(sz, group, place, src, out, sends, recv, local, h):
    @pl.when(h == group)
    def _():
        pltpu.make_async_copy(src.at[h], out.at[h], local).start()

    copy = remote(src.at[h], out.at[group], sends.at[h], recv.at[group], {"ctx": h * sz.per + place})

    @pl.when(h != group)
    def _():
        copy.start()


def swap_wait(sz, group, place, src, out, sends, recv, local):
    for h in range(GROUPS):
        copy = remote(src.at[h], out.at[h], sends.at[h], recv.at[h], {"ctx": h * sz.per + place})

        @pl.when(h == group)
        def _():
            pltpu.make_async_copy(src.at[h], out.at[h], local).wait()

        @pl.when(h != group)
        def _():
            copy.wait_send()
            copy.wait_recv()


def forward_kernel(
    sz, lengths, inverse, tokens, cot, routes_t, wq_send, wo_send, ffn_send,
    g_all, mix_all, cw_all, ffn_all, normed_o, qt_o, kt_o, vt_o, prob_o, wt_o, wo_o, small_o, attn_o, resid_o, mixed_o, route_o, table_o,
    x_all, wq_all, wo_all, wq, wt, wo, small, normed, qt, kt, vt, prob, o_send, attn, resid, mixed, route, cw, g_own, table,
    *sems,
):
    pos = Place(sz.columns)
    ctx = lax.axis_index("ctx")
    group, place = ctx // sz.per, ctx % sz.per
    rows, width, share = sz.rows, sz.width, sz.share
    sizes, ends = scalars(sz, lengths)
    group_of = lambda a: a // (sz.columns // GROUPS)

    greet(all_partners(pos))
    s = [Sends(sems[3 * i]) for i in range(7)]
    r = lambda i: (sems[3 * i + 1], sems[3 * i + 2])
    swap_sems = sems[21:24]
    out = Copies(sems[24])

    early = [
        gather_ctx(pos, tokens, x_all, s[0], *r(0)),
        gather_all(pos, wq_send, wq_all, s[1], *r(1), group_of=group_of),
        gather_all(pos, wo_send, wo_all, s[2], *r(2)),
    ]
    ffn = gather_fsdp(pos, ffn_send, ffn_all, s[3], *r(3))
    for stream in early:
        next(stream)
    next(ffn)

    own_rows = ctx * rows + iota((rows, 1), 0)
    live = own_rows < ends[-1]
    g_own[...] = jnp.where(live, cot[...].astype(F32), 0.0).astype(BF)
    index = iota((1, sz.slot), 1)
    position = index - jnp.where(index < ends[-1], starts(index, sizes, ends), 0)
    angles = position.astype(F32) * inverse[:, :1]
    table[0] = jnp.cos(angles)
    table[1] = jnp.sin(angles)
    live_t = (ctx * rows + iota((1, rows), 1)) < ends[-1]
    before = (iota((rows, rows), 0) < iota((rows, rows), 1)).astype(BF)
    base = jnp.zeros((8, 1), F32)
    kept = jnp.zeros((8, rows), F32)
    for k in range(sz.top):
        hot = ((iota((8, rows), 0) == routes_t[k : k + 1, :]) & live_t).astype(F32)
        earlier = base + dot(hot.astype(BF), before, NN)
        kept = kept + jnp.where(earlier < sz.capacity, hot, 0.0)
        base = base + jnp.sum(hot, axis=1, keepdims=True)

    drive(early)
    cots = gather_ctx(pos, g_own, g_all, s[4], *r(4))
    next(cots)

    owned = sz.owned
    for i in range(sz.all):
        wq[i * owned : (i + 1) * owned, :] = wq_all[i, :owned, :].astype(F32)
        wo[i * owned : (i + 1) * owned, :] = wo_all[i, :owned, :].astype(F32)
    extra = wo_all[0, owned:, :].astype(F32)
    for i in range(1, sz.all):
        extra = extra + wo_all[i, owned:, :].astype(F32)
    small[...] = extra[:8]
    wt[...] = wq[...].T.astype(BF)
    gain_a, gain_m = small[0:1, :], small[1:2, :]

    for d in range(sz.nc):
        x = x_all[d].astype(F32)
        inv = lax.rsqrt(mean_square(x, width) + EPSILON)
        normed[d] = (x * inv * gain_a).astype(BF)
        part = slice(d * rows, (d + 1) * rows)
        kv = dot(wt[share:, :], normed[d], NT)
        for h in range(sz.heads):
            kt[head(h), part] = turn(kv[head(h)], table[0, :, part], table[1, :, part]).astype(BF)
        vt[:, part] = kv[share:].astype(BF)

    next(ffn)
    next(cots)
    for h_ in reversed(range(GROUPS)):
        d = h_ * sz.per + place
        part = blk(d, rows)
        qq = dot(wt[:share, :], normed[d], NT)
        keys = (h_ + 1) * sz.per * rows
        index = d * rows + iota((rows, 1), 0)
        low = starts(index, sizes, ends)
        key = iota((rows, keys), 1)
        allowed = (key >= low) & (key <= index)
        for h in range(sz.heads):
            q = turn(qq[head(h)], table[0, :, part], table[1, :, part]).astype(BF) * BF(1.0 / math.sqrt(HEAD_DIM))
            qt[h_, head(h), :] = q
            score = jnp.where(allowed, dot(q, kt[head(h), :keys], TN), MASKED)
            expo = jnp.exp(score - jnp.max(score, axis=1, keepdims=True))
            p = (expo * (1.0 / jnp.sum(expo, axis=1, keepdims=True))).astype(BF)
            prob[h_, h, :, :keys] = p
            o_send[h_, head(h), :] = dot(vt[head(h), :keys], p, NT).astype(BF)
        swap_send(sz, group, place, o_send, attn, *swap_sems, h_)
    drive([ffn, cots])
    swap_wait(sz, group, place, o_send, attn, *swap_sems)

    attn_t = attn[...].reshape(width, rows)
    wo_b = wo[...].astype(BF)
    res = tokens[...].astype(F32) + dot(attn_t, wo_b, TN)
    resid[...] = res
    inv = lax.rsqrt(mean_square(res, width) + EPSILON)
    mixed[...] = (res * inv * gain_m).astype(BF)
    row = iota((8, rows), 0)
    logits = dot(small[...].astype(BF), mixed[...], NT)
    logits = jnp.concatenate([logits[2:], logits[:2]], axis=0)
    logits = jnp.where(row < sz.experts, logits, MASKED)
    expo = jnp.exp(logits - jnp.max(logits, axis=0, keepdims=True))
    router_prob = expo * (1.0 / jnp.sum(expo, axis=0, keepdims=True))
    route[0] = router_prob
    route[1] = kept
    weight = router_prob * kept
    high = weight.astype(BF).astype(F32)
    high_row = jnp.where(row == sz.experts, 1.0, high)
    cw[...] = jnp.concatenate([high_row, weight - high], axis=0).astype(BF)
    late = [
        gather_ctx(pos, cw, cw_all, s[5], *r(5)),
        gather_ctx(pos, mixed, mix_all, s[6], *r(6)),
    ]
    for stream in late:
        next(stream)
    wo[...] = wo_b.astype(F32)
    for src, dst in zip(
        (normed, qt, kt, vt, prob, wt, wo, small, attn, resid, mixed, route, table),
        (normed_o, qt_o, kt_o, vt_o, prob_o, wt_o, wo_o, small_o, attn_o, resid_o, mixed_o, route_o, table_o),
    ):
        out.start(src, dst)
    drive(late)
    out.finish()
    for x in s:
        x.finish()


def forward(sz, collective_id, lengths, inverse, tokens, cot, routes_t, wq_send, wo_send, ffn_send):
    n, nc, rows, width = sz.columns, sz.nc, sz.rows, sz.width
    saved = [
        ((nc, rows, width), BF),
        ((GROUPS, sz.share, rows), BF),
        ((sz.share, sz.slot), BF),
        ((sz.share, sz.slot), BF),
        ((GROUPS, sz.heads, rows, sz.slot), BF),
        ((3 * sz.share, width), BF),
        ((width, width), F32),
        ((8, width), F32),
        ((GROUPS, sz.share, rows), BF),
        ((rows, width), F32),
        ((rows, width), BF),
        ((2, 8, rows), F32),
        ((2, HEAD_DIM // 2, sz.slot), F32),
    ]
    outs = [
        shaped((nc, rows, width)),
        shaped((nc, rows, width)),
        shaped((nc, 16, rows)),
        shaped((ffn_send.shape[0], sz.nf) + ffn_send.shape[1:]),
    ] + [shaped(*x) for x in saved]
    v = lambda shape, dtype=BF: pltpu.VMEM(tuple(shape), dtype)
    normed, qt, kt, vt, prob, wt, wo, small, attn, resid, mixed, route, table = (v(*x) for x in saved)
    scratch = [
        v((nc, rows, width)), v((sz.all,) + wq_send.shape[1:]), v((sz.all,) + wo_send.shape),
        v((width, 3 * sz.share), F32), wt, wo, small, normed, qt, kt, vt, prob, v((GROUPS, sz.share, rows)),
        attn, resid, mixed, route, v((16, rows)), v((rows, width)), table,
    ]
    sems = gather_ctx_sems(n) + gather_all_sems(n) * 2 + gather_fsdp_sems(ffn_send.shape[0]) + gather_ctx_sems(n) * 3
    sems += [DMA((GROUPS,)), DMA((GROUPS,)), DMA, DMA((len(saved),))]
    hbm, vmem = pl.BlockSpec(memory_space=pl.ANY), pl.BlockSpec(memory_space=pltpu.VMEM)
    return pl.pallas_call(
        functools.partial(forward_kernel, sz),
        out_shape=outs,
        in_specs=[pl.BlockSpec(memory_space=pltpu.SMEM), vmem, vmem, vmem, vmem, hbm, hbm, hbm],
        out_specs=[hbm] * len(outs),
        scratch_shapes=scratch + sems,
        compiler_params=pltpu.CompilerParams(collective_id=collective_id, has_side_effects=True, vmem_limit_bytes=62 << 20),
        name="forward",
    )(lengths, inverse, tokens, cot, routes_t, wq_send, wo_send, ffn_send)


def ffn_kernel(chunk, mix, cw, g, wg, wu, wd, spread, gm, yy, pair, dg_w, du_w, dd_w, hw_all, dg_all, du_all, wg_all, wu_all, wd_all, pair_acc):
    j = pl.program_id(0)
    hb = wg.shape[0]
    nc, rows, width = mix.shape
    per = chunk // rows
    at = blk(j, hb) if hb < wg_all.shape[0] else pl.ds(0, hb)
    wg_all[at, :] = wg[...]
    wu_all[at, :] = wu[...]
    wd_all[at, :] = wd[...]
    sp = spread[...]
    for m in range(nc // per):
        part = slice(m * per, (m + 1) * per)
        x = mix[part].reshape(chunk, width)
        gate = dot(x, wg[...], NT)
        up = dot(x, wu[...], NT)
        back = dot(g[part].reshape(chunk, width), wd[...], NT)
        weight = jnp.concatenate([dot(cw[m * per + i], sp[:16], TN) for i in range(per)], axis=0)
        sig = 1.0 / (1.0 + jnp.exp(-gate))
        act = gate * sig
        hid = act * up
        ms = slice(m * chunk, (m + 1) * chunk)
        product = dot(sp[16:], (hid * back).astype(BF), NT)

        @pl.when(j == 0)
        def _():
            pair_acc[:, ms] = product

        @pl.when(j > 0)
        def _():
            pair_acc[:, ms] = pair_acc[:, ms] + product

        hw_all[ms, at] = (hid * weight).astype(BF)
        back = back * weight
        dg_all[ms, at] = (back * up * sig * (1.0 + gate * (1.0 - sig))).astype(BF)
        du_all[ms, at] = (back * act).astype(BF)
    xs = mix[...].reshape(nc * rows, width)
    dg_w[...] = dot(dg_all[:, at], xs, TN).astype(BF)
    du_w[...] = dot(du_all[:, at], xs, TN).astype(BF)
    dd_w[...] = dot(hw_all[:, at], g[...].reshape(nc * rows, width), TN).astype(BF)

    @pl.when(j == pl.num_programs(0) - 1)
    def _():
        for m in range(nc // per):
            ms = slice(m * chunk, (m + 1) * chunk)
            part = slice(m * per, (m + 1) * per)
            total = dot(dg_all[ms], wg_all[...], NN) + dot(du_all[ms], wu_all[...], NN)
            gm[part] = total.astype(BF).reshape(per, rows, width)
            yy[part] = dot(hw_all[ms], wd_all[...], NN).astype(BF).reshape(per, rows, width)
        for d in range(nc):
            pair[d] = pair_acc[:, d * rows : (d + 1) * rows].astype(BF)


def feed_forward(mix, cw, g, w, spread):
    nc, rows, width = mix.shape
    units = w.shape[1]
    block = math.gcd(units, 256) if units % 256 == 0 else units
    chunk = 1024
    once = pl.Buffered(1)
    full = lambda a: pl.BlockSpec(a.shape, lambda j: (0,) * a.ndim, pipeline_mode=once)
    of = lambda p: pl.BlockSpec((None, block, width), lambda j: (p, j, 0))
    kept = lambda *shape: pl.BlockSpec(shape, lambda j: (0,) * len(shape), pipeline_mode=once)
    grads = pl.BlockSpec((block, width), lambda j: (j, 0))
    t = nc * rows
    flops = 2 * t * units * width * 9
    return pl.pallas_call(
        functools.partial(ffn_kernel, chunk),
        grid=(units // block,),
        out_shape=(shaped(mix.shape), shaped(mix.shape), shaped((nc, 16, rows))) + (shaped((units, width)),) * 3,
        in_specs=[full(mix), full(cw), full(g), of(0), of(1), of(2), pl.BlockSpec((32, block), lambda j: (0, j))],
        out_specs=(kept(nc, rows, width), kept(nc, rows, width), kept(nc, 16, rows), grads, grads, grads),
        scratch_shapes=[pltpu.VMEM((t, units), BF)] * 3 + [pltpu.VMEM((units, width), BF)] * 3 + [pltpu.VMEM((16, t), F32)],
        compiler_params=pltpu.CompilerParams(vmem_limit_bytes=62 << 20),
        cost_estimate=pl.CostEstimate(flops=flops, bytes_accessed=w.size * 4 + mix.size * 8, transcendentals=t * units),
        name="feed_forward",
    )(mix, cw, g, w, w, w, spread)


def backward_kernel(
    sz, lengths, tokens, cot, gm_part, pair_part, y_part, dg_w, du_w, dd_w,
    normed_i, qt_i, kt_i, vt_i, prob_i, wt_i, wo_i, small_i, attn_i, resid_i, mixed_i, route_i, table_i,
    o_out, o_tokens, o_wq, o_wo, o_ffn,
    normed, qt, kt, vt, prob, wt, wo, small, attn, resid, mixed, route, table,
    do_send, do, dkt, dvt, dqt_b, dkvt_b, normed_q, gn_part, wq_part, wo_part, gm_own, gp_own, gn_own, y_own,
    *scratch,
):
    pos = Place(sz.columns)
    ctx = lax.axis_index("ctx")
    group, place = ctx // sz.per, ctx % sz.per
    rows, width, share, n = sz.rows, sz.width, sz.share, sz.columns
    sizes, ends = scalars(sz, lengths)
    c_gm, c_gp, c_y, c_gn = (scratch[6 * i : 6 * i + 6] for i in range(4))
    a_wq, a_wo = scratch[24:32], scratch[32:40]
    f_ffn = scratch[40:46]
    swap_sems, loads = scratch[46:49], Copies(scratch[49])
    greet(all_partners(pos))
    s = {x: Sends(scratch[i]) for x, i in (("gm", 3), ("gp", 9), ("y", 15), ("gn", 21), ("wq", 29), ("wo", 37), ("ffn", 43))}

    def ctx_sum(name, part, out, x):
        return scatter_ctx(pos, part, out, *x[:3], s[name], *x[4:])

    early = [ctx_sum("gp", pair_part, gp_own, c_gp), ctx_sum("gm", gm_part, gm_own, c_gm)]
    ffn = scatter_fsdp(pos, (dg_w, du_w, dd_w), o_ffn, *f_ffn[:3], s["ffn"], *f_ffn[4:])
    for stream in early:
        next(stream)
    next(ffn)
    for src, dst in zip(
        (normed_i, qt_i, kt_i, vt_i, prob_i, wt_i, wo_i, small_i, attn_i, resid_i, mixed_i, route_i, table_i),
        (normed, qt, kt, vt, prob, wt, wo, small, attn, resid, mixed, route, table),
    ):
        loads.start(src, dst)
    drive(early)
    loads.finish()
    ys = ctx_sum("y", y_part, y_own, c_y)
    next(ys)

    gain_a, gain_m = small[0:1, :], small[1:2, :]
    live = (ctx * rows + iota((rows, 1), 0)) < ends[-1]
    router_prob, kept = route[0], route[1]
    grad_prob = gp_own[:8, :] * kept
    grad_logits = router_prob * (grad_prob - jnp.sum(router_prob * grad_prob, axis=0, keepdims=True))
    shifted = jnp.concatenate([jnp.zeros((2, rows), F32), grad_logits[:6]], axis=0).astype(BF)
    grad_small = dot(shifted, mixed[...], NN)
    grad_mixed = gm_own[...] + dot(shifted, small[...].astype(BF), TN)
    res = resid[...]
    inv = lax.rsqrt(mean_square(res, width) + EPSILON)
    w = grad_mixed * gain_m
    inner = jnp.sum(w * res, axis=-1, keepdims=True) * (1.0 / width)
    grad_resid = jnp.where(live, cot[...].astype(F32), 0.0) + inv * w - res * inner * inv * inv * inv
    grad_gain_m = jnp.sum(grad_mixed * res * inv, axis=0, keepdims=True)
    grad_resid_b = grad_resid.astype(BF)
    resid[...] = res
    wo_b = wo[...].astype(BF)
    grad_attn_t = dot(wo_b, grad_resid_b, NT).astype(BF)
    for h_ in range(GROUPS):
        do_send[h_] = grad_attn_t[h_ * share : (h_ + 1) * share]
    for h_ in range(GROUPS):
        swap_send(sz, group, place, do_send, do, *swap_sems, h_)
    next(ffn)
    next(ys)
    grad_wo = dot(attn[...].reshape(width, rows), grad_resid_b, NN)
    for i in range(sz.all):
        wo_part[i, : sz.owned, :] = grad_wo[i * sz.owned : (i + 1) * sz.owned].astype(BF)
    for h_ in range(GROUPS):
        normed_q[h_] = normed[h_ * sz.per + place]
    next(ffn)
    swap_wait(sz, group, place, do_send, do, *swap_sems)

    for h_ in reversed(range(GROUPS)):
        keys = (h_ + 1) * sz.per * rows
        part = blk(h_ * sz.per + place, rows)
        for h in range(sz.heads):
            d_o = do[h_, head(h), :]
            p = prob[h_, h, :, :keys]
            pf = p.astype(F32)
            grad_p = dot(d_o, vt[head(h), :keys], TN)
            delta = jnp.sum(pf * grad_p, axis=1, keepdims=True)
            grad_s = (pf * (grad_p - delta)).astype(BF)
            dq = dot(kt[head(h), :keys], grad_s, NT) * (1.0 / math.sqrt(HEAD_DIM))
            dqt_b[h_, head(h), :] = turn(dq, table[0, :, part], -table[1, :, part]).astype(BF)
            dk = dot(qt[h_, head(h), :], grad_s, NN)
            dv = dot(d_o, p, NN)
            if h_ == GROUPS - 1:
                dkt[head(h), :] = dk
                dvt[head(h), :] = dv
            else:
                dkt[head(h), :keys] = dkt[head(h), :keys] + dk
                dvt[head(h), :keys] = dvt[head(h), :keys] + dv
        if h_ == 2:
            next(ffn)
            next(ys)
    for h in range(sz.heads):
        dkvt_b[head(h), :] = turn(dkt[head(h), :], table[0], -table[1]).astype(BF)
    dkvt_b[share:, :] = dvt[...].astype(BF)

    grad_gain_a = jnp.zeros((1, width), F32)
    for step in range(sz.per):
        for h_ in range(GROUPS):
            other = lax.rem(place + 1 + step, sz.per)
            d = h_ * sz.per + other
            gn = dot(dkvt_b[:, blk(d, rows)], wt[share:, :], TN)
            if step == sz.per - 1:
                gn = gn + dot(dqt_b[h_], wt[:share, :], TN)
            grad_gain_a = grad_gain_a + jnp.sum(gn * normed[d].astype(F32), axis=0, keepdims=True)
            gn_part[d] = gn.astype(BF)
    grad_gain_a = grad_gain_a / gain_a
    gns = ctx_sum("gn", gn_part, gn_own, c_gn)
    next(gns)
    row = iota((8, width), 0)
    grad_small = jnp.where(row == 0, grad_gain_a, jnp.where(row == 1, grad_gain_m, grad_small))
    pad = jnp.zeros((sz.padded - sz.owned - 8, width), F32)
    grad_small = jnp.concatenate([grad_small, pad], axis=0).astype(BF) if pad.shape[0] else grad_small.astype(BF)
    for i in range(sz.all):
        wo_part[i, sz.owned :, :] = grad_small
    wos = scatter_all(pos, wo_part, o_wo, *a_wo[:5], s["wo"], *a_wo[6:])
    next(wos)
    grad_q = dot(dqt_b[0], normed_q[0], NN)
    for h_ in range(1, GROUPS):
        grad_q = grad_q + dot(dqt_b[h_], normed_q[h_], NN)
    grad_kv = dot(dkvt_b[...], normed[...].reshape(sz.slot, width), NN)
    grad_w = jnp.concatenate([grad_q, grad_kv], axis=0).T
    wq_part[...] = jnp.zeros_like(wq_part)
    for i in range(sz.all):
        wq_part[i, : sz.owned, :] = grad_w[i * sz.owned : (i + 1) * sz.owned].astype(BF)
    wqs = scatter_all(pos, wq_part, o_wq, *a_wq[:5], s["wq"], *a_wq[6:], per_group=True)
    drive([gns, wqs, wos, ffn, ys])

    o_out[...] = jnp.where(live, res + y_own[...], 0.0).astype(BF)
    x = tokens[...].astype(F32)
    inv = lax.rsqrt(mean_square(x, width) + EPSILON)
    w = gn_own[...] * gain_a
    inner = jnp.sum(w * x, axis=-1, keepdims=True) * (1.0 / width)
    o_tokens[...] = grad_resid + inv * w - x * inner * inv * inv * inv
    for x in s.values():
        x.finish()


def backward(sz, collective_id, lengths, tokens, cot, gm_part, pair_part, y_part, dg_w, du_w, dd_w, saved):
    n, rows, width = sz.columns, sz.rows, sz.width
    part = (3, sz.nf, dg_w.shape[1], width)
    outs = [
        shaped((rows, width)),
        shaped((rows, width), F32),
        shaped((GROUPS, sz.padded, 3 * sz.share), F32),
        shaped((sz.padded, width), F32),
        shaped((3,) + dg_w.shape[1:], F32),
    ]
    v = lambda shape, dtype=BF: pltpu.VMEM(tuple(shape), dtype)
    scratch = [v(x.shape, x.dtype) for x in saved] + [
        v((GROUPS, sz.share, rows)), v((GROUPS, sz.share, rows)), v((sz.share, sz.slot), F32), v((sz.share, sz.slot), F32),
        v((GROUPS, sz.share, rows)), v((2 * sz.share, sz.slot)), v((GROUPS, rows, width)), v((sz.nc, rows, width)),
        v((sz.all, sz.padded, 3 * sz.share)), v((sz.all, sz.padded, width)),
        v((rows, width), F32), v((16, rows), F32), v((rows, width), F32), v((rows, width), F32),
    ]
    scratch += scatter_ctx_scratch(n, (rows, width)) + scatter_ctx_scratch(n, (16, rows)) + scatter_ctx_scratch(n, (rows, width)) * 2
    scratch += scatter_all_scratch(n, (sz.padded, 3 * sz.share)) + scatter_all_scratch(n, (sz.padded, width))
    scratch += scatter_fsdp_scratch(3, dg_w.shape[1:])
    scratch += [DMA((GROUPS,)), DMA((GROUPS,)), DMA, DMA((len(saved),))]
    hbm, vmem = pl.BlockSpec(memory_space=pl.ANY), pl.BlockSpec(memory_space=pltpu.VMEM)
    return pl.pallas_call(
        functools.partial(backward_kernel, sz),
        out_shape=outs,
        in_specs=[pl.BlockSpec(memory_space=pltpu.SMEM), vmem, vmem] + [hbm] * (6 + len(saved)),
        out_specs=[vmem] * len(outs),
        scratch_shapes=scratch,
        compiler_params=pltpu.CompilerParams(collective_id=collective_id, has_side_effects=True, vmem_limit_bytes=62 << 20),
        name="backward",
    )(lengths, tokens, cot, gm_part, pair_part, y_part, dg_w, du_w, dd_w, *saved)


def gather_start_kernel(columns, group_of, tokens, wq, wo, ffn, cot, o_tokens, o_wq, o_wo, o_ffn, o_cot, *sems):
    pos = Place(columns)
    greet(all_partners(pos))
    s = [Sends(sems[3 * i]) for i in range(5)]
    r = lambda i: (sems[3 * i + 1], sems[3 * i + 2])
    streams = [
        gather_ctx(pos, tokens, o_tokens, s[0], *r(0)),
        gather_all(pos, wq, o_wq, s[1], *r(1), group_of=group_of),
        gather_all(pos, wo, o_wo, s[2], *r(2)),
        gather_fsdp(pos, ffn, o_ffn, s[3], *r(3)),
    ]
    drive(streams)
    drive([gather_ctx(pos, cot, o_cot, s[4], *r(4))])
    for x in s:
        x.finish()


def call(kernel, collective_id, ins, outs, scratch, name, space=pl.ANY, in_space=None):
    return pl.pallas_call(
        kernel,
        out_shape=outs,
        in_specs=[pl.BlockSpec(memory_space=in_space or space)] * len(ins),
        out_specs=jax.tree.map(lambda _: pl.BlockSpec(memory_space=space), outs),
        scratch_shapes=scratch,
        compiler_params=pltpu.CompilerParams(
            collective_id=collective_id, has_side_effects=True, vmem_limit_bytes=60 << 20
        ),
        name=name,
    )(*ins)


def gather_start(nc, tokens, wq, wo, ffn, cot):
    n = nc // 2
    group_of = lambda a: a // (n // GROUPS)
    sems = gather_ctx_sems(n) + gather_all_sems(n) * 2 + gather_fsdp_sems(ffn.shape[0]) + gather_ctx_sems(n)
    outs = (
        shaped((nc,) + tokens.shape),
        shaped((nc * 4,) + wq.shape[1:]),
        shaped((nc * 4,) + wo.shape),
        shaped((ffn.shape[0], 4) + ffn.shape[1:]),
        shaped((nc,) + cot.shape),
    )
    return call(functools.partial(gather_start_kernel, n, group_of), 1, (tokens, wq, wo, ffn, cot), outs, sems, "gather_start")


def gather_ctx_kernel(columns, src, out, send, recv, local):
    pos = Place(columns)
    greet([pos.column(k) for k in range(1, columns)] + [pos.flip_b()])
    s = Sends(send)
    drive([gather_ctx(pos, src, out, s, recv, local)])
    s.finish()


def gather_rows(nc, src, collective_id):
    n = nc // 2
    return call(functools.partial(gather_ctx_kernel, n), collective_id, (src,), shaped((nc,) + src.shape), gather_ctx_sems(n), "gather_rows")


def swap_kernel(nc, src, out, send, recv, local):
    per = nc // GROUPS
    ctx = lax.axis_index("ctx")
    group, place = ctx // per, ctx % per
    peer = lambda k: lax.rem(group + k, GROUPS)
    device = lambda k: {"ctx": peer(k) * per + place}
    greet([device(k) for k in range(1, GROUPS)])
    own = pltpu.make_async_copy(src.at[group], out.at[group], local)
    own.start()
    copies = []
    for k in range(1, GROUPS):
        copies.append(remote(src.at[peer(k)], out.at[group], send.at[k], recv.at[k], device(k)))
        copies[-1].start()
    for k in range(1, GROUPS):
        arrived(out.at[peer(GROUPS - k)], recv.at[k], device(k))
    own.wait()
    for copy in copies:
        copy.wait_send()


def swap(nc, src, collective_id):
    return call(functools.partial(swap_kernel, nc), collective_id, (src,), shaped(src.shape), [DMA((GROUPS,)), DMA((GROUPS,)), DMA], "swap")


def scatter_ctx_kernel(columns, part, out, acc, from_b, from_col, send, recv, local):
    pos = Place(columns)
    greet([pos.column(k) for k in range(1, columns)] + [pos.flip_b()])
    s = Sends(send)
    drive([scatter_ctx(pos, part, out, acc, from_b, from_col, s, recv, local)])
    s.finish()


def scatter_rows(nc, part, collective_id):
    n = nc // 2
    return pl.pallas_call(
        functools.partial(scatter_ctx_kernel, n),
        out_shape=shaped(part.shape[1:], F32),
        in_specs=[pl.BlockSpec(memory_space=pl.ANY)],
        out_specs=pl.BlockSpec(memory_space=pltpu.VMEM),
        scratch_shapes=scatter_ctx_scratch(n, part.shape[1:]),
        compiler_params=pltpu.CompilerParams(collective_id=collective_id, has_side_effects=True, vmem_limit_bytes=60 << 20),
        name="scatter_rows",
    )(part)


def scatter_end_kernel(columns, gn, wq, wo, ffn, yy, o_gn, o_wq, o_wo, o_ffn, o_yy, *scratch):
    pos = Place(columns)
    greet(all_partners(pos))
    c1, a1, a2, f1, c2 = scratch[0:6], scratch[6:14], scratch[14:22], scratch[22:28], scratch[28:34]
    s = [Sends(x[-3]) for x in (c1, a1, a2, f1, c2)]
    drive(
        [
            scatter_ctx(pos, gn, o_gn, *c1[:-3], s[0], *c1[-2:]),
            scatter_fsdp(pos, [ffn.at[p] for p in range(ffn.shape[0])], o_ffn, *f1[:-3], s[3], *f1[-2:]),
            scatter_all(pos, wq, o_wq, *a1[:-3], s[1], *a1[-2:], per_group=True),
            scatter_all(pos, wo, o_wo, *a2[:-3], s[2], *a2[-2:]),
            scatter_ctx(pos, yy, o_yy, *c2[:-3], s[4], *c2[-2:]),
        ]
    )
    for x in s:
        x.finish()


def scatter_end(nc, gn, wq, wo, ffn, yy):
    n = nc // 2
    scratch = (
        scatter_ctx_scratch(n, gn.shape[1:])
        + scatter_all_scratch(n, wq.shape[1:])
        + scatter_all_scratch(n, wo.shape[1:])
        + scatter_fsdp_scratch(ffn.shape[0], ffn.shape[2:])
        + scatter_ctx_scratch(n, yy.shape[1:])
    )
    outs = (
        shaped(gn.shape[1:], F32),
        shaped((GROUPS,) + wq.shape[1:], F32),
        shaped(wo.shape[1:], F32),
        shaped((ffn.shape[0],) + ffn.shape[2:], F32),
        shaped(yy.shape[1:], F32),
    )
    return call(
        functools.partial(scatter_end_kernel, n), 6, (gn, wq, wo, ffn, yy), outs, scratch, "scatter_end",
        space=pltpu.VMEM, in_space=pl.ANY,
    )


def doc_ids(row_index, doc_ends):
    return jnp.sum((row_index[:, None] >= doc_ends[None, :]).astype(jnp.int32), axis=1)


def positions(row_index, lengths):
    doc_ends = jnp.cumsum(lengths)
    doc_starts = doc_ends - lengths
    doc_num = doc_ids(row_index, doc_ends)
    column = jnp.arange(lengths.shape[0], dtype=jnp.int32)
    begins = jnp.sum(jnp.where(doc_num[:, None] == column[None, :], doc_starts[None, :], 0), axis=1)
    return doc_num, row_index - begins


def rope_tables(position):
    half_dim = HEAD_DIM // 2
    inverse = ROPE_BASE ** (-2.0 * jnp.arange(half_dim, dtype=F32) / HEAD_DIM)
    angles = position.astype(F32)[:, None] * inverse[None, :]
    return jnp.cos(angles), jnp.sin(angles)


def rotate(values, cosine, sine):
    half_dim = values.shape[-1] // 2
    lower, upper = values[..., :half_dim], values[..., half_dim:]
    cosine, sine = cosine[:, None, :], sine[:, None, :]
    return jnp.concatenate([lower * cosine - upper * sine, upper * cosine + lower * sine], axis=-1)


def kept_rows(route_rows, live_rows, experts, capacity):
    count, top = route_rows.shape
    hot = (route_rows[:, :, None] == jnp.arange(experts, dtype=jnp.int32)) & live_rows[:, None, None]
    hot = hot.astype(F32)
    before = jnp.tril(jnp.ones((count, count), F32), -1)
    kept = jnp.zeros((count, experts), F32)
    base = jnp.zeros((1, experts), F32)
    for k in range(top):
        earlier = base + jnp.dot(before, hot[:, k])
        kept = kept + hot[:, k] * (earlier < capacity)
        base = base + jnp.sum(hot[:, k], axis=0, keepdims=True)
    return kept


def pad_rows(x, rows):
    return jnp.pad(x, [(0, rows - x.shape[0])] + [(0, 0)] * (x.ndim - 1))


def body_wide(tokens, doc_lengths, routes, cotangent, attn_gain, w_qkv, w_out, mlp_gain, router, expert_in, expert_out, shared_in, shared_out):
    nc = lax.axis_size("ctx")
    nf = lax.axis_size("fsdp")
    rows, width = tokens.shape[1:]
    heads = width // HEAD_DIM
    experts = expert_in.shape[1]
    hidden = expert_in.shape[0]
    top = routes.shape[2]
    capacity = 5 * top * rows // (4 * experts)
    per = nc // GROUPS
    ctx = lax.axis_index("ctx")
    group, place = ctx // per, ctx % per
    slot = nc * rows
    mine = heads // GROUPS
    share = mine * HEAD_DIM
    scale = 1.0 / math.sqrt(HEAD_DIM)
    owned = w_out.shape[0]
    padded = -(-(owned + 2 + experts) // 16) * 16

    wq_send = w_qkv.reshape(owned, 3, GROUPS, share).transpose(2, 0, 1, 3).reshape(GROUPS, owned, 3 * share)
    wq_send = jnp.pad(wq_send, ((0, 0), (0, padded - owned), (0, 0)))
    small = jnp.concatenate([attn_gain[None], mlp_gain[None], router.T], axis=0)
    wo_send = pad_rows(jnp.concatenate([w_out, jnp.pad(small, ((0, 0), (0, width - owned)))], axis=0), padded)
    gate_up = jnp.concatenate([expert_in.transpose(2, 1, 0, 3), shared_in.transpose(1, 0, 2)[:, None]], axis=1)
    down = jnp.concatenate([expert_out.transpose(1, 0, 2), shared_out[None]], axis=0)
    ffn_send = jnp.concatenate([gate_up, down[None]], axis=0).reshape(3, (experts + 1) * hidden, width)

    x_all, wq_all, wo_all, ffn_all, cot_all = gather_start(nc, tokens[0], wq_send, wo_send, ffn_send, cotangent[0])
    units = nf * (experts + 1) * hidden
    w_gate, w_up, w_down = (ffn_all[p].reshape(units, width) for p in range(3))
    wq = wq_all[:, :owned].reshape(width, 3 * share)
    wo = wo_all[:, :owned].reshape(width, width)
    small = wo_all[:, owned : owned + 2 + experts, :owned].transpose(1, 0, 2).reshape(2 + experts, width)
    gain_a, gain_m = small[0].astype(F32), small[1].astype(F32)
    router_t = small[2:]

    all_rows = jnp.arange(slot, dtype=jnp.int32)
    doc_num, position = positions(all_rows, doc_lengths[0])
    cosine, sine = rope_tables(position)
    live_all = (doc_num < doc_lengths.shape[1]).astype(F32)[:, None]
    x_slot = x_all.reshape(slot, width).astype(F32)
    inv_attn = lax.rsqrt(jnp.mean(x_slot * x_slot, axis=-1, keepdims=True) + EPSILON)
    normed = (x_slot * inv_attn * gain_a).astype(BF)

    def queries(v):
        return lax.dynamic_index_in_dim(v.reshape((GROUPS, per, rows) + v.shape[1:]), place, 1, False).reshape((GROUPS * rows,) + v.shape[1:])

    normed_q = queries(normed)
    cos_q, sin_q = queries(cosine), queries(sine)
    q = rotate(dot(normed_q, wq[:, :share], ((1,), (0,))).reshape(-1, mine, HEAD_DIM), cos_q, sin_q).astype(BF)
    k = rotate(dot(normed, wq[:, share : 2 * share], ((1,), (0,))).reshape(slot, mine, HEAD_DIM), cosine, sine).astype(BF)
    v = dot(normed, wq[:, 2 * share :], ((1,), (0,))).reshape(slot, mine, HEAD_DIM).astype(BF)
    rows_q, doc_q = queries(all_rows), queries(doc_num)
    allowed = (doc_q[:, None] == doc_num[None, :]) & (all_rows[None, :] <= rows_q[:, None])
    scores = jnp.einsum("qhd,khd->hqk", q, k, preferred_element_type=F32) * scale
    scores = jnp.where(allowed[None], scores, MASKED)
    expo = jnp.exp(scores - jnp.max(scores, axis=-1, keepdims=True))
    prob = expo / jnp.sum(expo, axis=-1, keepdims=True)
    prob_b = prob.astype(BF)
    o = jnp.einsum("hqk,khd->qhd", prob_b, v, preferred_element_type=F32).astype(BF)

    o_own = swap(nc, o.reshape(GROUPS, rows, share), 2)
    attn = o_own.transpose(1, 0, 2).reshape(rows, width)

    row_index = ctx * rows + jnp.arange(rows, dtype=jnp.int32)
    doc_own, _ = positions(row_index, doc_lengths[0])
    live_rows = doc_own < doc_lengths.shape[1]
    live = live_rows.astype(F32)[:, None]
    x = tokens[0].astype(F32)
    resid = x + dot(attn, wo, ((1,), (0,)))
    inv_mlp = lax.rsqrt(jnp.mean(resid * resid, axis=-1, keepdims=True) + EPSILON)
    mixed = (resid * inv_mlp * gain_m).astype(BF)
    logits = dot(mixed, router_t, ((1,), (1,)))
    router_prob = jax.nn.softmax(logits, axis=-1)
    kept = kept_rows(routes[0], live_rows, experts, capacity)
    weight = router_prob * kept
    high = weight.astype(BF)
    low = (weight - high.astype(F32)).astype(BF)
    extra = pad_rows(jnp.pad(jnp.concatenate([high, low], axis=1).T, ((0, 0), (0, width - rows))), 16)
    mixed_all = gather_rows(nc, jnp.concatenate([mixed, extra], axis=0), 3)

    weights = mixed_all[:, rows : rows + 2 * experts, :rows].astype(F32)
    weights = (weights[:, :experts] + weights[:, experts:]).transpose(0, 2, 1).reshape(slot, experts)
    mix = mixed_all[:, :rows].reshape(slot, width)
    g = (cot_all.reshape(slot, width) * live_all.astype(BF)).astype(BF)
    unit_weight = jnp.concatenate([weights, jnp.ones((slot, 1), F32)], axis=1)
    unit_weight = jnp.tile(jnp.repeat(unit_weight, hidden, axis=1), (1, nf))
    gate = dot(mix, w_gate, ((1,), (1,)))
    up = dot(mix, w_up, ((1,), (1,)))
    sig = jax.nn.sigmoid(gate)
    hid = gate * sig * up
    hid_w = (hid * unit_weight).astype(BF)
    y_part = dot(hid_w, w_down, ((1,), (0,))).astype(BF)
    back = dot(g, w_down, ((1,), (1,)))
    pair = (hid * back).reshape(slot, nf, experts + 1, hidden).sum(axis=(1, 3))[:, :experts]
    back_w = back * unit_weight
    d_gate = (back_w * up * sig * (1.0 + gate * (1.0 - sig))).astype(BF)
    d_up = (back_w * gate * sig).astype(BF)
    gm_part = (dot(d_gate, w_gate, ((1,), (0,))) + dot(d_up, w_up, ((1,), (0,)))).astype(BF)
    d_w = jnp.stack([dot(d_gate, mix, ((0,), (0,))), dot(d_up, mix, ((0,), (0,))), dot(hid_w, g, ((0,), (0,)))]).astype(BF)
    pair_t = pair.reshape(nc, rows, experts).transpose(0, 2, 1)
    pair_t = jnp.pad(pair_t, ((0, 0), (0, 16 - experts), (0, width - rows))).astype(BF)
    gm_all = scatter_rows(nc, jnp.concatenate([gm_part.reshape(nc, rows, width), pair_t], axis=1), 4)

    grad_prob = gm_all[rows : rows + experts, :rows].T * kept
    grad_logits = (router_prob * (grad_prob - jnp.sum(router_prob * grad_prob, axis=-1, keepdims=True))).astype(BF)
    grad_router_t = dot(grad_logits, mixed, ((0,), (0,)))
    grad_mixed = gm_all[:rows] + dot(grad_logits, router_t, ((1,), (0,)))
    grad_top = cotangent[0].astype(F32) * live
    w = grad_mixed * gain_m
    grad_resid = grad_top + inv_mlp * w - resid * jnp.mean(w * resid, axis=-1, keepdims=True) * inv_mlp**3
    grad_gain_m = jnp.sum(grad_mixed * resid * inv_mlp, axis=0)
    grad_resid_b = grad_resid.astype(BF)
    grad_wo = dot(attn, grad_resid_b, ((0,), (0,)))
    grad_attn = dot(grad_resid_b, wo, ((1,), (1,))).astype(BF)
    do = swap(nc, grad_attn.reshape(rows, GROUPS, share).transpose(1, 0, 2), 5).reshape(GROUPS * rows, mine, HEAD_DIM)

    grad_p = jnp.einsum("qhd,khd->hqk", do, v, preferred_element_type=F32)
    delta = jnp.sum(prob * grad_p, axis=-1, keepdims=True)
    grad_s = (prob * (grad_p - delta)).astype(BF)
    dq = jnp.einsum("hqk,khd->qhd", grad_s, k, preferred_element_type=F32) * scale
    dk = jnp.einsum("hqk,qhd->khd", grad_s, q, preferred_element_type=F32) * scale
    dv = jnp.einsum("hqk,qhd->khd", prob_b, do, preferred_element_type=F32)
    dq = rotate(dq, cos_q, -sin_q).reshape(GROUPS * rows, share).astype(BF)
    dk = rotate(dk, cosine, -sine).reshape(slot, share)
    dkv = jnp.concatenate([dk, dv.reshape(slot, share)], axis=1).astype(BF)
    grad_wq = jnp.concatenate([dot(normed_q, dq, ((0,), (0,))), dot(normed, dkv, ((0,), (0,)))], axis=1)
    gn_q = dot(dq, wq[:, :share], ((1,), (1,))).reshape(GROUPS, 1, rows, width)
    here = (jnp.arange(per) == place).astype(F32)[None, :, None, None]
    gn = dot(dkv, wq[:, share:], ((1,), (1,))).reshape(GROUPS, per, rows, width) + gn_q * here
    gn_part = gn.reshape(nc, rows, width).astype(BF)

    gn_full = gn.reshape(slot, width)
    grad_gain_a = jnp.sum(gn_full * x_slot * inv_attn, axis=0)
    small = jnp.concatenate([grad_gain_a[None], grad_gain_m[None], grad_router_t], axis=0)
    small = small.reshape(2 + experts, nc * nf, owned).transpose(1, 0, 2)
    wo_part = jnp.concatenate([grad_wo.reshape(nc * nf, owned, width), jnp.pad(small, ((0, 0), (0, 0), (0, width - owned)))], axis=1)
    wo_part = jnp.pad(wo_part, ((0, 0), (0, padded - wo_part.shape[1]), (0, 0))).astype(BF)
    wq_part = jnp.pad(grad_wq.reshape(nc * nf, owned, 3 * share), ((0, 0), (0, padded - owned), (0, 0))).astype(BF)
    ffn_part = d_w.reshape(3, nf, (experts + 1) * hidden, width)
    gn_own, wq_own, wo_own, ffn_own, y_own = scatter_end(nc, gn_part, wq_part, wo_part, ffn_part, y_part.reshape(nc, rows, width))

    layer_out = (live * (resid + y_own)).astype(BF)[None]
    inv = lax.rsqrt(jnp.mean(x * x, axis=-1, keepdims=True) + EPSILON)
    w = gn_own * gain_a
    grad_tokens = (grad_resid + inv * w - x * jnp.mean(w * x, axis=-1, keepdims=True) * inv**3)[None]
    grad_w_qkv = wq_own[:, :owned].reshape(GROUPS, owned, 3, share).transpose(1, 2, 0, 3).reshape(owned, 3 * width)
    small = wo_own[owned : owned + 2 + experts, :owned]
    out = ffn_own.reshape(3, experts + 1, hidden, width)
    return (
        layer_out,
        grad_tokens,
        small[0],
        grad_w_qkv,
        wo_own[:owned],
        small[1],
        small[2:].T,
        out[:2, :experts].transpose(2, 1, 0, 3),
        out[2, :experts].transpose(1, 0, 2),
        out[:2, experts].transpose(1, 0, 2),
        out[2, experts],
    )


def body(tokens, doc_lengths, routes, cotangent, attn_gain, w_qkv, w_out, mlp_gain, router, expert_in, expert_out, shared_in, shared_out):
    nc, nf = lax.axis_size("ctx"), lax.axis_size("fsdp")
    rows, width = tokens.shape[1:]
    experts, hidden, top = expert_in.shape[1], expert_in.shape[0], routes.shape[2]
    owned = w_out.shape[0]
    if 2 * nc * rows * width > FUSED_BYTES:
        return body_wide(
            tokens, doc_lengths, routes, cotangent, attn_gain, w_qkv, w_out, mlp_gain, router, expert_in, expert_out, shared_in, shared_out
        )
    padded = -(-(owned + 8) // 16) * 16
    sz = Sizes(nc, nf, rows, width, experts, hidden, owned, padded, 5 * top * rows // (4 * experts), top, doc_lengths.shape[1])
    share = sz.share
    device = lax.axis_index("ctx") * nf + lax.axis_index("fsdp")

    wq_send = w_qkv.reshape(owned, 3, GROUPS, share).transpose(2, 0, 1, 3).reshape(GROUPS, owned, 3 * share)
    wq_send = jnp.pad(wq_send, ((0, 0), (0, padded - owned), (0, 0)))
    small = jnp.concatenate([attn_gain[None], mlp_gain[None], router.T], axis=0)
    small = lax.dynamic_update_slice(jnp.zeros((padded - owned, width), BF), small, (0, device * owned))
    wo_send = jnp.concatenate([w_out, small], axis=0)
    gate_up = jnp.concatenate([expert_in.transpose(2, 1, 0, 3), shared_in.transpose(1, 0, 2)[:, None]], axis=1)
    down = jnp.concatenate([expert_out.transpose(1, 0, 2), shared_out[None]], axis=0)
    ffn_send = jnp.concatenate([gate_up, down[None]], axis=0).reshape(3, (experts + 1) * hidden, width)

    half = HEAD_DIM // 2
    inverse = (ROPE_BASE ** (-2.0 * np.arange(half) / HEAD_DIM)).astype(np.float32)
    inverse = jnp.asarray(np.broadcast_to(inverse[:, None], (half, 128)))
    routes_t = jnp.pad(routes[0].T, ((0, 8 - top), (0, 0)))

    units = nf * (experts + 1) * hidden
    of = np.arange(units) // hidden % (experts + 1)
    spread = np.zeros((32, units), np.float32)
    for e in range(experts + 1):
        spread[e] = of == e
    for e in range(experts):
        spread[8 + e] = of == e
        spread[16 + e] = of == e

    g_all, mix_all, cw_all, ffn_all, *saved = forward(sz, 1, doc_lengths, inverse, tokens[0], cotangent[0], routes_t, wq_send, wo_send, ffn_send)
    gm_part, y_part, pair_part, dg_w, du_w, dd_w = feed_forward(mix_all, cw_all, g_all, ffn_all.reshape(3, units, width), jnp.asarray(spread, BF))
    by_owner = lambda v: v.reshape(nf, (experts + 1) * hidden, width)
    layer_out, grad_tokens, wq_own, wo_own, ffn_own = backward(
        sz, 2, doc_lengths, tokens[0], cotangent[0], gm_part, pair_part, y_part, by_owner(dg_w), by_owner(du_w), by_owner(dd_w), saved
    )

    grad_w_qkv = wq_own[:, :owned].reshape(GROUPS, owned, 3, share).transpose(1, 2, 0, 3).reshape(owned, 3 * width)
    small = lax.dynamic_slice(wo_own[owned:], (0, device * owned), (2 + experts, owned))
    out = ffn_own.reshape(3, experts + 1, hidden, width)
    return (
        layer_out[None],
        grad_tokens[None],
        small[0],
        grad_w_qkv,
        wo_own[:owned],
        small[1],
        small[2:].T,
        out[:2, :experts].transpose(2, 1, 0, 3),
        out[2, :experts].transpose(1, 0, 2),
        out[:2, experts].transpose(1, 0, 2),
        out[2, experts],
    )


def solution(mesh):
    rows = P("fsdp", "ctx", None)
    flat = ("ctx", "fsdp")
    weights = (P(flat), P(flat, None), P(flat, None), P(flat), P(flat, None))
    ffn = (P(flat, None, None, None), P(flat, None, None), P(flat, None, None), P(flat, None))
    return jax.shard_map(
        body,
        mesh=mesh,
        in_specs=(rows, P("fsdp", None), rows, rows) + weights + ffn,
        out_specs=(rows, rows) + weights + ffn,
        check_vma=False,
    )
```

```python
import functools
import math

import jax
import jax.numpy as jnp
import numpy as np
from jax import lax
from jax.experimental import pallas as pl
from jax.experimental.pallas import tpu as pltpu
from jax.sharding import PartitionSpec as P

HEAD_DIM = 64
EPSILON = 1e-05
ROPE_BASE = 10000.0
MASKED = -1e30
NN, NT, TN = ((1,), (0,)), ((1,), (1,)), ((0,), (0,))
FUSED_BYTES = 2 << 20
GROUPS = 4
MESH = pl.DeviceIdType.MESH
DMA = pltpu.SemaphoreType.DMA
BF = jnp.bfloat16
F32 = jnp.float32


class Place:
    def __init__(self, columns, balanced=True):
        ctx, fsdp = lax.axis_index("ctx"), lax.axis_index("fsdp")
        self.columns = columns
        self.a, self.b = ctx // 2, ctx % 2
        self.y, self.c = fsdp // 2, fsdp % 2
        flip_b = (1 - self.b, self.y)
        flip_y = (self.b, 1 - self.y)
        core = (self.c == 0) if balanced else (self.c >= 0)
        self.first = tuple(jnp.where(core, p, q) for p, q in zip(flip_b, flip_y))
        self.second = tuple(jnp.where(core, q, p) for p, q in zip(flip_b, flip_y))
        self.plane = [(self.b, self.y), self.first, self.second, (1 - self.b, 1 - self.y)]
        self.sib_plane = [(self.b, self.y), self.second, self.first, (1 - self.b, 1 - self.y)]

    def at(self, step):
        return lax.rem(self.a + step, self.columns)

    def device(self, a=None, plane=None, c=None):
        b, y = plane if plane is not None else (self.b, self.y)
        a = self.a if a is None else a
        c = self.c if c is None else c
        return {"ctx": a * 2 + b, "fsdp": y * 2 + c}

    def column(self, step):
        return self.device(a=self.at(step))

    def flip_b(self):
        return self.device(plane=(1 - self.b, self.y))

    def flip_y(self):
        return self.device(plane=(self.b, 1 - self.y))

    def sibling(self):
        return self.device(c=1 - self.c)

    def chunk(self, step, plane, c):
        return (self.at(step) * 2 + plane[0]) * 4 + plane[1] * 2 + c


def greet(devices):
    barrier = pltpu.get_barrier_semaphore()
    for device in devices:
        pl.semaphore_signal(barrier, inc=1, device_id=device, device_id_type=MESH)
    pl.semaphore_wait(barrier, len(devices))


def remote(src, dst, send, recv, device):
    return pltpu.make_async_remote_copy(
        src_ref=src, dst_ref=dst, send_sem=send, recv_sem=recv, device_id=device, device_id_type=MESH
    )


class Sends:
    def __init__(self, sems):
        self.sems, self.made = sems, []

    def start(self, src, dst, recv, device):
        copy = remote(src, dst, self.sems.at[len(self.made)], recv, device)
        copy.start()
        self.made.append(copy)

    def finish(self):
        for copy in self.made:
            copy.wait_send()


def arrived(dst, recv, device):
    remote(dst, dst, recv, recv, device).wait_recv()


def gather_ctx(pos, src, out, sends, recv, local, there=lambda slot: None):
    n = pos.columns
    me = pos.a * 2 + pos.b
    own = pltpu.make_async_copy(src, out.at[me], local)
    own.start()
    for k in range(1, n):
        sends.start(src, out.at[me], recv.at[k], pos.column(k))
    sends.start(src, out.at[me], recv.at[n], pos.flip_b())
    yield
    own.wait()
    there(me)
    for k in range(1, n):
        slot = pos.at(n - k) * 2 + pos.b
        arrived(out.at[slot], recv.at[k], pos.column(k))
        sends.start(out.at[slot], out.at[slot], recv.at[n + k], pos.flip_b())
        there(slot)
        yield
    for k in range(n):
        slot = pos.at(n - k) * 2 + 1 - pos.b
        arrived(out.at[slot], recv.at[n + k], pos.flip_b())
        there(slot)
        yield


def gather_ctx_sems(n):
    return [DMA((2 * n,)), DMA((2 * n,)), DMA]


def gather_fsdp(pos, src, out, sends, recv, local):
    parts = src.shape[0]
    if len(out.shape) == 3:
        out = [out.at[p] for p in range(parts)]
        at = lambda p, f: out[p].at[pl.ds(pl.multiple_of(f * src.shape[1], src.shape[1]), src.shape[1])]
    else:
        at = lambda p, f: out.at[p, f]
    me = pos.y * 2 + pos.c
    other = (1 - pos.y) * 2 + pos.c
    own = []
    for p in range(parts):
        own.append(pltpu.make_async_copy(src.at[p], at(p, me), local.at[p]))
        own[-1].start()
        sends.start(src.at[p], at(p, me), recv.at[p], pos.flip_y())
    for p in range(parts):
        sends.start(src.at[p], at(p, me), recv.at[parts + p], pos.sibling())
    yield
    for p in range(parts):
        arrived(at(p, other), recv.at[p], pos.flip_y())
        sends.start(at(p, other), at(p, other), recv.at[2 * parts + p], pos.sibling())
        yield
    for p in range(parts):
        arrived(at(p, pos.y * 2 + 1 - pos.c), recv.at[parts + p], pos.sibling())
        arrived(at(p, (1 - pos.y) * 2 + 1 - pos.c), recv.at[2 * parts + p], pos.sibling())
        own[p].wait()


def gather_fsdp_sems(parts):
    return [DMA((3 * parts,)), DMA((3 * parts,)), DMA((parts,))]


def gather_all(pos, src, out, sends, recv, local, group_of=None):
    n = pos.columns
    me = pos.chunk(0, pos.plane[0], pos.c)
    part = (lambda a: src) if group_of is None else (lambda a: src.at[group_of(a)])
    mine = part(pos.a)
    own = pltpu.make_async_copy(mine, out.at[me], local)
    own.start()
    first, second = pos.device(plane=pos.first), pos.device(plane=pos.second)
    sibling = pos.sibling()
    for k in range(1, n):
        sends.start(part(pos.at(k)), out.at[me], recv.at[k], pos.column(k))
    sends.start(mine, out.at[me], recv.at[n], first)
    sends.start(mine, out.at[me], recv.at[2 * n], second)
    sends.start(mine, out.at[me], recv.at[4 * n], sibling)
    yield
    for k in range(1, n):
        slot = pos.chunk(n - k, pos.plane[0], pos.c)
        arrived(out.at[slot], recv.at[k], first)
        sends.start(out.at[slot], out.at[slot], recv.at[n + k], first)
        sends.start(out.at[slot], out.at[slot], recv.at[2 * n + k], second)
        sends.start(out.at[slot], out.at[slot], recv.at[4 * n + k], sibling)
        yield
    for k in range(n):
        slot = pos.chunk(n - k, pos.first, pos.c)
        arrived(out.at[slot], recv.at[n + k], first)
        sends.start(out.at[slot], out.at[slot], recv.at[3 * n + k], second)
        sends.start(out.at[slot], out.at[slot], recv.at[5 * n + k], sibling)
        yield
    for r in range(2):
        for k in range(n):
            slot = pos.chunk(n - k, pos.plane[2 + r], pos.c)
            arrived(out.at[slot], recv.at[(2 + r) * n + k], second)
            sends.start(out.at[slot], out.at[slot], recv.at[(6 + r) * n + k], sibling)
            yield
    own.wait()
    for r in range(4):
        for k in range(n):
            slot = pos.chunk(n - k, pos.sib_plane[r], 1 - pos.c)
            arrived(out.at[slot], recv.at[(4 + r) * n + k], sibling)


def gather_all_sems(n):
    return [DMA((8 * n,)), DMA((8 * n,)), DMA]


def drive(streams):
    streams = list(streams)
    while streams:
        for stream in list(streams):
            if next(stream, streams) is streams:
                streams.remove(stream)


def all_partners(pos):
    return [pos.column(k) for k in range(1, pos.columns)] + [pos.flip_b(), pos.flip_y(), pos.sibling()]


def shaped(shape, dtype=BF):
    return jax.ShapeDtypeStruct(tuple(shape), dtype)


def dot(a, b, dims):
    return lax.dot_general(a, b, (dims, ((), ())), preferred_element_type=F32)


def add(acc, *others):
    total = acc[...].astype(F32)
    for other in others:
        total = total + other[...].astype(F32)
    acc[...] = total.astype(acc.dtype)


def scatter_ctx(pos, part, out, acc, from_b, from_col, sends, recv, local):
    n = pos.columns
    loads = []
    for k in range(n):
        loads.append(pltpu.make_async_copy(part.at[pos.at(k) * 2 + pos.b], acc.at[k], local.at[k]))
        loads[-1].start()
    for k in [*range(1, n), 0]:
        sends.start(part.at[pos.at(k) * 2 + 1 - pos.b], from_b.at[k], recv.at[k], pos.flip_b())
    yield
    for k in [*range(1, n), 0]:
        loads[k].wait()
        arrived(from_b.at[k], recv.at[k], pos.flip_b())
        if k:
            add(acc.at[k], from_b.at[k])
            sends.start(acc.at[k], from_col.at[k], recv.at[n + k], pos.column(k))
            yield
    total = acc[0].astype(F32) + from_b[0].astype(F32)
    for k in range(1, n):
        arrived(from_col.at[k], recv.at[n + k], pos.column(k))
        total = total + from_col[k].astype(F32)
        yield
    out[...] = total.astype(out.dtype)


def scatter_ctx_scratch(n, shape):
    v = lambda m: pltpu.VMEM((m,) + tuple(shape), BF)
    return [v(n), v(n), v(n), DMA((2 * n,)), DMA((2 * n,)), DMA((n,))]


def scatter_fsdp(pos, part, out, acc, from_sib, from_y, sends, recv, local):
    parts = len(part)
    loads = []
    mine = [(1 - pos.y) * 2 + pos.c, pos.y * 2 + pos.c]
    his = [(1 - pos.y) * 2 + 1 - pos.c, pos.y * 2 + 1 - pos.c]
    for t in range(2):
        for p in range(parts):
            i = t * parts + p
            loads.append(pltpu.make_async_copy(part[p].at[mine[t]], acc.at[i], local.at[i]))
            loads[-1].start()
            sends.start(part[p].at[his[t]], from_sib.at[i], recv.at[i], pos.sibling())
    yield
    for p in range(parts):
        loads[p].wait()
        arrived(from_sib.at[p], recv.at[p], pos.sibling())
        add(acc.at[p], from_sib.at[p])
        sends.start(acc.at[p], from_y.at[p], recv.at[2 * parts + p], pos.flip_y())
        yield
    for p in range(parts):
        loads[parts + p].wait()
        arrived(from_sib.at[parts + p], recv.at[parts + p], pos.sibling())
        add(acc.at[parts + p], from_sib.at[parts + p])
        yield
    for p in range(parts):
        arrived(from_y.at[p], recv.at[2 * parts + p], pos.flip_y())
        out[p] = acc[parts + p].astype(F32) + from_y[p].astype(F32)
        yield


def scatter_fsdp_scratch(parts, shape):
    v = lambda m: pltpu.VMEM((m,) + tuple(shape), BF)
    return [v(2 * parts), v(2 * parts), v(parts), DMA((3 * parts,)), DMA((3 * parts,)), DMA((2 * parts,))]


def scatter_all(pos, part, out, acc, from_sib, from_2, from_1, from_col, sends, recv, local, per_group=False):
    n = pos.columns
    sibling = pos.sibling()
    first, second = pos.device(plane=pos.first), pos.device(plane=pos.second)
    loads = {}
    for r in (3, 2, 1, 0):
        for k in range(n):
            i = r * n + k
            loads[i] = pltpu.make_async_copy(part.at[pos.chunk(k, pos.plane[r], pos.c)], acc.at[i], local.at[i])
            loads[i].start()
            sends.start(part.at[pos.chunk(k, pos.sib_plane[r], 1 - pos.c)], from_sib.at[i], recv.at[i], sibling)
    yield
    for r in (3, 2):
        for k in range(n):
            i = r * n + k
            loads[i].wait()
            arrived(from_sib.at[i], recv.at[i], sibling)
            add(acc.at[i], from_sib.at[i])
            j = (r - 2) * n + k
            sends.start(acc.at[i], from_2.at[j], recv.at[4 * n + j], second)
        yield
    for k in range(n):
        i = n + k
        loads[i].wait()
        arrived(from_sib.at[i], recv.at[i], sibling)
        arrived(from_2.at[i], recv.at[4 * n + i], second)
        add(acc.at[i], from_sib.at[i], from_2.at[i])
        sends.start(acc.at[i], from_1.at[k], recv.at[6 * n + k], first)
    yield
    for k in [*range(1, n), 0]:
        loads[k].wait()
        arrived(from_sib.at[k], recv.at[k], sibling)
        arrived(from_2.at[k], recv.at[4 * n + k], second)
        arrived(from_1.at[k], recv.at[6 * n + k], first)
        if k:
            add(acc.at[k], from_sib.at[k], from_2.at[k], from_1.at[k])
            sends.start(acc.at[k], from_col.at[k], recv.at[7 * n + k], pos.column(k))
    total = acc[0].astype(F32) + from_sib[0].astype(F32) + from_2[0].astype(F32) + from_1[0].astype(F32)
    yield
    if not per_group:
        for k in range(1, n):
            arrived(from_col.at[k], recv.at[7 * n + k], pos.column(k))
            total = total + from_col[k].astype(F32)
        out[...] = total
        return
    each = n // GROUPS
    for k in range(1, n):
        arrived(from_col.at[k], recv.at[7 * n + k], pos.column(k))
    out[...] = jnp.zeros_like(out)
    for k in range(n):
        value = total if k == 0 else from_col[k].astype(F32)
        group = pos.at(n - k) // each
        out[group] = out[group] + value


def scatter_all_scratch(n, shape):
    v = lambda m: pltpu.VMEM((m,) + tuple(shape), BF)
    return [v(4 * n), v(4 * n), v(2 * n), v(n), v(n), DMA((8 * n,)), DMA((8 * n,)), DMA((4 * n,))]


class GatherLine:
    def __init__(self, pos, bufs, send, recv, parts=2):
        self.pos, self.bufs, self.send, self.recv, self.parts = pos, bufs, send, recv, parts
        self.made = []

    def cut(self, ref, p):
        rows = ref.shape[0] // self.parts
        return ref.at[pl.ds(p * rows, rows)]

    def copy(self, i, p, src, a, kind, device):
        out = self.bufs[i][1]
        n = self.pos.columns
        dst = self.cut(out.at[2 * a + self.pos.b], p)
        at = ((i * 2 + kind) * n + a) * self.parts + p
        made = remote(dst if src is None else self.cut(src, p), dst, self.send.at[len(self.made)], self.recv.at[at], device)
        return made

    def go(self, i, p, src, a, kind, device, when=None):
        made = self.copy(i, p, src, a, kind, device)
        self.made.append((made, when))
        if when is None:
            made.start()
        else:
            pl.when(when)(made.start)

    def start(self):
        pos, n = self.pos, self.pos.columns
        up, down = pos.device(a=jnp.minimum(pos.a + 1, n - 1)), pos.device(a=jnp.maximum(pos.a - 1, 0))
        self.up, self.down = up, down
        for p in range(self.parts):
            for i, (src, _) in enumerate(self.bufs):
                self.go(i, p, src, pos.a, 0, up, pos.a < n - 1)
                self.go(i, p, src, pos.a, 0, down, pos.a > 0)
                self.go(i, p, src, pos.a, 1, pos.flip_b())

    def here(self, i, p, a, kind, device):
        b = self.pos.b if kind == 0 else 1 - self.pos.b
        out = self.bufs[i][1]
        at = ((i * 2 + kind) * self.pos.columns + a) * self.parts + p
        arrived(self.cut(out.at[2 * a + b], p), self.recv.at[at], device)

    def relay(self, d):
        pos, n = self.pos, self.pos.columns
        for p in range(self.parts):
            for sign, device, end in ((-1, self.up, pos.a < n - 1), (1, self.down, pos.a > 0)):
                a = pos.a + sign * d
                there = (a >= 0) & (a < n)
                a = jnp.clip(a, 0, n - 1)
                for i in range(len(self.bufs)):
                    pl.when(there)(functools.partial(self.here, i, p, a, 0, device))
                    if d < n - 1:
                        self.go(i, p, None, a, 0, device, there & end)
                    self.go(i, p, None, a, 1, pos.flip_b(), there)

    def across(self, a):
        for p in range(self.parts):
            for i in range(len(self.bufs)):
                self.here(i, p, a, 1, self.pos.flip_b())

    def finish(self):
        for made, when in self.made:
            if when is None:
                made.wait_send()
            else:
                pl.when(when)(made.wait_send)


def gather_line_sems(n, bufs=1, parts=2):
    return [DMA((parts * bufs * (3 + 4 * (n - 1)),)), DMA((2 * bufs * n * parts,))]


def gather_tree(pos, src, out, sends, recv, local, group_of=None):
    n = pos.columns
    b, y = pos.plane[0]
    part = (lambda a: src) if group_of is None else (lambda a: src.at[group_of(a)])
    first, second, sibling = pos.device(plane=pos.first), pos.device(plane=pos.second), pos.sibling()
    mine = out.at[pos.c, b, y, pos.a]
    own = pltpu.make_async_copy(part(pos.a), mine, local)
    own.start()
    for k in range(1, n):
        sends.start(part(pos.at(k)), mine, recv.at[k], pos.column(k))
    yield
    for k in range(1, n):
        arrived(out.at[pos.c, b, y, pos.at(n - k)], recv.at[k], first)
    own.wait()
    column = out.at[pos.c, b, y]
    sends.start(column, column, recv.at[n], first)
    sends.start(column, column, recv.at[n + 1], second)
    yield
    column = out.at[pos.c, pos.first[0], pos.first[1]]
    arrived(column, recv.at[n], first)
    sends.start(column, column, recv.at[n + 2], second)
    yield
    for r in range(2):
        arrived(out.at[pos.c, pos.plane[2 + r][0], pos.plane[2 + r][1]], recv.at[n + 1 + r], second)
    sends.start(out.at[pos.c], out.at[pos.c], recv.at[n + 3], sibling)
    yield
    arrived(out.at[1 - pos.c], recv.at[n + 3], sibling)


def gather_tree_sems(n):
    return [DMA((n + 4,)), DMA((n + 4,)), DMA]


def scatter_tree(pos, part, out, from_sib, from_2, from_1, from_col, sends, recv, per_group=False):
    n = pos.columns
    c = pos.c
    first, second, sibling = pos.device(plane=pos.first), pos.device(plane=pos.second), pos.sibling()
    sends.start(part.at[1 - c], from_sib, recv.at[0], sibling)
    yield
    arrived(from_sib, recv.at[0], sibling)
    at = lambda r: (c, pos.plane[r][0], pos.plane[r][1])
    sib = lambda r: (pos.plane[r][0], pos.plane[r][1])
    for r in (3, 2):
        part[at(r)] = (part[at(r)].astype(F32) + from_sib[sib(r)].astype(F32)).astype(BF)
        sends.start(part.at[at(r)], from_2.at[r - 2], recv.at[1 + r - 2], second)
    yield
    arrived(from_2.at[1], recv.at[2], second)
    part[at(1)] = (part[at(1)].astype(F32) + from_sib[sib(1)].astype(F32) + from_2[1].astype(F32)).astype(BF)
    sends.start(part.at[at(1)], from_1, recv.at[3], first)
    arrived(from_2.at[0], recv.at[1], second)
    yield
    arrived(from_1, recv.at[3], first)
    total = part[at(0)].astype(F32) + from_sib[sib(0)].astype(F32) + from_2[0].astype(F32) + from_1[...].astype(F32)
    part[at(0)] = total.astype(BF)
    mine = part.at[at(0)]
    for k in range(1, n):
        sends.start(mine.at[pos.at(k)], from_col.at[k], recv.at[3 + k], pos.column(k))
    yield
    total = mine[pos.a].astype(F32)
    if per_group:
        out[pos.a // (n // GROUPS)] = total
    for k in range(1, n):
        arrived(from_col.at[k], recv.at[3 + k], pos.column(k))
        if per_group:
            out[pos.at(n - k) // (n // GROUPS)] = from_col[k].astype(F32)
        else:
            total = total + from_col[k].astype(F32)
    if not per_group:
        out[...] = total


def scatter_tree_scratch(n, shape):
    v = lambda *lead: pltpu.VMEM(lead + tuple(shape), BF)
    return [v(2, 2, n), v(2, n), v(n), v(n), DMA((n + 4,)), DMA((n + 4,))]


class SumCtx:
    def __init__(self, pos, parts, send, recv):
        self.pos, self.parts, self.send, self.recv = pos, parts, send, recv

    def copies(self, a, way):
        pos, n = self.pos, self.pos.columns
        for i, (part, from_b, from_col) in enumerate(self.parts):
            base = 2 * n * i
            if way == "b":
                yield remote(part.at[2 * a + 1 - pos.b], from_b.at[a], self.send.at[base + a], self.recv.at[base + a], pos.flip_b())
            else:
                device = pos.device(a=a)
                yield remote(part.at[2 * a + pos.b], from_col.at[pos.a], self.send.at[base + n + a], self.recv.at[base + n + pos.a], device)

    def push(self, a):
        for copy in self.copies(a, "b"):
            copy.start()

    def pass_on(self, a, other=None):
        pos = self.pos
        for copy, (part, from_b, _) in zip(self.copies(a, "b"), self.parts):
            copy.wait_recv()

        def send():
            for copy, (part, from_b, _) in zip(self.copies(a, "column"), self.parts):
                at = 2 * a + pos.b
                part[at] = (part[at].astype(F32) + from_b[a].astype(F32)).astype(BF)
                copy.start()

        if other is None:
            pl.when(a != pos.a)(send)
        elif other:
            send()

    def total(self):
        pos, n = self.pos, self.pos.columns
        sums = []
        for i, (part, from_b, from_col) in enumerate(self.parts):
            total = part[2 * pos.a + pos.b].astype(F32) + from_b[pos.a].astype(F32)
            for k in range(1, n):
                a = pos.at(k)
                sem = self.recv.at[2 * n * i + n + a]
                arrived(from_col.at[a], sem, pos.column(k))
                total = total + from_col[a].astype(F32)
            sums.append(total)
        return sums

    def finish(self):
        pos, n = self.pos, self.pos.columns
        for a in range(n):
            for copy in self.copies(a, "b"):
                copy.wait_send()
        for k in range(1, n):
            for copy in self.copies(pos.at(k), "column"):
                copy.wait_send()


def sum_ctx_scratch(n, *shapes):
    v = lambda shape: pltpu.VMEM((n,) + tuple(shape), BF)
    out = []
    for shape in shapes:
        out += [v(shape), v(shape)]
    return out + [DMA((2 * n * len(shapes),)), DMA((2 * n * len(shapes),))]


class Sizes:
    def __init__(self, nc, nf, rows, width, experts, hidden, owned, padded, capacity, top, docs):
        self.nc, self.nf, self.rows, self.width = nc, nf, rows, width
        self.experts, self.hidden, self.owned, self.padded = experts, hidden, owned, padded
        self.capacity, self.top, self.docs = capacity, top, docs
        self.columns, self.per = nc // 2, nc // GROUPS
        self.heads = width // HEAD_DIM // GROUPS
        self.share = self.heads * HEAD_DIM
        self.slot = nc * rows
        self.all = nc * nf


def scalars(sz, lengths):
    sizes = [lengths[0, d] for d in range(sz.docs)]
    ends, total = [], 0
    for size in sizes:
        total = total + size
        ends.append(total)
    return sizes, ends


def starts(index, sizes, ends):
    low = jnp.zeros_like(index)
    for size, end in zip(sizes, ends):
        low = low + jnp.where(index >= end, size, 0)
    return low


def iota(shape, dim):
    return lax.broadcasted_iota(jnp.int32, shape, dim)


def mean_square(x, width):
    return jnp.sum(x * x, axis=-1, keepdims=True) * (1.0 / width)


def turn(value, cosine, sine):
    half = HEAD_DIM // 2
    lower, upper = value[:half], value[half:]
    return jnp.concatenate([lower * cosine - upper * sine, upper * cosine + lower * sine], axis=0)


def head(h):
    return slice(h * HEAD_DIM, (h + 1) * HEAD_DIM)


def blk(index, rows):
    return pl.ds(pl.multiple_of(index * rows, rows), rows)


class Copies:
    def __init__(self, sems):
        self.sems, self.made = sems, []

    def start(self, src, dst):
        self.made.append(pltpu.make_async_copy(src, dst, self.sems.at[len(self.made)]))
        self.made[-1].start()

    def finish(self):
        for copy in self.made:
            copy.wait()


def swap_send(sz, group, place, src, out, sends, recv, local, h):
    @pl.when(h == group)
    def _():
        pltpu.make_async_copy(src.at[h], out.at[h], local).start()

    copy = remote(src.at[h], out.at[group], sends.at[h], recv.at[group], {"ctx": h * sz.per + place})

    @pl.when(h != group)
    def _():
        copy.start()


def swap_wait(sz, group, place, src, out, sends, recv, local):
    for h in range(GROUPS):
        copy = remote(src.at[h], out.at[h], sends.at[h], recv.at[h], {"ctx": h * sz.per + place})

        @pl.when(h == group)
        def _():
            pltpu.make_async_copy(src.at[h], out.at[h], local).wait()

        @pl.when(h != group)
        def _():
            copy.wait_send()
            copy.wait_recv()


def forward_kernel(
    sz, lengths, tokens, cot, routes, small_own, spread, wq_send, wo_own, ffn_send,
    gm_o, gp_o, y_o, dw_o, normed_o, qt_o, kt_o, vt_o, prob_o, wt_o, wo_o, small_o, attn_o, resid_o, mixed_o, route_o, table_o,
    x_all, wq_all, wo_all, wo_send, wq, wt, wo, small, normed, qt, kt, vt, prob, o_send, attn, resid, route, g_own, table,
    g_all, mix_all, cw_all, ffn_w, hw, dg, du, gm_part, gp_part, y_part, dw,
    *sems,
):
    pos, pos_b = Place(sz.columns), Place(sz.columns, balanced=False)
    ctx = lax.axis_index("ctx")
    group, place = ctx // sz.per, ctx % sz.per
    rows, width, share, n = sz.rows, sz.width, sz.share, sz.columns
    sizes, ends = scalars(sz, lengths)
    group_of = lambda a: a // (n // GROUPS)

    owned = sz.owned
    me = ctx * sz.nf + lax.axis_index("fsdp")
    place_of = (iota((owned, width), 1) == me * owned + iota((owned, width), 0)).astype(BF)
    wo_send[:owned, :] = wo_own[...]
    wo_send[owned:, :] = dot(small_own[...], place_of, NN).astype(BF)

    greet(all_partners(pos))
    s = [Sends(sems[3 * i]) for i in range(3)]
    r = lambda i: (sems[3 * i + 1], sems[3 * i + 2])
    swap_sems, out = sems[9:12], Copies(sems[12])
    gm_sum = SumCtx(pos, [(gm_part, sems[13], sems[14]), (gp_part, sems[15], sems[16])], sems[17], sems[18])
    toks = GatherLine(pos, [(tokens, x_all)], sems[19], sems[20])
    cots = GatherLine(pos, [(None, g_all)], sems[21], sems[22])
    mixes = GatherLine(pos, [(None, mix_all)], sems[23], sems[24])
    weights = GatherLine(pos, [(None, cw_all)], sems[25], sems[26], parts=1)

    wqs = gather_tree(pos_b, wq_send, wq_all, s[0], *r(0), group_of=group_of)
    wos = gather_tree(pos_b, wo_send, wo_all, s[1], *r(1))
    ffn = gather_fsdp(pos, ffn_send, ffn_w, s[2], *r(2))
    next(wqs)
    toks.start()
    next(ffn)
    x_all[ctx] = tokens[...]

    own_rows = ctx * rows + iota((rows, 1), 0)
    live = own_rows < ends[-1]
    g_all[ctx] = jnp.where(live, cot[...].astype(F32), 0.0).astype(BF)
    index = iota((1, sz.slot), 1)
    position = index - jnp.where(index < ends[-1], starts(index, sizes, ends), 0)
    half = HEAD_DIM // 2
    inverse = jnp.exp(iota((half, 1), 0).astype(F32) * (-2.0 * math.log(ROPE_BASE) / HEAD_DIM))
    angles = position.astype(F32) * inverse
    table[0] = jnp.cos(angles)
    table[1] = jnp.sin(angles)
    before = (iota((rows, rows), 0) < iota((rows, rows), 1)).astype(BF)
    same = (iota((rows, rows), 0) == iota((rows, rows), 1)).astype(BF)
    base = jnp.zeros((8, 1), F32)
    kept = jnp.zeros((8, rows), F32)
    for k in range(sz.top):
        hot = ((iota((rows, 8), 1) == routes[:, k : k + 1]) & live).astype(BF)
        earlier = base + dot(hot, before, TN)
        hot = dot(hot, same, TN)
        kept = kept + jnp.where(earlier < sz.capacity, hot, 0.0)
        base = base + jnp.sum(hot, axis=1, keepdims=True)
    route[1] = kept
    step(wqs)
    for k in range(1, n):
        toks.relay(k)
        step(wqs)
    cots.start()
    step(wos)
    for k in range(n):
        toks.across(k)
    drive([wqs])

    def spot(i):
        a_b, y_c = divmod(i, sz.nf)
        return y_c % 2, a_b % 2, y_c // 2, a_b // 2

    for i in range(sz.all):
        wq[i * owned : (i + 1) * owned, :] = wq_all[spot(i)][:owned, :].astype(F32)
    wt[...] = wq[...].T.astype(BF)
    for d in range(sz.nc):
        x = x_all[d].astype(F32)
        inv = lax.rsqrt(mean_square(x, width) + EPSILON)
        normed[d] = (x * inv).astype(BF)
        part = slice(d * rows, (d + 1) * rows)
        kv = dot(wt[share:, :], normed[d], NT)
        for h in range(sz.heads):
            kt[head(h), part] = turn(kv[head(h)], table[0, :, part], table[1, :, part]).astype(BF)
        vt[:, part] = kv[share:].astype(BF)
    step(wos, ffn)
    cots.relay(1)

    for h_ in reversed(range(GROUPS)):
        d = h_ * sz.per + place
        part = blk(d, rows)
        qq = dot(wt[:share, :], normed[d], NT)
        keys = (h_ + 1) * sz.per * rows
        index = d * rows + iota((rows, 1), 0)
        low = starts(index, sizes, ends)
        key = iota((rows, keys), 1)
        allowed = (key >= low) & (key <= index)
        for h in range(sz.heads):
            q = turn(qq[head(h)], table[0, :, part], table[1, :, part]).astype(BF) * BF(1.0 / math.sqrt(HEAD_DIM))
            qt[h_, head(h), :] = q
            score = jnp.where(allowed, dot(q, kt[head(h), :keys], TN), MASKED)
            expo = jnp.exp(score - jnp.max(score, axis=1, keepdims=True))
            p = (expo * (1.0 / jnp.sum(expo, axis=1, keepdims=True))).astype(BF)
            prob[h_, h, :, :keys] = p
            o_send[h_, head(h), :] = dot(vt[head(h), :keys], p, NT).astype(BF)
        swap_send(sz, group, place, o_send, attn, *swap_sems, h_)
        step(wos)
        if h_ in (1, 2):
            cots.relay(n - h_)
            step(ffn)
    for i in range(sz.all):
        wo[i * owned : (i + 1) * owned, :] = wo_all[spot(i)][:owned, :].astype(F32)
    drive([wos])
    extra = wo_all[spot(0)][owned:, :].astype(F32)
    for i in range(1, sz.all):
        extra = extra + wo_all[spot(i)][owned:, :].astype(F32)
    small[...] = extra[:8]
    gain_m = small[1:2, :]
    wo_b = wo[...].astype(BF)
    swap_wait(sz, group, place, o_send, attn, *swap_sems)

    attn_t = attn[...].reshape(width, rows)
    res = tokens[...].astype(F32) + dot(attn_t, wo_b, TN)
    resid[...] = res
    inv = lax.rsqrt(mean_square(res, width) + EPSILON)
    mixed = (res * inv * gain_m).astype(BF)
    mix_all[ctx] = mixed
    row = iota((8, rows), 0)
    logits = dot(small[...].astype(BF), mixed, NT)
    logits = jnp.concatenate([logits[2:], logits[:2]], axis=0)
    logits = jnp.where(row < sz.experts, logits, MASKED)
    expo = jnp.exp(logits - jnp.max(logits, axis=0, keepdims=True))
    router_prob = expo * (1.0 / jnp.sum(expo, axis=0, keepdims=True))
    route[0] = router_prob
    weight = router_prob * kept
    high = weight.astype(BF).astype(F32)
    high_row = jnp.where(row == sz.experts, 1.0, high)
    cw_all[ctx] = jnp.concatenate([high_row, weight - high], axis=0).astype(BF)

    weights.start()
    mixes.start()
    wo[...] = wo_b.astype(F32)
    for src, dst in zip(
        (normed, qt, kt, vt, prob, wt, wo, small, attn, resid, mix_all.at[ctx], route, table),
        (normed_o, qt_o, kt_o, vt_o, prob_o, wt_o, wo_o, small_o, attn_o, resid_o, mixed_o, route_o, table_o),
    ):
        out.start(src, dst)
    drive([ffn])

    block = 256
    chunk = 2 * rows

    def hidden_units(a):
        at_rows = blk(a, chunk)
        x = mix_all[pl.ds(2 * a, 2)].reshape(chunk, width)
        g = g_all[pl.ds(2 * a, 2)].reshape(chunk, width)

        def units(j, pair):
            at = blk(j, block)
            gate = dot(x, ffn_w[0, at, :], NT)
            up = dot(x, ffn_w[1, at, :], NT)
            back = dot(g, ffn_w[2, at, :], NT)
            weight = jnp.concatenate([dot(cw_all[2 * a + i], spread[:16, at], TN) for i in range(2)], axis=0)
            sig = 1.0 / (1.0 + jnp.exp(-gate))
            act = gate * sig
            hid = act * up
            pair = pair + dot(spread[16:, at], (hid * back).astype(BF), NT)
            hw[at_rows, at] = (hid * weight).astype(BF)
            back = back * weight
            dg[at_rows, at] = (back * up * sig * (1.0 + gate * (1.0 - sig))).astype(BF)
            du[at_rows, at] = (back * act).astype(BF)
            return pair

        pair = lax.fori_loop(0, ffn_w.shape[1] // block, units, jnp.zeros((16, chunk), F32))
        for i in range(2):
            gp_part[2 * a + i] = pair[:, i * rows : (i + 1) * rows].astype(BF)

    def input_grad(a):
        at_rows = blk(a, chunk)
        total = dot(dg[at_rows, :], ffn_w[0], NN) + dot(du[at_rows, :], ffn_w[1], NN)
        gm_part[pl.ds(2 * a, 2)] = total.astype(BF).reshape(2, rows, width)
        gm_sum.push(a)

    near = [pos.a, jnp.where(pos.a == 0, 1, jnp.where(pos.a == 1, 0, jnp.where(pos.a == 2, 3, 2)))]
    near += [jnp.where(pos.a < 2, 2, 1), jnp.where(pos.a < 2, 3, 0)]
    for i in range(n):
        if i + 1 < n:
            weights.relay(i + 1)
            mixes.relay(i + 1)
        for stream in (cots, weights, mixes):
            stream.across(near[i])
        hidden_units(near[i])
        input_grad(near[i])
        if i > 1:
            gm_sum.pass_on(near[i - 1], other=True)
    xs = mix_all[...].reshape(sz.slot, width)
    gs = g_all[...].reshape(sz.slot, width)
    total_units = ffn_w.shape[1]

    def unit_grads(j, _):
        at = blk(j, block)
        dw[0, at, :] = dot(dg[:, at], xs, TN).astype(BF)
        dw[1, at, :] = dot(du[:, at], xs, TN).astype(BF)
        dw[2, at, :] = dot(hw[:, at], gs, TN).astype(BF)
        return 0

    lax.fori_loop(0, total_units // block // 2, unit_grads, 0)
    gm_sum.pass_on(near[-1], other=True)
    gm_sum.pass_on(pos.a, other=False)
    lax.fori_loop(total_units // block // 2, total_units // block, unit_grads, 0)
    out.start(dw, dw_o)
    for a in range(n):
        part = slice(a * chunk, (a + 1) * chunk)
        y_part[2 * a : 2 * a + 2] = dot(hw[part, :], ffn_w[2], NN).astype(BF).reshape(2, rows, width)
    out.start(y_part, y_o)
    gm_o[...], gp_o[...] = gm_sum.total()
    out.finish()
    gm_sum.finish()
    for x in (*s, toks, cots, mixes, weights):
        x.finish()


def step(*streams):
    for stream in streams:
        next(stream, None)


def saved_shapes(sz):
    rows, width = sz.rows, sz.width
    return [
        ((sz.nc, rows, width), BF),
        ((GROUPS, sz.share, rows), BF),
        ((sz.share, sz.slot), BF),
        ((sz.share, sz.slot), BF),
        ((GROUPS, sz.heads, rows, sz.slot), BF),
        ((3 * sz.share, width), BF),
        ((width, width), F32),
        ((8, width), F32),
        ((GROUPS, sz.share, rows), BF),
        ((rows, width), F32),
        ((rows, width), BF),
        ((2, 8, rows), F32),
        ((2, HEAD_DIM // 2, sz.slot), F32),
    ]


def forward(sz, collective_id, lengths, tokens, cot, routes, small_own, spread, wq_send, wo_own, ffn_send):
    n, nc, rows, width = sz.columns, sz.nc, sz.rows, sz.width
    units = sz.nf * ffn_send.shape[1]
    saved = saved_shapes(sz)
    outs = [
        shaped((rows, width), F32),
        shaped((16, rows), F32),
        shaped((nc, rows, width)),
        shaped((3, units, width)),
    ] + [shaped(*x) for x in saved]
    v = lambda shape, dtype=BF: pltpu.VMEM(tuple(shape), dtype)
    normed, qt, kt, vt, prob, wt, wo, small, attn, resid, mixed, route, table = (v(*x) for x in saved)
    tree = (2, 2, 2, n)
    scratch = [
        v((nc, rows, width)), v(tree + wq_send.shape[1:]), v(tree + (sz.padded, width)), v((sz.padded, width)),
        v((width, 3 * sz.share), F32), wt, wo, small, normed, qt, kt, vt, prob, v((GROUPS, sz.share, rows)),
        attn, resid, route, v((rows, width)), table,
        v((nc, rows, width)), v((nc, rows, width)), v((nc, 16, rows)), v((3, units, width)),
        v((sz.slot, units)), v((sz.slot, units)), v((sz.slot, units)),
        v((nc, rows, width)), v((nc, 16, rows)), v((nc, rows, width)), v((3, units, width)),
    ]
    sems = gather_tree_sems(n) * 2 + gather_fsdp_sems(3)
    sems += [DMA((GROUPS,)), DMA((GROUPS,)), DMA, DMA((len(saved) + 2,))]
    sems += sum_ctx_scratch(n, (rows, width), (16, rows)) + gather_line_sems(n) * 3 + gather_line_sems(n, parts=1)
    hbm, vmem = pl.BlockSpec(memory_space=pl.ANY), pl.BlockSpec(memory_space=pltpu.VMEM)
    return pl.pallas_call(
        functools.partial(forward_kernel, sz),
        out_shape=outs,
        in_specs=[pl.BlockSpec(memory_space=pltpu.SMEM), vmem, vmem, vmem, vmem, vmem, hbm, vmem, hbm],
        out_specs=[vmem, vmem] + [hbm] * (len(outs) - 2),
        scratch_shapes=scratch + sems,
        compiler_params=pltpu.CompilerParams(collective_id=collective_id, has_side_effects=True, vmem_limit_bytes=62 << 20),
        name="forward",
    )(lengths, tokens, cot, routes, small_own, spread, wq_send, wo_own, ffn_send)


def backward_kernel(
    sz, lengths, tokens, cot, gm_own, gp_own, y_part, dw,
    normed_i, qt_i, kt_i, vt_i, prob_i, wt_i, wo_i, small_i, attn_i, resid_i, mixed_i, route_i, table_i,
    o_out, o_tokens, o_wq, o_wo, o_in, o_down,
    normed, qt, kt, vt, prob, wt, wo, small, attn, resid, mixed, route, table,
    do_send, do, dkt, dvt, dqt_b, dkvt_b, normed_q, gn_part, wq_part, wo_part, y_own, ffn_own,
    *scratch,
):
    pos = Place(sz.columns)
    ctx = lax.axis_index("ctx")
    group, place = ctx // sz.per, ctx % sz.per
    rows, width, share, n = sz.rows, sz.width, sz.share, sz.columns
    owned = sz.owned
    sizes, ends = scalars(sz, lengths)
    c_y, g_sum, t_wq, t_wo, f_ffn = scratch[:6], scratch[6:10], scratch[10:16], scratch[16:22], scratch[22:28]
    swap_sems, first, later = scratch[28:31], Copies(scratch[31]), Copies(scratch[32])
    saved = (normed_i, qt_i, kt_i, vt_i, prob_i, wt_i, wo_i, small_i, attn_i, resid_i, mixed_i, route_i, table_i)
    held = (normed, qt, kt, vt, prob, wt, wo, small, attn, resid, mixed, route, table)
    for i in (7, 6, 9, 10, 11):
        first.start(saved[i], held[i])
    for i in (8, 0, 2, 3, 1, 4, 5, 12):
        later.start(saved[i], held[i])
    greet(all_partners(pos))
    s = {x: Sends(y) for x, y in (("y", c_y[3]), ("wq", t_wq[4]), ("wo", t_wo[4]), ("ffn", f_ffn[3]))}
    ys = scatter_ctx(pos, y_part, y_own, *c_y[:3], s["y"], *c_y[4:])
    by_owner = [dw.at[p] for p in range(3)]
    ffn = scatter_fsdp(pos, by_owner, ffn_own, *f_ffn[:3], s["ffn"], *f_ffn[4:])
    wos = scatter_tree(pos, wo_part, o_wo, *t_wo[:4], s["wo"], t_wo[5])
    wqs = scatter_tree(pos, wq_part, o_wq, *t_wq[:4], s["wq"], t_wq[5], per_group=True)
    gn_sum = SumCtx(pos, [(gn_part, g_sum[0], g_sum[1])], g_sum[2], g_sum[3])
    step(ffn)
    first.finish()

    gain_m = small[1:2, :]
    live = (ctx * rows + iota((rows, 1), 0)) < ends[-1]
    router_prob, kept = route[0], route[1]
    grad_prob = gp_own[:8, :] * kept
    grad_logits = router_prob * (grad_prob - jnp.sum(router_prob * grad_prob, axis=0, keepdims=True))
    shifted = jnp.concatenate([jnp.zeros((2, rows), F32), grad_logits[:6]], axis=0).astype(BF)
    grad_small = dot(shifted, mixed[...], NN)
    grad_mixed = gm_own[...] + dot(shifted, small[...].astype(BF), TN)
    res = resid[...]
    inv = lax.rsqrt(mean_square(res, width) + EPSILON)
    w = grad_mixed * gain_m
    inner = jnp.sum(w * res, axis=-1, keepdims=True) * (1.0 / width)
    grad_resid = jnp.where(live, cot[...].astype(F32), 0.0) + inv * w - res * inner * inv * inv * inv
    grad_gain_m = jnp.sum(grad_mixed * res * inv, axis=0, keepdims=True)
    grad_resid_b = grad_resid.astype(BF)
    grad_attn_t = dot(wo[...].astype(BF), grad_resid_b, NT).astype(BF)
    for h_ in range(GROUPS):
        do_send[h_] = grad_attn_t[h_ * share : (h_ + 1) * share]
    for h_ in range(GROUPS):
        swap_send(sz, group, place, do_send, do, *swap_sems, h_)
    step(ys)

    later.finish()
    grad_wo = dot(attn[...].reshape(width, rows), grad_resid_b, NN)
    row = iota((sz.padded - owned, width), 0)
    grad_small = jnp.where(row == 1, grad_gain_m, jnp.concatenate([grad_small] * ((sz.padded - owned) // 8), axis=0)).astype(BF)

    def spot(i):
        a_b, y_c = divmod(i, sz.nf)
        return y_c % 2, a_b % 2, y_c // 2, a_b // 2

    for i in range(sz.all):
        wo_part[spot(i) + (slice(0, owned),)] = grad_wo[i * owned : (i + 1) * owned].astype(BF)
        wo_part[spot(i) + (slice(owned, None),)] = grad_small
    step(wos)
    for h_ in range(GROUPS):
        normed_q[h_] = normed[h_ * sz.per + place]
    step(ffn)
    swap_wait(sz, group, place, do_send, do, *swap_sems)

    dkt[...] = jnp.zeros_like(dkt)
    dvt[...] = jnp.zeros_like(dvt)
    for h_ in reversed(range(GROUPS)):
        keys = (h_ + 1) * sz.per * rows
        done = slice(h_ * sz.per * rows, keys)
        part = blk(h_ * sz.per + place, rows)
        for h in range(sz.heads):
            d_o = do[h_, head(h), :]
            p = prob[h_, h, :, :keys]
            pf = p.astype(F32)
            grad_p = dot(d_o, vt[head(h), :keys], TN)
            delta = jnp.sum(pf * grad_p, axis=1, keepdims=True)
            grad_s = (pf * (grad_p - delta)).astype(BF)
            dq = dot(kt[head(h), :keys], grad_s, NT) * (1.0 / math.sqrt(HEAD_DIM))
            dqt_b[h_, head(h), :] = turn(dq, table[0, :, part], -table[1, :, part]).astype(BF)
            dkt[head(h), :keys] = dkt[head(h), :keys] + dot(qt[h_, head(h), :], grad_s, NN)
            dvt[head(h), :keys] = dvt[head(h), :keys] + dot(d_o, p, NN)
        for h in range(sz.heads):
            dkvt_b[head(h), done] = turn(dkt[head(h), done], table[0, :, done], -table[1, :, done]).astype(BF)
        dkvt_b[share:, done] = dvt[:, done].astype(BF)
        for t in range(2):
            d = h_ * sz.per + lax.rem(place + 1 + t, 2)
            gn = dot(dkvt_b[:, blk(d, rows)], wt[share:, :], TN)
            if t == 1:
                gn = gn + dot(dqt_b[h_], wt[:share, :], TN)
            gn_part[d] = gn.astype(BF)
        gn_sum.push(h_)
        if h_ < GROUPS - 1:
            gn_sum.pass_on(h_ + 1)
        step(wos, ffn, ys)
    grad_q = dot(dqt_b[0], normed_q[0], NN)
    for h_ in range(1, GROUPS):
        grad_q = grad_q + dot(dqt_b[h_], normed_q[h_], NN)
    grad_kv = dot(dkvt_b[...], normed[...].reshape(sz.slot, width), NN)
    grad_w = jnp.concatenate([grad_q, grad_kv], axis=0).T
    wq_part[...] = jnp.zeros_like(wq_part)
    for i in range(sz.all):
        wq_part[spot(i) + (slice(0, owned),)] = grad_w[i * owned : (i + 1) * owned].astype(BF)
    step(wqs)
    gn_sum.pass_on(0)
    drive([wqs, wos, ys, ffn])
    o_in[...] = ffn_own[:2]
    o_down[...] = ffn_own[2]
    o_out[...] = jnp.where(live, res + y_own[...], 0.0).astype(BF)
    x = tokens[...].astype(F32)
    inv = lax.rsqrt(mean_square(x, width) + EPSILON)
    (gn_own,) = gn_sum.total()
    w = gn_own
    inner = jnp.sum(w * x, axis=-1, keepdims=True) * (1.0 / width)
    o_tokens[...] = grad_resid + inv * w - x * inner * inv * inv * inv
    gn_sum.finish()
    for x in s.values():
        x.finish()


def backward(sz, collective_id, lengths, tokens, cot, gm_own, gp_own, y_part, dw, saved):
    n, rows, width = sz.columns, sz.rows, sz.width
    units = dw.shape[2]
    outs = [
        shaped((rows, width)),
        shaped((rows, width), F32),
        shaped((GROUPS, sz.padded, 3 * sz.share), F32),
        shaped((sz.padded, width), F32),
        shaped((2, units, width), F32),
        shaped((units, width), F32),
    ]
    v = lambda shape, dtype=BF: pltpu.VMEM(tuple(shape), dtype)
    tree = (2, 2, 2, n)
    scratch = [v(x.shape, x.dtype) for x in saved] + [
        v((GROUPS, sz.share, rows)), v((GROUPS, sz.share, rows)), v((sz.share, sz.slot), F32), v((sz.share, sz.slot), F32),
        v((GROUPS, sz.share, rows)), v((2 * sz.share, sz.slot)), v((GROUPS, rows, width)), v((sz.nc, rows, width)),
        v(tree + (sz.padded, 3 * sz.share)), v(tree + (sz.padded, width)), v((rows, width), F32), v((3, units, width), F32),
    ]
    scratch += scatter_ctx_scratch(n, (rows, width)) + sum_ctx_scratch(n, (rows, width))
    scratch += scatter_tree_scratch(n, (sz.padded, 3 * sz.share)) + scatter_tree_scratch(n, (sz.padded, width))
    scratch += scatter_fsdp_scratch(3, dw.shape[2:])
    scratch += [DMA((GROUPS,)), DMA((GROUPS,)), DMA, DMA((len(saved),)), DMA((len(saved),))]
    hbm, vmem = pl.BlockSpec(memory_space=pl.ANY), pl.BlockSpec(memory_space=pltpu.VMEM)
    return pl.pallas_call(
        functools.partial(backward_kernel, sz),
        out_shape=outs,
        in_specs=[pl.BlockSpec(memory_space=pltpu.SMEM)] + [vmem] * 4 + [hbm] * (2 + len(saved)),
        out_specs=[vmem] * len(outs),
        scratch_shapes=scratch,
        compiler_params=pltpu.CompilerParams(collective_id=collective_id, has_side_effects=True, vmem_limit_bytes=62 << 20),
        name="backward",
    )(lengths, tokens, cot, gm_own, gp_own, y_part, dw, *saved)


def gather_start_kernel(columns, group_of, tokens, wq, wo, ffn, cot, o_tokens, o_wq, o_wo, o_ffn, o_cot, *sems):
    pos = Place(columns)
    greet(all_partners(pos))
    s = [Sends(sems[3 * i]) for i in range(5)]
    r = lambda i: (sems[3 * i + 1], sems[3 * i + 2])
    streams = [
        gather_ctx(pos, tokens, o_tokens, s[0], *r(0)),
        gather_all(pos, wq, o_wq, s[1], *r(1), group_of=group_of),
        gather_all(pos, wo, o_wo, s[2], *r(2)),
        gather_fsdp(pos, ffn, o_ffn, s[3], *r(3)),
    ]
    drive(streams)
    drive([gather_ctx(pos, cot, o_cot, s[4], *r(4))])
    for x in s:
        x.finish()


def call(kernel, collective_id, ins, outs, scratch, name, space=pl.ANY, in_space=None):
    return pl.pallas_call(
        kernel,
        out_shape=outs,
        in_specs=[pl.BlockSpec(memory_space=in_space or space)] * len(ins),
        out_specs=jax.tree.map(lambda _: pl.BlockSpec(memory_space=space), outs),
        scratch_shapes=scratch,
        compiler_params=pltpu.CompilerParams(
            collective_id=collective_id, has_side_effects=True, vmem_limit_bytes=60 << 20
        ),
        name=name,
    )(*ins)


def gather_start(nc, tokens, wq, wo, ffn, cot):
    n = nc // 2
    group_of = lambda a: a // (n // GROUPS)
    sems = gather_ctx_sems(n) + gather_all_sems(n) * 2 + gather_fsdp_sems(ffn.shape[0]) + gather_ctx_sems(n)
    outs = (
        shaped((nc,) + tokens.shape),
        shaped((nc * 4,) + wq.shape[1:]),
        shaped((nc * 4,) + wo.shape),
        shaped((ffn.shape[0], 4) + ffn.shape[1:]),
        shaped((nc,) + cot.shape),
    )
    return call(functools.partial(gather_start_kernel, n, group_of), 1, (tokens, wq, wo, ffn, cot), outs, sems, "gather_start")


def gather_ctx_kernel(columns, src, out, send, recv, local):
    pos = Place(columns)
    greet([pos.column(k) for k in range(1, columns)] + [pos.flip_b()])
    s = Sends(send)
    drive([gather_ctx(pos, src, out, s, recv, local)])
    s.finish()


def gather_rows(nc, src, collective_id):
    n = nc // 2
    return call(functools.partial(gather_ctx_kernel, n), collective_id, (src,), shaped((nc,) + src.shape), gather_ctx_sems(n), "gather_rows")


def swap_kernel(nc, src, out, send, recv, local):
    per = nc // GROUPS
    ctx = lax.axis_index("ctx")
    group, place = ctx // per, ctx % per
    peer = lambda k: lax.rem(group + k, GROUPS)
    device = lambda k: {"ctx": peer(k) * per + place}
    greet([device(k) for k in range(1, GROUPS)])
    own = pltpu.make_async_copy(src.at[group], out.at[group], local)
    own.start()
    copies = []
    for k in range(1, GROUPS):
        copies.append(remote(src.at[peer(k)], out.at[group], send.at[k], recv.at[k], device(k)))
        copies[-1].start()
    for k in range(1, GROUPS):
        arrived(out.at[peer(GROUPS - k)], recv.at[k], device(k))
    own.wait()
    for copy in copies:
        copy.wait_send()


def swap(nc, src, collective_id):
    return call(functools.partial(swap_kernel, nc), collective_id, (src,), shaped(src.shape), [DMA((GROUPS,)), DMA((GROUPS,)), DMA], "swap")


def scatter_ctx_kernel(columns, part, out, acc, from_b, from_col, send, recv, local):
    pos = Place(columns)
    greet([pos.column(k) for k in range(1, columns)] + [pos.flip_b()])
    s = Sends(send)
    drive([scatter_ctx(pos, part, out, acc, from_b, from_col, s, recv, local)])
    s.finish()


def scatter_rows(nc, part, collective_id):
    n = nc // 2
    return pl.pallas_call(
        functools.partial(scatter_ctx_kernel, n),
        out_shape=shaped(part.shape[1:], F32),
        in_specs=[pl.BlockSpec(memory_space=pl.ANY)],
        out_specs=pl.BlockSpec(memory_space=pltpu.VMEM),
        scratch_shapes=scatter_ctx_scratch(n, part.shape[1:]),
        compiler_params=pltpu.CompilerParams(collective_id=collective_id, has_side_effects=True, vmem_limit_bytes=60 << 20),
        name="scatter_rows",
    )(part)


def scatter_end_kernel(columns, gn, wq, wo, ffn, yy, o_gn, o_wq, o_wo, o_ffn, o_yy, *scratch):
    pos = Place(columns)
    greet(all_partners(pos))
    c1, a1, a2, f1, c2 = scratch[0:6], scratch[6:14], scratch[14:22], scratch[22:28], scratch[28:34]
    s = [Sends(x[-3]) for x in (c1, a1, a2, f1, c2)]
    drive(
        [
            scatter_ctx(pos, gn, o_gn, *c1[:-3], s[0], *c1[-2:]),
            scatter_fsdp(pos, [ffn.at[p] for p in range(ffn.shape[0])], o_ffn, *f1[:-3], s[3], *f1[-2:]),
            scatter_all(pos, wq, o_wq, *a1[:-3], s[1], *a1[-2:], per_group=True),
            scatter_all(pos, wo, o_wo, *a2[:-3], s[2], *a2[-2:]),
            scatter_ctx(pos, yy, o_yy, *c2[:-3], s[4], *c2[-2:]),
        ]
    )
    for x in s:
        x.finish()


def scatter_end(nc, gn, wq, wo, ffn, yy):
    n = nc // 2
    scratch = (
        scatter_ctx_scratch(n, gn.shape[1:])
        + scatter_all_scratch(n, wq.shape[1:])
        + scatter_all_scratch(n, wo.shape[1:])
        + scatter_fsdp_scratch(ffn.shape[0], ffn.shape[2:])
        + scatter_ctx_scratch(n, yy.shape[1:])
    )
    outs = (
        shaped(gn.shape[1:], F32),
        shaped((GROUPS,) + wq.shape[1:], F32),
        shaped(wo.shape[1:], F32),
        shaped((ffn.shape[0],) + ffn.shape[2:], F32),
        shaped(yy.shape[1:], F32),
    )
    return call(
        functools.partial(scatter_end_kernel, n), 6, (gn, wq, wo, ffn, yy), outs, scratch, "scatter_end",
        space=pltpu.VMEM, in_space=pl.ANY,
    )


def doc_ids(row_index, doc_ends):
    return jnp.sum((row_index[:, None] >= doc_ends[None, :]).astype(jnp.int32), axis=1)


def positions(row_index, lengths):
    doc_ends = jnp.cumsum(lengths)
    doc_starts = doc_ends - lengths
    doc_num = doc_ids(row_index, doc_ends)
    column = jnp.arange(lengths.shape[0], dtype=jnp.int32)
    begins = jnp.sum(jnp.where(doc_num[:, None] == column[None, :], doc_starts[None, :], 0), axis=1)
    return doc_num, row_index - begins


def rope_tables(position):
    half_dim = HEAD_DIM // 2
    inverse = ROPE_BASE ** (-2.0 * jnp.arange(half_dim, dtype=F32) / HEAD_DIM)
    angles = position.astype(F32)[:, None] * inverse[None, :]
    return jnp.cos(angles), jnp.sin(angles)


def rotate(values, cosine, sine):
    half_dim = values.shape[-1] // 2
    lower, upper = values[..., :half_dim], values[..., half_dim:]
    cosine, sine = cosine[:, None, :], sine[:, None, :]
    return jnp.concatenate([lower * cosine - upper * sine, upper * cosine + lower * sine], axis=-1)


def kept_rows(route_rows, live_rows, experts, capacity):
    count, top = route_rows.shape
    hot = (route_rows[:, :, None] == jnp.arange(experts, dtype=jnp.int32)) & live_rows[:, None, None]
    hot = hot.astype(F32)
    before = jnp.tril(jnp.ones((count, count), F32), -1)
    kept = jnp.zeros((count, experts), F32)
    base = jnp.zeros((1, experts), F32)
    for k in range(top):
        earlier = base + jnp.dot(before, hot[:, k])
        kept = kept + hot[:, k] * (earlier < capacity)
        base = base + jnp.sum(hot[:, k], axis=0, keepdims=True)
    return kept


def pad_rows(x, rows):
    return jnp.pad(x, [(0, rows - x.shape[0])] + [(0, 0)] * (x.ndim - 1))


def body_wide(tokens, doc_lengths, routes, cotangent, attn_gain, w_qkv, w_out, mlp_gain, router, expert_in, expert_out, shared_in, shared_out):
    nc = lax.axis_size("ctx")
    nf = lax.axis_size("fsdp")
    rows, width = tokens.shape[1:]
    heads = width // HEAD_DIM
    experts = expert_in.shape[1]
    hidden = expert_in.shape[0]
    top = routes.shape[2]
    capacity = 5 * top * rows // (4 * experts)
    per = nc // GROUPS
    ctx = lax.axis_index("ctx")
    group, place = ctx // per, ctx % per
    slot = nc * rows
    mine = heads // GROUPS
    share = mine * HEAD_DIM
    scale = 1.0 / math.sqrt(HEAD_DIM)
    owned = w_out.shape[0]
    padded = -(-(owned + 2 + experts) // 16) * 16

    wq_send = w_qkv.reshape(owned, 3, GROUPS, share).transpose(2, 0, 1, 3).reshape(GROUPS, owned, 3 * share)
    wq_send = jnp.pad(wq_send, ((0, 0), (0, padded - owned), (0, 0)))
    small = jnp.concatenate([attn_gain[None], mlp_gain[None], router.T], axis=0)
    wo_send = pad_rows(jnp.concatenate([w_out, jnp.pad(small, ((0, 0), (0, width - owned)))], axis=0), padded)
    gate_up = jnp.concatenate([expert_in.transpose(2, 1, 0, 3), shared_in.transpose(1, 0, 2)[:, None]], axis=1)
    down = jnp.concatenate([expert_out.transpose(1, 0, 2), shared_out[None]], axis=0)
    ffn_send = jnp.concatenate([gate_up, down[None]], axis=0).reshape(3, (experts + 1) * hidden, width)

    x_all, wq_all, wo_all, ffn_all, cot_all = gather_start(nc, tokens[0], wq_send, wo_send, ffn_send, cotangent[0])
    units = nf * (experts + 1) * hidden
    w_gate, w_up, w_down = (ffn_all[p].reshape(units, width) for p in range(3))
    wq = wq_all[:, :owned].reshape(width, 3 * share)
    wo = wo_all[:, :owned].reshape(width, width)
    small = wo_all[:, owned : owned + 2 + experts, :owned].transpose(1, 0, 2).reshape(2 + experts, width)
    gain_a, gain_m = small[0].astype(F32), small[1].astype(F32)
    router_t = small[2:]

    all_rows = jnp.arange(slot, dtype=jnp.int32)
    doc_num, position = positions(all_rows, doc_lengths[0])
    cosine, sine = rope_tables(position)
    live_all = (doc_num < doc_lengths.shape[1]).astype(F32)[:, None]
    x_slot = x_all.reshape(slot, width).astype(F32)
    inv_attn = lax.rsqrt(jnp.mean(x_slot * x_slot, axis=-1, keepdims=True) + EPSILON)
    normed = (x_slot * inv_attn * gain_a).astype(BF)

    def queries(v):
        return lax.dynamic_index_in_dim(v.reshape((GROUPS, per, rows) + v.shape[1:]), place, 1, False).reshape((GROUPS * rows,) + v.shape[1:])

    normed_q = queries(normed)
    cos_q, sin_q = queries(cosine), queries(sine)
    q = rotate(dot(normed_q, wq[:, :share], ((1,), (0,))).reshape(-1, mine, HEAD_DIM), cos_q, sin_q).astype(BF)
    k = rotate(dot(normed, wq[:, share : 2 * share], ((1,), (0,))).reshape(slot, mine, HEAD_DIM), cosine, sine).astype(BF)
    v = dot(normed, wq[:, 2 * share :], ((1,), (0,))).reshape(slot, mine, HEAD_DIM).astype(BF)
    rows_q, doc_q = queries(all_rows), queries(doc_num)
    allowed = (doc_q[:, None] == doc_num[None, :]) & (all_rows[None, :] <= rows_q[:, None])
    scores = jnp.einsum("qhd,khd->hqk", q, k, preferred_element_type=F32) * scale
    scores = jnp.where(allowed[None], scores, MASKED)
    expo = jnp.exp(scores - jnp.max(scores, axis=-1, keepdims=True))
    prob = expo / jnp.sum(expo, axis=-1, keepdims=True)
    prob_b = prob.astype(BF)
    o = jnp.einsum("hqk,khd->qhd", prob_b, v, preferred_element_type=F32).astype(BF)

    o_own = swap(nc, o.reshape(GROUPS, rows, share), 2)
    attn = o_own.transpose(1, 0, 2).reshape(rows, width)

    row_index = ctx * rows + jnp.arange(rows, dtype=jnp.int32)
    doc_own, _ = positions(row_index, doc_lengths[0])
    live_rows = doc_own < doc_lengths.shape[1]
    live = live_rows.astype(F32)[:, None]
    x = tokens[0].astype(F32)
    resid = x + dot(attn, wo, ((1,), (0,)))
    inv_mlp = lax.rsqrt(jnp.mean(resid * resid, axis=-1, keepdims=True) + EPSILON)
    mixed = (resid * inv_mlp * gain_m).astype(BF)
    logits = dot(mixed, router_t, ((1,), (1,)))
    router_prob = jax.nn.softmax(logits, axis=-1)
    kept = kept_rows(routes[0], live_rows, experts, capacity)
    weight = router_prob * kept
    high = weight.astype(BF)
    low = (weight - high.astype(F32)).astype(BF)
    extra = pad_rows(jnp.pad(jnp.concatenate([high, low], axis=1).T, ((0, 0), (0, width - rows))), 16)
    mixed_all = gather_rows(nc, jnp.concatenate([mixed, extra], axis=0), 3)

    weights = mixed_all[:, rows : rows + 2 * experts, :rows].astype(F32)
    weights = (weights[:, :experts] + weights[:, experts:]).transpose(0, 2, 1).reshape(slot, experts)
    mix = mixed_all[:, :rows].reshape(slot, width)
    g = (cot_all.reshape(slot, width) * live_all.astype(BF)).astype(BF)
    unit_weight = jnp.concatenate([weights, jnp.ones((slot, 1), F32)], axis=1)
    unit_weight = jnp.tile(jnp.repeat(unit_weight, hidden, axis=1), (1, nf))
    gate = dot(mix, w_gate, ((1,), (1,)))
    up = dot(mix, w_up, ((1,), (1,)))
    sig = jax.nn.sigmoid(gate)
    hid = gate * sig * up
    hid_w = (hid * unit_weight).astype(BF)
    y_part = dot(hid_w, w_down, ((1,), (0,))).astype(BF)
    back = dot(g, w_down, ((1,), (1,)))
    pair = (hid * back).reshape(slot, nf, experts + 1, hidden).sum(axis=(1, 3))[:, :experts]
    back_w = back * unit_weight
    d_gate = (back_w * up * sig * (1.0 + gate * (1.0 - sig))).astype(BF)
    d_up = (back_w * gate * sig).astype(BF)
    gm_part = (dot(d_gate, w_gate, ((1,), (0,))) + dot(d_up, w_up, ((1,), (0,)))).astype(BF)
    d_w = jnp.stack([dot(d_gate, mix, ((0,), (0,))), dot(d_up, mix, ((0,), (0,))), dot(hid_w, g, ((0,), (0,)))]).astype(BF)
    pair_t = pair.reshape(nc, rows, experts).transpose(0, 2, 1)
    pair_t = jnp.pad(pair_t, ((0, 0), (0, 16 - experts), (0, width - rows))).astype(BF)
    gm_all = scatter_rows(nc, jnp.concatenate([gm_part.reshape(nc, rows, width), pair_t], axis=1), 4)

    grad_prob = gm_all[rows : rows + experts, :rows].T * kept
    grad_logits = (router_prob * (grad_prob - jnp.sum(router_prob * grad_prob, axis=-1, keepdims=True))).astype(BF)
    grad_router_t = dot(grad_logits, mixed, ((0,), (0,)))
    grad_mixed = gm_all[:rows] + dot(grad_logits, router_t, ((1,), (0,)))
    grad_top = cotangent[0].astype(F32) * live
    w = grad_mixed * gain_m
    grad_resid = grad_top + inv_mlp * w - resid * jnp.mean(w * resid, axis=-1, keepdims=True) * inv_mlp**3
    grad_gain_m = jnp.sum(grad_mixed * resid * inv_mlp, axis=0)
    grad_resid_b = grad_resid.astype(BF)
    grad_wo = dot(attn, grad_resid_b, ((0,), (0,)))
    grad_attn = dot(grad_resid_b, wo, ((1,), (1,))).astype(BF)
    do = swap(nc, grad_attn.reshape(rows, GROUPS, share).transpose(1, 0, 2), 5).reshape(GROUPS * rows, mine, HEAD_DIM)

    grad_p = jnp.einsum("qhd,khd->hqk", do, v, preferred_element_type=F32)
    delta = jnp.sum(prob * grad_p, axis=-1, keepdims=True)
    grad_s = (prob * (grad_p - delta)).astype(BF)
    dq = jnp.einsum("hqk,khd->qhd", grad_s, k, preferred_element_type=F32) * scale
    dk = jnp.einsum("hqk,qhd->khd", grad_s, q, preferred_element_type=F32) * scale
    dv = jnp.einsum("hqk,qhd->khd", prob_b, do, preferred_element_type=F32)
    dq = rotate(dq, cos_q, -sin_q).reshape(GROUPS * rows, share).astype(BF)
    dk = rotate(dk, cosine, -sine).reshape(slot, share)
    dkv = jnp.concatenate([dk, dv.reshape(slot, share)], axis=1).astype(BF)
    grad_wq = jnp.concatenate([dot(normed_q, dq, ((0,), (0,))), dot(normed, dkv, ((0,), (0,)))], axis=1)
    gn_q = dot(dq, wq[:, :share], ((1,), (1,))).reshape(GROUPS, 1, rows, width)
    here = (jnp.arange(per) == place).astype(F32)[None, :, None, None]
    gn = dot(dkv, wq[:, share:], ((1,), (1,))).reshape(GROUPS, per, rows, width) + gn_q * here
    gn_part = gn.reshape(nc, rows, width).astype(BF)

    gn_full = gn.reshape(slot, width)
    grad_gain_a = jnp.sum(gn_full * x_slot * inv_attn, axis=0)
    small = jnp.concatenate([grad_gain_a[None], grad_gain_m[None], grad_router_t], axis=0)
    small = small.reshape(2 + experts, nc * nf, owned).transpose(1, 0, 2)
    wo_part = jnp.concatenate([grad_wo.reshape(nc * nf, owned, width), jnp.pad(small, ((0, 0), (0, 0), (0, width - owned)))], axis=1)
    wo_part = jnp.pad(wo_part, ((0, 0), (0, padded - wo_part.shape[1]), (0, 0))).astype(BF)
    wq_part = jnp.pad(grad_wq.reshape(nc * nf, owned, 3 * share), ((0, 0), (0, padded - owned), (0, 0))).astype(BF)
    ffn_part = d_w.reshape(3, nf, (experts + 1) * hidden, width)
    gn_own, wq_own, wo_own, ffn_own, y_own = scatter_end(nc, gn_part, wq_part, wo_part, ffn_part, y_part.reshape(nc, rows, width))

    layer_out = (live * (resid + y_own)).astype(BF)[None]
    inv = lax.rsqrt(jnp.mean(x * x, axis=-1, keepdims=True) + EPSILON)
    w = gn_own * gain_a
    grad_tokens = (grad_resid + inv * w - x * jnp.mean(w * x, axis=-1, keepdims=True) * inv**3)[None]
    grad_w_qkv = wq_own[:, :owned].reshape(GROUPS, owned, 3, share).transpose(1, 2, 0, 3).reshape(owned, 3 * width)
    small = wo_own[owned : owned + 2 + experts, :owned]
    out = ffn_own.reshape(3, experts + 1, hidden, width)
    return (
        layer_out,
        grad_tokens,
        small[0],
        grad_w_qkv,
        wo_own[:owned],
        small[1],
        small[2:].T,
        out[:2, :experts].transpose(2, 1, 0, 3),
        out[2, :experts].transpose(1, 0, 2),
        out[:2, experts].transpose(1, 0, 2),
        out[2, experts],
    )


def body(tokens, doc_lengths, routes, cotangent, attn_gain, w_qkv, w_out, mlp_gain, router, expert_in, expert_out, shared_in, shared_out):
    nc, nf = lax.axis_size("ctx"), lax.axis_size("fsdp")
    rows, width = tokens.shape[1:]
    experts, hidden, top = expert_in.shape[1], expert_in.shape[0], routes.shape[2]
    owned = w_out.shape[0]
    if nc != 2 * GROUPS or 2 * nc * rows * width > FUSED_BYTES:
        return body_wide(
            tokens, doc_lengths, routes, cotangent, attn_gain, w_qkv, w_out, mlp_gain, router, expert_in, expert_out, shared_in, shared_out
        )
    padded = -(-(owned + 8) // 16) * 16
    sz = Sizes(nc, nf, rows, width, experts, hidden, owned, padded, 5 * top * rows // (4 * experts), top, doc_lengths.shape[1])
    share = sz.share
    device = lax.axis_index("ctx") * nf + lax.axis_index("fsdp")

    gain = attn_gain.astype(F32)[:, None]
    wq_send = (w_qkv.astype(F32) * gain).astype(BF).reshape(owned, 3, GROUPS, share).transpose(2, 0, 1, 3).reshape(GROUPS, owned, 3 * share)
    wq_send = jnp.pad(wq_send, ((0, 0), (0, padded - owned), (0, 0)))
    small = jnp.concatenate([attn_gain[None], mlp_gain[None], router.T, jnp.zeros((padded - owned - 2 - experts, owned), BF)], axis=0)
    gate_up = jnp.concatenate([expert_in.transpose(2, 1, 0, 3), shared_in.transpose(1, 0, 2)[:, None]], axis=1)
    down = jnp.concatenate([expert_out.transpose(1, 0, 2), shared_out[None]], axis=0)
    ffn_send = jnp.concatenate([gate_up, down[None]], axis=0).reshape(3, (experts + 1) * hidden, width)

    units = nf * (experts + 1) * hidden
    of = np.arange(units) // hidden % (experts + 1)
    spread = np.zeros((32, units), np.float32)
    for e in range(experts + 1):
        spread[e] = of == e
    for e in range(experts):
        spread[8 + e] = of == e
        spread[16 + e] = of == e

    gm_own, gp_own, y_part, dw, *saved = forward(
        sz, 1, doc_lengths, tokens[0], cotangent[0], routes[0], small, jnp.asarray(spread, BF), wq_send, w_out, ffn_send
    )
    dw = dw.reshape(3, nf, (experts + 1) * hidden, width)
    layer_out, grad_tokens, wq_own, wo_own, grad_in, grad_down = backward(
        sz, 2, doc_lengths, tokens[0], cotangent[0], gm_own, gp_own, y_part, dw, saved
    )

    grad_w = wq_own[:, :owned].reshape(GROUPS, owned, 3, share).transpose(1, 2, 0, 3).reshape(owned, 3 * width)
    gain_a = jnp.sum(grad_w * w_qkv.astype(F32), axis=1)
    grad_w_qkv = grad_w * gain
    small = lax.dynamic_slice(wo_own[owned:], (0, device * owned), (2 + experts, owned))
    grad_in = grad_in.reshape(2, experts + 1, hidden, width)
    grad_down = grad_down.reshape(experts + 1, hidden, width)
    return (
        layer_out[None],
        grad_tokens[None],
        gain_a,
        grad_w_qkv,
        wo_own[:owned],
        small[1],
        small[2:].T,
        grad_in[:, :experts].transpose(2, 1, 0, 3),
        grad_down[:experts].transpose(1, 0, 2),
        grad_in[:, experts].transpose(1, 0, 2),
        grad_down[experts],
    )


def solution(mesh):
    rows = P("fsdp", "ctx", None)
    flat = ("ctx", "fsdp")
    weights = (P(flat), P(flat, None), P(flat, None), P(flat), P(flat, None))
    ffn = (P(flat, None, None, None), P(flat, None, None), P(flat, None, None), P(flat, None))
    return jax.shard_map(
        body,
        mesh=mesh,
        in_specs=(rows, P("fsdp", None), rows, rows) + weights + ffn,
        out_specs=(rows, rows) + weights + ffn,
        check_vma=False,
    )
```

```python
import functools
import math

import jax
import jax.numpy as jnp
import numpy as np
from jax import lax
from jax.experimental import pallas as pl
from jax.experimental.pallas import tpu as pltpu
from jax.sharding import PartitionSpec as P

HEAD_DIM = 64
EPSILON = 1e-05
ROPE_BASE = 10000.0
MASKED = -1e30
NN, NT, TN = ((1,), (0,)), ((1,), (1,)), ((0,), (0,))
FUSED_BYTES = 2 << 20
GROUPS = 4
MESH = pl.DeviceIdType.MESH
DMA = pltpu.SemaphoreType.DMA
BF = jnp.bfloat16
F32 = jnp.float32


class Place:
    def __init__(self, columns, balanced=True):
        ctx, fsdp = lax.axis_index("ctx"), lax.axis_index("fsdp")
        self.columns = columns
        self.a, self.b = ctx // 2, ctx % 2
        self.y, self.c = fsdp // 2, fsdp % 2
        flip_b = (1 - self.b, self.y)
        flip_y = (self.b, 1 - self.y)
        core = (self.c == 0) if balanced else (self.c >= 0)
        self.first = tuple(jnp.where(core, p, q) for p, q in zip(flip_b, flip_y))
        self.second = tuple(jnp.where(core, q, p) for p, q in zip(flip_b, flip_y))
        self.plane = [(self.b, self.y), self.first, self.second, (1 - self.b, 1 - self.y)]
        self.sib_plane = [(self.b, self.y), self.second, self.first, (1 - self.b, 1 - self.y)]

    def at(self, step):
        return lax.rem(self.a + step, self.columns)

    def device(self, a=None, plane=None, c=None):
        b, y = plane if plane is not None else (self.b, self.y)
        a = self.a if a is None else a
        c = self.c if c is None else c
        return {"ctx": a * 2 + b, "fsdp": y * 2 + c}

    def column(self, step):
        return self.device(a=self.at(step))

    def flip_b(self):
        return self.device(plane=(1 - self.b, self.y))

    def flip_y(self):
        return self.device(plane=(self.b, 1 - self.y))

    def sibling(self):
        return self.device(c=1 - self.c)

    def chunk(self, step, plane, c):
        return (self.at(step) * 2 + plane[0]) * 4 + plane[1] * 2 + c


def greet(devices):
    barrier = pltpu.get_barrier_semaphore()
    for device in devices:
        pl.semaphore_signal(barrier, inc=1, device_id=device, device_id_type=MESH)
    pl.semaphore_wait(barrier, len(devices))


def remote(src, dst, send, recv, device):
    return pltpu.make_async_remote_copy(
        src_ref=src, dst_ref=dst, send_sem=send, recv_sem=recv, device_id=device, device_id_type=MESH
    )


class Sends:
    def __init__(self, sems):
        self.sems, self.made = sems, []

    def start(self, src, dst, recv, device):
        copy = remote(src, dst, self.sems.at[len(self.made)], recv, device)
        copy.start()
        self.made.append(copy)

    def finish(self):
        for copy in self.made:
            copy.wait_send()


def arrived(dst, recv, device):
    remote(dst, dst, recv, recv, device).wait_recv()


def gather_ctx(pos, src, out, sends, recv, local, there=lambda slot: None):
    n = pos.columns
    me = pos.a * 2 + pos.b
    own = pltpu.make_async_copy(src, out.at[me], local)
    own.start()
    for k in range(1, n):
        sends.start(src, out.at[me], recv.at[k], pos.column(k))
    sends.start(src, out.at[me], recv.at[n], pos.flip_b())
    yield
    own.wait()
    there(me)
    for k in range(1, n):
        slot = pos.at(n - k) * 2 + pos.b
        arrived(out.at[slot], recv.at[k], pos.column(k))
        sends.start(out.at[slot], out.at[slot], recv.at[n + k], pos.flip_b())
        there(slot)
        yield
    for k in range(n):
        slot = pos.at(n - k) * 2 + 1 - pos.b
        arrived(out.at[slot], recv.at[n + k], pos.flip_b())
        there(slot)
        yield


def gather_ctx_sems(n):
    return [DMA((2 * n,)), DMA((2 * n,)), DMA]


def gather_fsdp(pos, src, out, sends, recv, local):
    parts = src.shape[0]
    if len(out.shape) == 3:
        out = [out.at[p] for p in range(parts)]
        at = lambda p, f: out[p].at[pl.ds(pl.multiple_of(f * src.shape[1], src.shape[1]), src.shape[1])]
    else:
        at = lambda p, f: out.at[p, f]
    me = pos.y * 2 + pos.c
    other = (1 - pos.y) * 2 + pos.c
    own = []
    for p in range(parts):
        own.append(pltpu.make_async_copy(src.at[p], at(p, me), local.at[p]))
        own[-1].start()
        sends.start(src.at[p], at(p, me), recv.at[p], pos.flip_y())
    for p in range(parts):
        sends.start(src.at[p], at(p, me), recv.at[parts + p], pos.sibling())
    yield
    for p in range(parts):
        arrived(at(p, pos.y * 2 + 1 - pos.c), recv.at[parts + p], pos.sibling())
        own[p].wait()
    yield
    for p in range(parts):
        arrived(at(p, other), recv.at[p], pos.flip_y())
        sends.start(at(p, other), at(p, other), recv.at[2 * parts + p], pos.sibling())
        yield
    for p in range(parts):
        arrived(at(p, (1 - pos.y) * 2 + 1 - pos.c), recv.at[2 * parts + p], pos.sibling())


def gather_fsdp_sems(parts):
    return [DMA((3 * parts,)), DMA((3 * parts,)), DMA((parts,))]


def gather_all(pos, src, out, sends, recv, local, group_of=None):
    n = pos.columns
    me = pos.chunk(0, pos.plane[0], pos.c)
    part = (lambda a: src) if group_of is None else (lambda a: src.at[group_of(a)])
    mine = part(pos.a)
    own = pltpu.make_async_copy(mine, out.at[me], local)
    own.start()
    first, second = pos.device(plane=pos.first), pos.device(plane=pos.second)
    sibling = pos.sibling()
    for k in range(1, n):
        sends.start(part(pos.at(k)), out.at[me], recv.at[k], pos.column(k))
    sends.start(mine, out.at[me], recv.at[n], first)
    sends.start(mine, out.at[me], recv.at[2 * n], second)
    sends.start(mine, out.at[me], recv.at[4 * n], sibling)
    yield
    for k in range(1, n):
        slot = pos.chunk(n - k, pos.plane[0], pos.c)
        arrived(out.at[slot], recv.at[k], first)
        sends.start(out.at[slot], out.at[slot], recv.at[n + k], first)
        sends.start(out.at[slot], out.at[slot], recv.at[2 * n + k], second)
        sends.start(out.at[slot], out.at[slot], recv.at[4 * n + k], sibling)
        yield
    for k in range(n):
        slot = pos.chunk(n - k, pos.first, pos.c)
        arrived(out.at[slot], recv.at[n + k], first)
        sends.start(out.at[slot], out.at[slot], recv.at[3 * n + k], second)
        sends.start(out.at[slot], out.at[slot], recv.at[5 * n + k], sibling)
        yield
    for r in range(2):
        for k in range(n):
            slot = pos.chunk(n - k, pos.plane[2 + r], pos.c)
            arrived(out.at[slot], recv.at[(2 + r) * n + k], second)
            sends.start(out.at[slot], out.at[slot], recv.at[(6 + r) * n + k], sibling)
            yield
    own.wait()
    for r in range(4):
        for k in range(n):
            slot = pos.chunk(n - k, pos.sib_plane[r], 1 - pos.c)
            arrived(out.at[slot], recv.at[(4 + r) * n + k], sibling)


def gather_all_sems(n):
    return [DMA((8 * n,)), DMA((8 * n,)), DMA]


def drive(streams):
    streams = list(streams)
    while streams:
        for stream in list(streams):
            if next(stream, streams) is streams:
                streams.remove(stream)


def all_partners(pos):
    return [pos.column(k) for k in range(1, pos.columns)] + [pos.flip_b(), pos.flip_y(), pos.sibling()]


def shaped(shape, dtype=BF):
    return jax.ShapeDtypeStruct(tuple(shape), dtype)


def dot(a, b, dims):
    return lax.dot_general(a, b, (dims, ((), ())), preferred_element_type=F32)


def add(acc, *others):
    total = acc[...].astype(F32)
    for other in others:
        total = total + other[...].astype(F32)
    acc[...] = total.astype(acc.dtype)


def scatter_ctx(pos, part, out, acc, from_b, from_col, sends, recv, local):
    n = pos.columns
    loads = []
    for k in range(n):
        loads.append(pltpu.make_async_copy(part.at[pos.at(k) * 2 + pos.b], acc.at[k], local.at[k]))
        loads[-1].start()
    for k in [*range(1, n), 0]:
        sends.start(part.at[pos.at(k) * 2 + 1 - pos.b], from_b.at[k], recv.at[k], pos.flip_b())
    yield
    for k in [*range(1, n), 0]:
        loads[k].wait()
        arrived(from_b.at[k], recv.at[k], pos.flip_b())
        if k:
            add(acc.at[k], from_b.at[k])
            sends.start(acc.at[k], from_col.at[k], recv.at[n + k], pos.column(k))
            yield
    total = acc[0].astype(F32) + from_b[0].astype(F32)
    for k in range(1, n):
        arrived(from_col.at[k], recv.at[n + k], pos.column(k))
        total = total + from_col[k].astype(F32)
        yield
    out[...] = total.astype(out.dtype)


def scatter_ctx_scratch(n, shape):
    v = lambda m: pltpu.VMEM((m,) + tuple(shape), BF)
    return [v(n), v(n), v(n), DMA((2 * n,)), DMA((2 * n,)), DMA((n,))]


def scatter_fsdp(pos, part, out, acc, from_sib, from_y, sends, recv, local):
    parts = len(part)
    loads = []
    mine = [(1 - pos.y) * 2 + pos.c, pos.y * 2 + pos.c]
    his = [(1 - pos.y) * 2 + 1 - pos.c, pos.y * 2 + 1 - pos.c]
    for t in range(2):
        for p in range(parts):
            i = t * parts + p
            loads.append(pltpu.make_async_copy(part[p].at[mine[t]], acc.at[i], local.at[i]))
            loads[-1].start()
            sends.start(part[p].at[his[t]], from_sib.at[i], recv.at[i], pos.sibling())
    yield
    for p in range(parts):
        loads[p].wait()
        arrived(from_sib.at[p], recv.at[p], pos.sibling())
        add(acc.at[p], from_sib.at[p])
        sends.start(acc.at[p], from_y.at[p], recv.at[2 * parts + p], pos.flip_y())
        yield
    for p in range(parts):
        loads[parts + p].wait()
        arrived(from_sib.at[parts + p], recv.at[parts + p], pos.sibling())
        add(acc.at[parts + p], from_sib.at[parts + p])
        yield
    for p in range(parts):
        arrived(from_y.at[p], recv.at[2 * parts + p], pos.flip_y())
        out[p] = acc[parts + p].astype(F32) + from_y[p].astype(F32)
        yield


def scatter_fsdp_scratch(parts, shape):
    v = lambda m: pltpu.VMEM((m,) + tuple(shape), BF)
    return [v(2 * parts), v(2 * parts), v(parts), DMA((3 * parts,)), DMA((3 * parts,)), DMA((2 * parts,))]


def scatter_all(pos, part, out, acc, from_sib, from_2, from_1, from_col, sends, recv, local, per_group=False):
    n = pos.columns
    sibling = pos.sibling()
    first, second = pos.device(plane=pos.first), pos.device(plane=pos.second)
    loads = {}
    for r in (3, 2, 1, 0):
        for k in range(n):
            i = r * n + k
            loads[i] = pltpu.make_async_copy(part.at[pos.chunk(k, pos.plane[r], pos.c)], acc.at[i], local.at[i])
            loads[i].start()
            sends.start(part.at[pos.chunk(k, pos.sib_plane[r], 1 - pos.c)], from_sib.at[i], recv.at[i], sibling)
    yield
    for r in (3, 2):
        for k in range(n):
            i = r * n + k
            loads[i].wait()
            arrived(from_sib.at[i], recv.at[i], sibling)
            add(acc.at[i], from_sib.at[i])
            j = (r - 2) * n + k
            sends.start(acc.at[i], from_2.at[j], recv.at[4 * n + j], second)
        yield
    for k in range(n):
        i = n + k
        loads[i].wait()
        arrived(from_sib.at[i], recv.at[i], sibling)
        arrived(from_2.at[i], recv.at[4 * n + i], second)
        add(acc.at[i], from_sib.at[i], from_2.at[i])
        sends.start(acc.at[i], from_1.at[k], recv.at[6 * n + k], first)
    yield
    for k in [*range(1, n), 0]:
        loads[k].wait()
        arrived(from_sib.at[k], recv.at[k], sibling)
        arrived(from_2.at[k], recv.at[4 * n + k], second)
        arrived(from_1.at[k], recv.at[6 * n + k], first)
        if k:
            add(acc.at[k], from_sib.at[k], from_2.at[k], from_1.at[k])
            sends.start(acc.at[k], from_col.at[k], recv.at[7 * n + k], pos.column(k))
    total = acc[0].astype(F32) + from_sib[0].astype(F32) + from_2[0].astype(F32) + from_1[0].astype(F32)
    yield
    if not per_group:
        for k in range(1, n):
            arrived(from_col.at[k], recv.at[7 * n + k], pos.column(k))
            total = total + from_col[k].astype(F32)
        out[...] = total
        return
    each = n // GROUPS
    for k in range(1, n):
        arrived(from_col.at[k], recv.at[7 * n + k], pos.column(k))
    out[...] = jnp.zeros_like(out)
    for k in range(n):
        value = total if k == 0 else from_col[k].astype(F32)
        group = pos.at(n - k) // each
        out[group] = out[group] + value


def scatter_all_scratch(n, shape):
    v = lambda m: pltpu.VMEM((m,) + tuple(shape), BF)
    return [v(4 * n), v(4 * n), v(2 * n), v(n), v(n), DMA((8 * n,)), DMA((8 * n,)), DMA((4 * n,))]


class GatherLine:
    def __init__(self, pos, bufs, send, recv, parts=2):
        self.pos, self.bufs, self.send, self.recv, self.parts = pos, bufs, send, recv, parts
        self.made = []

    def cut(self, ref, p):
        rows = ref.shape[0] // self.parts
        return ref.at[pl.ds(p * rows, rows)]

    def copy(self, i, p, src, a, kind, device):
        out = self.bufs[i][1]
        n = self.pos.columns
        dst = self.cut(out.at[2 * a + self.pos.b], p)
        at = ((i * 2 + kind) * n + a) * self.parts + p
        made = remote(dst if src is None else self.cut(src, p), dst, self.send.at[len(self.made)], self.recv.at[at], device)
        return made

    def go(self, i, p, src, a, kind, device, when=None):
        made = self.copy(i, p, src, a, kind, device)
        self.made.append((made, when))
        if when is None:
            made.start()
        else:
            pl.when(when)(made.start)

    def start(self):
        pos, n = self.pos, self.pos.columns
        up, down = pos.device(a=jnp.minimum(pos.a + 1, n - 1)), pos.device(a=jnp.maximum(pos.a - 1, 0))
        self.up, self.down = up, down
        for p in range(self.parts):
            for i, (src, _) in enumerate(self.bufs):
                self.go(i, p, src, pos.a, 0, up, pos.a < n - 1)
                self.go(i, p, src, pos.a, 0, down, pos.a > 0)
                self.go(i, p, src, pos.a, 1, pos.flip_b())

    def here(self, i, p, a, kind, device):
        b = self.pos.b if kind == 0 else 1 - self.pos.b
        out = self.bufs[i][1]
        at = ((i * 2 + kind) * self.pos.columns + a) * self.parts + p
        arrived(self.cut(out.at[2 * a + b], p), self.recv.at[at], device)

    def relay(self, d):
        pos, n = self.pos, self.pos.columns
        for p in range(self.parts):
            for sign, device, end in ((-1, self.up, pos.a < n - 1), (1, self.down, pos.a > 0)):
                a = pos.a + sign * d
                there = (a >= 0) & (a < n)
                a = jnp.clip(a, 0, n - 1)
                for i in range(len(self.bufs)):
                    pl.when(there)(functools.partial(self.here, i, p, a, 0, device))
                    if d < n - 1:
                        self.go(i, p, None, a, 0, device, there & end)
                    self.go(i, p, None, a, 1, pos.flip_b(), there)

    def across(self, a):
        for p in range(self.parts):
            for i in range(len(self.bufs)):
                self.here(i, p, a, 1, self.pos.flip_b())

    def finish(self):
        for made, when in self.made:
            if when is None:
                made.wait_send()
            else:
                pl.when(when)(made.wait_send)


def gather_line_sems(n, bufs=1, parts=2):
    return [DMA((parts * bufs * (3 + 4 * (n - 1)),)), DMA((2 * bufs * n * parts,))]


def gather_tree(pos, src, out, sends, recv, local, group_of=None):
    n = pos.columns
    b, y = pos.plane[0]
    part = (lambda a: src) if group_of is None else (lambda a: src.at[group_of(a)])
    first, second, sibling = pos.device(plane=pos.first), pos.device(plane=pos.second), pos.sibling()
    mine = out.at[pos.c, b, y, pos.a]
    own = pltpu.make_async_copy(part(pos.a), mine, local)
    own.start()
    for k in range(1, n):
        sends.start(part(pos.at(k)), mine, recv.at[k], pos.column(k))
    yield
    for k in range(1, n):
        arrived(out.at[pos.c, b, y, pos.at(n - k)], recv.at[k], first)
    own.wait()
    column = out.at[pos.c, b, y]
    sends.start(column, column, recv.at[n], first)
    sends.start(column, column, recv.at[n + 1], second)
    yield
    column = out.at[pos.c, pos.first[0], pos.first[1]]
    arrived(column, recv.at[n], first)
    sends.start(column, column, recv.at[n + 2], second)
    yield
    for r in range(2):
        arrived(out.at[pos.c, pos.plane[2 + r][0], pos.plane[2 + r][1]], recv.at[n + 1 + r], second)
    sends.start(out.at[pos.c], out.at[pos.c], recv.at[n + 3], sibling)
    yield
    arrived(out.at[1 - pos.c], recv.at[n + 3], sibling)


def gather_tree_sems(n):
    return [DMA((n + 4,)), DMA((n + 4,)), DMA]


def scatter_tree(pos, part, out, from_sib, from_2, from_1, from_col, sends, recv, per_group=False):
    n = pos.columns
    c = pos.c
    first, second, sibling = pos.device(plane=pos.first), pos.device(plane=pos.second), pos.sibling()
    sends.start(part.at[1 - c], from_sib, recv.at[0], sibling)
    yield
    arrived(from_sib, recv.at[0], sibling)
    at = lambda r: (c, pos.plane[r][0], pos.plane[r][1])
    sib = lambda r: (pos.plane[r][0], pos.plane[r][1])
    for r in (3, 2):
        part[at(r)] = (part[at(r)].astype(F32) + from_sib[sib(r)].astype(F32)).astype(BF)
        sends.start(part.at[at(r)], from_2.at[r - 2], recv.at[1 + r - 2], second)
    yield
    arrived(from_2.at[1], recv.at[2], second)
    part[at(1)] = (part[at(1)].astype(F32) + from_sib[sib(1)].astype(F32) + from_2[1].astype(F32)).astype(BF)
    sends.start(part.at[at(1)], from_1, recv.at[3], first)
    arrived(from_2.at[0], recv.at[1], second)
    yield
    arrived(from_1, recv.at[3], first)
    total = part[at(0)].astype(F32) + from_sib[sib(0)].astype(F32) + from_2[0].astype(F32) + from_1[...].astype(F32)
    part[at(0)] = total.astype(BF)
    mine = part.at[at(0)]
    for k in range(1, n):
        sends.start(mine.at[pos.at(k)], from_col.at[k], recv.at[3 + k], pos.column(k))
    yield
    total = mine[pos.a].astype(F32)
    if per_group:
        out[pos.a // (n // GROUPS)] = total
    for k in range(1, n):
        arrived(from_col.at[k], recv.at[3 + k], pos.column(k))
        if per_group:
            out[pos.at(n - k) // (n // GROUPS)] = from_col[k].astype(F32)
        else:
            total = total + from_col[k].astype(F32)
    if not per_group:
        out[...] = total
    sends.finish()


def scatter_tree_scratch(n, shape):
    v = lambda *lead: pltpu.VMEM(lead + tuple(shape), BF)
    return [v(2, 2, n), v(2, n), v(n), v(n), DMA((n + 4,)), DMA((n + 4,))]


class SumCtx:
    def __init__(self, pos, parts, send, recv):
        self.pos, self.parts, self.send, self.recv = pos, parts, send, recv

    def copies(self, a, way):
        pos, n = self.pos, self.pos.columns
        for i, (part, from_b, from_col) in enumerate(self.parts):
            base = 2 * n * i
            if way == "b":
                yield remote(part.at[2 * a + 1 - pos.b], from_b.at[a], self.send.at[base + a], self.recv.at[base + a], pos.flip_b())
            else:
                device = pos.device(a=a)
                yield remote(part.at[2 * a + pos.b], from_col.at[pos.a], self.send.at[base + n + a], self.recv.at[base + n + pos.a], device)

    def push(self, a):
        for copy in self.copies(a, "b"):
            copy.start()

    def pass_on(self, a, other=None):
        pos = self.pos
        for copy, (part, from_b, _) in zip(self.copies(a, "b"), self.parts):
            copy.wait_recv()

        def send():
            for copy, (part, from_b, _) in zip(self.copies(a, "column"), self.parts):
                at = 2 * a + pos.b
                part[at] = (part[at].astype(F32) + from_b[a].astype(F32)).astype(BF)
                copy.start()

        if other is None:
            pl.when(a != pos.a)(send)
        elif other:
            send()

    def total(self):
        pos, n = self.pos, self.pos.columns
        sums = []
        for i, (part, from_b, from_col) in enumerate(self.parts):
            total = part[2 * pos.a + pos.b].astype(F32) + from_b[pos.a].astype(F32)
            for k in range(1, n):
                a = pos.at(k)
                sem = self.recv.at[2 * n * i + n + a]
                arrived(from_col.at[a], sem, pos.column(k))
                total = total + from_col[a].astype(F32)
            sums.append(total)
        return sums

    def finish(self):
        pos, n = self.pos, self.pos.columns
        for a in range(n):
            for copy in self.copies(a, "b"):
                copy.wait_send()
        for k in range(1, n):
            for copy in self.copies(pos.at(k), "column"):
                copy.wait_send()


def sum_ctx_scratch(n, *shapes):
    v = lambda shape: pltpu.VMEM((n,) + tuple(shape), BF)
    out = []
    for shape in shapes:
        out += [v(shape), v(shape)]
    return out + [DMA((2 * n * len(shapes),)), DMA((2 * n * len(shapes),))]


class Sizes:
    def __init__(self, nc, nf, rows, width, experts, hidden, owned, padded, capacity, top, docs):
        self.nc, self.nf, self.rows, self.width = nc, nf, rows, width
        self.experts, self.hidden, self.owned, self.padded = experts, hidden, owned, padded
        self.capacity, self.top, self.docs = capacity, top, docs
        self.columns, self.per = nc // 2, nc // GROUPS
        self.heads = width // HEAD_DIM // GROUPS
        self.share = self.heads * HEAD_DIM
        self.slot = nc * rows
        self.all = nc * nf


def scalars(sz, lengths):
    sizes = [lengths[0, d] for d in range(sz.docs)]
    ends, total = [], 0
    for size in sizes:
        total = total + size
        ends.append(total)
    return sizes, ends


def starts(index, sizes, ends):
    low = jnp.zeros_like(index)
    for size, end in zip(sizes, ends):
        low = low + jnp.where(index >= end, size, 0)
    return low


def iota(shape, dim):
    return lax.broadcasted_iota(jnp.int32, shape, dim)


def mean_square(x, width):
    return jnp.sum(x * x, axis=-1, keepdims=True) * (1.0 / width)


def turn(value, cosine, sine):
    half = HEAD_DIM // 2
    lower, upper = value[:half], value[half:]
    return jnp.concatenate([lower * cosine - upper * sine, upper * cosine + lower * sine], axis=0)


def head(h):
    return slice(h * HEAD_DIM, (h + 1) * HEAD_DIM)


def blk(index, rows):
    return pl.ds(pl.multiple_of(index * rows, rows), rows)


class Copies:
    def __init__(self, sems):
        self.sems, self.made = sems, []

    def start(self, src, dst):
        self.made.append(pltpu.make_async_copy(src, dst, self.sems.at[len(self.made)]))
        self.made[-1].start()

    def finish(self):
        for copy in self.made:
            copy.wait()


def swap_send(sz, group, place, src, out, sends, recv, local, h):
    @pl.when(h == group)
    def _():
        pltpu.make_async_copy(src.at[h], out.at[h], local).start()

    copy = remote(src.at[h], out.at[group], sends.at[h], recv.at[group], {"ctx": h * sz.per + place})

    @pl.when(h != group)
    def _():
        copy.start()


def swap_wait(sz, group, place, src, out, sends, recv, local):
    for h in range(GROUPS):
        copy = remote(src.at[h], out.at[h], sends.at[h], recv.at[h], {"ctx": h * sz.per + place})

        @pl.when(h == group)
        def _():
            pltpu.make_async_copy(src.at[h], out.at[h], local).wait()

        @pl.when(h != group)
        def _():
            copy.wait_send()
            copy.wait_recv()


def scatter_owner(pos, part, outs, stage, from_sib, from_y, sends, recv, local):
    parts = len(outs)
    rows = outs[0].shape[0]
    of = lambda p, y, c: part.at[p, blk(y * 2 + c, rows)]
    for t, y in enumerate((1 - pos.y, pos.y)):
        for p in range(parts):
            sends.start(of(p, y, 1 - pos.c), from_sib.at[t, p], recv.at[t * parts + p], pos.sibling())
        yield
    for t, y in enumerate((1 - pos.y, pos.y)):
        for p in range(parts):
            arrived(from_sib.at[t, p], recv.at[t * parts + p], pos.sibling())
            mine = of(p, y, pos.c)
            mine[...] = (mine[...].astype(F32) + from_sib[t, p].astype(F32)).astype(BF)
            if t == 0:
                sends.start(mine, from_y.at[p], recv.at[2 * parts + p], pos.flip_y())
        yield
    copies = []
    for p in range(parts):
        arrived(from_y.at[p], recv.at[2 * parts + p], pos.flip_y())
        if p > 1:
            copies[p - 2].wait()
        held = stage.at[pl.ds(p % 2 * rows, rows)]
        held[...] = of(p, pos.y, pos.c)[...].astype(F32) + from_y[p].astype(F32)
        copies.append(pltpu.make_async_copy(held, outs[p], local.at[p]))
        copies[p].start()
        yield
    for copy in copies[-2:]:
        copy.wait()
    sends.finish()


def scatter_owner_scratch(parts, shape):
    v = lambda *lead: pltpu.VMEM(lead + tuple(shape), BF)
    return [v(2, parts), v(parts), DMA((3 * parts,)), DMA((3 * parts,)), DMA((parts,))]


def step(*streams):
    for stream in streams:
        next(stream, None)


def layer_kernel(
    sz, lengths, tokens, cot, routes, small_own, spread, wq_send, wo_own, ffn_send,
    o_out, o_tokens, o_wq, o_wo, o_in, o_down,
    x_all, wq_all, wo_all, wo_send, stage, wt, wo, small, normed, qt, kt, vt, prob, o_send, attn, resid, table,
    g_all, mix_all, cw_all, ffn_w, hw, dg, du, gm_part, gp_part, dw,
    do_send, do, dkt, dvt, dqt_b, dkvt_b,
    *sems,
):
    pos, pos_b = Place(sz.columns), Place(sz.columns, balanced=False)
    ctx = lax.axis_index("ctx")
    group, place = ctx // sz.per, ctx % sz.per
    rows, width, share, n = sz.rows, sz.width, sz.share, sz.columns
    sizes, ends = scalars(sz, lengths)
    group_of = lambda a: a // (n // GROUPS)

    owned = sz.owned
    me = ctx * sz.nf + lax.axis_index("fsdp")
    place_of = (iota((owned, width), 1) == me * owned + iota((owned, width), 0)).astype(BF)
    wo_send[:owned, :] = wo_own[...]
    wo_send[owned:, :] = dot(small_own[...], place_of, NN).astype(BF)

    greet(all_partners(pos))
    s = [Sends(sems[3 * i]) for i in range(3)]
    r = lambda i: (sems[3 * i + 1], sems[3 * i + 2])
    swap_sems, swap_back = sems[9:12], sems[12:15]
    gm_sum = SumCtx(pos, [(gm_part, sems[27], sems[28]), (gp_part, sems[29], sems[30])], sems[31], sems[32])
    gn_part, wq_part, wo_part, y_part = x_all, wq_all, wo_all, gm_part
    y_sum = SumCtx(pos, [(y_part, sems[33], sems[34])], sems[35], sems[36])
    gn_sum = SumCtx(pos, [(gn_part, sems[37], sems[38])], sems[39], sems[40])
    t_wq, t_wo, t_ffn = sems[41:47], sems[47:53], sems[53:58]
    toks = GatherLine(pos, [(tokens, x_all)], sems[15], sems[16])
    cots = GatherLine(pos, [(None, g_all)], sems[17], sems[18])
    mixes = GatherLine(pos, [(None, mix_all)], sems[19], sems[20])
    weights = GatherLine(pos, [(None, cw_all)], sems[21], sems[22], parts=1)

    wqs = gather_tree(pos_b, wq_send, wq_all, s[0], *r(0), group_of=group_of)
    wos = gather_tree(pos_b, wo_send, wo_all, s[1], *r(1))
    ffn = gather_fsdp(pos, ffn_send, ffn_w, s[2], *r(2))
    next(wqs)
    toks.start()
    next(wos)
    x_all[ctx] = tokens[...]

    own_rows = ctx * rows + iota((rows, 1), 0)
    live = own_rows < ends[-1]
    g_all[ctx] = jnp.where(live, cot[...].astype(F32), 0.0).astype(BF)
    index = iota((1, sz.slot), 1)
    position = index - jnp.where(index < ends[-1], starts(index, sizes, ends), 0)
    half = HEAD_DIM // 2
    inverse = jnp.exp(iota((half, 1), 0).astype(F32) * (-2.0 * math.log(ROPE_BASE) / HEAD_DIM))
    angles = position.astype(F32) * inverse
    table[0] = jnp.cos(angles)
    table[1] = jnp.sin(angles)
    before = (iota((rows, rows), 0) < iota((rows, rows), 1)).astype(BF)
    same = (iota((rows, rows), 0) == iota((rows, rows), 1)).astype(BF)
    base = jnp.zeros((8, 1), F32)
    kept = jnp.zeros((8, rows), F32)
    for k in range(sz.top):
        hot = ((iota((rows, 8), 1) == routes[:, k : k + 1]) & live).astype(BF)
        earlier = base + dot(hot, before, TN)
        hot = dot(hot, same, TN)
        kept = kept + jnp.where(earlier < sz.capacity, hot, 0.0)
        base = base + jnp.sum(hot, axis=1, keepdims=True)
    step(wqs, wos)
    toks.relay(1)
    step(wqs, wos)
    toks.relay(2)
    step(wqs, wos)
    next(ffn)
    toks.relay(3)
    cots.start()
    for k in range(n):
        toks.across(k)
    drive([wqs])

    def packed(h_):
        each = sz.per * rows
        return slice(each * h_ * (h_ + 1) // 2, each * (h_ + 1) * (h_ + 2) // 2)

    def spot(i):
        a_b, y_c = divmod(i, sz.nf)
        return y_c % 2, a_b % 2, y_c // 2, a_b // 2

    for i in range(sz.all):
        stage[i * owned : (i + 1) * owned, : 3 * share] = wq_all[spot(i)][:owned, :].astype(F32)
    wt[...] = stage[:, : 3 * share].T.astype(BF)
    for d in range(sz.nc):
        x = x_all[d].astype(F32)
        inv = lax.rsqrt(mean_square(x, width) + EPSILON)
        normed[d] = (x * inv).astype(BF)
        part = slice(d * rows, (d + 1) * rows)
        kv = dot(wt[share:, :], normed[d], NT)
        for h in range(sz.heads):
            kt[head(h), part] = turn(kv[head(h)], table[0, :, part], table[1, :, part]).astype(BF)
        vt[:, part] = kv[share:].astype(BF)

    for h_ in reversed(range(GROUPS)):
        d = h_ * sz.per + place
        part = blk(d, rows)
        qq = dot(wt[:share, :], normed[d], NT)
        keys = (h_ + 1) * sz.per * rows
        index = d * rows + iota((rows, 1), 0)
        low = starts(index, sizes, ends)
        key = iota((rows, keys), 1)
        allowed = (key >= low) & (key <= index)
        for h in range(sz.heads):
            q = turn(qq[head(h)], table[0, :, part], table[1, :, part]).astype(BF) * BF(1.0 / math.sqrt(HEAD_DIM))
            qt[h_, head(h), :] = q
            score = jnp.where(allowed, dot(q, kt[head(h), :keys], TN), MASKED)
            expo = jnp.exp(score - jnp.max(score, axis=1, keepdims=True))
            p = (expo * (1.0 / jnp.sum(expo, axis=1, keepdims=True))).astype(BF)
            prob[h, :, packed(h_)] = p
            o_send[h_, head(h), :] = dot(vt[head(h), :keys], p, NT).astype(BF)
        swap_send(sz, group, place, o_send, attn, *swap_sems, h_)
        if h_ == 3:
            cots.relay(1)
        if h_ == 1:
            cots.relay(2)
    swap_wait(sz, group, place, o_send, attn, *swap_sems)
    cots.relay(3)
    drive([wos])
    for i in range(sz.all):
        stage[i * owned : (i + 1) * owned, :] = wo_all[spot(i)][:owned, :].astype(F32)
    extra = wo_all[spot(0)][owned:, :].astype(F32)
    for i in range(1, sz.all):
        extra = extra + wo_all[spot(i)][owned:, :].astype(F32)
    small[...] = extra[:8]
    gain_m = small[1:2, :]
    wo[...] = stage[...].astype(BF)

    attn_t = attn[...].reshape(width, rows)
    res = tokens[...].astype(F32) + dot(attn_t, wo[...], TN)
    resid[...] = res
    inv = lax.rsqrt(mean_square(res, width) + EPSILON)
    mixed = (res * inv * gain_m).astype(BF)
    mix_all[ctx] = mixed
    row = iota((8, rows), 0)
    logits = dot(small[...].astype(BF), mixed, NT)
    logits = jnp.concatenate([logits[2:], logits[:2]], axis=0)
    logits = jnp.where(row < sz.experts, logits, MASKED)
    expo = jnp.exp(logits - jnp.max(logits, axis=0, keepdims=True))
    router_prob = expo * (1.0 / jnp.sum(expo, axis=0, keepdims=True))
    weight = router_prob * kept
    high = weight.astype(BF).astype(F32)
    high_row = jnp.where(row == sz.experts, 1.0, high)
    cw_all[ctx] = jnp.concatenate([high_row, weight - high], axis=0).astype(BF)

    weights.start()
    mixes.start()
    step(ffn)

    chunk = 2 * rows

    half_units = sz.nf // 2 * ffn_send.shape[1]
    cuts = ((0, 384), (384, half_units - 384))

    def units_at(y, cut):
        return pl.ds(pl.multiple_of(y * half_units + cut[0], 128), cut[1])

    def hidden_units(a, y):
        at_rows = blk(a, chunk)
        x = mix_all[pl.ds(2 * a, 2)].reshape(chunk, width)
        g = g_all[pl.ds(2 * a, 2)].reshape(chunk, width)
        pair = jnp.zeros((16, chunk), F32)
        for cut in cuts:
            at = units_at(y, cut)
            gate = dot(x, ffn_w[0, at, :], NT)
            up = dot(x, ffn_w[1, at, :], NT)
            back = dot(g, ffn_w[2, at, :], NT)
            weight = jnp.concatenate([dot(cw_all[2 * a + i], spread[:16, at], TN) for i in range(2)], axis=0)
            sig = 1.0 / (1.0 + jnp.exp(-gate))
            act = gate * sig
            hid = act * up
            pair = pair + dot(spread[16:, at], (hid * back).astype(BF), NT)
            hw[at_rows, at] = (hid * weight).astype(BF)
            back = back * weight
            dg[at_rows, at] = (back * up * sig * (1.0 + gate * (1.0 - sig))).astype(BF)
            du[at_rows, at] = (back * act).astype(BF)
        return pair

    def input_grad(a):
        at_rows = blk(a, chunk)
        total = dot(dg[at_rows, :], ffn_w[0], NN) + dot(du[at_rows, :], ffn_w[1], NN)
        gm_part[pl.ds(2 * a, 2)] = total.astype(BF).reshape(2, rows, width)
        gm_sum.push(a)

    near = [pos.a, jnp.where(pos.a == 0, 1, jnp.where(pos.a == 1, 0, jnp.where(pos.a == 2, 3, 2)))]
    near += [jnp.where(pos.a < 2, 2, 1), jnp.where(pos.a < 2, 3, 0)]
    for i in range(n):
        if i + 1 < n:
            weights.relay(i + 1)
            mixes.relay(i + 1)
        for stream in (cots, weights, mixes):
            stream.across(near[i])
        pair = hidden_units(near[i], pos.y)
        if i == 0:
            drive([ffn])
        pair = (pair + hidden_units(near[i], 1 - pos.y)).astype(BF)
        for t in range(2):
            gp_part[2 * near[i] + t] = pair[:, t * rows : (t + 1) * rows]
        input_grad(near[i])
        if i > 1:
            gm_sum.pass_on(near[i - 1], other=True)
    xs = mix_all[...].reshape(sz.slot, width)
    gs = g_all[...].reshape(sz.slot, width)

    ffn_back = scatter_owner(pos, dw, (o_in.at[0], o_in.at[1], o_down), stage, *t_ffn[:2], Sends(t_ffn[2]), *t_ffn[3:])
    for y in (1 - pos.y, pos.y):
        for cut in cuts:
            at = units_at(y, cut)
            for p, (units, rows_of) in enumerate(((dg, xs), (du, xs), (hw, gs))):
                dw[p, at, :] = dot(units[:, at], rows_of, TN).astype(BF)
        step(ffn_back)
        if y is not pos.y:
            gm_sum.pass_on(near[-1], other=True)
            gm_sum.pass_on(pos.a, other=False)
    step(ffn_back)

    gm_own, gp_own = gm_sum.total()
    grad_prob = gp_own[:8, :] * kept
    grad_logits = router_prob * (grad_prob - jnp.sum(router_prob * grad_prob, axis=0, keepdims=True))
    shifted = jnp.concatenate([jnp.zeros((2, rows), F32), grad_logits[:6]], axis=0).astype(BF)
    grad_small = dot(shifted, mix_all[ctx], NN)
    grad_mixed = gm_own + dot(shifted, small[...].astype(BF), TN)
    res = resid[...]
    inv = lax.rsqrt(mean_square(res, width) + EPSILON)
    w = grad_mixed * gain_m
    inner = jnp.sum(w * res, axis=-1, keepdims=True) * (1.0 / width)
    grad_resid = jnp.where(live, cot[...].astype(F32), 0.0) + inv * w - res * inner * inv * inv * inv
    grad_gain_m = jnp.sum(grad_mixed * res * inv, axis=0, keepdims=True)
    grad_resid_b = grad_resid.astype(BF)
    grad_attn_t = dot(wo[...], grad_resid_b, NT).astype(BF)
    for h_ in range(GROUPS):
        do_send[h_] = grad_attn_t[h_ * share : (h_ + 1) * share]
    for h_ in range(GROUPS):
        swap_send(sz, group, place, do_send, do, *swap_back, h_)
    gm_sum.finish()
    for a in (*near[1:], pos.a):
        y_part[pl.ds(2 * a, 2)] = dot(hw[blk(a, chunk), :], ffn_w[2], NN).astype(BF).reshape(2, rows, width)
        y_sum.push(a)
    for x in (*s, toks):
        x.finish()
    wos = scatter_tree(pos, wo_part, o_wo, *t_wo[:4], Sends(t_wo[4]), t_wo[5])
    wqs = scatter_tree(pos, wq_part, o_wq, *t_wq[:4], Sends(t_wq[4]), t_wq[5], per_group=True)
    grad_wo = dot(attn[...].reshape(width, rows), grad_resid_b, NN)
    row = iota((sz.padded - owned, width), 0)
    grad_small = jnp.where(row == 1, grad_gain_m, jnp.concatenate([grad_small] * ((sz.padded - owned) // 8), axis=0)).astype(BF)

    for i in range(sz.all):
        wo_part[spot(i) + (slice(0, owned),)] = grad_wo[i * owned : (i + 1) * owned].astype(BF)
        wo_part[spot(i) + (slice(owned, None),)] = grad_small
    step(wos)
    swap_wait(sz, group, place, do_send, do, *swap_back)

    dkt[...] = jnp.zeros_like(dkt)
    dvt[...] = jnp.zeros_like(dvt)
    for h_ in reversed(range(GROUPS)):
        keys = (h_ + 1) * sz.per * rows
        done = slice(h_ * sz.per * rows, keys)
        part = blk(h_ * sz.per + place, rows)
        for h in range(sz.heads):
            d_o = do[h_, head(h), :]
            p = prob[h, :, packed(h_)]
            pf = p.astype(F32)
            grad_p = dot(d_o, vt[head(h), :keys], TN)
            delta = jnp.sum(pf * grad_p, axis=1, keepdims=True)
            grad_s = (pf * (grad_p - delta)).astype(BF)
            dq = dot(kt[head(h), :keys], grad_s, NT) * (1.0 / math.sqrt(HEAD_DIM))
            dqt_b[h_, head(h), :] = turn(dq, table[0, :, part], -table[1, :, part]).astype(BF)
            dkt[head(h), :keys] = dkt[head(h), :keys] + dot(qt[h_, head(h), :], grad_s, NN)
            dvt[head(h), :keys] = dvt[head(h), :keys] + dot(d_o, p, NN)
        for h in range(sz.heads):
            dkvt_b[head(h), done] = turn(dkt[head(h), done], table[0, :, done], -table[1, :, done]).astype(BF)
        dkvt_b[share:, done] = dvt[:, done].astype(BF)
        for t in range(2):
            d = h_ * sz.per + lax.rem(place + 1 + t, 2)
            gn = dot(dkvt_b[:, blk(d, rows)], wt[share:, :], TN)
            if t == 1:
                gn = gn + dot(dqt_b[h_], wt[:share, :], TN)
            gn_part[d] = gn.astype(BF)
        gn_sum.push(h_)
        if h_ < GROUPS - 2:
            gn_sum.pass_on(h_ + 2)
        if h_ < GROUPS - 1:
            y_sum.pass_on(near[GROUPS - 1 - h_], other=True)
        if h_ % 2:
            step(wos)
        if h_ == GROUPS - 1:
            step(ffn_back)
    grad_q = dot(dqt_b[0], normed[place], NN)
    for h_ in range(1, GROUPS):
        grad_q = grad_q + dot(dqt_b[h_], normed[h_ * sz.per + place], NN)
    grad_kv = dot(dkvt_b[...], normed[...].reshape(sz.slot, width), NN)
    grad_w = jnp.concatenate([grad_q, grad_kv], axis=0).T
    wq_part[...] = jnp.zeros_like(wq_part)
    for i in range(sz.all):
        wq_part[spot(i) + (slice(0, owned),)] = grad_w[i * owned : (i + 1) * owned].astype(BF)
    step(wqs)
    gn_sum.pass_on(1)
    gn_sum.pass_on(0)
    drive([wos])
    step(wqs, ffn_back, wqs, ffn_back, wqs)
    drive([wqs, ffn_back])
    y_sum.pass_on(pos.a, other=False)
    (y_own,) = y_sum.total()
    o_out[...] = jnp.where(live, res + y_own, 0.0).astype(BF)
    x = tokens[...].astype(F32)
    inv = lax.rsqrt(mean_square(x, width) + EPSILON)
    (gn_own,) = gn_sum.total()
    w = gn_own
    inner = jnp.sum(w * x, axis=-1, keepdims=True) * (1.0 / width)
    o_tokens[...] = grad_resid + inv * w - x * inner * inv * inv * inv
    for x in (y_sum, gn_sum, cots, mixes, weights):
        x.finish()


def layer(sz, collective_id, lengths, tokens, cot, routes, small_own, spread, wq_send, wo_own, ffn_send):
    n, nc, rows, width, share, slot = sz.columns, sz.nc, sz.rows, sz.width, sz.share, sz.slot
    own_units = ffn_send.shape[1]
    units = sz.nf * own_units
    outs = [
        shaped((rows, width)),
        shaped((rows, width), F32),
        shaped((GROUPS, sz.padded, 3 * share), F32),
        shaped((sz.padded, width), F32),
        shaped((2, own_units, width), F32),
        shaped((own_units, width), F32),
    ]
    v = lambda *shape, dtype=BF: pltpu.VMEM(shape, dtype)
    tree = (2, 2, 2, n, sz.padded)
    blocks = v(nc, rows, width)
    scratch = [
        blocks, v(*tree, 3 * share), v(*tree, width), v(sz.padded, width), v(width, width, dtype=F32),
        v(3 * share, width), v(width, width), v(8, width, dtype=F32), blocks,
        v(GROUPS, share, rows), v(share, slot), v(share, slot), v(sz.heads, rows, slot * (GROUPS + 1) // 2), v(GROUPS, share, rows),
        v(GROUPS, share, rows), v(rows, width, dtype=F32), v(2, HEAD_DIM // 2, slot, dtype=F32),
        blocks, blocks, v(nc, 16, rows), v(3, units, width), v(slot, units), v(slot, units), v(slot, units),
        blocks, v(nc, 16, rows), v(3, units, width),
        v(GROUPS, share, rows), v(GROUPS, share, rows), v(share, slot, dtype=F32), v(share, slot, dtype=F32),
        v(GROUPS, share, rows), v(2 * share, slot),
    ]
    sems = gather_tree_sems(n) * 2 + gather_fsdp_sems(3)
    sems += [DMA((GROUPS,)), DMA((GROUPS,)), DMA] * 2
    sems += gather_line_sems(n) * 3 + gather_line_sems(n, parts=1) + [DMA] * 4
    sems += sum_ctx_scratch(n, (rows, width), (16, rows)) + sum_ctx_scratch(n, (rows, width)) * 2
    sems += scatter_tree_scratch(n, (sz.padded, 3 * share)) + scatter_tree_scratch(n, (sz.padded, width))
    sems += scatter_owner_scratch(3, (own_units, width))
    hbm, vmem = pl.BlockSpec(memory_space=pl.ANY), pl.BlockSpec(memory_space=pltpu.VMEM)
    return pl.pallas_call(
        functools.partial(layer_kernel, sz),
        out_shape=outs,
        in_specs=[pl.BlockSpec(memory_space=pltpu.SMEM), vmem, vmem, vmem, vmem, vmem, hbm, vmem, hbm],
        out_specs=[vmem] * 4 + [hbm] * 2,
        scratch_shapes=scratch + sems,
        compiler_params=pltpu.CompilerParams(collective_id=collective_id, has_side_effects=True, vmem_limit_bytes=63 << 20),
        name="layer",
    )(lengths, tokens, cot, routes, small_own, spread, wq_send, wo_own, ffn_send)


def gather_start_kernel(columns, group_of, tokens, wq, wo, ffn, cot, o_tokens, o_wq, o_wo, o_ffn, o_cot, *sems):
    pos = Place(columns)
    greet(all_partners(pos))
    s = [Sends(sems[3 * i]) for i in range(5)]
    r = lambda i: (sems[3 * i + 1], sems[3 * i + 2])
    streams = [
        gather_ctx(pos, tokens, o_tokens, s[0], *r(0)),
        gather_all(pos, wq, o_wq, s[1], *r(1), group_of=group_of),
        gather_all(pos, wo, o_wo, s[2], *r(2)),
        gather_fsdp(pos, ffn, o_ffn, s[3], *r(3)),
    ]
    drive(streams)
    drive([gather_ctx(pos, cot, o_cot, s[4], *r(4))])
    for x in s:
        x.finish()


def call(kernel, collective_id, ins, outs, scratch, name, space=pl.ANY, in_space=None):
    return pl.pallas_call(
        kernel,
        out_shape=outs,
        in_specs=[pl.BlockSpec(memory_space=in_space or space)] * len(ins),
        out_specs=jax.tree.map(lambda _: pl.BlockSpec(memory_space=space), outs),
        scratch_shapes=scratch,
        compiler_params=pltpu.CompilerParams(
            collective_id=collective_id, has_side_effects=True, vmem_limit_bytes=60 << 20
        ),
        name=name,
    )(*ins)


def gather_start(nc, tokens, wq, wo, ffn, cot):
    n = nc // 2
    group_of = lambda a: a // (n // GROUPS)
    sems = gather_ctx_sems(n) + gather_all_sems(n) * 2 + gather_fsdp_sems(ffn.shape[0]) + gather_ctx_sems(n)
    outs = (
        shaped((nc,) + tokens.shape),
        shaped((nc * 4,) + wq.shape[1:]),
        shaped((nc * 4,) + wo.shape),
        shaped((ffn.shape[0], 4) + ffn.shape[1:]),
        shaped((nc,) + cot.shape),
    )
    return call(functools.partial(gather_start_kernel, n, group_of), 1, (tokens, wq, wo, ffn, cot), outs, sems, "gather_start")


def gather_ctx_kernel(columns, src, out, send, recv, local):
    pos = Place(columns)
    greet([pos.column(k) for k in range(1, columns)] + [pos.flip_b()])
    s = Sends(send)
    drive([gather_ctx(pos, src, out, s, recv, local)])
    s.finish()


def gather_rows(nc, src, collective_id):
    n = nc // 2
    return call(functools.partial(gather_ctx_kernel, n), collective_id, (src,), shaped((nc,) + src.shape), gather_ctx_sems(n), "gather_rows")


def swap_kernel(nc, src, out, send, recv, local):
    per = nc // GROUPS
    ctx = lax.axis_index("ctx")
    group, place = ctx // per, ctx % per
    peer = lambda k: lax.rem(group + k, GROUPS)
    device = lambda k: {"ctx": peer(k) * per + place}
    greet([device(k) for k in range(1, GROUPS)])
    own = pltpu.make_async_copy(src.at[group], out.at[group], local)
    own.start()
    copies = []
    for k in range(1, GROUPS):
        copies.append(remote(src.at[peer(k)], out.at[group], send.at[k], recv.at[k], device(k)))
        copies[-1].start()
    for k in range(1, GROUPS):
        arrived(out.at[peer(GROUPS - k)], recv.at[k], device(k))
    own.wait()
    for copy in copies:
        copy.wait_send()


def swap(nc, src, collective_id):
    return call(functools.partial(swap_kernel, nc), collective_id, (src,), shaped(src.shape), [DMA((GROUPS,)), DMA((GROUPS,)), DMA], "swap")


def scatter_ctx_kernel(columns, part, out, acc, from_b, from_col, send, recv, local):
    pos = Place(columns)
    greet([pos.column(k) for k in range(1, columns)] + [pos.flip_b()])
    s = Sends(send)
    drive([scatter_ctx(pos, part, out, acc, from_b, from_col, s, recv, local)])
    s.finish()


def scatter_rows(nc, part, collective_id):
    n = nc // 2
    return pl.pallas_call(
        functools.partial(scatter_ctx_kernel, n),
        out_shape=shaped(part.shape[1:], F32),
        in_specs=[pl.BlockSpec(memory_space=pl.ANY)],
        out_specs=pl.BlockSpec(memory_space=pltpu.VMEM),
        scratch_shapes=scatter_ctx_scratch(n, part.shape[1:]),
        compiler_params=pltpu.CompilerParams(collective_id=collective_id, has_side_effects=True, vmem_limit_bytes=60 << 20),
        name="scatter_rows",
    )(part)


def scatter_end_kernel(columns, gn, wq, wo, ffn, yy, o_gn, o_wq, o_wo, o_ffn, o_yy, *scratch):
    pos = Place(columns)
    greet(all_partners(pos))
    c1, a1, a2, f1, c2 = scratch[0:6], scratch[6:14], scratch[14:22], scratch[22:28], scratch[28:34]
    s = [Sends(x[-3]) for x in (c1, a1, a2, f1, c2)]
    drive(
        [
            scatter_ctx(pos, gn, o_gn, *c1[:-3], s[0], *c1[-2:]),
            scatter_fsdp(pos, [ffn.at[p] for p in range(ffn.shape[0])], o_ffn, *f1[:-3], s[3], *f1[-2:]),
            scatter_all(pos, wq, o_wq, *a1[:-3], s[1], *a1[-2:], per_group=True),
            scatter_all(pos, wo, o_wo, *a2[:-3], s[2], *a2[-2:]),
            scatter_ctx(pos, yy, o_yy, *c2[:-3], s[4], *c2[-2:]),
        ]
    )
    for x in s:
        x.finish()


def scatter_end(nc, gn, wq, wo, ffn, yy):
    n = nc // 2
    scratch = (
        scatter_ctx_scratch(n, gn.shape[1:])
        + scatter_all_scratch(n, wq.shape[1:])
        + scatter_all_scratch(n, wo.shape[1:])
        + scatter_fsdp_scratch(ffn.shape[0], ffn.shape[2:])
        + scatter_ctx_scratch(n, yy.shape[1:])
    )
    outs = (
        shaped(gn.shape[1:], F32),
        shaped((GROUPS,) + wq.shape[1:], F32),
        shaped(wo.shape[1:], F32),
        shaped((ffn.shape[0],) + ffn.shape[2:], F32),
        shaped(yy.shape[1:], F32),
    )
    return call(
        functools.partial(scatter_end_kernel, n), 6, (gn, wq, wo, ffn, yy), outs, scratch, "scatter_end",
        space=pltpu.VMEM, in_space=pl.ANY,
    )


def doc_ids(row_index, doc_ends):
    return jnp.sum((row_index[:, None] >= doc_ends[None, :]).astype(jnp.int32), axis=1)


def positions(row_index, lengths):
    doc_ends = jnp.cumsum(lengths)
    doc_starts = doc_ends - lengths
    doc_num = doc_ids(row_index, doc_ends)
    column = jnp.arange(lengths.shape[0], dtype=jnp.int32)
    begins = jnp.sum(jnp.where(doc_num[:, None] == column[None, :], doc_starts[None, :], 0), axis=1)
    return doc_num, row_index - begins


def rope_tables(position):
    half_dim = HEAD_DIM // 2
    inverse = ROPE_BASE ** (-2.0 * jnp.arange(half_dim, dtype=F32) / HEAD_DIM)
    angles = position.astype(F32)[:, None] * inverse[None, :]
    return jnp.cos(angles), jnp.sin(angles)


def rotate(values, cosine, sine):
    half_dim = values.shape[-1] // 2
    lower, upper = values[..., :half_dim], values[..., half_dim:]
    cosine, sine = cosine[:, None, :], sine[:, None, :]
    return jnp.concatenate([lower * cosine - upper * sine, upper * cosine + lower * sine], axis=-1)


def kept_rows(route_rows, live_rows, experts, capacity):
    count, top = route_rows.shape
    hot = (route_rows[:, :, None] == jnp.arange(experts, dtype=jnp.int32)) & live_rows[:, None, None]
    hot = hot.astype(F32)
    before = jnp.tril(jnp.ones((count, count), F32), -1)
    kept = jnp.zeros((count, experts), F32)
    base = jnp.zeros((1, experts), F32)
    for k in range(top):
        earlier = base + jnp.dot(before, hot[:, k])
        kept = kept + hot[:, k] * (earlier < capacity)
        base = base + jnp.sum(hot[:, k], axis=0, keepdims=True)
    return kept


def pad_rows(x, rows):
    return jnp.pad(x, [(0, rows - x.shape[0])] + [(0, 0)] * (x.ndim - 1))


def body_wide(tokens, doc_lengths, routes, cotangent, attn_gain, w_qkv, w_out, mlp_gain, router, expert_in, expert_out, shared_in, shared_out):
    nc = lax.axis_size("ctx")
    nf = lax.axis_size("fsdp")
    rows, width = tokens.shape[1:]
    heads = width // HEAD_DIM
    experts = expert_in.shape[1]
    hidden = expert_in.shape[0]
    top = routes.shape[2]
    capacity = 5 * top * rows // (4 * experts)
    per = nc // GROUPS
    ctx = lax.axis_index("ctx")
    group, place = ctx // per, ctx % per
    slot = nc * rows
    mine = heads // GROUPS
    share = mine * HEAD_DIM
    scale = 1.0 / math.sqrt(HEAD_DIM)
    owned = w_out.shape[0]
    padded = -(-(owned + 2 + experts) // 16) * 16

    wq_send = w_qkv.reshape(owned, 3, GROUPS, share).transpose(2, 0, 1, 3).reshape(GROUPS, owned, 3 * share)
    wq_send = jnp.pad(wq_send, ((0, 0), (0, padded - owned), (0, 0)))
    small = jnp.concatenate([attn_gain[None], mlp_gain[None], router.T], axis=0)
    wo_send = pad_rows(jnp.concatenate([w_out, jnp.pad(small, ((0, 0), (0, width - owned)))], axis=0), padded)
    gate_up = jnp.concatenate([expert_in.transpose(2, 1, 0, 3), shared_in.transpose(1, 0, 2)[:, None]], axis=1)
    down = jnp.concatenate([expert_out.transpose(1, 0, 2), shared_out[None]], axis=0)
    ffn_send = jnp.concatenate([gate_up, down[None]], axis=0).reshape(3, (experts + 1) * hidden, width)

    x_all, wq_all, wo_all, ffn_all, cot_all = gather_start(nc, tokens[0], wq_send, wo_send, ffn_send, cotangent[0])
    units = nf * (experts + 1) * hidden
    w_gate, w_up, w_down = (ffn_all[p].reshape(units, width) for p in range(3))
    wq = wq_all[:, :owned].reshape(width, 3 * share)
    wo = wo_all[:, :owned].reshape(width, width)
    small = wo_all[:, owned : owned + 2 + experts, :owned].transpose(1, 0, 2).reshape(2 + experts, width)
    gain_a, gain_m = small[0].astype(F32), small[1].astype(F32)
    router_t = small[2:]

    all_rows = jnp.arange(slot, dtype=jnp.int32)
    doc_num, position = positions(all_rows, doc_lengths[0])
    cosine, sine = rope_tables(position)
    live_all = (doc_num < doc_lengths.shape[1]).astype(F32)[:, None]
    x_slot = x_all.reshape(slot, width).astype(F32)
    inv_attn = lax.rsqrt(jnp.mean(x_slot * x_slot, axis=-1, keepdims=True) + EPSILON)
    normed = (x_slot * inv_attn * gain_a).astype(BF)

    def queries(v):
        return lax.dynamic_index_in_dim(v.reshape((GROUPS, per, rows) + v.shape[1:]), place, 1, False).reshape((GROUPS * rows,) + v.shape[1:])

    normed_q = queries(normed)
    cos_q, sin_q = queries(cosine), queries(sine)
    q = rotate(dot(normed_q, wq[:, :share], ((1,), (0,))).reshape(-1, mine, HEAD_DIM), cos_q, sin_q).astype(BF)
    k = rotate(dot(normed, wq[:, share : 2 * share], ((1,), (0,))).reshape(slot, mine, HEAD_DIM), cosine, sine).astype(BF)
    v = dot(normed, wq[:, 2 * share :], ((1,), (0,))).reshape(slot, mine, HEAD_DIM).astype(BF)
    rows_q, doc_q = queries(all_rows), queries(doc_num)
    allowed = (doc_q[:, None] == doc_num[None, :]) & (all_rows[None, :] <= rows_q[:, None])
    scores = jnp.einsum("qhd,khd->hqk", q, k, preferred_element_type=F32) * scale
    scores = jnp.where(allowed[None], scores, MASKED)
    expo = jnp.exp(scores - jnp.max(scores, axis=-1, keepdims=True))
    prob = expo / jnp.sum(expo, axis=-1, keepdims=True)
    prob_b = prob.astype(BF)
    o = jnp.einsum("hqk,khd->qhd", prob_b, v, preferred_element_type=F32).astype(BF)

    o_own = swap(nc, o.reshape(GROUPS, rows, share), 2)
    attn = o_own.transpose(1, 0, 2).reshape(rows, width)

    row_index = ctx * rows + jnp.arange(rows, dtype=jnp.int32)
    doc_own, _ = positions(row_index, doc_lengths[0])
    live_rows = doc_own < doc_lengths.shape[1]
    live = live_rows.astype(F32)[:, None]
    x = tokens[0].astype(F32)
    resid = x + dot(attn, wo, ((1,), (0,)))
    inv_mlp = lax.rsqrt(jnp.mean(resid * resid, axis=-1, keepdims=True) + EPSILON)
    mixed = (resid * inv_mlp * gain_m).astype(BF)
    logits = dot(mixed, router_t, ((1,), (1,)))
    router_prob = jax.nn.softmax(logits, axis=-1)
    kept = kept_rows(routes[0], live_rows, experts, capacity)
    weight = router_prob * kept
    high = weight.astype(BF)
    low = (weight - high.astype(F32)).astype(BF)
    extra = pad_rows(jnp.pad(jnp.concatenate([high, low], axis=1).T, ((0, 0), (0, width - rows))), 16)
    mixed_all = gather_rows(nc, jnp.concatenate([mixed, extra], axis=0), 3)

    weights = mixed_all[:, rows : rows + 2 * experts, :rows].astype(F32)
    weights = (weights[:, :experts] + weights[:, experts:]).transpose(0, 2, 1).reshape(slot, experts)
    mix = mixed_all[:, :rows].reshape(slot, width)
    g = (cot_all.reshape(slot, width) * live_all.astype(BF)).astype(BF)
    unit_weight = jnp.concatenate([weights, jnp.ones((slot, 1), F32)], axis=1)
    unit_weight = jnp.tile(jnp.repeat(unit_weight, hidden, axis=1), (1, nf))
    gate = dot(mix, w_gate, ((1,), (1,)))
    up = dot(mix, w_up, ((1,), (1,)))
    sig = jax.nn.sigmoid(gate)
    hid = gate * sig * up
    hid_w = (hid * unit_weight).astype(BF)
    y_part = dot(hid_w, w_down, ((1,), (0,))).astype(BF)
    back = dot(g, w_down, ((1,), (1,)))
    pair = (hid * back).reshape(slot, nf, experts + 1, hidden).sum(axis=(1, 3))[:, :experts]
    back_w = back * unit_weight
    d_gate = (back_w * up * sig * (1.0 + gate * (1.0 - sig))).astype(BF)
    d_up = (back_w * gate * sig).astype(BF)
    gm_part = (dot(d_gate, w_gate, ((1,), (0,))) + dot(d_up, w_up, ((1,), (0,)))).astype(BF)
    d_w = jnp.stack([dot(d_gate, mix, ((0,), (0,))), dot(d_up, mix, ((0,), (0,))), dot(hid_w, g, ((0,), (0,)))]).astype(BF)
    pair_t = pair.reshape(nc, rows, experts).transpose(0, 2, 1)
    pair_t = jnp.pad(pair_t, ((0, 0), (0, 16 - experts), (0, width - rows))).astype(BF)
    gm_all = scatter_rows(nc, jnp.concatenate([gm_part.reshape(nc, rows, width), pair_t], axis=1), 4)

    grad_prob = gm_all[rows : rows + experts, :rows].T * kept
    grad_logits = (router_prob * (grad_prob - jnp.sum(router_prob * grad_prob, axis=-1, keepdims=True))).astype(BF)
    grad_router_t = dot(grad_logits, mixed, ((0,), (0,)))
    grad_mixed = gm_all[:rows] + dot(grad_logits, router_t, ((1,), (0,)))
    grad_top = cotangent[0].astype(F32) * live
    w = grad_mixed * gain_m
    grad_resid = grad_top + inv_mlp * w - resid * jnp.mean(w * resid, axis=-1, keepdims=True) * inv_mlp**3
    grad_gain_m = jnp.sum(grad_mixed * resid * inv_mlp, axis=0)
    grad_resid_b = grad_resid.astype(BF)
    grad_wo = dot(attn, grad_resid_b, ((0,), (0,)))
    grad_attn = dot(grad_resid_b, wo, ((1,), (1,))).astype(BF)
    do = swap(nc, grad_attn.reshape(rows, GROUPS, share).transpose(1, 0, 2), 5).reshape(GROUPS * rows, mine, HEAD_DIM)

    grad_p = jnp.einsum("qhd,khd->hqk", do, v, preferred_element_type=F32)
    delta = jnp.sum(prob * grad_p, axis=-1, keepdims=True)
    grad_s = (prob * (grad_p - delta)).astype(BF)
    dq = jnp.einsum("hqk,khd->qhd", grad_s, k, preferred_element_type=F32) * scale
    dk = jnp.einsum("hqk,qhd->khd", grad_s, q, preferred_element_type=F32) * scale
    dv = jnp.einsum("hqk,qhd->khd", prob_b, do, preferred_element_type=F32)
    dq = rotate(dq, cos_q, -sin_q).reshape(GROUPS * rows, share).astype(BF)
    dk = rotate(dk, cosine, -sine).reshape(slot, share)
    dkv = jnp.concatenate([dk, dv.reshape(slot, share)], axis=1).astype(BF)
    grad_wq = jnp.concatenate([dot(normed_q, dq, ((0,), (0,))), dot(normed, dkv, ((0,), (0,)))], axis=1)
    gn_q = dot(dq, wq[:, :share], ((1,), (1,))).reshape(GROUPS, 1, rows, width)
    here = (jnp.arange(per) == place).astype(F32)[None, :, None, None]
    gn = dot(dkv, wq[:, share:], ((1,), (1,))).reshape(GROUPS, per, rows, width) + gn_q * here
    gn_part = gn.reshape(nc, rows, width).astype(BF)

    gn_full = gn.reshape(slot, width)
    grad_gain_a = jnp.sum(gn_full * x_slot * inv_attn, axis=0)
    small = jnp.concatenate([grad_gain_a[None], grad_gain_m[None], grad_router_t], axis=0)
    small = small.reshape(2 + experts, nc * nf, owned).transpose(1, 0, 2)
    wo_part = jnp.concatenate([grad_wo.reshape(nc * nf, owned, width), jnp.pad(small, ((0, 0), (0, 0), (0, width - owned)))], axis=1)
    wo_part = jnp.pad(wo_part, ((0, 0), (0, padded - wo_part.shape[1]), (0, 0))).astype(BF)
    wq_part = jnp.pad(grad_wq.reshape(nc * nf, owned, 3 * share), ((0, 0), (0, padded - owned), (0, 0))).astype(BF)
    ffn_part = d_w.reshape(3, nf, (experts + 1) * hidden, width)
    gn_own, wq_own, wo_own, ffn_own, y_own = scatter_end(nc, gn_part, wq_part, wo_part, ffn_part, y_part.reshape(nc, rows, width))

    layer_out = (live * (resid + y_own)).astype(BF)[None]
    inv = lax.rsqrt(jnp.mean(x * x, axis=-1, keepdims=True) + EPSILON)
    w = gn_own * gain_a
    grad_tokens = (grad_resid + inv * w - x * jnp.mean(w * x, axis=-1, keepdims=True) * inv**3)[None]
    grad_w_qkv = wq_own[:, :owned].reshape(GROUPS, owned, 3, share).transpose(1, 2, 0, 3).reshape(owned, 3 * width)
    small = wo_own[owned : owned + 2 + experts, :owned]
    out = ffn_own.reshape(3, experts + 1, hidden, width)
    return (
        layer_out,
        grad_tokens,
        small[0],
        grad_w_qkv,
        wo_own[:owned],
        small[1],
        small[2:].T,
        out[:2, :experts].transpose(2, 1, 0, 3),
        out[2, :experts].transpose(1, 0, 2),
        out[:2, experts].transpose(1, 0, 2),
        out[2, experts],
    )


def body(tokens, doc_lengths, routes, cotangent, attn_gain, w_qkv, w_out, mlp_gain, router, expert_in, expert_out, shared_in, shared_out):
    nc, nf = lax.axis_size("ctx"), lax.axis_size("fsdp")
    rows, width = tokens.shape[1:]
    experts, hidden, top = expert_in.shape[1], expert_in.shape[0], routes.shape[2]
    owned = w_out.shape[0]
    if nc != 2 * GROUPS or 2 * nc * rows * width > FUSED_BYTES:
        return body_wide(
            tokens, doc_lengths, routes, cotangent, attn_gain, w_qkv, w_out, mlp_gain, router, expert_in, expert_out, shared_in, shared_out
        )
    padded = -(-(owned + 8) // 16) * 16
    sz = Sizes(nc, nf, rows, width, experts, hidden, owned, padded, 5 * top * rows // (4 * experts), top, doc_lengths.shape[1])
    share = sz.share
    device = lax.axis_index("ctx") * nf + lax.axis_index("fsdp")

    gain = attn_gain.astype(F32)[:, None]
    wq_send = (w_qkv.astype(F32) * gain).astype(BF).reshape(owned, 3, GROUPS, share).transpose(2, 0, 1, 3).reshape(GROUPS, owned, 3 * share)
    wq_send = jnp.pad(wq_send, ((0, 0), (0, padded - owned), (0, 0)))
    small = jnp.concatenate([attn_gain[None], mlp_gain[None], router.T, jnp.zeros((padded - owned - 2 - experts, owned), BF)], axis=0)
    gate_up = jnp.concatenate([expert_in.transpose(2, 1, 0, 3), shared_in.transpose(1, 0, 2)[:, None]], axis=1)
    down = jnp.concatenate([expert_out.transpose(1, 0, 2), shared_out[None]], axis=0)
    ffn_send = jnp.concatenate([gate_up, down[None]], axis=0).reshape(3, (experts + 1) * hidden, width)

    units = nf * (experts + 1) * hidden
    of = np.arange(units) // hidden % (experts + 1)
    spread = np.zeros((32, units), np.float32)
    for e in range(experts + 1):
        spread[e] = of == e
    for e in range(experts):
        spread[8 + e] = of == e
        spread[16 + e] = of == e

    layer_out, grad_tokens, wq_own, wo_own, grad_in, grad_down = layer(
        sz, 1, doc_lengths, tokens[0], cotangent[0], routes[0], small, jnp.asarray(spread, BF), wq_send, w_out, ffn_send
    )

    grad_w = wq_own[:, :owned].reshape(GROUPS, owned, 3, share).transpose(1, 2, 0, 3).reshape(owned, 3 * width)
    gain_a = jnp.sum(grad_w * w_qkv.astype(F32), axis=1)
    grad_w_qkv = grad_w * gain
    small = lax.dynamic_slice(wo_own[owned:], (0, device * owned), (2 + experts, owned))
    grad_in = grad_in.reshape(2, experts + 1, hidden, width)
    grad_down = grad_down.reshape(experts + 1, hidden, width)
    return (
        layer_out[None],
        grad_tokens[None],
        gain_a,
        grad_w_qkv,
        wo_own[:owned],
        small[1],
        small[2:].T,
        grad_in[:, :experts].transpose(2, 1, 0, 3),
        grad_down[:experts].transpose(1, 0, 2),
        grad_in[:, experts].transpose(1, 0, 2),
        grad_down[experts],
    )


def solution(mesh):
    rows = P("fsdp", "ctx", None)
    flat = ("ctx", "fsdp")
    weights = (P(flat), P(flat, None), P(flat, None), P(flat), P(flat, None))
    ffn = (P(flat, None, None, None), P(flat, None, None), P(flat, None, None), P(flat, None))
    return jax.shard_map(
        body,
        mesh=mesh,
        in_specs=(rows, P("fsdp", None), rows, rows) + weights + ffn,
        out_specs=(rows, rows) + weights + ffn,
        check_vma=False,
    )
```

```python
import functools
import math

import jax
import jax.numpy as jnp
import numpy as np
from jax import lax
from jax.experimental import pallas as pl
from jax.experimental.pallas import tpu as pltpu
from jax.sharding import PartitionSpec as P

HEAD_DIM = 64
EPSILON = 1e-05
ROPE_BASE = 10000.0
MASKED = -1e30
NN, NT, TN = ((1,), (0,)), ((1,), (1,)), ((0,), (0,))
FUSED_BYTES = 2 << 20
GROUPS = 4
MESH = pl.DeviceIdType.MESH
DMA = pltpu.SemaphoreType.DMA
BF = jnp.bfloat16
F32 = jnp.float32


class Place:
    def __init__(self, columns, balanced=True):
        ctx, fsdp = lax.axis_index("ctx"), lax.axis_index("fsdp")
        self.columns = columns
        self.a, self.b = ctx // 2, ctx % 2
        self.y, self.c = fsdp // 2, fsdp % 2
        flip_b = (1 - self.b, self.y)
        flip_y = (self.b, 1 - self.y)
        core = (self.c == 0) if balanced else (self.c >= 0)
        self.first = tuple(jnp.where(core, p, q) for p, q in zip(flip_b, flip_y))
        self.second = tuple(jnp.where(core, q, p) for p, q in zip(flip_b, flip_y))
        self.plane = [(self.b, self.y), self.first, self.second, (1 - self.b, 1 - self.y)]
        self.sib_plane = [(self.b, self.y), self.second, self.first, (1 - self.b, 1 - self.y)]

    def at(self, step):
        return lax.rem(self.a + step, self.columns)

    def device(self, a=None, plane=None, c=None):
        b, y = plane if plane is not None else (self.b, self.y)
        a = self.a if a is None else a
        c = self.c if c is None else c
        return {"ctx": a * 2 + b, "fsdp": y * 2 + c}

    def column(self, step):
        return self.device(a=self.at(step))

    def flip_b(self):
        return self.device(plane=(1 - self.b, self.y))

    def flip_y(self):
        return self.device(plane=(self.b, 1 - self.y))

    def sibling(self):
        return self.device(c=1 - self.c)

    def chunk(self, step, plane, c):
        return (self.at(step) * 2 + plane[0]) * 4 + plane[1] * 2 + c


def greet(devices):
    barrier = pltpu.get_barrier_semaphore()
    for device in devices:
        pl.semaphore_signal(barrier, inc=1, device_id=device, device_id_type=MESH)
    pl.semaphore_wait(barrier, len(devices))


def remote(src, dst, send, recv, device):
    return pltpu.make_async_remote_copy(
        src_ref=src, dst_ref=dst, send_sem=send, recv_sem=recv, device_id=device, device_id_type=MESH
    )


class Sends:
    def __init__(self, sems):
        self.sems, self.made = sems, []

    def start(self, src, dst, recv, device):
        copy = remote(src, dst, self.sems.at[len(self.made)], recv, device)
        copy.start()
        self.made.append(copy)

    def finish(self):
        for copy in self.made:
            copy.wait_send()


def arrived(dst, recv, device):
    remote(dst, dst, recv, recv, device).wait_recv()


def gather_ctx(pos, src, out, sends, recv, local, there=lambda slot: None):
    n = pos.columns
    me = pos.a * 2 + pos.b
    own = pltpu.make_async_copy(src, out.at[me], local)
    own.start()
    for k in range(1, n):
        sends.start(src, out.at[me], recv.at[k], pos.column(k))
    sends.start(src, out.at[me], recv.at[n], pos.flip_b())
    yield
    own.wait()
    there(me)
    for k in range(1, n):
        slot = pos.at(n - k) * 2 + pos.b
        arrived(out.at[slot], recv.at[k], pos.column(k))
        sends.start(out.at[slot], out.at[slot], recv.at[n + k], pos.flip_b())
        there(slot)
        yield
    for k in range(n):
        slot = pos.at(n - k) * 2 + 1 - pos.b
        arrived(out.at[slot], recv.at[n + k], pos.flip_b())
        there(slot)
        yield


def gather_ctx_sems(n):
    return [DMA((2 * n,)), DMA((2 * n,)), DMA]


def gather_fsdp(pos, src, out, sends, recv, local):
    parts = src.shape[0]
    if len(out.shape) == 3:
        out = [out.at[p] for p in range(parts)]
        at = lambda p, f: out[p].at[pl.ds(pl.multiple_of(f * src.shape[1], src.shape[1]), src.shape[1])]
    else:
        at = lambda p, f: out.at[p, f]
    me = pos.y * 2 + pos.c
    other = (1 - pos.y) * 2 + pos.c
    own = []
    for p in range(parts):
        own.append(pltpu.make_async_copy(src.at[p], at(p, me), local.at[p]))
        own[-1].start()
        sends.start(src.at[p], at(p, me), recv.at[p], pos.flip_y())
    for p in range(parts):
        sends.start(src.at[p], at(p, me), recv.at[parts + p], pos.sibling())
    yield
    for p in range(parts):
        arrived(at(p, pos.y * 2 + 1 - pos.c), recv.at[parts + p], pos.sibling())
        own[p].wait()
    yield
    for p in range(parts):
        arrived(at(p, other), recv.at[p], pos.flip_y())
        sends.start(at(p, other), at(p, other), recv.at[2 * parts + p], pos.sibling())
        yield
    for p in range(parts):
        arrived(at(p, (1 - pos.y) * 2 + 1 - pos.c), recv.at[2 * parts + p], pos.sibling())


def gather_fsdp_sems(parts):
    return [DMA((3 * parts,)), DMA((3 * parts,)), DMA((parts,))]


def gather_all(pos, src, out, sends, recv, local, group_of=None):
    n = pos.columns
    me = pos.chunk(0, pos.plane[0], pos.c)
    part = (lambda a: src) if group_of is None else (lambda a: src.at[group_of(a)])
    mine = part(pos.a)
    own = pltpu.make_async_copy(mine, out.at[me], local)
    own.start()
    first, second = pos.device(plane=pos.first), pos.device(plane=pos.second)
    sibling = pos.sibling()
    for k in range(1, n):
        sends.start(part(pos.at(k)), out.at[me], recv.at[k], pos.column(k))
    sends.start(mine, out.at[me], recv.at[n], first)
    sends.start(mine, out.at[me], recv.at[2 * n], second)
    sends.start(mine, out.at[me], recv.at[4 * n], sibling)
    yield
    for k in range(1, n):
        slot = pos.chunk(n - k, pos.plane[0], pos.c)
        arrived(out.at[slot], recv.at[k], first)
        sends.start(out.at[slot], out.at[slot], recv.at[n + k], first)
        sends.start(out.at[slot], out.at[slot], recv.at[2 * n + k], second)
        sends.start(out.at[slot], out.at[slot], recv.at[4 * n + k], sibling)
        yield
    for k in range(n):
        slot = pos.chunk(n - k, pos.first, pos.c)
        arrived(out.at[slot], recv.at[n + k], first)
        sends.start(out.at[slot], out.at[slot], recv.at[3 * n + k], second)
        sends.start(out.at[slot], out.at[slot], recv.at[5 * n + k], sibling)
        yield
    for r in range(2):
        for k in range(n):
            slot = pos.chunk(n - k, pos.plane[2 + r], pos.c)
            arrived(out.at[slot], recv.at[(2 + r) * n + k], second)
            sends.start(out.at[slot], out.at[slot], recv.at[(6 + r) * n + k], sibling)
            yield
    own.wait()
    for r in range(4):
        for k in range(n):
            slot = pos.chunk(n - k, pos.sib_plane[r], 1 - pos.c)
            arrived(out.at[slot], recv.at[(4 + r) * n + k], sibling)


def gather_all_sems(n):
    return [DMA((8 * n,)), DMA((8 * n,)), DMA]


def drive(streams):
    streams = list(streams)
    while streams:
        for stream in list(streams):
            if next(stream, streams) is streams:
                streams.remove(stream)


def all_partners(pos):
    return [pos.column(k) for k in range(1, pos.columns)] + [pos.flip_b(), pos.flip_y(), pos.sibling()]


def shaped(shape, dtype=BF):
    return jax.ShapeDtypeStruct(tuple(shape), dtype)


def dot(a, b, dims):
    return lax.dot_general(a, b, (dims, ((), ())), preferred_element_type=F32)


def add(acc, *others):
    total = acc[...].astype(F32)
    for other in others:
        total = total + other[...].astype(F32)
    acc[...] = total.astype(acc.dtype)


def scatter_ctx(pos, part, out, acc, from_b, from_col, sends, recv, local):
    n = pos.columns
    loads = []
    for k in range(n):
        loads.append(pltpu.make_async_copy(part.at[pos.at(k) * 2 + pos.b], acc.at[k], local.at[k]))
        loads[-1].start()
    for k in [*range(1, n), 0]:
        sends.start(part.at[pos.at(k) * 2 + 1 - pos.b], from_b.at[k], recv.at[k], pos.flip_b())
    yield
    for k in [*range(1, n), 0]:
        loads[k].wait()
        arrived(from_b.at[k], recv.at[k], pos.flip_b())
        if k:
            add(acc.at[k], from_b.at[k])
            sends.start(acc.at[k], from_col.at[k], recv.at[n + k], pos.column(k))
            yield
    total = acc[0].astype(F32) + from_b[0].astype(F32)
    for k in range(1, n):
        arrived(from_col.at[k], recv.at[n + k], pos.column(k))
        total = total + from_col[k].astype(F32)
        yield
    out[...] = total.astype(out.dtype)


def scatter_ctx_scratch(n, shape):
    v = lambda m: pltpu.VMEM((m,) + tuple(shape), BF)
    return [v(n), v(n), v(n), DMA((2 * n,)), DMA((2 * n,)), DMA((n,))]


def scatter_fsdp(pos, part, out, acc, from_sib, from_y, sends, recv, local):
    parts = len(part)
    loads = []
    mine = [(1 - pos.y) * 2 + pos.c, pos.y * 2 + pos.c]
    his = [(1 - pos.y) * 2 + 1 - pos.c, pos.y * 2 + 1 - pos.c]
    for t in range(2):
        for p in range(parts):
            i = t * parts + p
            loads.append(pltpu.make_async_copy(part[p].at[mine[t]], acc.at[i], local.at[i]))
            loads[-1].start()
            sends.start(part[p].at[his[t]], from_sib.at[i], recv.at[i], pos.sibling())
    yield
    for p in range(parts):
        loads[p].wait()
        arrived(from_sib.at[p], recv.at[p], pos.sibling())
        add(acc.at[p], from_sib.at[p])
        sends.start(acc.at[p], from_y.at[p], recv.at[2 * parts + p], pos.flip_y())
        yield
    for p in range(parts):
        loads[parts + p].wait()
        arrived(from_sib.at[parts + p], recv.at[parts + p], pos.sibling())
        add(acc.at[parts + p], from_sib.at[parts + p])
        yield
    for p in range(parts):
        arrived(from_y.at[p], recv.at[2 * parts + p], pos.flip_y())
        out[p] = acc[parts + p].astype(F32) + from_y[p].astype(F32)
        yield


def scatter_fsdp_scratch(parts, shape):
    v = lambda m: pltpu.VMEM((m,) + tuple(shape), BF)
    return [v(2 * parts), v(2 * parts), v(parts), DMA((3 * parts,)), DMA((3 * parts,)), DMA((2 * parts,))]


def scatter_all(pos, part, out, acc, from_sib, from_2, from_1, from_col, sends, recv, local, per_group=False):
    n = pos.columns
    sibling = pos.sibling()
    first, second = pos.device(plane=pos.first), pos.device(plane=pos.second)
    loads = {}
    for r in (3, 2, 1, 0):
        for k in range(n):
            i = r * n + k
            loads[i] = pltpu.make_async_copy(part.at[pos.chunk(k, pos.plane[r], pos.c)], acc.at[i], local.at[i])
            loads[i].start()
            sends.start(part.at[pos.chunk(k, pos.sib_plane[r], 1 - pos.c)], from_sib.at[i], recv.at[i], sibling)
    yield
    for r in (3, 2):
        for k in range(n):
            i = r * n + k
            loads[i].wait()
            arrived(from_sib.at[i], recv.at[i], sibling)
            add(acc.at[i], from_sib.at[i])
            j = (r - 2) * n + k
            sends.start(acc.at[i], from_2.at[j], recv.at[4 * n + j], second)
        yield
    for k in range(n):
        i = n + k
        loads[i].wait()
        arrived(from_sib.at[i], recv.at[i], sibling)
        arrived(from_2.at[i], recv.at[4 * n + i], second)
        add(acc.at[i], from_sib.at[i], from_2.at[i])
        sends.start(acc.at[i], from_1.at[k], recv.at[6 * n + k], first)
    yield
    for k in [*range(1, n), 0]:
        loads[k].wait()
        arrived(from_sib.at[k], recv.at[k], sibling)
        arrived(from_2.at[k], recv.at[4 * n + k], second)
        arrived(from_1.at[k], recv.at[6 * n + k], first)
        if k:
            add(acc.at[k], from_sib.at[k], from_2.at[k], from_1.at[k])
            sends.start(acc.at[k], from_col.at[k], recv.at[7 * n + k], pos.column(k))
    total = acc[0].astype(F32) + from_sib[0].astype(F32) + from_2[0].astype(F32) + from_1[0].astype(F32)
    yield
    if not per_group:
        for k in range(1, n):
            arrived(from_col.at[k], recv.at[7 * n + k], pos.column(k))
            total = total + from_col[k].astype(F32)
        out[...] = total
        return
    each = n // GROUPS
    for k in range(1, n):
        arrived(from_col.at[k], recv.at[7 * n + k], pos.column(k))
    out[...] = jnp.zeros_like(out)
    for k in range(n):
        value = total if k == 0 else from_col[k].astype(F32)
        group = pos.at(n - k) // each
        out[group] = out[group] + value


def scatter_all_scratch(n, shape):
    v = lambda m: pltpu.VMEM((m,) + tuple(shape), BF)
    return [v(4 * n), v(4 * n), v(2 * n), v(n), v(n), DMA((8 * n,)), DMA((8 * n,)), DMA((4 * n,))]


class GatherLine:
    def __init__(self, pos, bufs, send, recv, parts=2):
        self.pos, self.bufs, self.send, self.recv, self.parts = pos, bufs, send, recv, parts
        self.made = []

    def cut(self, ref, p):
        rows = ref.shape[0] // self.parts
        return ref.at[pl.ds(p * rows, rows)]

    def copy(self, i, p, src, a, kind, device):
        out = self.bufs[i][1]
        n = self.pos.columns
        dst = self.cut(out.at[2 * a + self.pos.b], p)
        at = ((i * 2 + kind) * n + a) * self.parts + p
        made = remote(dst if src is None else self.cut(src, p), dst, self.send.at[len(self.made)], self.recv.at[at], device)
        return made

    def go(self, i, p, src, a, kind, device, when=None):
        made = self.copy(i, p, src, a, kind, device)
        self.made.append((made, when))
        if when is None:
            made.start()
        else:
            pl.when(when)(made.start)

    def start(self):
        pos, n = self.pos, self.pos.columns
        up, down = pos.device(a=jnp.minimum(pos.a + 1, n - 1)), pos.device(a=jnp.maximum(pos.a - 1, 0))
        self.up, self.down = up, down
        for p in range(self.parts):
            for i, (src, _) in enumerate(self.bufs):
                self.go(i, p, src, pos.a, 0, up, pos.a < n - 1)
                self.go(i, p, src, pos.a, 0, down, pos.a > 0)
                self.go(i, p, src, pos.a, 1, pos.flip_b())

    def here(self, i, p, a, kind, device):
        b = self.pos.b if kind == 0 else 1 - self.pos.b
        out = self.bufs[i][1]
        at = ((i * 2 + kind) * self.pos.columns + a) * self.parts + p
        arrived(self.cut(out.at[2 * a + b], p), self.recv.at[at], device)

    def relay(self, d):
        pos, n = self.pos, self.pos.columns
        for p in range(self.parts):
            for sign, device, end in ((-1, self.up, pos.a < n - 1), (1, self.down, pos.a > 0)):
                a = pos.a + sign * d
                there = (a >= 0) & (a < n)
                a = jnp.clip(a, 0, n - 1)
                for i in range(len(self.bufs)):
                    pl.when(there)(functools.partial(self.here, i, p, a, 0, device))
                    if d < n - 1:
                        self.go(i, p, None, a, 0, device, there & end)
                    self.go(i, p, None, a, 1, pos.flip_b(), there)

    def across(self, a):
        for p in range(self.parts):
            for i in range(len(self.bufs)):
                self.here(i, p, a, 1, self.pos.flip_b())

    def finish(self):
        for made, when in self.made:
            if when is None:
                made.wait_send()
            else:
                pl.when(when)(made.wait_send)


def gather_line_sems(n, bufs=1, parts=2):
    return [DMA((parts * bufs * (3 + 4 * (n - 1)),)), DMA((2 * bufs * n * parts,))]


def gather_tree(pos, src, out, sends, recv, local, group_of=None):
    n = pos.columns
    b, y = pos.plane[0]
    part = (lambda a: src) if group_of is None else (lambda a: src.at[group_of(a)])
    first, second, sibling = pos.device(plane=pos.first), pos.device(plane=pos.second), pos.sibling()
    mine = out.at[pos.c, b, y, pos.a]
    own = pltpu.make_async_copy(part(pos.a), mine, local)
    own.start()
    for k in range(1, n):
        sends.start(part(pos.at(k)), mine, recv.at[k], pos.column(k))
    yield
    for k in range(1, n):
        arrived(out.at[pos.c, b, y, pos.at(n - k)], recv.at[k], first)
    own.wait()
    column = out.at[pos.c, b, y]
    sends.start(column, column, recv.at[n], first)
    sends.start(column, column, recv.at[n + 1], second)
    yield
    column = out.at[pos.c, pos.first[0], pos.first[1]]
    arrived(column, recv.at[n], first)
    sends.start(column, column, recv.at[n + 2], second)
    yield
    for r in range(2):
        arrived(out.at[pos.c, pos.plane[2 + r][0], pos.plane[2 + r][1]], recv.at[n + 1 + r], second)
    sends.start(out.at[pos.c], out.at[pos.c], recv.at[n + 3], sibling)
    yield
    arrived(out.at[1 - pos.c], recv.at[n + 3], sibling)


def gather_tree_sems(n):
    return [DMA((n + 4,)), DMA((n + 4,)), DMA]


def scatter_tree(pos, part, out, from_sib, from_2, from_1, from_col, sends, recv, per_group=False):
    n = pos.columns
    c = pos.c
    first, second, sibling = pos.device(plane=pos.first), pos.device(plane=pos.second), pos.sibling()
    sends.start(part.at[1 - c], from_sib, recv.at[0], sibling)
    yield
    arrived(from_sib, recv.at[0], sibling)
    at = lambda r: (c, pos.plane[r][0], pos.plane[r][1])
    sib = lambda r: (pos.plane[r][0], pos.plane[r][1])
    for r in (3, 2):
        part[at(r)] = (part[at(r)].astype(F32) + from_sib[sib(r)].astype(F32)).astype(BF)
        sends.start(part.at[at(r)], from_2.at[r - 2], recv.at[1 + r - 2], second)
    yield
    arrived(from_2.at[1], recv.at[2], second)
    part[at(1)] = (part[at(1)].astype(F32) + from_sib[sib(1)].astype(F32) + from_2[1].astype(F32)).astype(BF)
    sends.start(part.at[at(1)], from_1, recv.at[3], first)
    arrived(from_2.at[0], recv.at[1], second)
    yield
    arrived(from_1, recv.at[3], first)
    total = part[at(0)].astype(F32) + from_sib[sib(0)].astype(F32) + from_2[0].astype(F32) + from_1[...].astype(F32)
    part[at(0)] = total.astype(BF)
    mine = part.at[at(0)]
    for k in range(1, n):
        sends.start(mine.at[pos.at(k)], from_col.at[k], recv.at[3 + k], pos.column(k))
    yield
    total = mine[pos.a].astype(F32)
    if per_group:
        out[pos.a // (n // GROUPS)] = total[: out.shape[1]]
    for k in range(1, n):
        arrived(from_col.at[k], recv.at[3 + k], pos.column(k))
        if per_group:
            out[pos.at(n - k) // (n // GROUPS)] = from_col[k].astype(F32)[: out.shape[1]]
        else:
            total = total + from_col[k].astype(F32)
    if not per_group:
        cut = out[0].shape[0]
        out[0][...] = total[:cut]
        out[1][...] = total[cut:]
    sends.finish()


def scatter_tree_scratch(n, shape):
    v = lambda *lead: pltpu.VMEM(lead + tuple(shape), BF)
    return [v(2, 2, n), v(2, n), v(n), v(n), DMA((n + 4,)), DMA((n + 4,))]


class SumCtx:
    def __init__(self, pos, parts, send, recv):
        self.pos, self.parts, self.send, self.recv = pos, parts, send, recv

    def copies(self, a, way):
        pos, n = self.pos, self.pos.columns
        for i, (part, from_b, from_col) in enumerate(self.parts):
            base = 2 * n * i
            if way == "b":
                yield remote(part.at[2 * a + 1 - pos.b], from_b.at[a], self.send.at[base + a], self.recv.at[base + a], pos.flip_b())
            else:
                device = pos.device(a=a)
                yield remote(part.at[2 * a + pos.b], from_col.at[pos.a], self.send.at[base + n + a], self.recv.at[base + n + pos.a], device)

    def push(self, a):
        for copy in self.copies(a, "b"):
            copy.start()

    def pass_on(self, a, other=None):
        pos = self.pos
        for copy, (part, from_b, _) in zip(self.copies(a, "b"), self.parts):
            copy.wait_recv()

        def send():
            for copy, (part, from_b, _) in zip(self.copies(a, "column"), self.parts):
                at = 2 * a + pos.b
                part[at] = (part[at].astype(F32) + from_b[a].astype(F32)).astype(BF)
                copy.start()

        if other is None:
            pl.when(a != pos.a)(send)
        elif other:
            send()

    def total(self):
        pos, n = self.pos, self.pos.columns
        sums = []
        for i, (part, from_b, from_col) in enumerate(self.parts):
            total = part[2 * pos.a + pos.b].astype(F32) + from_b[pos.a].astype(F32)
            for k in range(1, n):
                a = pos.at(k)
                sem = self.recv.at[2 * n * i + n + a]
                arrived(from_col.at[a], sem, pos.column(k))
                total = total + from_col[a].astype(F32)
            sums.append(total)
        return sums

    def finish(self):
        pos, n = self.pos, self.pos.columns
        for a in range(n):
            for copy in self.copies(a, "b"):
                copy.wait_send()
        for k in range(1, n):
            for copy in self.copies(pos.at(k), "column"):
                copy.wait_send()


def sum_ctx_scratch(n, *shapes):
    v = lambda shape: pltpu.VMEM((n,) + tuple(shape), BF)
    out = []
    for shape in shapes:
        out += [v(shape), v(shape)]
    return out + [DMA((2 * n * len(shapes),)), DMA((2 * n * len(shapes),))]


class Sizes:
    def __init__(self, nc, nf, rows, width, experts, hidden, owned, padded, capacity, top, docs):
        self.nc, self.nf, self.rows, self.width = nc, nf, rows, width
        self.experts, self.hidden, self.owned, self.padded = experts, hidden, owned, padded
        self.capacity, self.top, self.docs = capacity, top, docs
        self.columns, self.per = nc // 2, nc // GROUPS
        self.heads = width // HEAD_DIM // GROUPS
        self.share = self.heads * HEAD_DIM
        self.slot = nc * rows
        self.all = nc * nf


def scalars(sz, lengths):
    sizes = [lengths[0, d] for d in range(sz.docs)]
    ends, total = [], 0
    for size in sizes:
        total = total + size
        ends.append(total)
    return sizes, ends


def starts(index, sizes, ends):
    low = jnp.zeros_like(index)
    for size, end in zip(sizes, ends):
        low = low + jnp.where(index >= end, size, 0)
    return low


def iota(shape, dim):
    return lax.broadcasted_iota(jnp.int32, shape, dim)


def mean_square(x, width):
    return jnp.sum(x * x, axis=-1, keepdims=True) * (1.0 / width)


def turn(value, cosine, sine):
    half = HEAD_DIM // 2
    lower, upper = value[:half], value[half:]
    return jnp.concatenate([lower * cosine - upper * sine, upper * cosine + lower * sine], axis=0)


def head(h):
    return slice(h * HEAD_DIM, (h + 1) * HEAD_DIM)


def blk(index, rows):
    return pl.ds(pl.multiple_of(index * rows, rows), rows)


class Copies:
    def __init__(self, sems):
        self.sems, self.made = sems, []

    def start(self, src, dst):
        self.made.append(pltpu.make_async_copy(src, dst, self.sems.at[len(self.made)]))
        self.made[-1].start()

    def finish(self):
        for copy in self.made:
            copy.wait()


def swap_send(sz, group, place, src, out, sends, recv, local, h):
    @pl.when(h == group)
    def _():
        pltpu.make_async_copy(src.at[h], out.at[h], local).start()

    copy = remote(src.at[h], out.at[group], sends.at[h], recv.at[group], {"ctx": h * sz.per + place})

    @pl.when(h != group)
    def _():
        copy.start()


def swap_wait(sz, group, place, src, out, sends, recv, local):
    for h in range(GROUPS):
        copy = remote(src.at[h], out.at[h], sends.at[h], recv.at[h], {"ctx": h * sz.per + place})

        @pl.when(h == group)
        def _():
            pltpu.make_async_copy(src.at[h], out.at[h], local).wait()

        @pl.when(h != group)
        def _():
            copy.wait_send()
            copy.wait_recv()


def scatter_owner(pos, part, outs, stage, from_sib, from_y, sends, recv, local):
    parts = len(outs)
    rows = outs[0][0].shape[0] + outs[0][1].shape[0]
    of = lambda p, y, c: part.at[p, blk(y * 2 + c, rows)]
    for t, y in enumerate((1 - pos.y, pos.y)):
        for p in range(parts):
            sends.start(of(p, y, 1 - pos.c), from_sib.at[t, p], recv.at[t * parts + p], pos.sibling())
        yield
    for t, y in enumerate((1 - pos.y, pos.y)):
        for p in range(parts):
            arrived(from_sib.at[t, p], recv.at[t * parts + p], pos.sibling())
            mine = of(p, y, pos.c)
            mine[...] = (mine[...].astype(F32) + from_sib[t, p].astype(F32)).astype(BF)
            if t == 0:
                sends.start(mine, from_y.at[p], recv.at[2 * parts + p], pos.flip_y())
        yield
    copies = []
    for p in range(parts):
        arrived(from_y.at[p], recv.at[2 * parts + p], pos.flip_y())
        if p > 1:
            for copy in copies[p - 2]:
                copy.wait()
        held = stage.at[pl.ds(p % 2 * rows, rows)]
        held[...] = of(p, pos.y, pos.c)[...].astype(F32) + from_y[p].astype(F32)
        cut = outs[p][0].shape[0]
        parts_of = (held.at[pl.ds(0, cut)], held.at[pl.ds(cut, rows - cut)])
        copies.append([pltpu.make_async_copy(src, dst, local.at[p, t]) for t, (src, dst) in enumerate(zip(parts_of, outs[p]))])
        for copy in copies[p]:
            copy.start()
        yield
    for pair in copies[-2:]:
        for copy in pair:
            copy.wait()
    sends.finish()


def scatter_owner_scratch(parts, shape):
    v = lambda *lead: pltpu.VMEM(lead + tuple(shape), BF)
    return [v(2, parts), v(parts), DMA((3 * parts,)), DMA((3 * parts,)), DMA((parts, 2))]


def step(*streams):
    for stream in streams:
        next(stream, None)


def layer_kernel(
    sz, lengths, tokens, cot, routes, gain_own, router_own, spread, wq_send, wo_own, ffn_send,
    o_out, o_tokens, o_wq, o_wo, o_small, o_in, o_down, o_shared_in, o_shared_down,
    x_all, wq_all, wo_all, wo_send, stage, wt, wo, small, normed, qt, kt, vt, prob, o_send, attn, resid, table,
    g_all, mix_all, cw_all, ffn_w, hw, dg, du, gm_part, gp_part, y_hold, dw,
    do_send, do, dkt, dvt, dqt_b, dkvt_b,
    *sems,
):
    pos, pos_b = Place(sz.columns), Place(sz.columns, balanced=False)
    ctx = lax.axis_index("ctx")
    group, place = ctx // sz.per, ctx % sz.per
    rows, width, share, n = sz.rows, sz.width, sz.share, sz.columns
    sizes, ends = scalars(sz, lengths)
    group_of = lambda a: a // (n // GROUPS)

    owned = sz.owned
    me = ctx * sz.nf + lax.axis_index("fsdp")
    place_of = (iota((owned, width), 1) == me * owned + iota((owned, width), 0)).astype(BF)
    wo_send[:owned, :] = wo_own[...]
    rest = jnp.zeros((sz.padded - owned - 2 - sz.experts, width), F32)
    first = jnp.zeros((1, width), F32)
    wo_send[owned:, :] = jnp.concatenate([first, dot(gain_own[...], place_of, NN), dot(router_own[...], place_of, NN), rest], axis=0).astype(BF)

    greet(all_partners(pos))
    s = [Sends(sems[3 * i]) for i in range(3)]
    r = lambda i: (sems[3 * i + 1], sems[3 * i + 2])
    swap_sems, swap_back = sems[9:12], sems[12:15]
    gm_sum = SumCtx(pos, [(gm_part, sems[27], sems[28]), (gp_part, sems[29], sems[30])], sems[31], sems[32])
    gn_part, wq_part, wo_part, y_part = x_all, wq_all, wo_all, y_hold
    y_sum = SumCtx(pos, [(y_part, sems[33], sems[34])], sems[35], sems[36])
    gn_sum = SumCtx(pos, [(gn_part, sems[37], sems[38])], sems[39], sems[40])
    t_wq, t_wo, t_ffn = sems[41:47], sems[47:53], sems[53:58]
    toks = GatherLine(pos, [(tokens, x_all)], sems[15], sems[16])
    cots = GatherLine(pos, [(None, g_all)], sems[17], sems[18])
    mixes = GatherLine(pos, [(None, mix_all)], sems[19], sems[20])
    weights = GatherLine(pos, [(None, cw_all)], sems[21], sems[22], parts=1)

    wqs = gather_tree(pos_b, wq_send, wq_all, s[0], *r(0), group_of=group_of)
    wos = gather_tree(pos_b, wo_send, wo_all, s[1], *r(1))
    ffn = gather_fsdp(pos, ffn_send, ffn_w, s[2], *r(2))
    next(wqs)
    toks.start()
    next(wos)
    x_all[ctx] = tokens[...]

    own_rows = ctx * rows + iota((rows, 1), 0)
    live = own_rows < ends[-1]
    g_all[ctx] = jnp.where(live, cot[...].astype(F32), 0.0).astype(BF)
    index = iota((1, sz.slot), 1)
    position = index - jnp.where(index < ends[-1], starts(index, sizes, ends), 0)
    half = HEAD_DIM // 2
    inverse = jnp.exp(iota((half, 1), 0).astype(F32) * (-2.0 * math.log(ROPE_BASE) / HEAD_DIM))
    angles = position.astype(F32) * inverse
    table[0] = jnp.cos(angles)
    table[1] = jnp.sin(angles)
    before = (iota((rows, rows), 0) < iota((rows, rows), 1)).astype(BF)
    live_t = (ctx * rows + iota((1, rows), 1)) < ends[-1]
    base = jnp.zeros((8, 1), F32)
    kept = jnp.zeros((8, rows), F32)
    for k in range(sz.top):
        hot = ((iota((8, rows), 0) == routes[k : k + 1, :]) & live_t).astype(F32)
        earlier = base + dot(hot.astype(BF), before, NN)
        kept = kept + jnp.where(earlier < sz.capacity, hot, 0.0)
        base = base + jnp.sum(hot, axis=1, keepdims=True)
    step(wqs, wos)
    toks.relay(1)
    step(wqs, wos)
    toks.relay(2)
    step(wqs, wos)
    next(ffn)
    toks.relay(3)
    cots.start()
    for k in range(n):
        toks.across(k)
    drive([wqs])

    def packed(h_):
        each = sz.per * rows
        return slice(each * h_ * (h_ + 1) // 2, each * (h_ + 1) * (h_ + 2) // 2)

    def spot(i):
        a_b, y_c = divmod(i, sz.nf)
        return y_c % 2, a_b % 2, y_c // 2, a_b // 2

    for i in range(sz.all):
        stage[i * owned : (i + 1) * owned, : 3 * share] = wq_all[spot(i)][:owned, :].astype(F32)
    wt[...] = stage[:, : 3 * share].T.astype(BF)
    for d in range(sz.nc):
        x = x_all[d].astype(F32)
        inv = lax.rsqrt(mean_square(x, width) + EPSILON)
        normed[d] = (x * inv).astype(BF)
        part = slice(d * rows, (d + 1) * rows)
        kv = dot(wt[share:, :], normed[d], NT)
        for h in range(sz.heads):
            kt[head(h), part] = turn(kv[head(h)], table[0, :, part], table[1, :, part]).astype(BF)
        vt[:, part] = kv[share:].astype(BF)

    for h_ in reversed(range(GROUPS)):
        d = h_ * sz.per + place
        part = blk(d, rows)
        qq = dot(wt[:share, :], normed[d], NT)
        keys = (h_ + 1) * sz.per * rows
        index = d * rows + iota((rows, 1), 0)
        low = starts(index, sizes, ends)
        key = iota((rows, keys), 1)
        allowed = (key >= low) & (key <= index)
        for h in range(sz.heads):
            q = turn(qq[head(h)], table[0, :, part], table[1, :, part]).astype(BF) * BF(1.0 / math.sqrt(HEAD_DIM))
            qt[h_, head(h), :] = q
            score = jnp.where(allowed, dot(q, kt[head(h), :keys], TN), MASKED)
            expo = jnp.exp(score - jnp.max(score, axis=1, keepdims=True))
            p = (expo * (1.0 / jnp.sum(expo, axis=1, keepdims=True))).astype(BF)
            prob[h, :, packed(h_)] = p
            o_send[h_, head(h), :] = dot(vt[head(h), :keys], p, NT).astype(BF)
        swap_send(sz, group, place, o_send, attn, *swap_sems, h_)
        if h_ == 3:
            cots.relay(1)
        if h_ == 1:
            cots.relay(2)
    swap_wait(sz, group, place, o_send, attn, *swap_sems)
    cots.relay(3)
    drive([wos])
    for i in range(sz.all):
        stage[i * owned : (i + 1) * owned, :] = wo_all[spot(i)][:owned, :].astype(F32)
    extra = wo_all[spot(0)][owned:, :].astype(F32)
    for i in range(1, sz.all):
        extra = extra + wo_all[spot(i)][owned:, :].astype(F32)
    small[...] = extra[:8]
    gain_m = small[1:2, :]
    wo[...] = stage[...].astype(BF)

    attn_t = attn[...].reshape(width, rows)
    res = tokens[...].astype(F32) + dot(attn_t, wo[...], TN)
    resid[...] = res
    inv = lax.rsqrt(mean_square(res, width) + EPSILON)
    mixed = (res * inv * gain_m).astype(BF)
    mix_all[ctx] = mixed
    row = iota((8, rows), 0)
    logits = dot(small[...].astype(BF), mixed, NT)
    logits = jnp.concatenate([logits[2:], logits[:2]], axis=0)
    logits = jnp.where(row < sz.experts, logits, MASKED)
    expo = jnp.exp(logits - jnp.max(logits, axis=0, keepdims=True))
    router_prob = expo * (1.0 / jnp.sum(expo, axis=0, keepdims=True))
    weight = router_prob * kept
    high = weight.astype(BF).astype(F32)
    high_row = jnp.where(row == sz.experts, 1.0, high)
    cw_all[ctx] = jnp.concatenate([high_row, weight - high], axis=0).astype(BF)

    weights.start()
    mixes.start()
    step(ffn)

    chunk = 2 * rows

    half_units = sz.nf // 2 * ffn_send.shape[1]
    cuts = ((0, 384), (384, half_units - 384))

    def units_at(y, cut):
        return pl.ds(pl.multiple_of(y * half_units + cut[0], 128), cut[1])

    def hidden_units(a, y):
        at_rows = blk(a, chunk)
        x = mix_all[pl.ds(2 * a, 2)].reshape(chunk, width)
        g = g_all[pl.ds(2 * a, 2)].reshape(chunk, width)
        pair = jnp.zeros((16, chunk), F32)
        for cut in cuts:
            at = units_at(y, cut)
            gate = dot(x, ffn_w[0, at, :], NT)
            up = dot(x, ffn_w[1, at, :], NT)
            back = dot(g, ffn_w[2, at, :], NT)
            weight = jnp.concatenate([dot(cw_all[2 * a + i], spread[:16, at], TN) for i in range(2)], axis=0)
            sig = 1.0 / (1.0 + jnp.exp(-gate))
            act = gate * sig
            hid = act * up
            pair = pair + dot(spread[16:, at], (hid * back).astype(BF), NT)
            hw[at_rows, at] = (hid * weight).astype(BF)
            back = back * weight
            dg[at_rows, at] = (back * up * sig * (1.0 + gate * (1.0 - sig))).astype(BF)
            du[at_rows, at] = (back * act).astype(BF)
        return pair

    def input_grad(a):
        at_rows = blk(a, chunk)
        total = dot(dg[at_rows, :], ffn_w[0], NN) + dot(du[at_rows, :], ffn_w[1], NN)
        gm_part[pl.ds(2 * a, 2)] = total.astype(BF).reshape(2, rows, width)
        gm_sum.push(a)

    near = [pos.a, jnp.where(pos.a == 0, 1, jnp.where(pos.a == 1, 0, jnp.where(pos.a == 2, 3, 2)))]
    near += [jnp.where(pos.a < 2, 2, 1), jnp.where(pos.a < 2, 3, 0)]
    for i in range(n):
        if i + 1 < n:
            weights.relay(i + 1)
            mixes.relay(i + 1)
        for stream in (cots, weights, mixes):
            stream.across(near[i])
        pair = hidden_units(near[i], pos.y)
        if i == 0:
            drive([ffn])
        pair = (pair + hidden_units(near[i], 1 - pos.y)).astype(BF)
        for t in range(2):
            gp_part[2 * near[i] + t] = pair[:, t * rows : (t + 1) * rows]
        input_grad(near[i])
        if i > 1:
            gm_sum.pass_on(near[i - 1], other=True)
    xs = mix_all[...].reshape(sz.slot, width)
    gs = g_all[...].reshape(sz.slot, width)

    ffn_back = scatter_owner(pos, dw, ((o_in.at[0], o_shared_in.at[0]), (o_in.at[1], o_shared_in.at[1]), (o_down, o_shared_down)), stage, *t_ffn[:2], Sends(t_ffn[2]), *t_ffn[3:])
    for y in (1 - pos.y, pos.y):
        for cut in cuts:
            at = units_at(y, cut)
            for p, (units, rows_of) in enumerate(((dg, xs), (du, xs), (hw, gs))):
                dw[p, at, :] = dot(units[:, at], rows_of, TN).astype(BF)
        step(ffn_back)
        if y is not pos.y:
            gm_sum.pass_on(near[-1], other=True)
            gm_sum.pass_on(pos.a, other=False)
            for a in (*near[1:], pos.a):
                y_part[pl.ds(2 * a, 2)] = dot(hw[blk(a, chunk), :], ffn_w[2], NN).astype(BF).reshape(2, rows, width)
                y_sum.push(a)
    step(ffn_back)

    gm_own, gp_own = gm_sum.total()
    grad_prob = gp_own[:8, :] * kept
    grad_logits = router_prob * (grad_prob - jnp.sum(router_prob * grad_prob, axis=0, keepdims=True))
    shifted = jnp.concatenate([jnp.zeros((2, rows), F32), grad_logits[:6]], axis=0).astype(BF)
    grad_small = dot(shifted, mix_all[ctx], NN)
    grad_mixed = gm_own + dot(shifted, small[...].astype(BF), TN)
    res = resid[...]
    inv = lax.rsqrt(mean_square(res, width) + EPSILON)
    w = grad_mixed * gain_m
    inner = jnp.sum(w * res, axis=-1, keepdims=True) * (1.0 / width)
    grad_resid = jnp.where(live, cot[...].astype(F32), 0.0) + inv * w - res * inner * inv * inv * inv
    grad_gain_m = jnp.sum(grad_mixed * res * inv, axis=0, keepdims=True)
    grad_resid_b = grad_resid.astype(BF)
    grad_attn_t = dot(wo[...], grad_resid_b, NT).astype(BF)
    for h_ in range(GROUPS):
        do_send[h_] = grad_attn_t[h_ * share : (h_ + 1) * share]
    for h_ in range(GROUPS):
        swap_send(sz, group, place, do_send, do, *swap_back, h_)
    gm_sum.finish()
    for x in (*s, toks):
        x.finish()
    wos = scatter_tree(pos, wo_part, (o_wo, o_small), *t_wo[:4], Sends(t_wo[4]), t_wo[5])
    wqs = scatter_tree(pos, wq_part, o_wq, *t_wq[:4], Sends(t_wq[4]), t_wq[5], per_group=True)
    grad_wo = dot(attn[...].reshape(width, rows), grad_resid_b, NN)
    row = iota((sz.padded - owned, width), 0)
    grad_small = jnp.where(row == 1, grad_gain_m, jnp.concatenate([grad_small] * ((sz.padded - owned) // 8), axis=0)).astype(BF)

    for i in range(sz.all):
        wo_part[spot(i) + (slice(0, owned),)] = grad_wo[i * owned : (i + 1) * owned].astype(BF)
        wo_part[spot(i) + (slice(owned, None),)] = grad_small
    step(wos)
    swap_wait(sz, group, place, do_send, do, *swap_back)

    dkt[...] = jnp.zeros_like(dkt)
    dvt[...] = jnp.zeros_like(dvt)
    for h_ in reversed(range(GROUPS)):
        keys = (h_ + 1) * sz.per * rows
        done = slice(h_ * sz.per * rows, keys)
        part = blk(h_ * sz.per + place, rows)
        for h in range(sz.heads):
            d_o = do[h_, head(h), :]
            p = prob[h, :, packed(h_)]
            pf = p.astype(F32)
            grad_p = dot(d_o, vt[head(h), :keys], TN)
            delta = jnp.sum(pf * grad_p, axis=1, keepdims=True)
            grad_s = (pf * (grad_p - delta)).astype(BF)
            dq = dot(kt[head(h), :keys], grad_s, NT) * (1.0 / math.sqrt(HEAD_DIM))
            dqt_b[h_, head(h), :] = turn(dq, table[0, :, part], -table[1, :, part]).astype(BF)
            dkt[head(h), :keys] = dkt[head(h), :keys] + dot(qt[h_, head(h), :], grad_s, NN)
            dvt[head(h), :keys] = dvt[head(h), :keys] + dot(d_o, p, NN)
        for h in range(sz.heads):
            dkvt_b[head(h), done] = turn(dkt[head(h), done], table[0, :, done], -table[1, :, done]).astype(BF)
        dkvt_b[share:, done] = dvt[:, done].astype(BF)
        for t in range(2):
            d = h_ * sz.per + lax.rem(place + 1 + t, 2)
            gn = dot(dkvt_b[:, blk(d, rows)], wt[share:, :], TN)
            if t == 1:
                gn = gn + dot(dqt_b[h_], wt[:share, :], TN)
            gn_part[d] = gn.astype(BF)
        gn_sum.push(h_)
        if h_ < GROUPS - 2:
            gn_sum.pass_on(h_ + 2)
        if h_ < GROUPS - 1:
            y_sum.pass_on(near[GROUPS - 1 - h_], other=True)
        if h_ % 2:
            step(wos)
        if h_ == GROUPS - 1:
            step(ffn_back)
    grad_q = dot(dqt_b[0], normed[place], NN)
    for h_ in range(1, GROUPS):
        grad_q = grad_q + dot(dqt_b[h_], normed[h_ * sz.per + place], NN)
    grad_kv = dot(dkvt_b[...], normed[...].reshape(sz.slot, width), NN)
    grad_w = jnp.concatenate([grad_q, grad_kv], axis=0).T
    wq_part[...] = jnp.zeros_like(wq_part)
    for i in range(sz.all):
        wq_part[spot(i) + (slice(0, owned),)] = grad_w[i * owned : (i + 1) * owned].astype(BF)
    step(wqs)
    gn_sum.pass_on(1)
    gn_sum.pass_on(0)
    drive([wos])
    step(wqs, ffn_back, wqs, ffn_back, wqs)
    drive([wqs, ffn_back])
    y_sum.pass_on(pos.a, other=False)
    (y_own,) = y_sum.total()
    o_out[...] = jnp.where(live, res + y_own, 0.0).astype(BF)
    x = tokens[...].astype(F32)
    inv = lax.rsqrt(mean_square(x, width) + EPSILON)
    (gn_own,) = gn_sum.total()
    w = gn_own
    inner = jnp.sum(w * x, axis=-1, keepdims=True) * (1.0 / width)
    o_tokens[...] = grad_resid + inv * w - x * inner * inv * inv * inv
    for x in (y_sum, gn_sum, cots, mixes, weights):
        x.finish()


def layer(sz, collective_id, lengths, tokens, cot, routes, gain_own, router_own, spread, wq_send, wo_own, ffn_send):
    n, nc, rows, width, share, slot = sz.columns, sz.nc, sz.rows, sz.width, sz.share, sz.slot
    own_units = ffn_send.shape[1]
    units = sz.nf * own_units
    outs = [
        shaped((rows, width)),
        shaped((rows, width), F32),
        shaped((GROUPS, sz.owned, 3 * share), F32),
        shaped((sz.owned, width), F32),
        shaped((sz.padded - sz.owned, width), F32),
        shaped((2, own_units - sz.hidden, width), F32),
        shaped((own_units - sz.hidden, width), F32),
        shaped((2, sz.hidden, width), F32),
        shaped((sz.hidden, width), F32),
    ]
    v = lambda *shape, dtype=BF: pltpu.VMEM(shape, dtype)
    tree = (2, 2, 2, n, sz.padded)
    blocks = v(nc, rows, width)
    scratch = [
        blocks, v(*tree, 3 * share), v(*tree, width), v(sz.padded, width), v(width, width, dtype=F32),
        v(3 * share, width), v(width, width), v(8, width, dtype=F32), blocks,
        v(GROUPS, share, rows), v(share, slot), v(share, slot), v(sz.heads, rows, slot * (GROUPS + 1) // 2), v(GROUPS, share, rows),
        v(GROUPS, share, rows), v(rows, width, dtype=F32), v(2, HEAD_DIM // 2, slot, dtype=F32),
        blocks, blocks, v(nc, 16, rows), v(3, units, width), v(slot, units), v(slot, units), v(slot, units),
        blocks, v(nc, 16, rows), blocks, v(3, units, width),
        v(GROUPS, share, rows), v(GROUPS, share, rows), v(share, slot, dtype=F32), v(share, slot, dtype=F32),
        v(GROUPS, share, rows), v(2 * share, slot),
    ]
    sems = gather_tree_sems(n) * 2 + gather_fsdp_sems(3)
    sems += [DMA((GROUPS,)), DMA((GROUPS,)), DMA] * 2
    sems += gather_line_sems(n) * 3 + gather_line_sems(n, parts=1) + [DMA] * 4
    sems += sum_ctx_scratch(n, (rows, width), (16, rows)) + sum_ctx_scratch(n, (rows, width)) * 2
    sems += scatter_tree_scratch(n, (sz.padded, 3 * share)) + scatter_tree_scratch(n, (sz.padded, width))
    sems += scatter_owner_scratch(3, (own_units, width))
    hbm, vmem = pl.BlockSpec(memory_space=pl.ANY), pl.BlockSpec(memory_space=pltpu.VMEM)
    return pl.pallas_call(
        functools.partial(layer_kernel, sz),
        out_shape=outs,
        in_specs=[pl.BlockSpec(memory_space=pltpu.SMEM)] + [vmem] * 6 + [hbm, vmem, hbm],
        out_specs=[vmem] * 5 + [hbm] * 4,
        scratch_shapes=scratch + sems,
        compiler_params=pltpu.CompilerParams(collective_id=collective_id, has_side_effects=True, vmem_limit_bytes=63 << 20),
        name="layer",
    )(lengths, tokens, cot, routes, gain_own, router_own, spread, wq_send, wo_own, ffn_send)


def gather_start_kernel(columns, group_of, tokens, wq, wo, ffn, cot, o_tokens, o_wq, o_wo, o_ffn, o_cot, *sems):
    pos = Place(columns)
    greet(all_partners(pos))
    s = [Sends(sems[3 * i]) for i in range(5)]
    r = lambda i: (sems[3 * i + 1], sems[3 * i + 2])
    streams = [
        gather_ctx(pos, tokens, o_tokens, s[0], *r(0)),
        gather_all(pos, wq, o_wq, s[1], *r(1), group_of=group_of),
        gather_all(pos, wo, o_wo, s[2], *r(2)),
        gather_fsdp(pos, ffn, o_ffn, s[3], *r(3)),
    ]
    drive(streams)
    drive([gather_ctx(pos, cot, o_cot, s[4], *r(4))])
    for x in s:
        x.finish()


def call(kernel, collective_id, ins, outs, scratch, name, space=pl.ANY, in_space=None):
    return pl.pallas_call(
        kernel,
        out_shape=outs,
        in_specs=[pl.BlockSpec(memory_space=in_space or space)] * len(ins),
        out_specs=jax.tree.map(lambda _: pl.BlockSpec(memory_space=space), outs),
        scratch_shapes=scratch,
        compiler_params=pltpu.CompilerParams(
            collective_id=collective_id, has_side_effects=True, vmem_limit_bytes=60 << 20
        ),
        name=name,
    )(*ins)


def gather_start(nc, tokens, wq, wo, ffn, cot):
    n = nc // 2
    group_of = lambda a: a // (n // GROUPS)
    sems = gather_ctx_sems(n) + gather_all_sems(n) * 2 + gather_fsdp_sems(ffn.shape[0]) + gather_ctx_sems(n)
    outs = (
        shaped((nc,) + tokens.shape),
        shaped((nc * 4,) + wq.shape[1:]),
        shaped((nc * 4,) + wo.shape),
        shaped((ffn.shape[0], 4) + ffn.shape[1:]),
        shaped((nc,) + cot.shape),
    )
    return call(functools.partial(gather_start_kernel, n, group_of), 1, (tokens, wq, wo, ffn, cot), outs, sems, "gather_start")


def gather_ctx_kernel(columns, src, out, send, recv, local):
    pos = Place(columns)
    greet([pos.column(k) for k in range(1, columns)] + [pos.flip_b()])
    s = Sends(send)
    drive([gather_ctx(pos, src, out, s, recv, local)])
    s.finish()


def gather_rows(nc, src, collective_id):
    n = nc // 2
    return call(functools.partial(gather_ctx_kernel, n), collective_id, (src,), shaped((nc,) + src.shape), gather_ctx_sems(n), "gather_rows")


def swap_kernel(nc, src, out, send, recv, local):
    per = nc // GROUPS
    ctx = lax.axis_index("ctx")
    group, place = ctx // per, ctx % per
    peer = lambda k: lax.rem(group + k, GROUPS)
    device = lambda k: {"ctx": peer(k) * per + place}
    greet([device(k) for k in range(1, GROUPS)])
    own = pltpu.make_async_copy(src.at[group], out.at[group], local)
    own.start()
    copies = []
    for k in range(1, GROUPS):
        copies.append(remote(src.at[peer(k)], out.at[group], send.at[k], recv.at[k], device(k)))
        copies[-1].start()
    for k in range(1, GROUPS):
        arrived(out.at[peer(GROUPS - k)], recv.at[k], device(k))
    own.wait()
    for copy in copies:
        copy.wait_send()


def swap(nc, src, collective_id):
    return call(functools.partial(swap_kernel, nc), collective_id, (src,), shaped(src.shape), [DMA((GROUPS,)), DMA((GROUPS,)), DMA], "swap")


def scatter_ctx_kernel(columns, part, out, acc, from_b, from_col, send, recv, local):
    pos = Place(columns)
    greet([pos.column(k) for k in range(1, columns)] + [pos.flip_b()])
    s = Sends(send)
    drive([scatter_ctx(pos, part, out, acc, from_b, from_col, s, recv, local)])
    s.finish()


def scatter_rows(nc, part, collective_id):
    n = nc // 2
    return pl.pallas_call(
        functools.partial(scatter_ctx_kernel, n),
        out_shape=shaped(part.shape[1:], F32),
        in_specs=[pl.BlockSpec(memory_space=pl.ANY)],
        out_specs=pl.BlockSpec(memory_space=pltpu.VMEM),
        scratch_shapes=scatter_ctx_scratch(n, part.shape[1:]),
        compiler_params=pltpu.CompilerParams(collective_id=collective_id, has_side_effects=True, vmem_limit_bytes=60 << 20),
        name="scatter_rows",
    )(part)


def scatter_end_kernel(columns, gn, wq, wo, ffn, yy, o_gn, o_wq, o_wo, o_ffn, o_yy, *scratch):
    pos = Place(columns)
    greet(all_partners(pos))
    c1, a1, a2, f1, c2 = scratch[0:6], scratch[6:14], scratch[14:22], scratch[22:28], scratch[28:34]
    s = [Sends(x[-3]) for x in (c1, a1, a2, f1, c2)]
    drive(
        [
            scatter_ctx(pos, gn, o_gn, *c1[:-3], s[0], *c1[-2:]),
            scatter_fsdp(pos, [ffn.at[p] for p in range(ffn.shape[0])], o_ffn, *f1[:-3], s[3], *f1[-2:]),
            scatter_all(pos, wq, o_wq, *a1[:-3], s[1], *a1[-2:], per_group=True),
            scatter_all(pos, wo, o_wo, *a2[:-3], s[2], *a2[-2:]),
            scatter_ctx(pos, yy, o_yy, *c2[:-3], s[4], *c2[-2:]),
        ]
    )
    for x in s:
        x.finish()


def scatter_end(nc, gn, wq, wo, ffn, yy):
    n = nc // 2
    scratch = (
        scatter_ctx_scratch(n, gn.shape[1:])
        + scatter_all_scratch(n, wq.shape[1:])
        + scatter_all_scratch(n, wo.shape[1:])
        + scatter_fsdp_scratch(ffn.shape[0], ffn.shape[2:])
        + scatter_ctx_scratch(n, yy.shape[1:])
    )
    outs = (
        shaped(gn.shape[1:], F32),
        shaped((GROUPS,) + wq.shape[1:], F32),
        shaped(wo.shape[1:], F32),
        shaped((ffn.shape[0],) + ffn.shape[2:], F32),
        shaped(yy.shape[1:], F32),
    )
    return call(
        functools.partial(scatter_end_kernel, n), 6, (gn, wq, wo, ffn, yy), outs, scratch, "scatter_end",
        space=pltpu.VMEM, in_space=pl.ANY,
    )


def doc_ids(row_index, doc_ends):
    return jnp.sum((row_index[:, None] >= doc_ends[None, :]).astype(jnp.int32), axis=1)


def positions(row_index, lengths):
    doc_ends = jnp.cumsum(lengths)
    doc_starts = doc_ends - lengths
    doc_num = doc_ids(row_index, doc_ends)
    column = jnp.arange(lengths.shape[0], dtype=jnp.int32)
    begins = jnp.sum(jnp.where(doc_num[:, None] == column[None, :], doc_starts[None, :], 0), axis=1)
    return doc_num, row_index - begins


def rope_tables(position):
    half_dim = HEAD_DIM // 2
    inverse = ROPE_BASE ** (-2.0 * jnp.arange(half_dim, dtype=F32) / HEAD_DIM)
    angles = position.astype(F32)[:, None] * inverse[None, :]
    return jnp.cos(angles), jnp.sin(angles)


def rotate(values, cosine, sine):
    half_dim = values.shape[-1] // 2
    lower, upper = values[..., :half_dim], values[..., half_dim:]
    cosine, sine = cosine[:, None, :], sine[:, None, :]
    return jnp.concatenate([lower * cosine - upper * sine, upper * cosine + lower * sine], axis=-1)


def kept_rows(route_rows, live_rows, experts, capacity):
    count, top = route_rows.shape
    hot = (route_rows[:, :, None] == jnp.arange(experts, dtype=jnp.int32)) & live_rows[:, None, None]
    hot = hot.astype(F32)
    before = jnp.tril(jnp.ones((count, count), F32), -1)
    kept = jnp.zeros((count, experts), F32)
    base = jnp.zeros((1, experts), F32)
    for k in range(top):
        earlier = base + jnp.dot(before, hot[:, k])
        kept = kept + hot[:, k] * (earlier < capacity)
        base = base + jnp.sum(hot[:, k], axis=0, keepdims=True)
    return kept


def pad_rows(x, rows):
    return jnp.pad(x, [(0, rows - x.shape[0])] + [(0, 0)] * (x.ndim - 1))


def body_wide(tokens, doc_lengths, routes, cotangent, attn_gain, w_qkv, w_out, mlp_gain, router, expert_in, expert_out, shared_in, shared_out):
    nc = lax.axis_size("ctx")
    nf = lax.axis_size("fsdp")
    rows, width = tokens.shape[1:]
    heads = width // HEAD_DIM
    experts = expert_in.shape[1]
    hidden = expert_in.shape[0]
    top = routes.shape[2]
    capacity = 5 * top * rows // (4 * experts)
    per = nc // GROUPS
    ctx = lax.axis_index("ctx")
    group, place = ctx // per, ctx % per
    slot = nc * rows
    mine = heads // GROUPS
    share = mine * HEAD_DIM
    scale = 1.0 / math.sqrt(HEAD_DIM)
    owned = w_out.shape[0]
    padded = -(-(owned + 2 + experts) // 16) * 16

    wq_send = w_qkv.reshape(owned, 3, GROUPS, share).transpose(2, 0, 1, 3).reshape(GROUPS, owned, 3 * share)
    wq_send = jnp.pad(wq_send, ((0, 0), (0, padded - owned), (0, 0)))
    small = jnp.concatenate([attn_gain[None], mlp_gain[None], router.T], axis=0)
    wo_send = pad_rows(jnp.concatenate([w_out, jnp.pad(small, ((0, 0), (0, width - owned)))], axis=0), padded)
    gate_up = jnp.concatenate([expert_in.transpose(2, 1, 0, 3), shared_in.transpose(1, 0, 2)[:, None]], axis=1)
    down = jnp.concatenate([expert_out.transpose(1, 0, 2), shared_out[None]], axis=0)
    ffn_send = jnp.concatenate([gate_up, down[None]], axis=0).reshape(3, (experts + 1) * hidden, width)

    x_all, wq_all, wo_all, ffn_all, cot_all = gather_start(nc, tokens[0], wq_send, wo_send, ffn_send, cotangent[0])
    units = nf * (experts + 1) * hidden
    w_gate, w_up, w_down = (ffn_all[p].reshape(units, width) for p in range(3))
    wq = wq_all[:, :owned].reshape(width, 3 * share)
    wo = wo_all[:, :owned].reshape(width, width)
    small = wo_all[:, owned : owned + 2 + experts, :owned].transpose(1, 0, 2).reshape(2 + experts, width)
    gain_a, gain_m = small[0].astype(F32), small[1].astype(F32)
    router_t = small[2:]

    all_rows = jnp.arange(slot, dtype=jnp.int32)
    doc_num, position = positions(all_rows, doc_lengths[0])
    cosine, sine = rope_tables(position)
    live_all = (doc_num < doc_lengths.shape[1]).astype(F32)[:, None]
    x_slot = x_all.reshape(slot, width).astype(F32)
    inv_attn = lax.rsqrt(jnp.mean(x_slot * x_slot, axis=-1, keepdims=True) + EPSILON)
    normed = (x_slot * inv_attn * gain_a).astype(BF)

    def queries(v):
        return lax.dynamic_index_in_dim(v.reshape((GROUPS, per, rows) + v.shape[1:]), place, 1, False).reshape((GROUPS * rows,) + v.shape[1:])

    normed_q = queries(normed)
    cos_q, sin_q = queries(cosine), queries(sine)
    q = rotate(dot(normed_q, wq[:, :share], ((1,), (0,))).reshape(-1, mine, HEAD_DIM), cos_q, sin_q).astype(BF)
    k = rotate(dot(normed, wq[:, share : 2 * share], ((1,), (0,))).reshape(slot, mine, HEAD_DIM), cosine, sine).astype(BF)
    v = dot(normed, wq[:, 2 * share :], ((1,), (0,))).reshape(slot, mine, HEAD_DIM).astype(BF)
    rows_q, doc_q = queries(all_rows), queries(doc_num)
    allowed = (doc_q[:, None] == doc_num[None, :]) & (all_rows[None, :] <= rows_q[:, None])
    scores = jnp.einsum("qhd,khd->hqk", q, k, preferred_element_type=F32) * scale
    scores = jnp.where(allowed[None], scores, MASKED)
    expo = jnp.exp(scores - jnp.max(scores, axis=-1, keepdims=True))
    prob = expo / jnp.sum(expo, axis=-1, keepdims=True)
    prob_b = prob.astype(BF)
    o = jnp.einsum("hqk,khd->qhd", prob_b, v, preferred_element_type=F32).astype(BF)

    o_own = swap(nc, o.reshape(GROUPS, rows, share), 2)
    attn = o_own.transpose(1, 0, 2).reshape(rows, width)

    row_index = ctx * rows + jnp.arange(rows, dtype=jnp.int32)
    doc_own, _ = positions(row_index, doc_lengths[0])
    live_rows = doc_own < doc_lengths.shape[1]
    live = live_rows.astype(F32)[:, None]
    x = tokens[0].astype(F32)
    resid = x + dot(attn, wo, ((1,), (0,)))
    inv_mlp = lax.rsqrt(jnp.mean(resid * resid, axis=-1, keepdims=True) + EPSILON)
    mixed = (resid * inv_mlp * gain_m).astype(BF)
    logits = dot(mixed, router_t, ((1,), (1,)))
    router_prob = jax.nn.softmax(logits, axis=-1)
    kept = kept_rows(routes[0], live_rows, experts, capacity)
    weight = router_prob * kept
    high = weight.astype(BF)
    low = (weight - high.astype(F32)).astype(BF)
    extra = pad_rows(jnp.pad(jnp.concatenate([high, low], axis=1).T, ((0, 0), (0, width - rows))), 16)
    mixed_all = gather_rows(nc, jnp.concatenate([mixed, extra], axis=0), 3)

    weights = mixed_all[:, rows : rows + 2 * experts, :rows].astype(F32)
    weights = (weights[:, :experts] + weights[:, experts:]).transpose(0, 2, 1).reshape(slot, experts)
    mix = mixed_all[:, :rows].reshape(slot, width)
    g = (cot_all.reshape(slot, width) * live_all.astype(BF)).astype(BF)
    unit_weight = jnp.concatenate([weights, jnp.ones((slot, 1), F32)], axis=1)
    unit_weight = jnp.tile(jnp.repeat(unit_weight, hidden, axis=1), (1, nf))
    gate = dot(mix, w_gate, ((1,), (1,)))
    up = dot(mix, w_up, ((1,), (1,)))
    sig = jax.nn.sigmoid(gate)
    hid = gate * sig * up
    hid_w = (hid * unit_weight).astype(BF)
    y_part = dot(hid_w, w_down, ((1,), (0,))).astype(BF)
    back = dot(g, w_down, ((1,), (1,)))
    pair = (hid * back).reshape(slot, nf, experts + 1, hidden).sum(axis=(1, 3))[:, :experts]
    back_w = back * unit_weight
    d_gate = (back_w * up * sig * (1.0 + gate * (1.0 - sig))).astype(BF)
    d_up = (back_w * gate * sig).astype(BF)
    gm_part = (dot(d_gate, w_gate, ((1,), (0,))) + dot(d_up, w_up, ((1,), (0,)))).astype(BF)
    d_w = jnp.stack([dot(d_gate, mix, ((0,), (0,))), dot(d_up, mix, ((0,), (0,))), dot(hid_w, g, ((0,), (0,)))]).astype(BF)
    pair_t = pair.reshape(nc, rows, experts).transpose(0, 2, 1)
    pair_t = jnp.pad(pair_t, ((0, 0), (0, 16 - experts), (0, width - rows))).astype(BF)
    gm_all = scatter_rows(nc, jnp.concatenate([gm_part.reshape(nc, rows, width), pair_t], axis=1), 4)

    grad_prob = gm_all[rows : rows + experts, :rows].T * kept
    grad_logits = (router_prob * (grad_prob - jnp.sum(router_prob * grad_prob, axis=-1, keepdims=True))).astype(BF)
    grad_router_t = dot(grad_logits, mixed, ((0,), (0,)))
    grad_mixed = gm_all[:rows] + dot(grad_logits, router_t, ((1,), (0,)))
    grad_top = cotangent[0].astype(F32) * live
    w = grad_mixed * gain_m
    grad_resid = grad_top + inv_mlp * w - resid * jnp.mean(w * resid, axis=-1, keepdims=True) * inv_mlp**3
    grad_gain_m = jnp.sum(grad_mixed * resid * inv_mlp, axis=0)
    grad_resid_b = grad_resid.astype(BF)
    grad_wo = dot(attn, grad_resid_b, ((0,), (0,)))
    grad_attn = dot(grad_resid_b, wo, ((1,), (1,))).astype(BF)
    do = swap(nc, grad_attn.reshape(rows, GROUPS, share).transpose(1, 0, 2), 5).reshape(GROUPS * rows, mine, HEAD_DIM)

    grad_p = jnp.einsum("qhd,khd->hqk", do, v, preferred_element_type=F32)
    delta = jnp.sum(prob * grad_p, axis=-1, keepdims=True)
    grad_s = (prob * (grad_p - delta)).astype(BF)
    dq = jnp.einsum("hqk,khd->qhd", grad_s, k, preferred_element_type=F32) * scale
    dk = jnp.einsum("hqk,qhd->khd", grad_s, q, preferred_element_type=F32) * scale
    dv = jnp.einsum("hqk,qhd->khd", prob_b, do, preferred_element_type=F32)
    dq = rotate(dq, cos_q, -sin_q).reshape(GROUPS * rows, share).astype(BF)
    dk = rotate(dk, cosine, -sine).reshape(slot, share)
    dkv = jnp.concatenate([dk, dv.reshape(slot, share)], axis=1).astype(BF)
    grad_wq = jnp.concatenate([dot(normed_q, dq, ((0,), (0,))), dot(normed, dkv, ((0,), (0,)))], axis=1)
    gn_q = dot(dq, wq[:, :share], ((1,), (1,))).reshape(GROUPS, 1, rows, width)
    here = (jnp.arange(per) == place).astype(F32)[None, :, None, None]
    gn = dot(dkv, wq[:, share:], ((1,), (1,))).reshape(GROUPS, per, rows, width) + gn_q * here
    gn_part = gn.reshape(nc, rows, width).astype(BF)

    gn_full = gn.reshape(slot, width)
    grad_gain_a = jnp.sum(gn_full * x_slot * inv_attn, axis=0)
    small = jnp.concatenate([grad_gain_a[None], grad_gain_m[None], grad_router_t], axis=0)
    small = small.reshape(2 + experts, nc * nf, owned).transpose(1, 0, 2)
    wo_part = jnp.concatenate([grad_wo.reshape(nc * nf, owned, width), jnp.pad(small, ((0, 0), (0, 0), (0, width - owned)))], axis=1)
    wo_part = jnp.pad(wo_part, ((0, 0), (0, padded - wo_part.shape[1]), (0, 0))).astype(BF)
    wq_part = jnp.pad(grad_wq.reshape(nc * nf, owned, 3 * share), ((0, 0), (0, padded - owned), (0, 0))).astype(BF)
    ffn_part = d_w.reshape(3, nf, (experts + 1) * hidden, width)
    gn_own, wq_own, wo_own, ffn_own, y_own = scatter_end(nc, gn_part, wq_part, wo_part, ffn_part, y_part.reshape(nc, rows, width))

    layer_out = (live * (resid + y_own)).astype(BF)[None]
    inv = lax.rsqrt(jnp.mean(x * x, axis=-1, keepdims=True) + EPSILON)
    w = gn_own * gain_a
    grad_tokens = (grad_resid + inv * w - x * jnp.mean(w * x, axis=-1, keepdims=True) * inv**3)[None]
    grad_w_qkv = wq_own[:, :owned].reshape(GROUPS, owned, 3, share).transpose(1, 2, 0, 3).reshape(owned, 3 * width)
    small = wo_own[owned : owned + 2 + experts, :owned]
    out = ffn_own.reshape(3, experts + 1, hidden, width)
    return (
        layer_out,
        grad_tokens,
        small[0],
        grad_w_qkv,
        wo_own[:owned],
        small[1],
        small[2:].T,
        out[:2, :experts].transpose(2, 1, 0, 3),
        out[2, :experts].transpose(1, 0, 2),
        out[:2, experts].transpose(1, 0, 2),
        out[2, experts],
    )


def body(tokens, doc_lengths, routes, cotangent, attn_gain, w_qkv, w_out, mlp_gain, router, expert_in, expert_out, shared_in, shared_out):
    nc, nf = lax.axis_size("ctx"), lax.axis_size("fsdp")
    rows, width = tokens.shape[1:]
    experts, hidden, top = expert_in.shape[1], expert_in.shape[0], routes.shape[2]
    owned = w_out.shape[0]
    if nc != 2 * GROUPS or 2 * nc * rows * width > FUSED_BYTES:
        return body_wide(
            tokens, doc_lengths, routes, cotangent, attn_gain, w_qkv, w_out, mlp_gain, router, expert_in, expert_out, shared_in, shared_out
        )
    padded = -(-(owned + 8) // 16) * 16
    sz = Sizes(nc, nf, rows, width, experts, hidden, owned, padded, 5 * top * rows // (4 * experts), top, doc_lengths.shape[1])
    share = sz.share
    device = lax.axis_index("ctx") * nf + lax.axis_index("fsdp")

    gain = attn_gain.astype(F32)[:, None]
    wq_send = (w_qkv.astype(F32) * gain).astype(BF).reshape(owned, 3, GROUPS, share).transpose(2, 0, 1, 3).reshape(GROUPS, owned, 3 * share)
    wq_send = jnp.pad(wq_send, ((0, 0), (0, padded - owned), (0, 0)))
    gate_up = jnp.concatenate([expert_in.transpose(2, 1, 0, 3), shared_in.transpose(1, 0, 2)[:, None]], axis=1)
    down = jnp.concatenate([expert_out.transpose(1, 0, 2), shared_out[None]], axis=0)
    ffn_send = jnp.concatenate([gate_up, down[None]], axis=0).reshape(3, (experts + 1) * hidden, width)

    units = nf * (experts + 1) * hidden
    of = np.arange(units) // hidden % (experts + 1)
    spread = np.zeros((32, units), np.float32)
    for e in range(experts + 1):
        spread[e] = of == e
    for e in range(experts):
        spread[8 + e] = of == e
        spread[16 + e] = of == e

    layer_out, grad_tokens, wq_own, grad_w_out, small, grad_in, grad_down, shared_in_own, shared_out_own = layer(
        sz, 1, doc_lengths, tokens[0], cotangent[0], routes[0].T, mlp_gain[None], router.T, jnp.asarray(spread, BF), wq_send, w_out, ffn_send
    )

    grad_w = wq_own.reshape(GROUPS, owned, 3, share).transpose(1, 2, 0, 3).reshape(owned, 3 * width)
    gain_a = jnp.sum(grad_w * w_qkv.astype(F32), axis=1)
    grad_w_qkv = grad_w * gain
    small = lax.dynamic_slice(small, (0, device * owned), (2 + experts, owned))
    grad_in = grad_in.reshape(2, experts, hidden, width)
    grad_down = grad_down.reshape(experts, hidden, width)
    return (
        layer_out[None],
        grad_tokens[None],
        gain_a,
        grad_w_qkv,
        grad_w_out,
        small[1],
        small[2:].T,
        grad_in.transpose(2, 1, 0, 3),
        grad_down.transpose(1, 0, 2),
        shared_in_own.transpose(1, 0, 2),
        shared_out_own,
    )


def solution(mesh):
    rows = P("fsdp", "ctx", None)
    flat = ("ctx", "fsdp")
    weights = (P(flat), P(flat, None), P(flat, None), P(flat), P(flat, None))
    ffn = (P(flat, None, None, None), P(flat, None, None), P(flat, None, None), P(flat, None))
    return jax.shard_map(
        body,
        mesh=mesh,
        in_specs=(rows, P("fsdp", None), rows, rows) + weights + ffn,
        out_specs=(rows, rows) + weights + ffn,
        check_vma=False,
    )
```

```python
import functools
import math

import jax
import jax.numpy as jnp
import numpy as np
from jax import lax
from jax.experimental import pallas as pl
from jax.experimental.pallas import tpu as pltpu
from jax.sharding import PartitionSpec as P

HEAD_DIM = 64
EPSILON = 1e-05
ROPE_BASE = 10000.0
MASKED = -1e30
NN, NT, TN = ((1,), (0,)), ((1,), (1,)), ((0,), (0,))
FUSED_BYTES = 2 << 20
GROUPS = 4
MESH = pl.DeviceIdType.MESH
DMA = pltpu.SemaphoreType.DMA
BF = jnp.bfloat16
F32 = jnp.float32


class Place:
    def __init__(self, columns, balanced=True):
        ctx, fsdp = lax.axis_index("ctx"), lax.axis_index("fsdp")
        self.columns = columns
        self.a, self.b = ctx // 2, ctx % 2
        self.y, self.c = fsdp // 2, fsdp % 2
        flip_b = (1 - self.b, self.y)
        flip_y = (self.b, 1 - self.y)
        core = (self.c == 0) if balanced else (self.c >= 0)
        self.first = tuple(jnp.where(core, p, q) for p, q in zip(flip_b, flip_y))
        self.second = tuple(jnp.where(core, q, p) for p, q in zip(flip_b, flip_y))
        self.plane = [(self.b, self.y), self.first, self.second, (1 - self.b, 1 - self.y)]
        self.sib_plane = [(self.b, self.y), self.second, self.first, (1 - self.b, 1 - self.y)]

    def at(self, step):
        return lax.rem(self.a + step, self.columns)

    def device(self, a=None, plane=None, c=None):
        b, y = plane if plane is not None else (self.b, self.y)
        a = self.a if a is None else a
        c = self.c if c is None else c
        return {"ctx": a * 2 + b, "fsdp": y * 2 + c}

    def column(self, step):
        return self.device(a=self.at(step))

    def flip_b(self):
        return self.device(plane=(1 - self.b, self.y))

    def flip_y(self):
        return self.device(plane=(self.b, 1 - self.y))

    def sibling(self):
        return self.device(c=1 - self.c)

    def chunk(self, step, plane, c):
        return (self.at(step) * 2 + plane[0]) * 4 + plane[1] * 2 + c


def greet(devices):
    barrier = pltpu.get_barrier_semaphore()
    for device in devices:
        pl.semaphore_signal(barrier, inc=1, device_id=device, device_id_type=MESH)
    pl.semaphore_wait(barrier, len(devices))


def remote(src, dst, send, recv, device):
    return pltpu.make_async_remote_copy(
        src_ref=src, dst_ref=dst, send_sem=send, recv_sem=recv, device_id=device, device_id_type=MESH
    )


class Sends:
    def __init__(self, sems):
        self.sems, self.made = sems, []

    def start(self, src, dst, recv, device):
        copy = remote(src, dst, self.sems.at[len(self.made)], recv, device)
        copy.start()
        self.made.append(copy)

    def finish(self):
        for copy in self.made:
            copy.wait_send()


def arrived(dst, recv, device):
    remote(dst, dst, recv, recv, device).wait_recv()


def gather_ctx(pos, src, out, sends, recv, local, there=lambda slot: None):
    n = pos.columns
    me = pos.a * 2 + pos.b
    own = pltpu.make_async_copy(src, out.at[me], local)
    own.start()
    for k in range(1, n):
        sends.start(src, out.at[me], recv.at[k], pos.column(k))
    sends.start(src, out.at[me], recv.at[n], pos.flip_b())
    yield
    own.wait()
    there(me)
    for k in range(1, n):
        slot = pos.at(n - k) * 2 + pos.b
        arrived(out.at[slot], recv.at[k], pos.column(k))
        sends.start(out.at[slot], out.at[slot], recv.at[n + k], pos.flip_b())
        there(slot)
        yield
    for k in range(n):
        slot = pos.at(n - k) * 2 + 1 - pos.b
        arrived(out.at[slot], recv.at[n + k], pos.flip_b())
        there(slot)
        yield


def gather_ctx_sems(n):
    return [DMA((2 * n,)), DMA((2 * n,)), DMA]


def gather_fsdp(pos, src, out, sends, recv, local):
    parts = src.shape[0]
    if len(out.shape) == 3:
        out = [out.at[p] for p in range(parts)]
        at = lambda p, f: out[p].at[pl.ds(pl.multiple_of(f * src.shape[1], src.shape[1]), src.shape[1])]
    else:
        at = lambda p, f: out.at[p, f]
    me = pos.y * 2 + pos.c
    other = (1 - pos.y) * 2 + pos.c
    own = []
    for p in range(parts):
        own.append(pltpu.make_async_copy(src.at[p], at(p, me), local.at[p]))
        own[-1].start()
        sends.start(src.at[p], at(p, me), recv.at[p], pos.flip_y())
    for p in range(parts):
        sends.start(src.at[p], at(p, me), recv.at[parts + p], pos.sibling())
    yield
    for p in range(parts):
        arrived(at(p, pos.y * 2 + 1 - pos.c), recv.at[parts + p], pos.sibling())
        own[p].wait()
    yield
    for p in range(parts):
        arrived(at(p, other), recv.at[p], pos.flip_y())
        sends.start(at(p, other), at(p, other), recv.at[2 * parts + p], pos.sibling())
        yield
    for p in range(parts):
        arrived(at(p, (1 - pos.y) * 2 + 1 - pos.c), recv.at[2 * parts + p], pos.sibling())


def gather_fsdp_sems(parts):
    return [DMA((3 * parts,)), DMA((3 * parts,)), DMA((parts,))]


def gather_all(pos, src, out, sends, recv, local, group_of=None):
    n = pos.columns
    me = pos.chunk(0, pos.plane[0], pos.c)
    part = (lambda a: src) if group_of is None else (lambda a: src.at[group_of(a)])
    mine = part(pos.a)
    own = pltpu.make_async_copy(mine, out.at[me], local)
    own.start()
    first, second = pos.device(plane=pos.first), pos.device(plane=pos.second)
    sibling = pos.sibling()
    for k in range(1, n):
        sends.start(part(pos.at(k)), out.at[me], recv.at[k], pos.column(k))
    sends.start(mine, out.at[me], recv.at[n], first)
    sends.start(mine, out.at[me], recv.at[2 * n], second)
    sends.start(mine, out.at[me], recv.at[4 * n], sibling)
    yield
    for k in range(1, n):
        slot = pos.chunk(n - k, pos.plane[0], pos.c)
        arrived(out.at[slot], recv.at[k], first)
        sends.start(out.at[slot], out.at[slot], recv.at[n + k], first)
        sends.start(out.at[slot], out.at[slot], recv.at[2 * n + k], second)
        sends.start(out.at[slot], out.at[slot], recv.at[4 * n + k], sibling)
        yield
    for k in range(n):
        slot = pos.chunk(n - k, pos.first, pos.c)
        arrived(out.at[slot], recv.at[n + k], first)
        sends.start(out.at[slot], out.at[slot], recv.at[3 * n + k], second)
        sends.start(out.at[slot], out.at[slot], recv.at[5 * n + k], sibling)
        yield
    for r in range(2):
        for k in range(n):
            slot = pos.chunk(n - k, pos.plane[2 + r], pos.c)
            arrived(out.at[slot], recv.at[(2 + r) * n + k], second)
            sends.start(out.at[slot], out.at[slot], recv.at[(6 + r) * n + k], sibling)
            yield
    own.wait()
    for r in range(4):
        for k in range(n):
            slot = pos.chunk(n - k, pos.sib_plane[r], 1 - pos.c)
            arrived(out.at[slot], recv.at[(4 + r) * n + k], sibling)


def gather_all_sems(n):
    return [DMA((8 * n,)), DMA((8 * n,)), DMA]


def drive(streams):
    streams = list(streams)
    while streams:
        for stream in list(streams):
            if next(stream, streams) is streams:
                streams.remove(stream)


def all_partners(pos):
    return [pos.column(k) for k in range(1, pos.columns)] + [pos.flip_b(), pos.flip_y(), pos.sibling()]


def shaped(shape, dtype=BF):
    return jax.ShapeDtypeStruct(tuple(shape), dtype)


def dot(a, b, dims):
    return lax.dot_general(a, b, (dims, ((), ())), preferred_element_type=F32)


def add(acc, *others):
    total = acc[...].astype(F32)
    for other in others:
        total = total + other[...].astype(F32)
    acc[...] = total.astype(acc.dtype)


def scatter_ctx(pos, part, out, acc, from_b, from_col, sends, recv, local):
    n = pos.columns
    loads = []
    for k in range(n):
        loads.append(pltpu.make_async_copy(part.at[pos.at(k) * 2 + pos.b], acc.at[k], local.at[k]))
        loads[-1].start()
    for k in [*range(1, n), 0]:
        sends.start(part.at[pos.at(k) * 2 + 1 - pos.b], from_b.at[k], recv.at[k], pos.flip_b())
    yield
    for k in [*range(1, n), 0]:
        loads[k].wait()
        arrived(from_b.at[k], recv.at[k], pos.flip_b())
        if k:
            add(acc.at[k], from_b.at[k])
            sends.start(acc.at[k], from_col.at[k], recv.at[n + k], pos.column(k))
            yield
    total = acc[0].astype(F32) + from_b[0].astype(F32)
    for k in range(1, n):
        arrived(from_col.at[k], recv.at[n + k], pos.column(k))
        total = total + from_col[k].astype(F32)
        yield
    out[...] = total.astype(out.dtype)


def scatter_ctx_scratch(n, shape):
    v = lambda m: pltpu.VMEM((m,) + tuple(shape), BF)
    return [v(n), v(n), v(n), DMA((2 * n,)), DMA((2 * n,)), DMA((n,))]


def scatter_fsdp(pos, part, out, acc, from_sib, from_y, sends, recv, local):
    parts = len(part)
    loads = []
    mine = [(1 - pos.y) * 2 + pos.c, pos.y * 2 + pos.c]
    his = [(1 - pos.y) * 2 + 1 - pos.c, pos.y * 2 + 1 - pos.c]
    for t in range(2):
        for p in range(parts):
            i = t * parts + p
            loads.append(pltpu.make_async_copy(part[p].at[mine[t]], acc.at[i], local.at[i]))
            loads[-1].start()
            sends.start(part[p].at[his[t]], from_sib.at[i], recv.at[i], pos.sibling())
    yield
    for p in range(parts):
        loads[p].wait()
        arrived(from_sib.at[p], recv.at[p], pos.sibling())
        add(acc.at[p], from_sib.at[p])
        sends.start(acc.at[p], from_y.at[p], recv.at[2 * parts + p], pos.flip_y())
        yield
    for p in range(parts):
        loads[parts + p].wait()
        arrived(from_sib.at[parts + p], recv.at[parts + p], pos.sibling())
        add(acc.at[parts + p], from_sib.at[parts + p])
        yield
    for p in range(parts):
        arrived(from_y.at[p], recv.at[2 * parts + p], pos.flip_y())
        out[p] = acc[parts + p].astype(F32) + from_y[p].astype(F32)
        yield


def scatter_fsdp_scratch(parts, shape):
    v = lambda m: pltpu.VMEM((m,) + tuple(shape), BF)
    return [v(2 * parts), v(2 * parts), v(parts), DMA((3 * parts,)), DMA((3 * parts,)), DMA((2 * parts,))]


def scatter_all(pos, part, out, acc, from_sib, from_2, from_1, from_col, sends, recv, local, per_group=False):
    n = pos.columns
    sibling = pos.sibling()
    first, second = pos.device(plane=pos.first), pos.device(plane=pos.second)
    loads = {}
    for r in (3, 2, 1, 0):
        for k in range(n):
            i = r * n + k
            loads[i] = pltpu.make_async_copy(part.at[pos.chunk(k, pos.plane[r], pos.c)], acc.at[i], local.at[i])
            loads[i].start()
            sends.start(part.at[pos.chunk(k, pos.sib_plane[r], 1 - pos.c)], from_sib.at[i], recv.at[i], sibling)
    yield
    for r in (3, 2):
        for k in range(n):
            i = r * n + k
            loads[i].wait()
            arrived(from_sib.at[i], recv.at[i], sibling)
            add(acc.at[i], from_sib.at[i])
            j = (r - 2) * n + k
            sends.start(acc.at[i], from_2.at[j], recv.at[4 * n + j], second)
        yield
    for k in range(n):
        i = n + k
        loads[i].wait()
        arrived(from_sib.at[i], recv.at[i], sibling)
        arrived(from_2.at[i], recv.at[4 * n + i], second)
        add(acc.at[i], from_sib.at[i], from_2.at[i])
        sends.start(acc.at[i], from_1.at[k], recv.at[6 * n + k], first)
    yield
    for k in [*range(1, n), 0]:
        loads[k].wait()
        arrived(from_sib.at[k], recv.at[k], sibling)
        arrived(from_2.at[k], recv.at[4 * n + k], second)
        arrived(from_1.at[k], recv.at[6 * n + k], first)
        if k:
            add(acc.at[k], from_sib.at[k], from_2.at[k], from_1.at[k])
            sends.start(acc.at[k], from_col.at[k], recv.at[7 * n + k], pos.column(k))
    total = acc[0].astype(F32) + from_sib[0].astype(F32) + from_2[0].astype(F32) + from_1[0].astype(F32)
    yield
    if not per_group:
        for k in range(1, n):
            arrived(from_col.at[k], recv.at[7 * n + k], pos.column(k))
            total = total + from_col[k].astype(F32)
        out[...] = total
        return
    each = n // GROUPS
    for k in range(1, n):
        arrived(from_col.at[k], recv.at[7 * n + k], pos.column(k))
    out[...] = jnp.zeros_like(out)
    for k in range(n):
        value = total if k == 0 else from_col[k].astype(F32)
        group = pos.at(n - k) // each
        out[group] = out[group] + value


def scatter_all_scratch(n, shape):
    v = lambda m: pltpu.VMEM((m,) + tuple(shape), BF)
    return [v(4 * n), v(4 * n), v(2 * n), v(n), v(n), DMA((8 * n,)), DMA((8 * n,)), DMA((4 * n,))]


class GatherLine:
    def __init__(self, pos, bufs, send, recv, parts=2):
        self.pos, self.bufs, self.send, self.recv, self.parts = pos, bufs, send, recv, parts
        self.made = []

    def cut(self, ref, p):
        rows = ref.shape[0] // self.parts
        return ref.at[pl.ds(p * rows, rows)]

    def copy(self, i, p, src, a, kind, device):
        out = self.bufs[i][1]
        n = self.pos.columns
        dst = self.cut(out.at[2 * a + self.pos.b], p)
        at = ((i * 2 + kind) * n + a) * self.parts + p
        made = remote(dst if src is None else self.cut(src, p), dst, self.send.at[len(self.made)], self.recv.at[at], device)
        return made

    def go(self, i, p, src, a, kind, device, when=None):
        made = self.copy(i, p, src, a, kind, device)
        self.made.append((made, when))
        if when is None:
            made.start()
        else:
            pl.when(when)(made.start)

    def start(self):
        pos, n = self.pos, self.pos.columns
        up, down = pos.device(a=jnp.minimum(pos.a + 1, n - 1)), pos.device(a=jnp.maximum(pos.a - 1, 0))
        self.up, self.down = up, down
        for p in range(self.parts):
            for i, (src, _) in enumerate(self.bufs):
                self.go(i, p, src, pos.a, 0, up, pos.a < n - 1)
                self.go(i, p, src, pos.a, 0, down, pos.a > 0)
                self.go(i, p, src, pos.a, 1, pos.flip_b())

    def here(self, i, p, a, kind, device):
        b = self.pos.b if kind == 0 else 1 - self.pos.b
        out = self.bufs[i][1]
        at = ((i * 2 + kind) * self.pos.columns + a) * self.parts + p
        arrived(self.cut(out.at[2 * a + b], p), self.recv.at[at], device)

    def relay(self, d):
        pos, n = self.pos, self.pos.columns
        for p in range(self.parts):
            for sign, device, end in ((-1, self.up, pos.a < n - 1), (1, self.down, pos.a > 0)):
                a = pos.a + sign * d
                there = (a >= 0) & (a < n)
                a = jnp.clip(a, 0, n - 1)
                for i in range(len(self.bufs)):
                    pl.when(there)(functools.partial(self.here, i, p, a, 0, device))
                    if d < n - 1:
                        self.go(i, p, None, a, 0, device, there & end)
                    self.go(i, p, None, a, 1, pos.flip_b(), there)

    def across(self, a):
        for p in range(self.parts):
            for i in range(len(self.bufs)):
                self.here(i, p, a, 1, self.pos.flip_b())

    def finish(self):
        for made, when in self.made:
            if when is None:
                made.wait_send()
            else:
                pl.when(when)(made.wait_send)


def gather_line_sems(n, bufs=1, parts=2):
    return [DMA((parts * bufs * (3 + 4 * (n - 1)),)), DMA((2 * bufs * n * parts,))]


def gather_tree(pos, src, out, sends, recv, local, group_of=None):
    n = pos.columns
    b, y = pos.plane[0]
    part = (lambda a: src) if group_of is None else (lambda a: src.at[group_of(a)])
    first, second, sibling = pos.device(plane=pos.first), pos.device(plane=pos.second), pos.sibling()
    mine = out.at[pos.c, b, y, pos.a]
    own = pltpu.make_async_copy(part(pos.a), mine, local)
    own.start()
    for k in range(1, n):
        sends.start(part(pos.at(k)), mine, recv.at[k], pos.column(k))
    yield
    for k in range(1, n):
        arrived(out.at[pos.c, b, y, pos.at(n - k)], recv.at[k], first)
    own.wait()
    column = out.at[pos.c, b, y]
    sends.start(column, column, recv.at[n], first)
    sends.start(column, column, recv.at[n + 1], second)
    yield
    column = out.at[pos.c, pos.first[0], pos.first[1]]
    arrived(column, recv.at[n], first)
    sends.start(column, column, recv.at[n + 2], second)
    yield
    for r in range(2):
        arrived(out.at[pos.c, pos.plane[2 + r][0], pos.plane[2 + r][1]], recv.at[n + 1 + r], second)
    sends.start(out.at[pos.c], out.at[pos.c], recv.at[n + 3], sibling)
    yield
    arrived(out.at[1 - pos.c], recv.at[n + 3], sibling)


def gather_tree_sems(n):
    return [DMA((n + 4,)), DMA((n + 4,)), DMA]


def scatter_tree(pos, part, out, from_sib, from_2, from_1, from_col, sends, recv, per_group=False):
    n = pos.columns
    c = pos.c
    first, second, sibling = pos.device(plane=pos.first), pos.device(plane=pos.second), pos.sibling()
    sends.start(part.at[1 - c], from_sib, recv.at[0], sibling)
    yield
    arrived(from_sib, recv.at[0], sibling)
    at = lambda r: (c, pos.plane[r][0], pos.plane[r][1])
    sib = lambda r: (pos.plane[r][0], pos.plane[r][1])
    for r in (3, 2):
        part[at(r)] = (part[at(r)].astype(F32) + from_sib[sib(r)].astype(F32)).astype(BF)
        sends.start(part.at[at(r)], from_2.at[r - 2], recv.at[1 + r - 2], second)
    yield
    arrived(from_2.at[1], recv.at[2], second)
    part[at(1)] = (part[at(1)].astype(F32) + from_sib[sib(1)].astype(F32) + from_2[1].astype(F32)).astype(BF)
    sends.start(part.at[at(1)], from_1, recv.at[3], first)
    arrived(from_2.at[0], recv.at[1], second)
    yield
    arrived(from_1, recv.at[3], first)
    total = part[at(0)].astype(F32) + from_sib[sib(0)].astype(F32) + from_2[0].astype(F32) + from_1[...].astype(F32)
    part[at(0)] = total.astype(BF)
    mine = part.at[at(0)]
    for k in range(1, n):
        sends.start(mine.at[pos.at(k)], from_col.at[k], recv.at[3 + k], pos.column(k))
    yield
    total = mine[pos.a].astype(F32)
    if per_group:
        out[pos.a // (n // GROUPS)] = total[: out.shape[1]]
    for k in range(1, n):
        arrived(from_col.at[k], recv.at[3 + k], pos.column(k))
        if per_group:
            out[pos.at(n - k) // (n // GROUPS)] = from_col[k].astype(F32)[: out.shape[1]]
        else:
            total = total + from_col[k].astype(F32)
    if not per_group:
        cut = out[0].shape[0]
        out[0][...] = total[:cut]
        out[1][...] = total[cut:]
    sends.finish()


def scatter_tree_scratch(n, shape):
    v = lambda *lead: pltpu.VMEM(lead + tuple(shape), BF)
    return [v(2, 2, n), v(2, n), v(n), v(n), DMA((n + 4,)), DMA((n + 4,))]


class SumCtx:
    def __init__(self, pos, parts, send, recv):
        self.pos, self.parts, self.send, self.recv = pos, parts, send, recv

    def copies(self, a, way):
        pos, n = self.pos, self.pos.columns
        for i, (part, from_b, from_col) in enumerate(self.parts):
            base = 2 * n * i
            if way == "b":
                yield remote(part.at[2 * a + 1 - pos.b], from_b.at[a], self.send.at[base + a], self.recv.at[base + a], pos.flip_b())
            else:
                device = pos.device(a=a)
                yield remote(part.at[2 * a + pos.b], from_col.at[pos.a], self.send.at[base + n + a], self.recv.at[base + n + pos.a], device)

    def push(self, a):
        for copy in self.copies(a, "b"):
            copy.start()

    def pass_on(self, a, other=None):
        pos = self.pos
        for copy, (part, from_b, _) in zip(self.copies(a, "b"), self.parts):
            copy.wait_recv()

        def send():
            for copy, (part, from_b, _) in zip(self.copies(a, "column"), self.parts):
                at = 2 * a + pos.b
                part[at] = (part[at].astype(F32) + from_b[a].astype(F32)).astype(BF)
                copy.start()

        if other is None:
            pl.when(a != pos.a)(send)
        elif other:
            send()

    def total(self):
        pos, n = self.pos, self.pos.columns
        sums = []
        for i, (part, from_b, from_col) in enumerate(self.parts):
            total = part[2 * pos.a + pos.b].astype(F32) + from_b[pos.a].astype(F32)
            for k in range(1, n):
                a = pos.at(k)
                sem = self.recv.at[2 * n * i + n + a]
                arrived(from_col.at[a], sem, pos.column(k))
                total = total + from_col[a].astype(F32)
            sums.append(total)
        return sums

    def finish(self):
        pos, n = self.pos, self.pos.columns
        for a in range(n):
            for copy in self.copies(a, "b"):
                copy.wait_send()
        for k in range(1, n):
            for copy in self.copies(pos.at(k), "column"):
                copy.wait_send()


def sum_ctx_scratch(n, *shapes):
    v = lambda shape: pltpu.VMEM((n,) + tuple(shape), BF)
    out = []
    for shape in shapes:
        out += [v(shape), v(shape)]
    return out + [DMA((2 * n * len(shapes),)), DMA((2 * n * len(shapes),))]


class Sizes:
    def __init__(self, nc, nf, rows, width, experts, hidden, owned, padded, capacity, top, docs):
        self.nc, self.nf, self.rows, self.width = nc, nf, rows, width
        self.experts, self.hidden, self.owned, self.padded = experts, hidden, owned, padded
        self.capacity, self.top, self.docs = capacity, top, docs
        self.columns, self.per = nc // 2, nc // GROUPS
        self.heads = width // HEAD_DIM // GROUPS
        self.share = self.heads * HEAD_DIM
        self.slot = nc * rows
        self.all = nc * nf


def scalars(sz, lengths):
    sizes = [lengths[0, d] for d in range(sz.docs)]
    ends, total = [], 0
    for size in sizes:
        total = total + size
        ends.append(total)
    return sizes, ends


def starts(index, sizes, ends):
    low = jnp.zeros_like(index)
    for size, end in zip(sizes, ends):
        low = low + jnp.where(index >= end, size, 0)
    return low


def iota(shape, dim):
    return lax.broadcasted_iota(jnp.int32, shape, dim)


def mean_square(x, width):
    return jnp.sum(x * x, axis=-1, keepdims=True) * (1.0 / width)


def turn(value, cosine, sine):
    half = HEAD_DIM // 2
    lower, upper = value[:half], value[half:]
    return jnp.concatenate([lower * cosine - upper * sine, upper * cosine + lower * sine], axis=0)


def head(h):
    return slice(h * HEAD_DIM, (h + 1) * HEAD_DIM)


def blk(index, rows):
    return pl.ds(pl.multiple_of(index * rows, rows), rows)


class Copies:
    def __init__(self, sems):
        self.sems, self.made = sems, []

    def start(self, src, dst):
        self.made.append(pltpu.make_async_copy(src, dst, self.sems.at[len(self.made)]))
        self.made[-1].start()

    def finish(self):
        for copy in self.made:
            copy.wait()


def swap_send(sz, group, place, src, out, sends, recv, local, h):
    @pl.when(h == group)
    def _():
        pltpu.make_async_copy(src.at[h], out.at[h], local).start()

    copy = remote(src.at[h], out.at[group], sends.at[h], recv.at[group], {"ctx": h * sz.per + place})

    @pl.when(h != group)
    def _():
        copy.start()


def swap_wait(sz, group, place, src, out, sends, recv, local):
    for h in range(GROUPS):
        copy = remote(src.at[h], out.at[h], sends.at[h], recv.at[h], {"ctx": h * sz.per + place})

        @pl.when(h == group)
        def _():
            pltpu.make_async_copy(src.at[h], out.at[h], local).wait()

        @pl.when(h != group)
        def _():
            copy.wait_send()
            copy.wait_recv()


def scatter_owner(pos, part, outs, stage, from_sib, from_y, sends, recv, local):
    parts = len(outs)
    rows = outs[0][0].shape[0] + outs[0][1].shape[0]
    of = lambda p, y, c: part.at[p, blk(y * 2 + c, rows)]
    for t, y in enumerate((1 - pos.y, pos.y)):
        for p in range(parts):
            sends.start(of(p, y, 1 - pos.c), from_sib.at[t, p], recv.at[t * parts + p], pos.sibling())
        yield
    for t, y in enumerate((1 - pos.y, pos.y)):
        for p in range(parts):
            arrived(from_sib.at[t, p], recv.at[t * parts + p], pos.sibling())
            mine = of(p, y, pos.c)
            mine[...] = (mine[...].astype(F32) + from_sib[t, p].astype(F32)).astype(BF)
            if t == 0:
                sends.start(mine, from_y.at[p], recv.at[2 * parts + p], pos.flip_y())
        yield
    copies = []
    for p in range(parts):
        arrived(from_y.at[p], recv.at[2 * parts + p], pos.flip_y())
        if p > 1:
            for copy in copies[p - 2]:
                copy.wait()
        held = stage.at[pl.ds(p % 2 * rows, rows)]
        held[...] = of(p, pos.y, pos.c)[...].astype(F32) + from_y[p].astype(F32)
        cut = outs[p][0].shape[0]
        parts_of = (held.at[pl.ds(0, cut)], held.at[pl.ds(cut, rows - cut)])
        copies.append([pltpu.make_async_copy(src, dst, local.at[p, t]) for t, (src, dst) in enumerate(zip(parts_of, outs[p]))])
        for copy in copies[p]:
            copy.start()
        yield
    for pair in copies[-2:]:
        for copy in pair:
            copy.wait()
    sends.finish()


def scatter_owner_scratch(parts, shape):
    v = lambda *lead: pltpu.VMEM(lead + tuple(shape), BF)
    return [v(2, parts), v(parts), DMA((3 * parts,)), DMA((3 * parts,)), DMA((parts, 2))]


def step(*streams):
    for stream in streams:
        next(stream, None)


def layer_kernel(
    sz, lengths, tokens, cot, routes, gain_own, router_own, spread, wq_send, wo_own, ffn_send,
    o_out, o_tokens, o_wq, o_wo, o_small, o_in, o_down, o_shared_in, o_shared_down,
    x_all, wq_all, wo_all, wo_send, stage, wt, wo, small, normed, qt, kt, vt, prob, o_send, attn, resid, table,
    g_all, mix_all, cw_all, ffn_w, hw, dg, du, gm_part, gp_part, y_hold, dw,
    do_send, do, dkt, dvt, dqt_b, dkvt_b,
    *sems,
):
    pos, pos_b = Place(sz.columns), Place(sz.columns, balanced=False)
    ctx = lax.axis_index("ctx")
    group, place = ctx // sz.per, ctx % sz.per
    rows, width, share, n = sz.rows, sz.width, sz.share, sz.columns
    sizes, ends = scalars(sz, lengths)
    group_of = lambda a: a // (n // GROUPS)

    owned = sz.owned
    me = ctx * sz.nf + lax.axis_index("fsdp")
    place_of = (iota((owned, width), 1) == me * owned + iota((owned, width), 0)).astype(BF)
    wo_send[:owned, :] = wo_own[...]
    rest = jnp.zeros((sz.padded - owned - 2 - sz.experts, width), F32)
    first = jnp.zeros((1, width), F32)
    wo_send[owned:, :] = jnp.concatenate([first, dot(gain_own[...], place_of, NN), dot(router_own[...], place_of, NN), rest], axis=0).astype(BF)

    greet(all_partners(pos))
    s = [Sends(sems[3 * i]) for i in range(3)]
    r = lambda i: (sems[3 * i + 1], sems[3 * i + 2])
    swap_sems, swap_back = sems[9:12], sems[12:15]
    gm_sum = SumCtx(pos, [(gm_part, sems[27], sems[28]), (gp_part, sems[29], sems[30])], sems[31], sems[32])
    gn_part, wq_part, wo_part, y_part = x_all, wq_all, wo_all, y_hold
    y_sum = SumCtx(pos, [(y_part, sems[33], sems[34])], sems[35], sems[36])
    gn_sum = SumCtx(pos, [(gn_part, sems[37], sems[38])], sems[39], sems[40])
    t_wq, t_wo, t_ffn = sems[41:47], sems[47:53], sems[53:58]
    toks = GatherLine(pos, [(tokens, x_all)], sems[15], sems[16])
    cots = GatherLine(pos, [(None, g_all)], sems[17], sems[18])
    mixes = GatherLine(pos, [(None, mix_all)], sems[19], sems[20])
    weights = GatherLine(pos, [(None, cw_all)], sems[21], sems[22], parts=1)

    wqs = gather_tree(pos_b, wq_send, wq_all, s[0], *r(0), group_of=group_of)
    wos = gather_tree(pos_b, wo_send, wo_all, s[1], *r(1))
    ffn = gather_fsdp(pos, ffn_send, ffn_w, s[2], *r(2))
    next(wqs)
    toks.start()
    next(wos)
    x_all[ctx] = tokens[...]

    own_rows = ctx * rows + iota((rows, 1), 0)
    live = own_rows < ends[-1]
    g_all[ctx] = jnp.where(live, cot[...].astype(F32), 0.0).astype(BF)
    index = iota((1, sz.slot), 1)
    position = index - jnp.where(index < ends[-1], starts(index, sizes, ends), 0)
    half = HEAD_DIM // 2
    inverse = jnp.exp(iota((half, 1), 0).astype(F32) * (-2.0 * math.log(ROPE_BASE) / HEAD_DIM))
    angles = position.astype(F32) * inverse
    table[0] = jnp.cos(angles)
    table[1] = jnp.sin(angles)
    before = (iota((rows, rows), 0) < iota((rows, rows), 1)).astype(BF)
    live_t = (ctx * rows + iota((1, rows), 1)) < ends[-1]
    base = jnp.zeros((8, 1), F32)
    kept = jnp.zeros((8, rows), F32)
    for k in range(sz.top):
        hot = ((iota((8, rows), 0) == routes[k : k + 1, :]) & live_t).astype(F32)
        earlier = base + dot(hot.astype(BF), before, NN)
        kept = kept + jnp.where(earlier < sz.capacity, hot, 0.0)
        base = base + jnp.sum(hot, axis=1, keepdims=True)
    step(wqs, wos)
    toks.relay(1)
    step(wqs, wos)
    toks.relay(2)
    step(wqs, wos)
    next(ffn)
    toks.relay(3)
    cots.start()
    for k in range(n):
        toks.across(k)
    drive([wqs])

    def packed(h_):
        each = sz.per * rows
        return slice(each * h_ * (h_ + 1) // 2, each * (h_ + 1) * (h_ + 2) // 2)

    def spot(i):
        a_b, y_c = divmod(i, sz.nf)
        return y_c % 2, a_b % 2, y_c // 2, a_b // 2

    for i in range(sz.all):
        stage[i * owned : (i + 1) * owned, : 3 * share] = wq_all[spot(i)][:owned, :].astype(F32)
    wt[...] = stage[:, : 3 * share].T.astype(BF)
    for d in range(sz.nc):
        x = x_all[d].astype(F32)
        inv = lax.rsqrt(mean_square(x, width) + EPSILON)
        normed[d] = (x * inv).astype(BF)
        part = slice(d * rows, (d + 1) * rows)
        kv = dot(wt[share:, :], normed[d], NT)
        for h in range(sz.heads):
            kt[head(h), part] = turn(kv[head(h)], table[0, :, part], table[1, :, part]).astype(BF)
        vt[:, part] = kv[share:].astype(BF)

    for h_ in reversed(range(GROUPS)):
        d = h_ * sz.per + place
        part = blk(d, rows)
        qq = dot(wt[:share, :], normed[d], NT)
        keys = (h_ + 1) * sz.per * rows
        index = d * rows + iota((rows, 1), 0)
        low = starts(index, sizes, ends)
        key = iota((rows, keys), 1)
        allowed = (key >= low) & (key <= index)
        for h in range(sz.heads):
            q = turn(qq[head(h)], table[0, :, part], table[1, :, part]).astype(BF) * BF(1.0 / math.sqrt(HEAD_DIM))
            qt[h_, head(h), :] = q
            score = jnp.where(allowed, dot(q, kt[head(h), :keys], TN), MASKED)
            expo = jnp.exp(score - jnp.max(score, axis=1, keepdims=True))
            p = (expo * (1.0 / jnp.sum(expo, axis=1, keepdims=True))).astype(BF)
            prob[h, :, packed(h_)] = p
            o_send[h_, head(h), :] = dot(vt[head(h), :keys], p, NT).astype(BF)
        swap_send(sz, group, place, o_send, attn, *swap_sems, h_)
        if h_ == 3:
            cots.relay(1)
        if h_ == 1:
            cots.relay(2)
    swap_wait(sz, group, place, o_send, attn, *swap_sems)
    cots.relay(3)
    drive([wos])
    for i in range(sz.all):
        stage[i * owned : (i + 1) * owned, :] = wo_all[spot(i)][:owned, :].astype(F32)
    extra = wo_all[spot(0)][owned:, :].astype(F32)
    for i in range(1, sz.all):
        extra = extra + wo_all[spot(i)][owned:, :].astype(F32)
    small[...] = extra[:8]
    gain_m = small[1:2, :]
    wo[...] = stage[...].astype(BF)

    attn_t = attn[...].reshape(width, rows)
    res = tokens[...].astype(F32) + dot(attn_t, wo[...], TN)
    resid[...] = res
    inv = lax.rsqrt(mean_square(res, width) + EPSILON)
    mixed = (res * inv * gain_m).astype(BF)
    mix_all[ctx] = mixed
    row = iota((8, rows), 0)
    logits = dot(small[...].astype(BF), mixed, NT)
    logits = jnp.concatenate([logits[2:], logits[:2]], axis=0)
    logits = jnp.where(row < sz.experts, logits, MASKED)
    expo = jnp.exp(logits - jnp.max(logits, axis=0, keepdims=True))
    router_prob = expo * (1.0 / jnp.sum(expo, axis=0, keepdims=True))
    weight = router_prob * kept
    high = weight.astype(BF).astype(F32)
    high_row = jnp.where(row == sz.experts, 1.0, high)
    cw_all[ctx] = jnp.concatenate([high_row, weight - high], axis=0).astype(BF)

    weights.start()
    mixes.start()
    step(ffn)

    chunk = 2 * rows

    half_units = sz.nf // 2 * ffn_send.shape[1]
    cuts = ((0, 384), (384, half_units - 384))

    def units_at(y, cut):
        return pl.ds(pl.multiple_of(y * half_units + cut[0], 128), cut[1])

    def hidden_units(a, y):
        at_rows = blk(a, chunk)
        x = mix_all[pl.ds(2 * a, 2)].reshape(chunk, width)
        g = g_all[pl.ds(2 * a, 2)].reshape(chunk, width)
        pair = jnp.zeros((16, chunk), F32)
        for cut in cuts:
            at = units_at(y, cut)
            gate = dot(x, ffn_w[0, at, :], NT)
            up = dot(x, ffn_w[1, at, :], NT)
            back = dot(g, ffn_w[2, at, :], NT)
            weight = jnp.concatenate([dot(cw_all[2 * a + i], spread[:16, at], TN) for i in range(2)], axis=0)
            sig = 1.0 / (1.0 + jnp.exp(-gate))
            act = gate * sig
            hid = act * up
            pair = pair + dot(spread[16:, at], (hid * back).astype(BF), NT)
            hw[at_rows, at] = (hid * weight).astype(BF)
            back = back * weight
            dg[at_rows, at] = (back * up * sig * (1.0 + gate * (1.0 - sig))).astype(BF)
            du[at_rows, at] = (back * act).astype(BF)
        return pair

    def input_grad(a):
        at_rows = blk(a, chunk)
        total = dot(dg[at_rows, :], ffn_w[0], NN) + dot(du[at_rows, :], ffn_w[1], NN)
        gm_part[pl.ds(2 * a, 2)] = total.astype(BF).reshape(2, rows, width)
        gm_sum.push(a)

    near = [pos.a, jnp.where(pos.a == 0, 1, jnp.where(pos.a == 1, 0, jnp.where(pos.a == 2, 3, 2)))]
    near += [jnp.where(pos.a < 2, 2, 1), jnp.where(pos.a < 2, 3, 0)]
    for i in range(n):
        if i + 1 < n:
            weights.relay(i + 1)
            mixes.relay(i + 1)
        for stream in (cots, weights, mixes):
            stream.across(near[i])
        pair = hidden_units(near[i], pos.y)
        if i == 0:
            drive([ffn])
        pair = (pair + hidden_units(near[i], 1 - pos.y)).astype(BF)
        for t in range(2):
            gp_part[2 * near[i] + t] = pair[:, t * rows : (t + 1) * rows]
        input_grad(near[i])
        if i > 1:
            gm_sum.pass_on(near[i - 1], other=True)
    xs = mix_all[...].reshape(sz.slot, width)
    gs = g_all[...].reshape(sz.slot, width)

    ffn_back = scatter_owner(pos, dw, ((o_in.at[0], o_shared_in.at[0]), (o_in.at[1], o_shared_in.at[1]), (o_down, o_shared_down)), stage, *t_ffn[:2], Sends(t_ffn[2]), *t_ffn[3:])
    for y in (1 - pos.y, pos.y):
        for cut in cuts:
            at = units_at(y, cut)
            for p, (units, rows_of) in enumerate(((dg, xs), (du, xs), (hw, gs))):
                dw[p, at, :] = dot(units[:, at], rows_of, TN).astype(BF)
        step(ffn_back)
        if y is not pos.y:
            gm_sum.pass_on(near[-1], other=True)
            gm_sum.pass_on(pos.a, other=False)
            for a in (*near[1:], pos.a):
                y_part[pl.ds(2 * a, 2)] = dot(hw[blk(a, chunk), :], ffn_w[2], NN).astype(BF).reshape(2, rows, width)
                y_sum.push(a)
    step(ffn_back)

    gm_own, gp_own = gm_sum.total()
    grad_prob = gp_own[:8, :] * kept
    grad_logits = router_prob * (grad_prob - jnp.sum(router_prob * grad_prob, axis=0, keepdims=True))
    shifted = jnp.concatenate([jnp.zeros((2, rows), F32), grad_logits[:6]], axis=0).astype(BF)
    grad_small = dot(shifted, mix_all[ctx], NN)
    grad_mixed = gm_own + dot(shifted, small[...].astype(BF), TN)
    res = resid[...]
    inv = lax.rsqrt(mean_square(res, width) + EPSILON)
    w = grad_mixed * gain_m
    inner = jnp.sum(w * res, axis=-1, keepdims=True) * (1.0 / width)
    grad_resid = jnp.where(live, cot[...].astype(F32), 0.0) + inv * w - res * inner * inv * inv * inv
    grad_gain_m = jnp.sum(grad_mixed * res * inv, axis=0, keepdims=True)
    grad_resid_b = grad_resid.astype(BF)
    grad_attn_t = dot(wo[...], grad_resid_b, NT).astype(BF)
    for h_ in range(GROUPS):
        do_send[h_] = grad_attn_t[h_ * share : (h_ + 1) * share]
    for h_ in range(GROUPS):
        swap_send(sz, group, place, do_send, do, *swap_back, h_)
    gm_sum.finish()
    for x in (*s, toks):
        x.finish()
    wos = scatter_tree(pos, wo_part, (o_wo, o_small), *t_wo[:4], Sends(t_wo[4]), t_wo[5])
    wqs = scatter_tree(pos, wq_part, o_wq, *t_wq[:4], Sends(t_wq[4]), t_wq[5], per_group=True)
    grad_wo = dot(attn[...].reshape(width, rows), grad_resid_b, NN)
    row = iota((sz.padded - owned, width), 0)
    grad_small = jnp.where(row == 1, grad_gain_m, jnp.concatenate([grad_small] * ((sz.padded - owned) // 8), axis=0)).astype(BF)

    for i in range(sz.all):
        wo_part[spot(i) + (slice(0, owned),)] = grad_wo[i * owned : (i + 1) * owned].astype(BF)
        wo_part[spot(i) + (slice(owned, None),)] = grad_small
    step(wos)
    swap_wait(sz, group, place, do_send, do, *swap_back)
    y_sum.pass_on(near[1], other=True)

    dkt[...] = jnp.zeros_like(dkt)
    dvt[...] = jnp.zeros_like(dvt)
    for h_ in reversed(range(GROUPS)):
        keys = (h_ + 1) * sz.per * rows
        done = slice(h_ * sz.per * rows, keys)
        part = blk(h_ * sz.per + place, rows)
        for h in range(sz.heads):
            d_o = do[h_, head(h), :]
            p = prob[h, :, packed(h_)]
            pf = p.astype(F32)
            grad_p = dot(d_o, vt[head(h), :keys], TN)
            delta = jnp.sum(pf * grad_p, axis=1, keepdims=True)
            grad_s = (pf * (grad_p - delta)).astype(BF)
            dq = dot(kt[head(h), :keys], grad_s, NT) * (1.0 / math.sqrt(HEAD_DIM))
            dqt_b[h_, head(h), :] = turn(dq, table[0, :, part], -table[1, :, part]).astype(BF)
            dkt[head(h), :keys] = dkt[head(h), :keys] + dot(qt[h_, head(h), :], grad_s, NN)
            dvt[head(h), :keys] = dvt[head(h), :keys] + dot(d_o, p, NN)
        for h in range(sz.heads):
            dkvt_b[head(h), done] = turn(dkt[head(h), done], table[0, :, done], -table[1, :, done]).astype(BF)
        dkvt_b[share:, done] = dvt[:, done].astype(BF)
        for t in range(2):
            d = h_ * sz.per + lax.rem(place + 1 + t, 2)
            gn = dot(dkvt_b[:, blk(d, rows)], wt[share:, :], TN)
            if t == 1:
                gn = gn + dot(dqt_b[h_], wt[:share, :], TN)
            gn_part[d] = gn.astype(BF)
        gn_sum.push(h_)
        if h_ < GROUPS - 2:
            gn_sum.pass_on(h_ + 2)
        if 1 < h_:
            y_sum.pass_on(near[GROUPS + 1 - h_], other=True)
        if h_ % 2:
            step(wos)
        if h_ == GROUPS - 1:
            step(ffn_back)
    grad_q = dot(dqt_b[0], normed[place], NN)
    for h_ in range(1, GROUPS):
        grad_q = grad_q + dot(dqt_b[h_], normed[h_ * sz.per + place], NN)
    grad_kv = dot(dkvt_b[...], normed[...].reshape(sz.slot, width), NN)
    grad_w = jnp.concatenate([grad_q, grad_kv], axis=0).T
    wq_part[...] = jnp.zeros_like(wq_part)
    for i in range(sz.all):
        wq_part[spot(i) + (slice(0, owned),)] = grad_w[i * owned : (i + 1) * owned].astype(BF)
    step(wqs)
    gn_sum.pass_on(1)
    gn_sum.pass_on(0)
    step(wqs, wqs)
    drive([wos])
    step(wqs)
    drive([ffn_back])
    drive([wqs])
    y_sum.pass_on(pos.a, other=False)
    (y_own,) = y_sum.total()
    o_out[...] = jnp.where(live, res + y_own, 0.0).astype(BF)
    x = tokens[...].astype(F32)
    inv = lax.rsqrt(mean_square(x, width) + EPSILON)
    (gn_own,) = gn_sum.total()
    w = gn_own
    inner = jnp.sum(w * x, axis=-1, keepdims=True) * (1.0 / width)
    o_tokens[...] = grad_resid + inv * w - x * inner * inv * inv * inv
    for x in (y_sum, gn_sum, cots, mixes, weights):
        x.finish()


def layer(sz, collective_id, lengths, tokens, cot, routes, gain_own, router_own, spread, wq_send, wo_own, ffn_send):
    n, nc, rows, width, share, slot = sz.columns, sz.nc, sz.rows, sz.width, sz.share, sz.slot
    own_units = ffn_send.shape[1]
    units = sz.nf * own_units
    outs = [
        shaped((rows, width)),
        shaped((rows, width), F32),
        shaped((GROUPS, sz.owned, 3 * share), F32),
        shaped((sz.owned, width), F32),
        shaped((sz.padded - sz.owned, width), F32),
        shaped((2, own_units - sz.hidden, width), F32),
        shaped((own_units - sz.hidden, width), F32),
        shaped((2, sz.hidden, width), F32),
        shaped((sz.hidden, width), F32),
    ]
    v = lambda *shape, dtype=BF: pltpu.VMEM(shape, dtype)
    tree = (2, 2, 2, n, sz.padded)
    blocks = v(nc, rows, width)
    scratch = [
        blocks, v(*tree, 3 * share), v(*tree, width), v(sz.padded, width), v(width, width, dtype=F32),
        v(3 * share, width), v(width, width), v(8, width, dtype=F32), blocks,
        v(GROUPS, share, rows), v(share, slot), v(share, slot), v(sz.heads, rows, slot * (GROUPS + 1) // 2), v(GROUPS, share, rows),
        v(GROUPS, share, rows), v(rows, width, dtype=F32), v(2, HEAD_DIM // 2, slot, dtype=F32),
        blocks, blocks, v(nc, 16, rows), v(3, units, width), v(slot, units), v(slot, units), v(slot, units),
        blocks, v(nc, 16, rows), blocks, v(3, units, width),
        v(GROUPS, share, rows), v(GROUPS, share, rows), v(share, slot, dtype=F32), v(share, slot, dtype=F32),
        v(GROUPS, share, rows), v(2 * share, slot),
    ]
    sems = gather_tree_sems(n) * 2 + gather_fsdp_sems(3)
    sems += [DMA((GROUPS,)), DMA((GROUPS,)), DMA] * 2
    sems += gather_line_sems(n) * 3 + gather_line_sems(n, parts=1) + [DMA] * 4
    sems += sum_ctx_scratch(n, (rows, width), (16, rows)) + sum_ctx_scratch(n, (rows, width)) * 2
    sems += scatter_tree_scratch(n, (sz.padded, 3 * share)) + scatter_tree_scratch(n, (sz.padded, width))
    sems += scatter_owner_scratch(3, (own_units, width))
    hbm, vmem = pl.BlockSpec(memory_space=pl.ANY), pl.BlockSpec(memory_space=pltpu.VMEM)
    return pl.pallas_call(
        functools.partial(layer_kernel, sz),
        out_shape=outs,
        in_specs=[pl.BlockSpec(memory_space=pltpu.SMEM)] + [vmem] * 6 + [hbm, vmem, hbm],
        out_specs=[vmem] * 5 + [hbm] * 4,
        scratch_shapes=scratch + sems,
        compiler_params=pltpu.CompilerParams(collective_id=collective_id, has_side_effects=True, vmem_limit_bytes=63 << 20),
        name="layer",
    )(lengths, tokens, cot, routes, gain_own, router_own, spread, wq_send, wo_own, ffn_send)


def gather_start_kernel(columns, group_of, tokens, wq, wo, ffn, cot, o_tokens, o_wq, o_wo, o_ffn, o_cot, *sems):
    pos = Place(columns)
    greet(all_partners(pos))
    s = [Sends(sems[3 * i]) for i in range(5)]
    r = lambda i: (sems[3 * i + 1], sems[3 * i + 2])
    streams = [
        gather_ctx(pos, tokens, o_tokens, s[0], *r(0)),
        gather_all(pos, wq, o_wq, s[1], *r(1), group_of=group_of),
        gather_all(pos, wo, o_wo, s[2], *r(2)),
        gather_fsdp(pos, ffn, o_ffn, s[3], *r(3)),
    ]
    drive(streams)
    drive([gather_ctx(pos, cot, o_cot, s[4], *r(4))])
    for x in s:
        x.finish()


def call(kernel, collective_id, ins, outs, scratch, name, space=pl.ANY, in_space=None):
    return pl.pallas_call(
        kernel,
        out_shape=outs,
        in_specs=[pl.BlockSpec(memory_space=in_space or space)] * len(ins),
        out_specs=jax.tree.map(lambda _: pl.BlockSpec(memory_space=space), outs),
        scratch_shapes=scratch,
        compiler_params=pltpu.CompilerParams(
            collective_id=collective_id, has_side_effects=True, vmem_limit_bytes=60 << 20
        ),
        name=name,
    )(*ins)


def gather_start(nc, tokens, wq, wo, ffn, cot):
    n = nc // 2
    group_of = lambda a: a // (n // GROUPS)
    sems = gather_ctx_sems(n) + gather_all_sems(n) * 2 + gather_fsdp_sems(ffn.shape[0]) + gather_ctx_sems(n)
    outs = (
        shaped((nc,) + tokens.shape),
        shaped((nc * 4,) + wq.shape[1:]),
        shaped((nc * 4,) + wo.shape),
        shaped((ffn.shape[0], 4) + ffn.shape[1:]),
        shaped((nc,) + cot.shape),
    )
    return call(functools.partial(gather_start_kernel, n, group_of), 1, (tokens, wq, wo, ffn, cot), outs, sems, "gather_start")


def gather_ctx_kernel(columns, src, out, send, recv, local):
    pos = Place(columns)
    greet([pos.column(k) for k in range(1, columns)] + [pos.flip_b()])
    s = Sends(send)
    drive([gather_ctx(pos, src, out, s, recv, local)])
    s.finish()


def gather_rows(nc, src, collective_id):
    n = nc // 2
    return call(functools.partial(gather_ctx_kernel, n), collective_id, (src,), shaped((nc,) + src.shape), gather_ctx_sems(n), "gather_rows")


def swap_kernel(nc, src, out, send, recv, local):
    per = nc // GROUPS
    ctx = lax.axis_index("ctx")
    group, place = ctx // per, ctx % per
    peer = lambda k: lax.rem(group + k, GROUPS)
    device = lambda k: {"ctx": peer(k) * per + place}
    greet([device(k) for k in range(1, GROUPS)])
    own = pltpu.make_async_copy(src.at[group], out.at[group], local)
    own.start()
    copies = []
    for k in range(1, GROUPS):
        copies.append(remote(src.at[peer(k)], out.at[group], send.at[k], recv.at[k], device(k)))
        copies[-1].start()
    for k in range(1, GROUPS):
        arrived(out.at[peer(GROUPS - k)], recv.at[k], device(k))
    own.wait()
    for copy in copies:
        copy.wait_send()


def swap(nc, src, collective_id):
    return call(functools.partial(swap_kernel, nc), collective_id, (src,), shaped(src.shape), [DMA((GROUPS,)), DMA((GROUPS,)), DMA], "swap")


def scatter_ctx_kernel(columns, part, out, acc, from_b, from_col, send, recv, local):
    pos = Place(columns)
    greet([pos.column(k) for k in range(1, columns)] + [pos.flip_b()])
    s = Sends(send)
    drive([scatter_ctx(pos, part, out, acc, from_b, from_col, s, recv, local)])
    s.finish()


def scatter_rows(nc, part, collective_id):
    n = nc // 2
    return pl.pallas_call(
        functools.partial(scatter_ctx_kernel, n),
        out_shape=shaped(part.shape[1:], F32),
        in_specs=[pl.BlockSpec(memory_space=pl.ANY)],
        out_specs=pl.BlockSpec(memory_space=pltpu.VMEM),
        scratch_shapes=scatter_ctx_scratch(n, part.shape[1:]),
        compiler_params=pltpu.CompilerParams(collective_id=collective_id, has_side_effects=True, vmem_limit_bytes=60 << 20),
        name="scatter_rows",
    )(part)


def scatter_end_kernel(columns, gn, wq, wo, ffn, yy, o_gn, o_wq, o_wo, o_ffn, o_yy, *scratch):
    pos = Place(columns)
    greet(all_partners(pos))
    c1, a1, a2, f1, c2 = scratch[0:6], scratch[6:14], scratch[14:22], scratch[22:28], scratch[28:34]
    s = [Sends(x[-3]) for x in (c1, a1, a2, f1, c2)]
    drive(
        [
            scatter_ctx(pos, gn, o_gn, *c1[:-3], s[0], *c1[-2:]),
            scatter_fsdp(pos, [ffn.at[p] for p in range(ffn.shape[0])], o_ffn, *f1[:-3], s[3], *f1[-2:]),
            scatter_all(pos, wq, o_wq, *a1[:-3], s[1], *a1[-2:], per_group=True),
            scatter_all(pos, wo, o_wo, *a2[:-3], s[2], *a2[-2:]),
            scatter_ctx(pos, yy, o_yy, *c2[:-3], s[4], *c2[-2:]),
        ]
    )
    for x in s:
        x.finish()


def scatter_end(nc, gn, wq, wo, ffn, yy):
    n = nc // 2
    scratch = (
        scatter_ctx_scratch(n, gn.shape[1:])
        + scatter_all_scratch(n, wq.shape[1:])
        + scatter_all_scratch(n, wo.shape[1:])
        + scatter_fsdp_scratch(ffn.shape[0], ffn.shape[2:])
        + scatter_ctx_scratch(n, yy.shape[1:])
    )
    outs = (
        shaped(gn.shape[1:], F32),
        shaped((GROUPS,) + wq.shape[1:], F32),
        shaped(wo.shape[1:], F32),
        shaped((ffn.shape[0],) + ffn.shape[2:], F32),
        shaped(yy.shape[1:], F32),
    )
    return call(
        functools.partial(scatter_end_kernel, n), 6, (gn, wq, wo, ffn, yy), outs, scratch, "scatter_end",
        space=pltpu.VMEM, in_space=pl.ANY,
    )


def doc_ids(row_index, doc_ends):
    return jnp.sum((row_index[:, None] >= doc_ends[None, :]).astype(jnp.int32), axis=1)


def positions(row_index, lengths):
    doc_ends = jnp.cumsum(lengths)
    doc_starts = doc_ends - lengths
    doc_num = doc_ids(row_index, doc_ends)
    column = jnp.arange(lengths.shape[0], dtype=jnp.int32)
    begins = jnp.sum(jnp.where(doc_num[:, None] == column[None, :], doc_starts[None, :], 0), axis=1)
    return doc_num, row_index - begins


def rope_tables(position):
    half_dim = HEAD_DIM // 2
    inverse = ROPE_BASE ** (-2.0 * jnp.arange(half_dim, dtype=F32) / HEAD_DIM)
    angles = position.astype(F32)[:, None] * inverse[None, :]
    return jnp.cos(angles), jnp.sin(angles)


def rotate(values, cosine, sine):
    half_dim = values.shape[-1] // 2
    lower, upper = values[..., :half_dim], values[..., half_dim:]
    cosine, sine = cosine[:, None, :], sine[:, None, :]
    return jnp.concatenate([lower * cosine - upper * sine, upper * cosine + lower * sine], axis=-1)


def kept_rows(route_rows, live_rows, experts, capacity):
    count, top = route_rows.shape
    hot = (route_rows[:, :, None] == jnp.arange(experts, dtype=jnp.int32)) & live_rows[:, None, None]
    hot = hot.astype(F32)
    before = jnp.tril(jnp.ones((count, count), F32), -1)
    kept = jnp.zeros((count, experts), F32)
    base = jnp.zeros((1, experts), F32)
    for k in range(top):
        earlier = base + jnp.dot(before, hot[:, k])
        kept = kept + hot[:, k] * (earlier < capacity)
        base = base + jnp.sum(hot[:, k], axis=0, keepdims=True)
    return kept


def pad_rows(x, rows):
    return jnp.pad(x, [(0, rows - x.shape[0])] + [(0, 0)] * (x.ndim - 1))


def body_wide(tokens, doc_lengths, routes, cotangent, attn_gain, w_qkv, w_out, mlp_gain, router, expert_in, expert_out, shared_in, shared_out):
    nc = lax.axis_size("ctx")
    nf = lax.axis_size("fsdp")
    rows, width = tokens.shape[1:]
    heads = width // HEAD_DIM
    experts = expert_in.shape[1]
    hidden = expert_in.shape[0]
    top = routes.shape[2]
    capacity = 5 * top * rows // (4 * experts)
    per = nc // GROUPS
    ctx = lax.axis_index("ctx")
    group, place = ctx // per, ctx % per
    slot = nc * rows
    mine = heads // GROUPS
    share = mine * HEAD_DIM
    scale = 1.0 / math.sqrt(HEAD_DIM)
    owned = w_out.shape[0]
    padded = -(-(owned + 2 + experts) // 16) * 16

    wq_send = w_qkv.reshape(owned, 3, GROUPS, share).transpose(2, 0, 1, 3).reshape(GROUPS, owned, 3 * share)
    wq_send = jnp.pad(wq_send, ((0, 0), (0, padded - owned), (0, 0)))
    small = jnp.concatenate([attn_gain[None], mlp_gain[None], router.T], axis=0)
    wo_send = pad_rows(jnp.concatenate([w_out, jnp.pad(small, ((0, 0), (0, width - owned)))], axis=0), padded)
    gate_up = jnp.concatenate([expert_in.transpose(2, 1, 0, 3), shared_in.transpose(1, 0, 2)[:, None]], axis=1)
    down = jnp.concatenate([expert_out.transpose(1, 0, 2), shared_out[None]], axis=0)
    ffn_send = jnp.concatenate([gate_up, down[None]], axis=0).reshape(3, (experts + 1) * hidden, width)

    x_all, wq_all, wo_all, ffn_all, cot_all = gather_start(nc, tokens[0], wq_send, wo_send, ffn_send, cotangent[0])
    units = nf * (experts + 1) * hidden
    w_gate, w_up, w_down = (ffn_all[p].reshape(units, width) for p in range(3))
    wq = wq_all[:, :owned].reshape(width, 3 * share)
    wo = wo_all[:, :owned].reshape(width, width)
    small = wo_all[:, owned : owned + 2 + experts, :owned].transpose(1, 0, 2).reshape(2 + experts, width)
    gain_a, gain_m = small[0].astype(F32), small[1].astype(F32)
    router_t = small[2:]

    all_rows = jnp.arange(slot, dtype=jnp.int32)
    doc_num, position = positions(all_rows, doc_lengths[0])
    cosine, sine = rope_tables(position)
    live_all = (doc_num < doc_lengths.shape[1]).astype(F32)[:, None]
    x_slot = x_all.reshape(slot, width).astype(F32)
    inv_attn = lax.rsqrt(jnp.mean(x_slot * x_slot, axis=-1, keepdims=True) + EPSILON)
    normed = (x_slot * inv_attn * gain_a).astype(BF)

    def queries(v):
        return lax.dynamic_index_in_dim(v.reshape((GROUPS, per, rows) + v.shape[1:]), place, 1, False).reshape((GROUPS * rows,) + v.shape[1:])

    normed_q = queries(normed)
    cos_q, sin_q = queries(cosine), queries(sine)
    q = rotate(dot(normed_q, wq[:, :share], ((1,), (0,))).reshape(-1, mine, HEAD_DIM), cos_q, sin_q).astype(BF)
    k = rotate(dot(normed, wq[:, share : 2 * share], ((1,), (0,))).reshape(slot, mine, HEAD_DIM), cosine, sine).astype(BF)
    v = dot(normed, wq[:, 2 * share :], ((1,), (0,))).reshape(slot, mine, HEAD_DIM).astype(BF)
    rows_q, doc_q = queries(all_rows), queries(doc_num)
    allowed = (doc_q[:, None] == doc_num[None, :]) & (all_rows[None, :] <= rows_q[:, None])
    scores = jnp.einsum("qhd,khd->hqk", q, k, preferred_element_type=F32) * scale
    scores = jnp.where(allowed[None], scores, MASKED)
    expo = jnp.exp(scores - jnp.max(scores, axis=-1, keepdims=True))
    prob = expo / jnp.sum(expo, axis=-1, keepdims=True)
    prob_b = prob.astype(BF)
    o = jnp.einsum("hqk,khd->qhd", prob_b, v, preferred_element_type=F32).astype(BF)

    o_own = swap(nc, o.reshape(GROUPS, rows, share), 2)
    attn = o_own.transpose(1, 0, 2).reshape(rows, width)

    row_index = ctx * rows + jnp.arange(rows, dtype=jnp.int32)
    doc_own, _ = positions(row_index, doc_lengths[0])
    live_rows = doc_own < doc_lengths.shape[1]
    live = live_rows.astype(F32)[:, None]
    x = tokens[0].astype(F32)
    resid = x + dot(attn, wo, ((1,), (0,)))
    inv_mlp = lax.rsqrt(jnp.mean(resid * resid, axis=-1, keepdims=True) + EPSILON)
    mixed = (resid * inv_mlp * gain_m).astype(BF)
    logits = dot(mixed, router_t, ((1,), (1,)))
    router_prob = jax.nn.softmax(logits, axis=-1)
    kept = kept_rows(routes[0], live_rows, experts, capacity)
    weight = router_prob * kept
    high = weight.astype(BF)
    low = (weight - high.astype(F32)).astype(BF)
    extra = pad_rows(jnp.pad(jnp.concatenate([high, low], axis=1).T, ((0, 0), (0, width - rows))), 16)
    mixed_all = gather_rows(nc, jnp.concatenate([mixed, extra], axis=0), 3)

    weights = mixed_all[:, rows : rows + 2 * experts, :rows].astype(F32)
    weights = (weights[:, :experts] + weights[:, experts:]).transpose(0, 2, 1).reshape(slot, experts)
    mix = mixed_all[:, :rows].reshape(slot, width)
    g = (cot_all.reshape(slot, width) * live_all.astype(BF)).astype(BF)
    unit_weight = jnp.concatenate([weights, jnp.ones((slot, 1), F32)], axis=1)
    unit_weight = jnp.tile(jnp.repeat(unit_weight, hidden, axis=1), (1, nf))
    gate = dot(mix, w_gate, ((1,), (1,)))
    up = dot(mix, w_up, ((1,), (1,)))
    sig = jax.nn.sigmoid(gate)
    hid = gate * sig * up
    hid_w = (hid * unit_weight).astype(BF)
    y_part = dot(hid_w, w_down, ((1,), (0,))).astype(BF)
    back = dot(g, w_down, ((1,), (1,)))
    pair = (hid * back).reshape(slot, nf, experts + 1, hidden).sum(axis=(1, 3))[:, :experts]
    back_w = back * unit_weight
    d_gate = (back_w * up * sig * (1.0 + gate * (1.0 - sig))).astype(BF)
    d_up = (back_w * gate * sig).astype(BF)
    gm_part = (dot(d_gate, w_gate, ((1,), (0,))) + dot(d_up, w_up, ((1,), (0,)))).astype(BF)
    d_w = jnp.stack([dot(d_gate, mix, ((0,), (0,))), dot(d_up, mix, ((0,), (0,))), dot(hid_w, g, ((0,), (0,)))]).astype(BF)
    pair_t = pair.reshape(nc, rows, experts).transpose(0, 2, 1)
    pair_t = jnp.pad(pair_t, ((0, 0), (0, 16 - experts), (0, width - rows))).astype(BF)
    gm_all = scatter_rows(nc, jnp.concatenate([gm_part.reshape(nc, rows, width), pair_t], axis=1), 4)

    grad_prob = gm_all[rows : rows + experts, :rows].T * kept
    grad_logits = (router_prob * (grad_prob - jnp.sum(router_prob * grad_prob, axis=-1, keepdims=True))).astype(BF)
    grad_router_t = dot(grad_logits, mixed, ((0,), (0,)))
    grad_mixed = gm_all[:rows] + dot(grad_logits, router_t, ((1,), (0,)))
    grad_top = cotangent[0].astype(F32) * live
    w = grad_mixed * gain_m
    grad_resid = grad_top + inv_mlp * w - resid * jnp.mean(w * resid, axis=-1, keepdims=True) * inv_mlp**3
    grad_gain_m = jnp.sum(grad_mixed * resid * inv_mlp, axis=0)
    grad_resid_b = grad_resid.astype(BF)
    grad_wo = dot(attn, grad_resid_b, ((0,), (0,)))
    grad_attn = dot(grad_resid_b, wo, ((1,), (1,))).astype(BF)
    do = swap(nc, grad_attn.reshape(rows, GROUPS, share).transpose(1, 0, 2), 5).reshape(GROUPS * rows, mine, HEAD_DIM)

    grad_p = jnp.einsum("qhd,khd->hqk", do, v, preferred_element_type=F32)
    delta = jnp.sum(prob * grad_p, axis=-1, keepdims=True)
    grad_s = (prob * (grad_p - delta)).astype(BF)
    dq = jnp.einsum("hqk,khd->qhd", grad_s, k, preferred_element_type=F32) * scale
    dk = jnp.einsum("hqk,qhd->khd", grad_s, q, preferred_element_type=F32) * scale
    dv = jnp.einsum("hqk,qhd->khd", prob_b, do, preferred_element_type=F32)
    dq = rotate(dq, cos_q, -sin_q).reshape(GROUPS * rows, share).astype(BF)
    dk = rotate(dk, cosine, -sine).reshape(slot, share)
    dkv = jnp.concatenate([dk, dv.reshape(slot, share)], axis=1).astype(BF)
    grad_wq = jnp.concatenate([dot(normed_q, dq, ((0,), (0,))), dot(normed, dkv, ((0,), (0,)))], axis=1)
    gn_q = dot(dq, wq[:, :share], ((1,), (1,))).reshape(GROUPS, 1, rows, width)
    here = (jnp.arange(per) == place).astype(F32)[None, :, None, None]
    gn = dot(dkv, wq[:, share:], ((1,), (1,))).reshape(GROUPS, per, rows, width) + gn_q * here
    gn_part = gn.reshape(nc, rows, width).astype(BF)

    gn_full = gn.reshape(slot, width)
    grad_gain_a = jnp.sum(gn_full * x_slot * inv_attn, axis=0)
    small = jnp.concatenate([grad_gain_a[None], grad_gain_m[None], grad_router_t], axis=0)
    small = small.reshape(2 + experts, nc * nf, owned).transpose(1, 0, 2)
    wo_part = jnp.concatenate([grad_wo.reshape(nc * nf, owned, width), jnp.pad(small, ((0, 0), (0, 0), (0, width - owned)))], axis=1)
    wo_part = jnp.pad(wo_part, ((0, 0), (0, padded - wo_part.shape[1]), (0, 0))).astype(BF)
    wq_part = jnp.pad(grad_wq.reshape(nc * nf, owned, 3 * share), ((0, 0), (0, padded - owned), (0, 0))).astype(BF)
    ffn_part = d_w.reshape(3, nf, (experts + 1) * hidden, width)
    gn_own, wq_own, wo_own, ffn_own, y_own = scatter_end(nc, gn_part, wq_part, wo_part, ffn_part, y_part.reshape(nc, rows, width))

    layer_out = (live * (resid + y_own)).astype(BF)[None]
    inv = lax.rsqrt(jnp.mean(x * x, axis=-1, keepdims=True) + EPSILON)
    w = gn_own * gain_a
    grad_tokens = (grad_resid + inv * w - x * jnp.mean(w * x, axis=-1, keepdims=True) * inv**3)[None]
    grad_w_qkv = wq_own[:, :owned].reshape(GROUPS, owned, 3, share).transpose(1, 2, 0, 3).reshape(owned, 3 * width)
    small = wo_own[owned : owned + 2 + experts, :owned]
    out = ffn_own.reshape(3, experts + 1, hidden, width)
    return (
        layer_out,
        grad_tokens,
        small[0],
        grad_w_qkv,
        wo_own[:owned],
        small[1],
        small[2:].T,
        out[:2, :experts].transpose(2, 1, 0, 3),
        out[2, :experts].transpose(1, 0, 2),
        out[:2, experts].transpose(1, 0, 2),
        out[2, experts],
    )


def body(tokens, doc_lengths, routes, cotangent, attn_gain, w_qkv, w_out, mlp_gain, router, expert_in, expert_out, shared_in, shared_out):
    nc, nf = lax.axis_size("ctx"), lax.axis_size("fsdp")
    rows, width = tokens.shape[1:]
    experts, hidden, top = expert_in.shape[1], expert_in.shape[0], routes.shape[2]
    owned = w_out.shape[0]
    if nc != 2 * GROUPS or 2 * nc * rows * width > FUSED_BYTES:
        return body_wide(
            tokens, doc_lengths, routes, cotangent, attn_gain, w_qkv, w_out, mlp_gain, router, expert_in, expert_out, shared_in, shared_out
        )
    padded = -(-(owned + 8) // 16) * 16
    sz = Sizes(nc, nf, rows, width, experts, hidden, owned, padded, 5 * top * rows // (4 * experts), top, doc_lengths.shape[1])
    share = sz.share
    device = lax.axis_index("ctx") * nf + lax.axis_index("fsdp")

    gain = attn_gain.astype(F32)[:, None]
    wq_send = (w_qkv.astype(F32) * gain).astype(BF).reshape(owned, 3, GROUPS, share).transpose(2, 0, 1, 3).reshape(GROUPS, owned, 3 * share)
    wq_send = jnp.pad(wq_send, ((0, 0), (0, padded - owned), (0, 0)))
    gate_up = jnp.concatenate([expert_in.transpose(2, 1, 0, 3), shared_in.transpose(1, 0, 2)[:, None]], axis=1)
    down = jnp.concatenate([expert_out.transpose(1, 0, 2), shared_out[None]], axis=0)
    ffn_send = jnp.concatenate([gate_up, down[None]], axis=0).reshape(3, (experts + 1) * hidden, width)

    units = nf * (experts + 1) * hidden
    of = np.arange(units) // hidden % (experts + 1)
    spread = np.zeros((32, units), np.float32)
    for e in range(experts + 1):
        spread[e] = of == e
    for e in range(experts):
        spread[8 + e] = of == e
        spread[16 + e] = of == e

    layer_out, grad_tokens, wq_own, grad_w_out, small, grad_in, grad_down, shared_in_own, shared_out_own = layer(
        sz, 1, doc_lengths, tokens[0], cotangent[0], routes[0].T, mlp_gain[None], router.T, jnp.asarray(spread, BF), wq_send, w_out, ffn_send
    )

    grad_w = wq_own.reshape(GROUPS, owned, 3, share).transpose(1, 2, 0, 3).reshape(owned, 3 * width)
    gain_a = jnp.sum(grad_w * w_qkv.astype(F32), axis=1)
    grad_w_qkv = grad_w * gain
    small = lax.dynamic_slice(small, (0, device * owned), (2 + experts, owned))
    grad_in = grad_in.reshape(2, experts, hidden, width)
    grad_down = grad_down.reshape(experts, hidden, width)
    return (
        layer_out[None],
        grad_tokens[None],
        gain_a,
        grad_w_qkv,
        grad_w_out,
        small[1],
        small[2:].T,
        grad_in.transpose(2, 1, 0, 3),
        grad_down.transpose(1, 0, 2),
        shared_in_own.transpose(1, 0, 2),
        shared_out_own,
    )


def solution(mesh):
    rows = P("fsdp", "ctx", None)
    flat = ("ctx", "fsdp")
    weights = (P(flat), P(flat, None), P(flat, None), P(flat), P(flat, None))
    ffn = (P(flat, None, None, None), P(flat, None, None), P(flat, None, None), P(flat, None))
    return jax.shard_map(
        body,
        mesh=mesh,
        in_specs=(rows, P("fsdp", None), rows, rows) + weights + ffn,
        out_specs=(rows, rows) + weights + ffn,
        check_vma=False,
    )
```

```python
import functools
import math

import jax
import jax.numpy as jnp
import numpy as np
from jax import lax
from jax.experimental import pallas as pl
from jax.experimental.pallas import tpu as pltpu
from jax.sharding import PartitionSpec as P

HEAD_DIM = 64
EPSILON = 1e-05
ROPE_BASE = 10000.0
MASKED = -1e30
NN, NT, TN = ((1,), (0,)), ((1,), (1,)), ((0,), (0,))
FUSED_BYTES = 2 << 20
GROUPS = 4
MESH = pl.DeviceIdType.MESH
DMA = pltpu.SemaphoreType.DMA
BF = jnp.bfloat16
F32 = jnp.float32


class Place:
    def __init__(self, columns, balanced=True):
        ctx, fsdp = lax.axis_index("ctx"), lax.axis_index("fsdp")
        self.columns = columns
        self.a, self.b = ctx // 2, ctx % 2
        self.y, self.c = fsdp // 2, fsdp % 2
        flip_b = (1 - self.b, self.y)
        flip_y = (self.b, 1 - self.y)
        core = (self.c == 0) if balanced else (self.c >= 0)
        self.first = tuple(jnp.where(core, p, q) for p, q in zip(flip_b, flip_y))
        self.second = tuple(jnp.where(core, q, p) for p, q in zip(flip_b, flip_y))
        self.plane = [(self.b, self.y), self.first, self.second, (1 - self.b, 1 - self.y)]
        self.sib_plane = [(self.b, self.y), self.second, self.first, (1 - self.b, 1 - self.y)]

    def at(self, step):
        return lax.rem(self.a + step, self.columns)

    def device(self, a=None, plane=None, c=None):
        b, y = plane if plane is not None else (self.b, self.y)
        a = self.a if a is None else a
        c = self.c if c is None else c
        return {"ctx": a * 2 + b, "fsdp": y * 2 + c}

    def column(self, step):
        return self.device(a=self.at(step))

    def flip_b(self):
        return self.device(plane=(1 - self.b, self.y))

    def flip_y(self):
        return self.device(plane=(self.b, 1 - self.y))

    def sibling(self):
        return self.device(c=1 - self.c)

    def chunk(self, step, plane, c):
        return (self.at(step) * 2 + plane[0]) * 4 + plane[1] * 2 + c


def greet(devices):
    barrier = pltpu.get_barrier_semaphore()
    for device in devices:
        pl.semaphore_signal(barrier, inc=1, device_id=device, device_id_type=MESH)
    pl.semaphore_wait(barrier, len(devices))


def remote(src, dst, send, recv, device):
    return pltpu.make_async_remote_copy(
        src_ref=src, dst_ref=dst, send_sem=send, recv_sem=recv, device_id=device, device_id_type=MESH
    )


class Sends:
    def __init__(self, sems):
        self.sems, self.made = sems, []

    def start(self, src, dst, recv, device):
        copy = remote(src, dst, self.sems.at[len(self.made)], recv, device)
        copy.start()
        self.made.append(copy)

    def finish(self):
        for copy in self.made:
            copy.wait_send()


def arrived(dst, recv, device):
    remote(dst, dst, recv, recv, device).wait_recv()


def gather_ctx(pos, src, out, sends, recv, local, there=lambda slot: None):
    n = pos.columns
    me = pos.a * 2 + pos.b
    own = pltpu.make_async_copy(src, out.at[me], local)
    own.start()
    for k in range(1, n):
        sends.start(src, out.at[me], recv.at[k], pos.column(k))
    sends.start(src, out.at[me], recv.at[n], pos.flip_b())
    yield
    own.wait()
    there(me)
    for k in range(1, n):
        slot = pos.at(n - k) * 2 + pos.b
        arrived(out.at[slot], recv.at[k], pos.column(k))
        sends.start(out.at[slot], out.at[slot], recv.at[n + k], pos.flip_b())
        there(slot)
        yield
    for k in range(n):
        slot = pos.at(n - k) * 2 + 1 - pos.b
        arrived(out.at[slot], recv.at[n + k], pos.flip_b())
        there(slot)
        yield


def gather_ctx_sems(n):
    return [DMA((2 * n,)), DMA((2 * n,)), DMA]


def gather_fsdp(pos, src, out, sends, recv, local):
    parts = src.shape[0]
    if len(out.shape) == 3:
        out = [out.at[p] for p in range(parts)]
        at = lambda p, f: out[p].at[pl.ds(pl.multiple_of(f * src.shape[1], src.shape[1]), src.shape[1])]
    else:
        at = lambda p, f: out.at[p, f]
    me = pos.y * 2 + pos.c
    other = (1 - pos.y) * 2 + pos.c
    own = []
    for p in range(parts):
        own.append(pltpu.make_async_copy(src.at[p], at(p, me), local.at[p]))
        own[-1].start()
        sends.start(src.at[p], at(p, me), recv.at[p], pos.flip_y())
    for p in range(parts):
        sends.start(src.at[p], at(p, me), recv.at[parts + p], pos.sibling())
    yield
    for p in range(parts):
        arrived(at(p, pos.y * 2 + 1 - pos.c), recv.at[parts + p], pos.sibling())
        own[p].wait()
    yield
    for p in range(parts):
        arrived(at(p, other), recv.at[p], pos.flip_y())
        sends.start(at(p, other), at(p, other), recv.at[2 * parts + p], pos.sibling())
        yield
    for p in range(parts):
        arrived(at(p, (1 - pos.y) * 2 + 1 - pos.c), recv.at[2 * parts + p], pos.sibling())


def gather_fsdp_sems(parts):
    return [DMA((3 * parts,)), DMA((3 * parts,)), DMA((parts,))]


def gather_all(pos, src, out, sends, recv, local, group_of=None):
    n = pos.columns
    me = pos.chunk(0, pos.plane[0], pos.c)
    part = (lambda a: src) if group_of is None else (lambda a: src.at[group_of(a)])
    mine = part(pos.a)
    own = pltpu.make_async_copy(mine, out.at[me], local)
    own.start()
    first, second = pos.device(plane=pos.first), pos.device(plane=pos.second)
    sibling = pos.sibling()
    for k in range(1, n):
        sends.start(part(pos.at(k)), out.at[me], recv.at[k], pos.column(k))
    sends.start(mine, out.at[me], recv.at[n], first)
    sends.start(mine, out.at[me], recv.at[2 * n], second)
    sends.start(mine, out.at[me], recv.at[4 * n], sibling)
    yield
    for k in range(1, n):
        slot = pos.chunk(n - k, pos.plane[0], pos.c)
        arrived(out.at[slot], recv.at[k], first)
        sends.start(out.at[slot], out.at[slot], recv.at[n + k], first)
        sends.start(out.at[slot], out.at[slot], recv.at[2 * n + k], second)
        sends.start(out.at[slot], out.at[slot], recv.at[4 * n + k], sibling)
        yield
    for k in range(n):
        slot = pos.chunk(n - k, pos.first, pos.c)
        arrived(out.at[slot], recv.at[n + k], first)
        sends.start(out.at[slot], out.at[slot], recv.at[3 * n + k], second)
        sends.start(out.at[slot], out.at[slot], recv.at[5 * n + k], sibling)
        yield
    for r in range(2):
        for k in range(n):
            slot = pos.chunk(n - k, pos.plane[2 + r], pos.c)
            arrived(out.at[slot], recv.at[(2 + r) * n + k], second)
            sends.start(out.at[slot], out.at[slot], recv.at[(6 + r) * n + k], sibling)
            yield
    own.wait()
    for r in range(4):
        for k in range(n):
            slot = pos.chunk(n - k, pos.sib_plane[r], 1 - pos.c)
            arrived(out.at[slot], recv.at[(4 + r) * n + k], sibling)


def gather_all_sems(n):
    return [DMA((8 * n,)), DMA((8 * n,)), DMA]


def drive(streams):
    streams = list(streams)
    while streams:
        for stream in list(streams):
            if next(stream, streams) is streams:
                streams.remove(stream)


def all_partners(pos):
    return [pos.column(k) for k in range(1, pos.columns)] + [pos.flip_b(), pos.flip_y(), pos.sibling()]


def shaped(shape, dtype=BF):
    return jax.ShapeDtypeStruct(tuple(shape), dtype)


def dot(a, b, dims):
    return lax.dot_general(a, b, (dims, ((), ())), preferred_element_type=F32)


def add(acc, *others):
    total = acc[...].astype(F32)
    for other in others:
        total = total + other[...].astype(F32)
    acc[...] = total.astype(acc.dtype)


def scatter_ctx(pos, part, out, acc, from_b, from_col, sends, recv, local):
    n = pos.columns
    loads = []
    for k in range(n):
        loads.append(pltpu.make_async_copy(part.at[pos.at(k) * 2 + pos.b], acc.at[k], local.at[k]))
        loads[-1].start()
    for k in [*range(1, n), 0]:
        sends.start(part.at[pos.at(k) * 2 + 1 - pos.b], from_b.at[k], recv.at[k], pos.flip_b())
    yield
    for k in [*range(1, n), 0]:
        loads[k].wait()
        arrived(from_b.at[k], recv.at[k], pos.flip_b())
        if k:
            add(acc.at[k], from_b.at[k])
            sends.start(acc.at[k], from_col.at[k], recv.at[n + k], pos.column(k))
            yield
    total = acc[0].astype(F32) + from_b[0].astype(F32)
    for k in range(1, n):
        arrived(from_col.at[k], recv.at[n + k], pos.column(k))
        total = total + from_col[k].astype(F32)
        yield
    out[...] = total.astype(out.dtype)


def scatter_ctx_scratch(n, shape):
    v = lambda m: pltpu.VMEM((m,) + tuple(shape), BF)
    return [v(n), v(n), v(n), DMA((2 * n,)), DMA((2 * n,)), DMA((n,))]


def scatter_fsdp(pos, part, out, acc, from_sib, from_y, sends, recv, local):
    parts = len(part)
    loads = []
    mine = [(1 - pos.y) * 2 + pos.c, pos.y * 2 + pos.c]
    his = [(1 - pos.y) * 2 + 1 - pos.c, pos.y * 2 + 1 - pos.c]
    for t in range(2):
        for p in range(parts):
            i = t * parts + p
            loads.append(pltpu.make_async_copy(part[p].at[mine[t]], acc.at[i], local.at[i]))
            loads[-1].start()
            sends.start(part[p].at[his[t]], from_sib.at[i], recv.at[i], pos.sibling())
    yield
    for p in range(parts):
        loads[p].wait()
        arrived(from_sib.at[p], recv.at[p], pos.sibling())
        add(acc.at[p], from_sib.at[p])
        sends.start(acc.at[p], from_y.at[p], recv.at[2 * parts + p], pos.flip_y())
        yield
    for p in range(parts):
        loads[parts + p].wait()
        arrived(from_sib.at[parts + p], recv.at[parts + p], pos.sibling())
        add(acc.at[parts + p], from_sib.at[parts + p])
        yield
    for p in range(parts):
        arrived(from_y.at[p], recv.at[2 * parts + p], pos.flip_y())
        out[p] = acc[parts + p].astype(F32) + from_y[p].astype(F32)
        yield


def scatter_fsdp_scratch(parts, shape):
    v = lambda m: pltpu.VMEM((m,) + tuple(shape), BF)
    return [v(2 * parts), v(2 * parts), v(parts), DMA((3 * parts,)), DMA((3 * parts,)), DMA((2 * parts,))]


def scatter_all(pos, part, out, acc, from_sib, from_2, from_1, from_col, sends, recv, local, per_group=False):
    n = pos.columns
    sibling = pos.sibling()
    first, second = pos.device(plane=pos.first), pos.device(plane=pos.second)
    loads = {}
    for r in (3, 2, 1, 0):
        for k in range(n):
            i = r * n + k
            loads[i] = pltpu.make_async_copy(part.at[pos.chunk(k, pos.plane[r], pos.c)], acc.at[i], local.at[i])
            loads[i].start()
            sends.start(part.at[pos.chunk(k, pos.sib_plane[r], 1 - pos.c)], from_sib.at[i], recv.at[i], sibling)
    yield
    for r in (3, 2):
        for k in range(n):
            i = r * n + k
            loads[i].wait()
            arrived(from_sib.at[i], recv.at[i], sibling)
            add(acc.at[i], from_sib.at[i])
            j = (r - 2) * n + k
            sends.start(acc.at[i], from_2.at[j], recv.at[4 * n + j], second)
        yield
    for k in range(n):
        i = n + k
        loads[i].wait()
        arrived(from_sib.at[i], recv.at[i], sibling)
        arrived(from_2.at[i], recv.at[4 * n + i], second)
        add(acc.at[i], from_sib.at[i], from_2.at[i])
        sends.start(acc.at[i], from_1.at[k], recv.at[6 * n + k], first)
    yield
    for k in [*range(1, n), 0]:
        loads[k].wait()
        arrived(from_sib.at[k], recv.at[k], sibling)
        arrived(from_2.at[k], recv.at[4 * n + k], second)
        arrived(from_1.at[k], recv.at[6 * n + k], first)
        if k:
            add(acc.at[k], from_sib.at[k], from_2.at[k], from_1.at[k])
            sends.start(acc.at[k], from_col.at[k], recv.at[7 * n + k], pos.column(k))
    total = acc[0].astype(F32) + from_sib[0].astype(F32) + from_2[0].astype(F32) + from_1[0].astype(F32)
    yield
    if not per_group:
        for k in range(1, n):
            arrived(from_col.at[k], recv.at[7 * n + k], pos.column(k))
            total = total + from_col[k].astype(F32)
        out[...] = total
        return
    each = n // GROUPS
    for k in range(1, n):
        arrived(from_col.at[k], recv.at[7 * n + k], pos.column(k))
    out[...] = jnp.zeros_like(out)
    for k in range(n):
        value = total if k == 0 else from_col[k].astype(F32)
        group = pos.at(n - k) // each
        out[group] = out[group] + value


def scatter_all_scratch(n, shape):
    v = lambda m: pltpu.VMEM((m,) + tuple(shape), BF)
    return [v(4 * n), v(4 * n), v(2 * n), v(n), v(n), DMA((8 * n,)), DMA((8 * n,)), DMA((4 * n,))]


class GatherLine:
    def __init__(self, pos, bufs, send, recv, parts=2):
        self.pos, self.bufs, self.send, self.recv, self.parts = pos, bufs, send, recv, parts
        self.made = []

    def cut(self, ref, p):
        rows = ref.shape[0] // self.parts
        return ref.at[pl.ds(p * rows, rows)]

    def copy(self, i, p, src, a, kind, device):
        out = self.bufs[i][1]
        n = self.pos.columns
        dst = self.cut(out.at[2 * a + self.pos.b], p)
        at = ((i * 2 + kind) * n + a) * self.parts + p
        made = remote(dst if src is None else self.cut(src, p), dst, self.send.at[len(self.made)], self.recv.at[at], device)
        return made

    def go(self, i, p, src, a, kind, device, when=None):
        made = self.copy(i, p, src, a, kind, device)
        self.made.append((made, when))
        if when is None:
            made.start()
        else:
            pl.when(when)(made.start)

    def start(self):
        pos, n = self.pos, self.pos.columns
        up, down = pos.device(a=jnp.minimum(pos.a + 1, n - 1)), pos.device(a=jnp.maximum(pos.a - 1, 0))
        self.up, self.down = up, down
        for p in range(self.parts):
            for i, (src, _) in enumerate(self.bufs):
                self.go(i, p, src, pos.a, 0, up, pos.a < n - 1)
                self.go(i, p, src, pos.a, 0, down, pos.a > 0)
                self.go(i, p, src, pos.a, 1, pos.flip_b())

    def here(self, i, p, a, kind, device):
        b = self.pos.b if kind == 0 else 1 - self.pos.b
        out = self.bufs[i][1]
        at = ((i * 2 + kind) * self.pos.columns + a) * self.parts + p
        arrived(self.cut(out.at[2 * a + b], p), self.recv.at[at], device)

    def relay(self, d):
        pos, n = self.pos, self.pos.columns
        for p in range(self.parts):
            for sign, device, end in ((-1, self.up, pos.a < n - 1), (1, self.down, pos.a > 0)):
                a = pos.a + sign * d
                there = (a >= 0) & (a < n)
                a = jnp.clip(a, 0, n - 1)
                for i in range(len(self.bufs)):
                    pl.when(there)(functools.partial(self.here, i, p, a, 0, device))
                    if d < n - 1:
                        self.go(i, p, None, a, 0, device, there & end)
                    self.go(i, p, None, a, 1, pos.flip_b(), there)

    def across(self, a):
        for p in range(self.parts):
            for i in range(len(self.bufs)):
                self.here(i, p, a, 1, self.pos.flip_b())

    def finish(self):
        for made, when in self.made:
            if when is None:
                made.wait_send()
            else:
                pl.when(when)(made.wait_send)


def gather_line_sems(n, bufs=1, parts=2):
    return [DMA((parts * bufs * (3 + 4 * (n - 1)),)), DMA((2 * bufs * n * parts,))]


def gather_tree(pos, src, out, sends, recv, local, group_of=None):
    n = pos.columns
    b, y = pos.plane[0]
    part = (lambda a: src) if group_of is None else (lambda a: src.at[group_of(a)])
    first, second, sibling = pos.device(plane=pos.first), pos.device(plane=pos.second), pos.sibling()
    mine = out.at[pos.c, b, y, pos.a]
    own = pltpu.make_async_copy(part(pos.a), mine, local)
    own.start()
    for k in range(1, n):
        sends.start(part(pos.at(k)), mine, recv.at[k], pos.column(k))
    yield
    for k in range(1, n):
        arrived(out.at[pos.c, b, y, pos.at(n - k)], recv.at[k], first)
    own.wait()
    column = out.at[pos.c, b, y]
    sends.start(column, column, recv.at[n], first)
    sends.start(column, column, recv.at[n + 1], second)
    yield
    column = out.at[pos.c, pos.first[0], pos.first[1]]
    arrived(column, recv.at[n], first)
    sends.start(column, column, recv.at[n + 2], second)
    yield
    for r in range(2):
        arrived(out.at[pos.c, pos.plane[2 + r][0], pos.plane[2 + r][1]], recv.at[n + 1 + r], second)
    sends.start(out.at[pos.c], out.at[pos.c], recv.at[n + 3], sibling)
    yield
    arrived(out.at[1 - pos.c], recv.at[n + 3], sibling)


def gather_tree_sems(n):
    return [DMA((n + 4,)), DMA((n + 4,)), DMA]


def scatter_tree(pos, part, out, from_sib, from_2, from_1, from_col, sends, recv, per_group=False):
    n = pos.columns
    c = pos.c
    first, second, sibling = pos.device(plane=pos.first), pos.device(plane=pos.second), pos.sibling()
    sends.start(part.at[1 - c], from_sib, recv.at[0], sibling)
    yield
    arrived(from_sib, recv.at[0], sibling)
    at = lambda r: (c, pos.plane[r][0], pos.plane[r][1])
    sib = lambda r: (pos.plane[r][0], pos.plane[r][1])
    for r in (3, 2):
        part[at(r)] = (part[at(r)].astype(F32) + from_sib[sib(r)].astype(F32)).astype(BF)
        sends.start(part.at[at(r)], from_2.at[r - 2], recv.at[1 + r - 2], second)
    yield
    arrived(from_2.at[1], recv.at[2], second)
    part[at(1)] = (part[at(1)].astype(F32) + from_sib[sib(1)].astype(F32) + from_2[1].astype(F32)).astype(BF)
    sends.start(part.at[at(1)], from_1, recv.at[3], first)
    arrived(from_2.at[0], recv.at[1], second)
    yield
    arrived(from_1, recv.at[3], first)
    total = part[at(0)].astype(F32) + from_sib[sib(0)].astype(F32) + from_2[0].astype(F32) + from_1[...].astype(F32)
    part[at(0)] = total.astype(BF)
    mine = part.at[at(0)]
    for k in range(1, n):
        sends.start(mine.at[pos.at(k)], from_col.at[k], recv.at[3 + k], pos.column(k))
    yield
    total = mine[pos.a].astype(F32)
    if per_group:
        out[pos.a // (n // GROUPS)] = total[: out.shape[1]]
    for k in range(1, n):
        arrived(from_col.at[k], recv.at[3 + k], pos.column(k))
        if per_group:
            out[pos.at(n - k) // (n // GROUPS)] = from_col[k].astype(F32)[: out.shape[1]]
        else:
            total = total + from_col[k].astype(F32)
    if not per_group:
        cut = out[0].shape[0]
        out[0][...] = total[:cut]
        out[1][...] = total[cut:]
    sends.finish()


def scatter_tree_scratch(n, shape):
    v = lambda *lead: pltpu.VMEM(lead + tuple(shape), BF)
    return [v(2, 2, n), v(2, n), v(n), v(n), DMA((n + 4,)), DMA((n + 4,))]


class SumCtx:
    def __init__(self, pos, parts, send, recv):
        self.pos, self.parts, self.send, self.recv = pos, parts, send, recv

    def copies(self, a, way):
        pos, n = self.pos, self.pos.columns
        for i, (part, from_b, from_col) in enumerate(self.parts):
            base = 2 * n * i
            if way == "b":
                yield remote(part.at[2 * a + 1 - pos.b], from_b.at[a], self.send.at[base + a], self.recv.at[base + a], pos.flip_b())
            else:
                device = pos.device(a=a)
                yield remote(part.at[2 * a + pos.b], from_col.at[pos.a], self.send.at[base + n + a], self.recv.at[base + n + pos.a], device)

    def push(self, a):
        for copy in self.copies(a, "b"):
            copy.start()

    def pass_on(self, a, other=None):
        pos = self.pos
        for copy, (part, from_b, _) in zip(self.copies(a, "b"), self.parts):
            copy.wait_recv()

        def send():
            for copy, (part, from_b, _) in zip(self.copies(a, "column"), self.parts):
                at = 2 * a + pos.b
                part[at] = (part[at].astype(F32) + from_b[a].astype(F32)).astype(BF)
                copy.start()

        if other is None:
            pl.when(a != pos.a)(send)
        elif other:
            send()

    def total(self):
        pos, n = self.pos, self.pos.columns
        sums = []
        for i, (part, from_b, from_col) in enumerate(self.parts):
            total = part[2 * pos.a + pos.b].astype(F32) + from_b[pos.a].astype(F32)
            for k in range(1, n):
                a = pos.at(k)
                sem = self.recv.at[2 * n * i + n + a]
                arrived(from_col.at[a], sem, pos.column(k))
                total = total + from_col[a].astype(F32)
            sums.append(total)
        return sums

    def finish(self):
        pos, n = self.pos, self.pos.columns
        for a in range(n):
            for copy in self.copies(a, "b"):
                copy.wait_send()
        for k in range(1, n):
            for copy in self.copies(pos.at(k), "column"):
                copy.wait_send()


def sum_ctx_scratch(n, *shapes):
    v = lambda shape: pltpu.VMEM((n,) + tuple(shape), BF)
    out = []
    for shape in shapes:
        out += [v(shape), v(shape)]
    return out + [DMA((2 * n * len(shapes),)), DMA((2 * n * len(shapes),))]


class Sizes:
    def __init__(self, nc, nf, rows, width, experts, hidden, owned, padded, capacity, top, docs):
        self.nc, self.nf, self.rows, self.width = nc, nf, rows, width
        self.experts, self.hidden, self.owned, self.padded = experts, hidden, owned, padded
        self.capacity, self.top, self.docs = capacity, top, docs
        self.columns, self.per = nc // 2, nc // GROUPS
        self.heads = width // HEAD_DIM // GROUPS
        self.share = self.heads * HEAD_DIM
        self.slot = nc * rows
        self.all = nc * nf


def scalars(sz, lengths):
    sizes = [lengths[0, d] for d in range(sz.docs)]
    ends, total = [], 0
    for size in sizes:
        total = total + size
        ends.append(total)
    return sizes, ends


def starts(index, sizes, ends):
    low = jnp.zeros_like(index)
    for size, end in zip(sizes, ends):
        low = low + jnp.where(index >= end, size, 0)
    return low


def iota(shape, dim):
    return lax.broadcasted_iota(jnp.int32, shape, dim)


def mean_square(x, width):
    return jnp.sum(x * x, axis=-1, keepdims=True) * (1.0 / width)


def turn(value, cosine, sine):
    half = HEAD_DIM // 2
    lower, upper = value[:half], value[half:]
    return jnp.concatenate([lower * cosine - upper * sine, upper * cosine + lower * sine], axis=0)


def head(h):
    return slice(h * HEAD_DIM, (h + 1) * HEAD_DIM)


def blk(index, rows):
    return pl.ds(pl.multiple_of(index * rows, rows), rows)


class Copies:
    def __init__(self, sems):
        self.sems, self.made = sems, []

    def start(self, src, dst):
        self.made.append(pltpu.make_async_copy(src, dst, self.sems.at[len(self.made)]))
        self.made[-1].start()

    def finish(self):
        for copy in self.made:
            copy.wait()


def swap_send(sz, group, place, src, out, sends, recv, local, h):
    @pl.when(h == group)
    def _():
        pltpu.make_async_copy(src.at[h], out.at[h], local).start()

    copy = remote(src.at[h], out.at[group], sends.at[h], recv.at[group], {"ctx": h * sz.per + place})

    @pl.when(h != group)
    def _():
        copy.start()


def swap_wait(sz, group, place, src, out, sends, recv, local):
    for h in range(GROUPS):
        copy = remote(src.at[h], out.at[h], sends.at[h], recv.at[h], {"ctx": h * sz.per + place})

        @pl.when(h == group)
        def _():
            pltpu.make_async_copy(src.at[h], out.at[h], local).wait()

        @pl.when(h != group)
        def _():
            copy.wait_send()
            copy.wait_recv()


def scatter_owner(pos, part, outs, stage, from_sib, from_y, sends, recv, local):
    parts = len(outs)
    rows = outs[0][0].shape[0] + outs[0][1].shape[0]
    of = lambda p, y, c: part.at[p, blk(y * 2 + c, rows)]
    for t, y in enumerate((1 - pos.y, pos.y)):
        for p in range(parts):
            sends.start(of(p, y, 1 - pos.c), from_sib.at[t, p], recv.at[t * parts + p], pos.sibling())
        yield
    for t, y in enumerate((1 - pos.y, pos.y)):
        for p in range(parts):
            arrived(from_sib.at[t, p], recv.at[t * parts + p], pos.sibling())
            mine = of(p, y, pos.c)
            mine[...] = (mine[...].astype(F32) + from_sib[t, p].astype(F32)).astype(BF)
            if t == 0:
                sends.start(mine, from_y.at[p], recv.at[2 * parts + p], pos.flip_y())
        yield
    copies = []
    for p in range(parts):
        arrived(from_y.at[p], recv.at[2 * parts + p], pos.flip_y())
        if p > 1:
            for copy in copies[p - 2]:
                copy.wait()
        held = stage.at[pl.ds(p % 2 * rows, rows)]
        held[...] = of(p, pos.y, pos.c)[...].astype(F32) + from_y[p].astype(F32)
        cut = outs[p][0].shape[0]
        parts_of = (held.at[pl.ds(0, cut)], held.at[pl.ds(cut, rows - cut)])
        copies.append([pltpu.make_async_copy(src, dst, local.at[p, t]) for t, (src, dst) in enumerate(zip(parts_of, outs[p]))])
        for copy in copies[p]:
            copy.start()
        yield
    for pair in copies[-2:]:
        for copy in pair:
            copy.wait()
    sends.finish()


def scatter_owner_scratch(parts, shape):
    v = lambda *lead: pltpu.VMEM(lead + tuple(shape), BF)
    return [v(2, parts), v(parts), DMA((3 * parts,)), DMA((3 * parts,)), DMA((parts, 2))]


def step(*streams):
    for stream in streams:
        next(stream, None)


def layer_kernel(
    sz, lengths, tokens, cot, routes, gain_own, router_own, spread, wq_send, wo_own, ffn_send,
    o_out, o_tokens, o_wq, o_wo, o_small, o_in, o_down, o_shared_in, o_shared_down,
    x_all, wq_all, wo_all, wo_send, stage, wt, wo, small, normed, qt, kt, vt, prob, o_send, attn, resid, table,
    g_all, mix_all, cw_all, ffn_w, hw, dg, du, gm_part, gp_part, y_hold, dw,
    do_send, do, dkt, dvt, dqt_b, dkvt_b,
    *sems,
):
    pos, pos_b = Place(sz.columns), Place(sz.columns, balanced=False)
    ctx = lax.axis_index("ctx")
    group, place = ctx // sz.per, ctx % sz.per
    rows, width, share, n = sz.rows, sz.width, sz.share, sz.columns
    sizes, ends = scalars(sz, lengths)
    group_of = lambda a: a // (n // GROUPS)

    owned = sz.owned
    me = ctx * sz.nf + lax.axis_index("fsdp")
    place_of = (iota((owned, width), 1) == me * owned + iota((owned, width), 0)).astype(BF)
    wo_send[:owned, :] = wo_own[...]
    rest = jnp.zeros((sz.padded - owned - 2 - sz.experts, width), F32)
    first = jnp.zeros((1, width), F32)
    wo_send[owned:, :] = jnp.concatenate([first, dot(gain_own[...], place_of, NN), dot(router_own[...], place_of, NN), rest], axis=0).astype(BF)

    greet(all_partners(pos))
    s = [Sends(sems[3 * i]) for i in range(3)]
    r = lambda i: (sems[3 * i + 1], sems[3 * i + 2])
    swap_sems, swap_back = sems[9:12], sems[12:15]
    gm_sum = SumCtx(pos, [(gm_part, sems[27], sems[28]), (gp_part, sems[29], sems[30])], sems[31], sems[32])
    gn_part, wq_part, wo_part, y_part = x_all, wq_all, wo_all, y_hold
    y_sum = SumCtx(pos, [(y_part, sems[33], sems[34])], sems[35], sems[36])
    gn_sum = SumCtx(pos, [(gn_part, sems[37], sems[38])], sems[39], sems[40])
    t_wq, t_wo, t_ffn = sems[41:47], sems[47:53], sems[53:58]
    toks = GatherLine(pos, [(tokens, x_all)], sems[15], sems[16])
    cots = GatherLine(pos, [(None, g_all)], sems[17], sems[18])
    mixes = GatherLine(pos, [(None, mix_all)], sems[19], sems[20])
    weights = GatherLine(pos, [(None, cw_all)], sems[21], sems[22], parts=1)

    wqs = gather_tree(pos_b, wq_send, wq_all, s[0], *r(0), group_of=group_of)
    wos = gather_tree(pos_b, wo_send, wo_all, s[1], *r(1))
    ffn = gather_fsdp(pos, ffn_send, ffn_w, s[2], *r(2))
    next(wqs)
    toks.start()
    next(wos)
    x_all[ctx] = tokens[...]

    own_rows = ctx * rows + iota((rows, 1), 0)
    live = own_rows < ends[-1]
    g_all[ctx] = jnp.where(live, cot[...].astype(F32), 0.0).astype(BF)
    index = iota((1, sz.slot), 1)
    position = index - jnp.where(index < ends[-1], starts(index, sizes, ends), 0)
    half = HEAD_DIM // 2
    inverse = jnp.exp(iota((half, 1), 0).astype(F32) * (-2.0 * math.log(ROPE_BASE) / HEAD_DIM))
    angles = position.astype(F32) * inverse
    table[0] = jnp.cos(angles)
    table[1] = jnp.sin(angles)
    before = (iota((rows, rows), 0) < iota((rows, rows), 1)).astype(BF)
    live_t = (ctx * rows + iota((1, rows), 1)) < ends[-1]
    base = jnp.zeros((8, 1), F32)
    kept = jnp.zeros((8, rows), F32)
    for k in range(sz.top):
        hot = ((iota((8, rows), 0) == routes[k : k + 1, :]) & live_t).astype(F32)
        earlier = base + dot(hot.astype(BF), before, NN)
        kept = kept + jnp.where(earlier < sz.capacity, hot, 0.0)
        base = base + jnp.sum(hot, axis=1, keepdims=True)
    step(wqs, wos)
    toks.relay(1)
    step(wqs, wos)
    toks.relay(2)
    step(wqs, wos)
    next(ffn)
    toks.relay(3)
    cots.start()
    for k in range(n):
        toks.across(k)
    drive([wqs])

    def packed(h_):
        each = sz.per * rows
        return slice(each * h_ * (h_ + 1) // 2, each * (h_ + 1) * (h_ + 2) // 2)

    def spot(i):
        a_b, y_c = divmod(i, sz.nf)
        return y_c % 2, a_b % 2, y_c // 2, a_b // 2

    for i in range(sz.all):
        stage[i * owned : (i + 1) * owned, : 3 * share] = wq_all[spot(i)][:owned, :].astype(F32)
    wt[...] = stage[:, : 3 * share].T.astype(BF)
    for d in range(sz.nc):
        x = x_all[d].astype(F32)
        inv = lax.rsqrt(mean_square(x, width) + EPSILON)
        normed[d] = (x * inv).astype(BF)
        part = slice(d * rows, (d + 1) * rows)
        kv = dot(wt[share:, :], normed[d], NT)
        for h in range(sz.heads):
            kt[head(h), part] = turn(kv[head(h)], table[0, :, part], table[1, :, part]).astype(BF)
        vt[:, part] = kv[share:].astype(BF)

    for h_ in reversed(range(GROUPS)):
        d = h_ * sz.per + place
        part = blk(d, rows)
        qq = dot(wt[:share, :], normed[d], NT)
        keys = (h_ + 1) * sz.per * rows
        index = d * rows + iota((rows, 1), 0)
        low = starts(index, sizes, ends)
        key = iota((rows, keys), 1)
        allowed = (key >= low) & (key <= index)
        for h in range(sz.heads):
            q = turn(qq[head(h)], table[0, :, part], table[1, :, part]).astype(BF) * BF(1.0 / math.sqrt(HEAD_DIM))
            qt[h_, head(h), :] = q
            score = jnp.where(allowed, dot(q, kt[head(h), :keys], TN), MASKED)
            expo = jnp.exp(score - jnp.max(score, axis=1, keepdims=True))
            p = (expo * (1.0 / jnp.sum(expo, axis=1, keepdims=True))).astype(BF)
            prob[h, :, packed(h_)] = p
            o_send[h_, head(h), :] = dot(vt[head(h), :keys], p, NT).astype(BF)
        swap_send(sz, group, place, o_send, attn, *swap_sems, h_)
        if h_ == 3:
            cots.relay(1)
        if h_ == 1:
            cots.relay(2)
    swap_wait(sz, group, place, o_send, attn, *swap_sems)
    cots.relay(3)
    drive([wos])
    for i in range(sz.all):
        stage[i * owned : (i + 1) * owned, :] = wo_all[spot(i)][:owned, :].astype(F32)
    extra = wo_all[spot(0)][owned:, :].astype(F32)
    for i in range(1, sz.all):
        extra = extra + wo_all[spot(i)][owned:, :].astype(F32)
    small[...] = extra[:8]
    gain_m = small[1:2, :]
    wo[...] = stage[...].astype(BF)

    attn_t = attn[...].reshape(width, rows)
    res = tokens[...].astype(F32) + dot(attn_t, wo[...], TN)
    resid[...] = res
    inv = lax.rsqrt(mean_square(res, width) + EPSILON)
    mixed = (res * inv * gain_m).astype(BF)
    mix_all[ctx] = mixed
    row = iota((8, rows), 0)
    logits = dot(small[...].astype(BF), mixed, NT)
    logits = jnp.concatenate([logits[2:], logits[:2]], axis=0)
    logits = jnp.where(row < sz.experts, logits, MASKED)
    expo = jnp.exp(logits - jnp.max(logits, axis=0, keepdims=True))
    router_prob = expo * (1.0 / jnp.sum(expo, axis=0, keepdims=True))
    weight = router_prob * kept
    high = weight.astype(BF).astype(F32)
    high_row = jnp.where(row == sz.experts, 1.0, high)
    cw_all[ctx] = jnp.concatenate([high_row, weight - high], axis=0).astype(BF)

    weights.start()
    mixes.start()
    step(ffn)

    chunk = 2 * rows

    half_units = sz.nf // 2 * ffn_send.shape[1]
    cuts = ((0, 384), (384, half_units - 384))

    def units_at(y, cut):
        return pl.ds(pl.multiple_of(y * half_units + cut[0], 128), cut[1])

    def hidden_units(a, y):
        at_rows = blk(a, chunk)
        x = mix_all[pl.ds(2 * a, 2)].reshape(chunk, width)
        g = g_all[pl.ds(2 * a, 2)].reshape(chunk, width)
        pair = jnp.zeros((16, chunk), F32)
        for cut in cuts:
            at = units_at(y, cut)
            gate = dot(x, ffn_w[0, at, :], NT)
            up = dot(x, ffn_w[1, at, :], NT)
            back = dot(g, ffn_w[2, at, :], NT)
            weight = jnp.concatenate([dot(cw_all[2 * a + i], spread[:16, at], TN) for i in range(2)], axis=0)
            sig = 1.0 / (1.0 + jnp.exp(-gate))
            act = gate * sig
            hid = act * up
            pair = pair + dot(spread[16:, at], (hid * back).astype(BF), NT)
            hw[at_rows, at] = (hid * weight).astype(BF)
            back = back * weight
            dg[at_rows, at] = (back * up * sig * (1.0 + gate * (1.0 - sig))).astype(BF)
            du[at_rows, at] = (back * act).astype(BF)
        return pair

    def input_grad(a):
        at_rows = blk(a, chunk)
        total = dot(dg[at_rows, :], ffn_w[0], NN) + dot(du[at_rows, :], ffn_w[1], NN)
        gm_part[pl.ds(2 * a, 2)] = total.astype(BF).reshape(2, rows, width)
        gm_sum.push(a)

    near = [pos.a, jnp.where(pos.a == 0, 1, jnp.where(pos.a == 1, 0, jnp.where(pos.a == 2, 3, 2)))]
    near += [jnp.where(pos.a < 2, 2, 1), jnp.where(pos.a < 2, 3, 0)]
    for i in range(n):
        if i + 1 < n:
            weights.relay(i + 1)
            mixes.relay(i + 1)
        for stream in (cots, weights, mixes):
            stream.across(near[i])
        pair = hidden_units(near[i], pos.y)
        if i == 0:
            drive([ffn])
        pair = (pair + hidden_units(near[i], 1 - pos.y)).astype(BF)
        for t in range(2):
            gp_part[2 * near[i] + t] = pair[:, t * rows : (t + 1) * rows]
        input_grad(near[i])
        if i > 1:
            gm_sum.pass_on(near[i - 1], other=True)
    xs = mix_all[...].reshape(sz.slot, width)
    gs = g_all[...].reshape(sz.slot, width)

    ffn_back = scatter_owner(pos, dw, ((o_in.at[0], o_shared_in.at[0]), (o_in.at[1], o_shared_in.at[1]), (o_down, o_shared_down)), stage, *t_ffn[:2], Sends(t_ffn[2]), *t_ffn[3:])
    for y in (1 - pos.y, pos.y):
        for cut in cuts:
            at = units_at(y, cut)
            for p, (units, rows_of) in enumerate(((dg, xs), (du, xs), (hw, gs))):
                dw[p, at, :] = dot(units[:, at], rows_of, TN).astype(BF)
        step(ffn_back)
        if y is not pos.y:
            gm_sum.pass_on(near[-1], other=True)
            gm_sum.pass_on(pos.a, other=False)
            for a in (*near[1:], pos.a):
                y_part[pl.ds(2 * a, 2)] = dot(hw[blk(a, chunk), :], ffn_w[2], NN).astype(BF).reshape(2, rows, width)
                y_sum.push(a)
    step(ffn_back)

    gm_own, gp_own = gm_sum.total()
    grad_prob = gp_own[:8, :] * kept
    grad_logits = router_prob * (grad_prob - jnp.sum(router_prob * grad_prob, axis=0, keepdims=True))
    shifted = jnp.concatenate([jnp.zeros((2, rows), F32), grad_logits[:6]], axis=0).astype(BF)
    grad_small = dot(shifted, mix_all[ctx], NN)
    grad_mixed = gm_own + dot(shifted, small[...].astype(BF), TN)
    res = resid[...]
    inv = lax.rsqrt(mean_square(res, width) + EPSILON)
    w = grad_mixed * gain_m
    inner = jnp.sum(w * res, axis=-1, keepdims=True) * (1.0 / width)
    grad_resid = jnp.where(live, cot[...].astype(F32), 0.0) + inv * w - res * inner * inv * inv * inv
    grad_gain_m = jnp.sum(grad_mixed * res * inv, axis=0, keepdims=True)
    grad_resid_b = grad_resid.astype(BF)
    grad_attn_t = dot(wo[...], grad_resid_b, NT).astype(BF)
    for h_ in range(GROUPS):
        do_send[h_] = grad_attn_t[h_ * share : (h_ + 1) * share]
    for h_ in range(GROUPS):
        swap_send(sz, group, place, do_send, do, *swap_back, h_)
    gm_sum.finish()
    for x in (*s, toks):
        x.finish()
    wos = scatter_tree(pos, wo_part, (o_wo, o_small), *t_wo[:4], Sends(t_wo[4]), t_wo[5])
    wqs = scatter_tree(pos, wq_part, o_wq, *t_wq[:4], Sends(t_wq[4]), t_wq[5], per_group=True)
    grad_wo = dot(attn[...].reshape(width, rows), grad_resid_b, NN)
    row = iota((sz.padded - owned, width), 0)
    grad_small = jnp.where(row == 1, grad_gain_m, jnp.concatenate([grad_small] * ((sz.padded - owned) // 8), axis=0)).astype(BF)

    for i in range(sz.all):
        wo_part[spot(i) + (slice(0, owned),)] = grad_wo[i * owned : (i + 1) * owned].astype(BF)
        wo_part[spot(i) + (slice(owned, None),)] = grad_small
    step(wos)
    swap_wait(sz, group, place, do_send, do, *swap_back)
    y_sum.pass_on(near[1], other=True)

    dkt[...] = jnp.zeros_like(dkt)
    dvt[...] = jnp.zeros_like(dvt)
    for h_ in reversed(range(GROUPS)):
        keys = (h_ + 1) * sz.per * rows
        done = slice(h_ * sz.per * rows, keys)
        part = blk(h_ * sz.per + place, rows)
        for h in range(sz.heads):
            d_o = do[h_, head(h), :]
            p = prob[h, :, packed(h_)]
            pf = p.astype(F32)
            grad_p = dot(d_o, vt[head(h), :keys], TN)
            delta = jnp.sum(pf * grad_p, axis=1, keepdims=True)
            grad_s = (pf * (grad_p - delta)).astype(BF)
            dq = dot(kt[head(h), :keys], grad_s, NT) * (1.0 / math.sqrt(HEAD_DIM))
            dqt_b[h_, head(h), :] = turn(dq, table[0, :, part], -table[1, :, part]).astype(BF)
            dkt[head(h), :keys] = dkt[head(h), :keys] + dot(qt[h_, head(h), :], grad_s, NN)
            dvt[head(h), :keys] = dvt[head(h), :keys] + dot(d_o, p, NN)
        for h in range(sz.heads):
            dkvt_b[head(h), done] = turn(dkt[head(h), done], table[0, :, done], -table[1, :, done]).astype(BF)
        dkvt_b[share:, done] = dvt[:, done].astype(BF)
        for t in range(2):
            d = h_ * sz.per + lax.rem(place + 1 + t, 2)
            gn = dot(dkvt_b[:, blk(d, rows)], wt[share:, :], TN)
            if t == 1:
                gn = gn + dot(dqt_b[h_], wt[:share, :], TN)
            gn_part[d] = gn.astype(BF)
        gn_sum.push(h_)
        if h_ < GROUPS - 2:
            gn_sum.pass_on(h_ + 2)
        if 1 < h_:
            y_sum.pass_on(near[GROUPS + 1 - h_], other=True)
        if h_ % 2:
            step(wos)
        if h_ == GROUPS - 1:
            step(ffn_back)
    grad_q = dot(dqt_b[0], normed[place], NN)
    for h_ in range(1, GROUPS):
        grad_q = grad_q + dot(dqt_b[h_], normed[h_ * sz.per + place], NN)
    grad_kv = dot(dkvt_b[...], normed[...].reshape(sz.slot, width), NN)
    grad_w = jnp.concatenate([grad_q, grad_kv], axis=0).T
    wq_part[...] = jnp.zeros_like(wq_part)
    for i in range(sz.all):
        wq_part[spot(i) + (slice(0, owned),)] = grad_w[i * owned : (i + 1) * owned].astype(BF)
    step(wqs)
    gn_sum.pass_on(1)
    step(wqs)
    gn_sum.pass_on(0)
    step(wqs)
    drive([wos])
    step(wqs)
    drive([ffn_back])
    drive([wqs])
    y_sum.pass_on(pos.a, other=False)
    (y_own,) = y_sum.total()
    o_out[...] = jnp.where(live, res + y_own, 0.0).astype(BF)
    x = tokens[...].astype(F32)
    inv = lax.rsqrt(mean_square(x, width) + EPSILON)
    (gn_own,) = gn_sum.total()
    w = gn_own
    inner = jnp.sum(w * x, axis=-1, keepdims=True) * (1.0 / width)
    o_tokens[...] = grad_resid + inv * w - x * inner * inv * inv * inv
    for x in (y_sum, gn_sum, cots, mixes, weights):
        x.finish()


def layer(sz, collective_id, lengths, tokens, cot, routes, gain_own, router_own, spread, wq_send, wo_own, ffn_send):
    n, nc, rows, width, share, slot = sz.columns, sz.nc, sz.rows, sz.width, sz.share, sz.slot
    own_units = ffn_send.shape[1]
    units = sz.nf * own_units
    outs = [
        shaped((rows, width)),
        shaped((rows, width), F32),
        shaped((GROUPS, sz.owned, 3 * share), F32),
        shaped((sz.owned, width), F32),
        shaped((sz.padded - sz.owned, width), F32),
        shaped((2, own_units - sz.hidden, width), F32),
        shaped((own_units - sz.hidden, width), F32),
        shaped((2, sz.hidden, width), F32),
        shaped((sz.hidden, width), F32),
    ]
    v = lambda *shape, dtype=BF: pltpu.VMEM(shape, dtype)
    tree = (2, 2, 2, n, sz.padded)
    blocks = v(nc, rows, width)
    scratch = [
        blocks, v(*tree, 3 * share), v(*tree, width), v(sz.padded, width), v(width, width, dtype=F32),
        v(3 * share, width), v(width, width), v(8, width, dtype=F32), blocks,
        v(GROUPS, share, rows), v(share, slot), v(share, slot), v(sz.heads, rows, slot * (GROUPS + 1) // 2), v(GROUPS, share, rows),
        v(GROUPS, share, rows), v(rows, width, dtype=F32), v(2, HEAD_DIM // 2, slot, dtype=F32),
        blocks, blocks, v(nc, 16, rows), v(3, units, width), v(slot, units), v(slot, units), v(slot, units),
        blocks, v(nc, 16, rows), blocks, v(3, units, width),
        v(GROUPS, share, rows), v(GROUPS, share, rows), v(share, slot, dtype=F32), v(share, slot, dtype=F32),
        v(GROUPS, share, rows), v(2 * share, slot),
    ]
    sems = gather_tree_sems(n) * 2 + gather_fsdp_sems(3)
    sems += [DMA((GROUPS,)), DMA((GROUPS,)), DMA] * 2
    sems += gather_line_sems(n) * 3 + gather_line_sems(n, parts=1) + [DMA] * 4
    sems += sum_ctx_scratch(n, (rows, width), (16, rows)) + sum_ctx_scratch(n, (rows, width)) * 2
    sems += scatter_tree_scratch(n, (sz.padded, 3 * share)) + scatter_tree_scratch(n, (sz.padded, width))
    sems += scatter_owner_scratch(3, (own_units, width))
    hbm, vmem = pl.BlockSpec(memory_space=pl.ANY), pl.BlockSpec(memory_space=pltpu.VMEM)
    return pl.pallas_call(
        functools.partial(layer_kernel, sz),
        out_shape=outs,
        in_specs=[pl.BlockSpec(memory_space=pltpu.SMEM)] + [vmem] * 6 + [hbm, vmem, hbm],
        out_specs=[vmem] * 5 + [hbm] * 4,
        scratch_shapes=scratch + sems,
        compiler_params=pltpu.CompilerParams(collective_id=collective_id, has_side_effects=True, vmem_limit_bytes=63 << 20),
        name="layer",
    )(lengths, tokens, cot, routes, gain_own, router_own, spread, wq_send, wo_own, ffn_send)


def gather_start_kernel(columns, group_of, tokens, wq, wo, ffn, cot, o_tokens, o_wq, o_wo, o_ffn, o_cot, *sems):
    pos = Place(columns)
    greet(all_partners(pos))
    s = [Sends(sems[3 * i]) for i in range(5)]
    r = lambda i: (sems[3 * i + 1], sems[3 * i + 2])
    streams = [
        gather_ctx(pos, tokens, o_tokens, s[0], *r(0)),
        gather_all(pos, wq, o_wq, s[1], *r(1), group_of=group_of),
        gather_all(pos, wo, o_wo, s[2], *r(2)),
        gather_fsdp(pos, ffn, o_ffn, s[3], *r(3)),
    ]
    drive(streams)
    drive([gather_ctx(pos, cot, o_cot, s[4], *r(4))])
    for x in s:
        x.finish()


def call(kernel, collective_id, ins, outs, scratch, name, space=pl.ANY, in_space=None):
    return pl.pallas_call(
        kernel,
        out_shape=outs,
        in_specs=[pl.BlockSpec(memory_space=in_space or space)] * len(ins),
        out_specs=jax.tree.map(lambda _: pl.BlockSpec(memory_space=space), outs),
        scratch_shapes=scratch,
        compiler_params=pltpu.CompilerParams(
            collective_id=collective_id, has_side_effects=True, vmem_limit_bytes=60 << 20
        ),
        name=name,
    )(*ins)


def gather_start(nc, tokens, wq, wo, ffn, cot):
    n = nc // 2
    group_of = lambda a: a // (n // GROUPS)
    sems = gather_ctx_sems(n) + gather_all_sems(n) * 2 + gather_fsdp_sems(ffn.shape[0]) + gather_ctx_sems(n)
    outs = (
        shaped((nc,) + tokens.shape),
        shaped((nc * 4,) + wq.shape[1:]),
        shaped((nc * 4,) + wo.shape),
        shaped((ffn.shape[0], 4) + ffn.shape[1:]),
        shaped((nc,) + cot.shape),
    )
    return call(functools.partial(gather_start_kernel, n, group_of), 1, (tokens, wq, wo, ffn, cot), outs, sems, "gather_start")


def gather_ctx_kernel(columns, src, out, send, recv, local):
    pos = Place(columns)
    greet([pos.column(k) for k in range(1, columns)] + [pos.flip_b()])
    s = Sends(send)
    drive([gather_ctx(pos, src, out, s, recv, local)])
    s.finish()


def gather_rows(nc, src, collective_id):
    n = nc // 2
    return call(functools.partial(gather_ctx_kernel, n), collective_id, (src,), shaped((nc,) + src.shape), gather_ctx_sems(n), "gather_rows")


def swap_kernel(nc, src, out, send, recv, local):
    per = nc // GROUPS
    ctx = lax.axis_index("ctx")
    group, place = ctx // per, ctx % per
    peer = lambda k: lax.rem(group + k, GROUPS)
    device = lambda k: {"ctx": peer(k) * per + place}
    greet([device(k) for k in range(1, GROUPS)])
    own = pltpu.make_async_copy(src.at[group], out.at[group], local)
    own.start()
    copies = []
    for k in range(1, GROUPS):
        copies.append(remote(src.at[peer(k)], out.at[group], send.at[k], recv.at[k], device(k)))
        copies[-1].start()
    for k in range(1, GROUPS):
        arrived(out.at[peer(GROUPS - k)], recv.at[k], device(k))
    own.wait()
    for copy in copies:
        copy.wait_send()


def swap(nc, src, collective_id):
    return call(functools.partial(swap_kernel, nc), collective_id, (src,), shaped(src.shape), [DMA((GROUPS,)), DMA((GROUPS,)), DMA], "swap")


def scatter_ctx_kernel(columns, part, out, acc, from_b, from_col, send, recv, local):
    pos = Place(columns)
    greet([pos.column(k) for k in range(1, columns)] + [pos.flip_b()])
    s = Sends(send)
    drive([scatter_ctx(pos, part, out, acc, from_b, from_col, s, recv, local)])
    s.finish()


def scatter_rows(nc, part, collective_id):
    n = nc // 2
    return pl.pallas_call(
        functools.partial(scatter_ctx_kernel, n),
        out_shape=shaped(part.shape[1:], F32),
        in_specs=[pl.BlockSpec(memory_space=pl.ANY)],
        out_specs=pl.BlockSpec(memory_space=pltpu.VMEM),
        scratch_shapes=scatter_ctx_scratch(n, part.shape[1:]),
        compiler_params=pltpu.CompilerParams(collective_id=collective_id, has_side_effects=True, vmem_limit_bytes=60 << 20),
        name="scatter_rows",
    )(part)


def scatter_end_kernel(columns, gn, wq, wo, ffn, yy, o_gn, o_wq, o_wo, o_ffn, o_yy, *scratch):
    pos = Place(columns)
    greet(all_partners(pos))
    c1, a1, a2, f1, c2 = scratch[0:6], scratch[6:14], scratch[14:22], scratch[22:28], scratch[28:34]
    s = [Sends(x[-3]) for x in (c1, a1, a2, f1, c2)]
    drive(
        [
            scatter_ctx(pos, gn, o_gn, *c1[:-3], s[0], *c1[-2:]),
            scatter_fsdp(pos, [ffn.at[p] for p in range(ffn.shape[0])], o_ffn, *f1[:-3], s[3], *f1[-2:]),
            scatter_all(pos, wq, o_wq, *a1[:-3], s[1], *a1[-2:], per_group=True),
            scatter_all(pos, wo, o_wo, *a2[:-3], s[2], *a2[-2:]),
            scatter_ctx(pos, yy, o_yy, *c2[:-3], s[4], *c2[-2:]),
        ]
    )
    for x in s:
        x.finish()


def scatter_end(nc, gn, wq, wo, ffn, yy):
    n = nc // 2
    scratch = (
        scatter_ctx_scratch(n, gn.shape[1:])
        + scatter_all_scratch(n, wq.shape[1:])
        + scatter_all_scratch(n, wo.shape[1:])
        + scatter_fsdp_scratch(ffn.shape[0], ffn.shape[2:])
        + scatter_ctx_scratch(n, yy.shape[1:])
    )
    outs = (
        shaped(gn.shape[1:], F32),
        shaped((GROUPS,) + wq.shape[1:], F32),
        shaped(wo.shape[1:], F32),
        shaped((ffn.shape[0],) + ffn.shape[2:], F32),
        shaped(yy.shape[1:], F32),
    )
    return call(
        functools.partial(scatter_end_kernel, n), 6, (gn, wq, wo, ffn, yy), outs, scratch, "scatter_end",
        space=pltpu.VMEM, in_space=pl.ANY,
    )


def doc_ids(row_index, doc_ends):
    return jnp.sum((row_index[:, None] >= doc_ends[None, :]).astype(jnp.int32), axis=1)


def positions(row_index, lengths):
    doc_ends = jnp.cumsum(lengths)
    doc_starts = doc_ends - lengths
    doc_num = doc_ids(row_index, doc_ends)
    column = jnp.arange(lengths.shape[0], dtype=jnp.int32)
    begins = jnp.sum(jnp.where(doc_num[:, None] == column[None, :], doc_starts[None, :], 0), axis=1)
    return doc_num, row_index - begins


def rope_tables(position):
    half_dim = HEAD_DIM // 2
    inverse = ROPE_BASE ** (-2.0 * jnp.arange(half_dim, dtype=F32) / HEAD_DIM)
    angles = position.astype(F32)[:, None] * inverse[None, :]
    return jnp.cos(angles), jnp.sin(angles)


def rotate(values, cosine, sine):
    half_dim = values.shape[-1] // 2
    lower, upper = values[..., :half_dim], values[..., half_dim:]
    cosine, sine = cosine[:, None, :], sine[:, None, :]
    return jnp.concatenate([lower * cosine - upper * sine, upper * cosine + lower * sine], axis=-1)


def kept_rows(route_rows, live_rows, experts, capacity):
    count, top = route_rows.shape
    hot = (route_rows[:, :, None] == jnp.arange(experts, dtype=jnp.int32)) & live_rows[:, None, None]
    hot = hot.astype(F32)
    before = jnp.tril(jnp.ones((count, count), F32), -1)
    kept = jnp.zeros((count, experts), F32)
    base = jnp.zeros((1, experts), F32)
    for k in range(top):
        earlier = base + jnp.dot(before, hot[:, k])
        kept = kept + hot[:, k] * (earlier < capacity)
        base = base + jnp.sum(hot[:, k], axis=0, keepdims=True)
    return kept


def pad_rows(x, rows):
    return jnp.pad(x, [(0, rows - x.shape[0])] + [(0, 0)] * (x.ndim - 1))


def body_wide(tokens, doc_lengths, routes, cotangent, attn_gain, w_qkv, w_out, mlp_gain, router, expert_in, expert_out, shared_in, shared_out):
    nc = lax.axis_size("ctx")
    nf = lax.axis_size("fsdp")
    rows, width = tokens.shape[1:]
    heads = width // HEAD_DIM
    experts = expert_in.shape[1]
    hidden = expert_in.shape[0]
    top = routes.shape[2]
    capacity = 5 * top * rows // (4 * experts)
    per = nc // GROUPS
    ctx = lax.axis_index("ctx")
    group, place = ctx // per, ctx % per
    slot = nc * rows
    mine = heads // GROUPS
    share = mine * HEAD_DIM
    scale = 1.0 / math.sqrt(HEAD_DIM)
    owned = w_out.shape[0]
    padded = -(-(owned + 2 + experts) // 16) * 16

    wq_send = w_qkv.reshape(owned, 3, GROUPS, share).transpose(2, 0, 1, 3).reshape(GROUPS, owned, 3 * share)
    wq_send = jnp.pad(wq_send, ((0, 0), (0, padded - owned), (0, 0)))
    small = jnp.concatenate([attn_gain[None], mlp_gain[None], router.T], axis=0)
    wo_send = pad_rows(jnp.concatenate([w_out, jnp.pad(small, ((0, 0), (0, width - owned)))], axis=0), padded)
    gate_up = jnp.concatenate([expert_in.transpose(2, 1, 0, 3), shared_in.transpose(1, 0, 2)[:, None]], axis=1)
    down = jnp.concatenate([expert_out.transpose(1, 0, 2), shared_out[None]], axis=0)
    ffn_send = jnp.concatenate([gate_up, down[None]], axis=0).reshape(3, (experts + 1) * hidden, width)

    x_all, wq_all, wo_all, ffn_all, cot_all = gather_start(nc, tokens[0], wq_send, wo_send, ffn_send, cotangent[0])
    units = nf * (experts + 1) * hidden
    w_gate, w_up, w_down = (ffn_all[p].reshape(units, width) for p in range(3))
    wq = wq_all[:, :owned].reshape(width, 3 * share)
    wo = wo_all[:, :owned].reshape(width, width)
    small = wo_all[:, owned : owned + 2 + experts, :owned].transpose(1, 0, 2).reshape(2 + experts, width)
    gain_a, gain_m = small[0].astype(F32), small[1].astype(F32)
    router_t = small[2:]

    all_rows = jnp.arange(slot, dtype=jnp.int32)
    doc_num, position = positions(all_rows, doc_lengths[0])
    cosine, sine = rope_tables(position)
    live_all = (doc_num < doc_lengths.shape[1]).astype(F32)[:, None]
    x_slot = x_all.reshape(slot, width).astype(F32)
    inv_attn = lax.rsqrt(jnp.mean(x_slot * x_slot, axis=-1, keepdims=True) + EPSILON)
    normed = (x_slot * inv_attn * gain_a).astype(BF)

    def queries(v):
        return lax.dynamic_index_in_dim(v.reshape((GROUPS, per, rows) + v.shape[1:]), place, 1, False).reshape((GROUPS * rows,) + v.shape[1:])

    normed_q = queries(normed)
    cos_q, sin_q = queries(cosine), queries(sine)
    q = rotate(dot(normed_q, wq[:, :share], ((1,), (0,))).reshape(-1, mine, HEAD_DIM), cos_q, sin_q).astype(BF)
    k = rotate(dot(normed, wq[:, share : 2 * share], ((1,), (0,))).reshape(slot, mine, HEAD_DIM), cosine, sine).astype(BF)
    v = dot(normed, wq[:, 2 * share :], ((1,), (0,))).reshape(slot, mine, HEAD_DIM).astype(BF)
    rows_q, doc_q = queries(all_rows), queries(doc_num)
    allowed = (doc_q[:, None] == doc_num[None, :]) & (all_rows[None, :] <= rows_q[:, None])
    scores = jnp.einsum("qhd,khd->hqk", q, k, preferred_element_type=F32) * scale
    scores = jnp.where(allowed[None], scores, MASKED)
    expo = jnp.exp(scores - jnp.max(scores, axis=-1, keepdims=True))
    prob = expo / jnp.sum(expo, axis=-1, keepdims=True)
    prob_b = prob.astype(BF)
    o = jnp.einsum("hqk,khd->qhd", prob_b, v, preferred_element_type=F32).astype(BF)

    o_own = swap(nc, o.reshape(GROUPS, rows, share), 2)
    attn = o_own.transpose(1, 0, 2).reshape(rows, width)

    row_index = ctx * rows + jnp.arange(rows, dtype=jnp.int32)
    doc_own, _ = positions(row_index, doc_lengths[0])
    live_rows = doc_own < doc_lengths.shape[1]
    live = live_rows.astype(F32)[:, None]
    x = tokens[0].astype(F32)
    resid = x + dot(attn, wo, ((1,), (0,)))
    inv_mlp = lax.rsqrt(jnp.mean(resid * resid, axis=-1, keepdims=True) + EPSILON)
    mixed = (resid * inv_mlp * gain_m).astype(BF)
    logits = dot(mixed, router_t, ((1,), (1,)))
    router_prob = jax.nn.softmax(logits, axis=-1)
    kept = kept_rows(routes[0], live_rows, experts, capacity)
    weight = router_prob * kept
    high = weight.astype(BF)
    low = (weight - high.astype(F32)).astype(BF)
    extra = pad_rows(jnp.pad(jnp.concatenate([high, low], axis=1).T, ((0, 0), (0, width - rows))), 16)
    mixed_all = gather_rows(nc, jnp.concatenate([mixed, extra], axis=0), 3)

    weights = mixed_all[:, rows : rows + 2 * experts, :rows].astype(F32)
    weights = (weights[:, :experts] + weights[:, experts:]).transpose(0, 2, 1).reshape(slot, experts)
    mix = mixed_all[:, :rows].reshape(slot, width)
    g = (cot_all.reshape(slot, width) * live_all.astype(BF)).astype(BF)
    unit_weight = jnp.concatenate([weights, jnp.ones((slot, 1), F32)], axis=1)
    unit_weight = jnp.tile(jnp.repeat(unit_weight, hidden, axis=1), (1, nf))
    gate = dot(mix, w_gate, ((1,), (1,)))
    up = dot(mix, w_up, ((1,), (1,)))
    sig = jax.nn.sigmoid(gate)
    hid = gate * sig * up
    hid_w = (hid * unit_weight).astype(BF)
    y_part = dot(hid_w, w_down, ((1,), (0,))).astype(BF)
    back = dot(g, w_down, ((1,), (1,)))
    pair = (hid * back).reshape(slot, nf, experts + 1, hidden).sum(axis=(1, 3))[:, :experts]
    back_w = back * unit_weight
    d_gate = (back_w * up * sig * (1.0 + gate * (1.0 - sig))).astype(BF)
    d_up = (back_w * gate * sig).astype(BF)
    gm_part = (dot(d_gate, w_gate, ((1,), (0,))) + dot(d_up, w_up, ((1,), (0,)))).astype(BF)
    d_w = jnp.stack([dot(d_gate, mix, ((0,), (0,))), dot(d_up, mix, ((0,), (0,))), dot(hid_w, g, ((0,), (0,)))]).astype(BF)
    pair_t = pair.reshape(nc, rows, experts).transpose(0, 2, 1)
    pair_t = jnp.pad(pair_t, ((0, 0), (0, 16 - experts), (0, width - rows))).astype(BF)
    gm_all = scatter_rows(nc, jnp.concatenate([gm_part.reshape(nc, rows, width), pair_t], axis=1), 4)

    grad_prob = gm_all[rows : rows + experts, :rows].T * kept
    grad_logits = (router_prob * (grad_prob - jnp.sum(router_prob * grad_prob, axis=-1, keepdims=True))).astype(BF)
    grad_router_t = dot(grad_logits, mixed, ((0,), (0,)))
    grad_mixed = gm_all[:rows] + dot(grad_logits, router_t, ((1,), (0,)))
    grad_top = cotangent[0].astype(F32) * live
    w = grad_mixed * gain_m
    grad_resid = grad_top + inv_mlp * w - resid * jnp.mean(w * resid, axis=-1, keepdims=True) * inv_mlp**3
    grad_gain_m = jnp.sum(grad_mixed * resid * inv_mlp, axis=0)
    grad_resid_b = grad_resid.astype(BF)
    grad_wo = dot(attn, grad_resid_b, ((0,), (0,)))
    grad_attn = dot(grad_resid_b, wo, ((1,), (1,))).astype(BF)
    do = swap(nc, grad_attn.reshape(rows, GROUPS, share).transpose(1, 0, 2), 5).reshape(GROUPS * rows, mine, HEAD_DIM)

    grad_p = jnp.einsum("qhd,khd->hqk", do, v, preferred_element_type=F32)
    delta = jnp.sum(prob * grad_p, axis=-1, keepdims=True)
    grad_s = (prob * (grad_p - delta)).astype(BF)
    dq = jnp.einsum("hqk,khd->qhd", grad_s, k, preferred_element_type=F32) * scale
    dk = jnp.einsum("hqk,qhd->khd", grad_s, q, preferred_element_type=F32) * scale
    dv = jnp.einsum("hqk,qhd->khd", prob_b, do, preferred_element_type=F32)
    dq = rotate(dq, cos_q, -sin_q).reshape(GROUPS * rows, share).astype(BF)
    dk = rotate(dk, cosine, -sine).reshape(slot, share)
    dkv = jnp.concatenate([dk, dv.reshape(slot, share)], axis=1).astype(BF)
    grad_wq = jnp.concatenate([dot(normed_q, dq, ((0,), (0,))), dot(normed, dkv, ((0,), (0,)))], axis=1)
    gn_q = dot(dq, wq[:, :share], ((1,), (1,))).reshape(GROUPS, 1, rows, width)
    here = (jnp.arange(per) == place).astype(F32)[None, :, None, None]
    gn = dot(dkv, wq[:, share:], ((1,), (1,))).reshape(GROUPS, per, rows, width) + gn_q * here
    gn_part = gn.reshape(nc, rows, width).astype(BF)

    gn_full = gn.reshape(slot, width)
    grad_gain_a = jnp.sum(gn_full * x_slot * inv_attn, axis=0)
    small = jnp.concatenate([grad_gain_a[None], grad_gain_m[None], grad_router_t], axis=0)
    small = small.reshape(2 + experts, nc * nf, owned).transpose(1, 0, 2)
    wo_part = jnp.concatenate([grad_wo.reshape(nc * nf, owned, width), jnp.pad(small, ((0, 0), (0, 0), (0, width - owned)))], axis=1)
    wo_part = jnp.pad(wo_part, ((0, 0), (0, padded - wo_part.shape[1]), (0, 0))).astype(BF)
    wq_part = jnp.pad(grad_wq.reshape(nc * nf, owned, 3 * share), ((0, 0), (0, padded - owned), (0, 0))).astype(BF)
    ffn_part = d_w.reshape(3, nf, (experts + 1) * hidden, width)
    gn_own, wq_own, wo_own, ffn_own, y_own = scatter_end(nc, gn_part, wq_part, wo_part, ffn_part, y_part.reshape(nc, rows, width))

    layer_out = (live * (resid + y_own)).astype(BF)[None]
    inv = lax.rsqrt(jnp.mean(x * x, axis=-1, keepdims=True) + EPSILON)
    w = gn_own * gain_a
    grad_tokens = (grad_resid + inv * w - x * jnp.mean(w * x, axis=-1, keepdims=True) * inv**3)[None]
    grad_w_qkv = wq_own[:, :owned].reshape(GROUPS, owned, 3, share).transpose(1, 2, 0, 3).reshape(owned, 3 * width)
    small = wo_own[owned : owned + 2 + experts, :owned]
    out = ffn_own.reshape(3, experts + 1, hidden, width)
    return (
        layer_out,
        grad_tokens,
        small[0],
        grad_w_qkv,
        wo_own[:owned],
        small[1],
        small[2:].T,
        out[:2, :experts].transpose(2, 1, 0, 3),
        out[2, :experts].transpose(1, 0, 2),
        out[:2, experts].transpose(1, 0, 2),
        out[2, experts],
    )


def body(tokens, doc_lengths, routes, cotangent, attn_gain, w_qkv, w_out, mlp_gain, router, expert_in, expert_out, shared_in, shared_out):
    nc, nf = lax.axis_size("ctx"), lax.axis_size("fsdp")
    rows, width = tokens.shape[1:]
    experts, hidden, top = expert_in.shape[1], expert_in.shape[0], routes.shape[2]
    owned = w_out.shape[0]
    if nc != 2 * GROUPS or 2 * nc * rows * width > FUSED_BYTES:
        return body_wide(
            tokens, doc_lengths, routes, cotangent, attn_gain, w_qkv, w_out, mlp_gain, router, expert_in, expert_out, shared_in, shared_out
        )
    padded = -(-(owned + 8) // 16) * 16
    sz = Sizes(nc, nf, rows, width, experts, hidden, owned, padded, 5 * top * rows // (4 * experts), top, doc_lengths.shape[1])
    share = sz.share
    device = lax.axis_index("ctx") * nf + lax.axis_index("fsdp")

    gain = attn_gain.astype(F32)[:, None]
    wq_send = (w_qkv.astype(F32) * gain).astype(BF).reshape(owned, 3, GROUPS, share).transpose(2, 0, 1, 3).reshape(GROUPS, owned, 3 * share)
    wq_send = jnp.pad(wq_send, ((0, 0), (0, padded - owned), (0, 0)))
    gate_up = jnp.concatenate([expert_in.transpose(2, 1, 0, 3), shared_in.transpose(1, 0, 2)[:, None]], axis=1)
    down = jnp.concatenate([expert_out.transpose(1, 0, 2), shared_out[None]], axis=0)
    ffn_send = jnp.concatenate([gate_up, down[None]], axis=0).reshape(3, (experts + 1) * hidden, width)

    units = nf * (experts + 1) * hidden
    of = np.arange(units) // hidden % (experts + 1)
    spread = np.zeros((32, units), np.float32)
    for e in range(experts + 1):
        spread[e] = of == e
    for e in range(experts):
        spread[8 + e] = of == e
        spread[16 + e] = of == e

    layer_out, grad_tokens, wq_own, grad_w_out, small, grad_in, grad_down, shared_in_own, shared_out_own = layer(
        sz, 1, doc_lengths, tokens[0], cotangent[0], routes[0].T, mlp_gain[None], router.T, jnp.asarray(spread, BF), wq_send, w_out, ffn_send
    )

    grad_w = wq_own.reshape(GROUPS, owned, 3, share).transpose(1, 2, 0, 3).reshape(owned, 3 * width)
    gain_a = jnp.sum(grad_w * w_qkv.astype(F32), axis=1)
    grad_w_qkv = grad_w * gain
    small = lax.dynamic_slice(small, (0, device * owned), (2 + experts, owned))
    grad_in = grad_in.reshape(2, experts, hidden, width)
    grad_down = grad_down.reshape(experts, hidden, width)
    return (
        layer_out[None],
        grad_tokens[None],
        gain_a,
        grad_w_qkv,
        grad_w_out,
        small[1],
        small[2:].T,
        grad_in.transpose(2, 1, 0, 3),
        grad_down.transpose(1, 0, 2),
        shared_in_own.transpose(1, 0, 2),
        shared_out_own,
    )


def solution(mesh):
    rows = P("fsdp", "ctx", None)
    flat = ("ctx", "fsdp")
    weights = (P(flat), P(flat, None), P(flat, None), P(flat), P(flat, None))
    ffn = (P(flat, None, None, None), P(flat, None, None), P(flat, None, None), P(flat, None))
    return jax.shard_map(
        body,
        mesh=mesh,
        in_specs=(rows, P("fsdp", None), rows, rows) + weights + ffn,
        out_specs=(rows, rows) + weights + ffn,
        check_vma=False,
    )
```
